32 devices in a mesh: gx: 4 (over z), gy: 4 (over x, core), gz: 2 (over y).
Axes of the slice: x: 2, y: 2, z: 4, core: 2. Of those that a mesh axis runs over, the one named last changes fastest.
Arguments:
- pops: float32 [19, 16, 32, 512], P(None, 'gz', 'gy', 'gx'), may hold values from 0.4 to 1.6
- coarse_pops: bfloat16 [19, 16, 32, 512], P(None, 'gz', 'gy', 'gx'), may hold values from 0.3984375 to 1.59375
- interface: int32 [16, 32, 512], P('gz', 'gy', 'gx'), may hold values 0 or 1
- drop_vel: float32 [3, 512, 128], P(None, ('gx', 'gy', 'gz')), may hold values from -1 to 1
- drop_frac: float32 [3, 512, 128], P(None, ('gx', 'gy', 'gz')), may hold values from 0 to 1
- home: int32 [512, 128], P(('gx', 'gy', 'gz')), may hold values from 0 to 8191, as said below
- counts: int32 [512], P(('gx', 'gy', 'gz')), may hold values from 1 to 128, 49152 in all
- dest: int32 [512], P(('gx', 'gy', 'gz')), may hold values from 0 to 26, as said below
Outputs:
- pops_out: float32 [19, 16, 32, 512], P(None, 'gz', 'gy', 'gx')
- force: float32 [3, 16, 32, 512], P(None, 'gz', 'gy', 'gx')
- arrived: float32 [6, 2176, 128], P(None, ('gx', 'gy', 'gz'))
The draws below stay inside these ranges and needn't reach their ends.
Inputs may be any that keep to these rules, and one draw needn't show every extreme that they name: All droplets of a block lie in one tile of 8 x 8 x 8 cells at tile-aligned offsets; home = (8 * z + y) * 128 + x in the device's brick. `counts`: live droplets fill the first slots of their block. `dest`: no block crosses a wall along z; apart from code 13, at most 2 blocks of one device share a code, and every device has exactly 2 blocks of some code other than 13.
All inputs are finite; a program needn't handle non-finite values. No bound on the sum of `interface` on one device may be relied on, other than what follows from the above.
Results may differ from the reference program's by a relative error of at most 0.0003.
Values sent between devices are 32-bit elements; how exact they have to be, the bound alone decides.
No kernel may reach another device: no remote copies, remote signals or barrier semaphores. Data moves between devices by JAX's collectives and lax.ppermute only.
A program may use at most 64 MiB of HBM per device.

```python
import math
import jax
import jax.numpy as jnp
import numpy as np
from jax import lax

CX = 128
CY = 8
CZ = 8
NBD = 16
TILE = 8
CAP = 2
NX = 512
NY = 32
NZ = 16
NBT = 512
SLOTS = 68
N_GX = 4
N_GY = 4
N_GZ = 2
DEVICES = 32


def draw_home(key, part):
    tiles_x = CX // TILE
    tiles_y = CY // TILE
    tiles_z = CZ // TILE
    key_tile, key_x, key_y, key_z = jax.random.split(key, 4)
    tile = jax.random.randint(key_tile, (NBT, 1), 0, tiles_x * tiles_y * tiles_z)
    tile_x = tile % tiles_x
    tile_y = tile // tiles_x % tiles_y
    tile_z = tile // (tiles_x * tiles_y)
    cell_x = tile_x * TILE + jax.random.randint(key_x, (NBT, 128), 0, TILE)
    cell_y = tile_y * TILE + jax.random.randint(key_y, (NBT, 128), 0, TILE)
    cell_z = tile_z * TILE + jax.random.randint(key_z, (NBT, 128), 0, TILE)
    return ((cell_z * CY + cell_y) * CX + cell_x).astype(jnp.int32)


def draw_dest(key, part):
    plane_codes = jnp.array([9, 10, 11, 12, 14, 15, 16, 17], dtype=jnp.int32)
    travel = jnp.concatenate([jnp.arange(13, dtype=jnp.int32), jnp.arange(14, 27, dtype=jnp.int32)])
    pool = jnp.concatenate([jnp.repeat(travel, CAP), jnp.full((NBD,), 13, dtype=jnp.int32)])

    def one_device(index):
        device_key = jax.random.fold_in(jax.random.fold_in(key, 7321), index)
        key_pick, key_pool, key_order = jax.random.split(device_key, 3)
        level = index % N_GZ
        chosen = plane_codes[jax.random.randint(key_pick, (), 0, 8)]
        options = jnp.where(pool == chosen, 13, pool)
        picked = options[jax.random.permutation(key_pool, options.shape[0])[:NBD - CAP]]
        codes = jnp.concatenate([jnp.full((CAP,), chosen, dtype=jnp.int32), picked])
        codes = codes[jax.random.permutation(key_order, NBD)]
        travel_z = codes // 9 - 1
        blocked = (level == 0) & (travel_z == -1) | (level == N_GZ - 1) & (travel_z == 1)
        return jnp.where(blocked, 13, codes).astype(jnp.int32)
    return jax.vmap(one_device)(jnp.arange(DEVICES, dtype=jnp.int32)).reshape(NBT)


def with_ends(result, rng, smallest, high):
    longest = result.shape.index(max(result.shape))
    spots = []
    for shift in (0, 1):
        where = [jax.random.randint(jax.random.fold_in(rng, axis), (), 0, length) for axis, length in enumerate(result.shape)]
        where[longest] = (where[longest] + shift) % result.shape[longest]
        spots.append(tuple(where))
    return result.at[spots[0]].set(smallest).at[spots[1]].set(high)


def block_scale(own_key, dims, shards, smallest, largest):
    def one(axis_at, parts):
        steps = jax.random.uniform(jax.random.fold_in(jax.random.fold_in(own_key, 6), axis_at), (parts,), jnp.float32, smallest / len(shards), largest / len(shards))
        return jnp.repeat(jnp.exp(steps), dims[axis_at] // parts).reshape((-1,) + (1,) * (len(dims) - axis_at - 1))

    level = one(*shards[0])
    for cut in shards[1:]:
        level = level * one(*cut)
    return level


def profile(count, total, bound, skew):
    portions = [(1 << 20) // math.isqrt(grade ** skew) + 1 for grade in range(2, count + 1)]
    surplus, holding = total - bound - (count - 1), [1] * (count - 1)
    while surplus > 0:
        free = [i for i in range(count - 1) if holding[i] < bound]
        whole, remaining = sum([portions[i] for i in free]), surplus
        for i in free:
            addition = min(bound - holding[i], max(1, remaining * portions[i] // whole), surplus)
            holding[i] = holding[i] + addition
            surplus = surplus - addition
    return np.array([bound] + holding)


def ragged(key, number_of, total, bound, slope):
    if number_of == 2:
        one = jax.random.randint(key, (), max(1, total - bound), min(bound, total - 1) + 1)
        return jnp.stack([one, total - one])
    lengths = jnp.asarray(profile(number_of, total, bound, slope), jnp.int32)
    couples = (number_of - 1) // 2
    giver, taker = lengths[1:1 + 2 * couples:2], lengths[2:2 + 2 * couples:2]
    margin = jnp.minimum(giver - 1, bound - taker)
    moved = jax.random.randint(jax.random.fold_in(key, 1), (couples,), 0, 1 << 20) % (margin + 1)
    lengths = lengths.at[1:1 + 2 * couples:2].set(giver - moved).at[2:2 + 2 * couples:2].set(taker + moved)
    return lengths[jax.random.permutation(jax.random.fold_in(key, 2), number_of)]


def scatter_about(key, dims, width, reach, cuts=(), kind=jnp.bfloat16):
    loudness = block_scale(key, dims, cuts, -0.22, 0.18) if cuts else 1.0
    values = jax.random.normal(key, dims, jnp.float32) * width * loudness
    return jnp.minimum(jnp.maximum(values, -reach), reach).astype(kind)


def setup_inputs(seed: int = 0) -> dict:
    key_of = jax.random.split(jax.random.key(seed), 9)
    pops = jnp.clip(0.4 + 1.2 * jax.random.uniform(key_of[0], (19, NZ, NY, NX), jnp.float32) ** block_scale(key_of[0], (19, NZ, NY, NX), ((1, 2), (2, 4), (3, 4)), -0.2, 0.2), 0.4, 1.6)
    coarse_pops = jnp.clip(0.3984375 + 1.1953125 * jax.random.uniform(key_of[1], (19, NZ, NY, NX), jnp.float32) ** block_scale(key_of[1], (19, NZ, NY, NX), ((1, 2), (2, 4), (3, 4)), -0.2, 0.2), 0.3984375, 1.59375).astype(jnp.bfloat16)
    interface = with_ends((jax.random.randint(key_of[2], (NZ, NY, NX), 0, 4) < 1).astype(jnp.int32), jax.random.fold_in(key_of[2], 1), 0, 1)
    drop_vel = scatter_about(key_of[3], (3, NBT, 128), 0.2, 1.0, ((1, 32),), jnp.float32)
    drop_frac = jnp.clip(1.0 * jax.random.uniform(key_of[4], (3, NBT, 128), jnp.float32) ** block_scale(key_of[4], (3, NBT, 128), ((1, 32),), -0.2, 0.2), 0.0, 1.0)
    home = draw_home(jax.random.fold_in(key_of[8], 71), 0)
    counts = ragged(key_of[6], NBT, NBT * 96, 128, 1).astype(jnp.int32)
    dest = draw_dest(jax.random.fold_in(key_of[8], 71), 0)
    return {"pops": pops, "coarse_pops": coarse_pops, "interface": interface, "drop_vel": drop_vel, "drop_frac": drop_frac, "home": home, "counts": counts, "dest": dest}


lattice = np.array([[0, 0, 0], [1, 0, 0], [-1, 0, 0], [0, 1, 0], [0, -1, 0], [0, 0, 1], [0, 0, -1],
                    [1, 1, 0], [-1, -1, 0], [1, -1, 0], [-1, 1, 0], [1, 0, 1], [-1, 0, -1], [1, 0, -1],
                    [-1, 0, 1], [0, 1, 1], [0, -1, -1], [0, 1, -1], [0, -1, 1]])
weights_table = np.array([1.0 / 3.0] + [1.0 / 18.0] * 6 + [1.0 / 36.0] * 12)
opposite = [0, 2, 1, 4, 3, 6, 5, 8, 7, 10, 9, 12, 11, 14, 13, 16, 15, 18, 17]
inverse_tau = 0.8
relax = 0.5
couple = 8.0


def kernel(distance):
    return 0.25 * (1.0 + jnp.cos(math.pi * 0.5 * distance))


def macroscopic(pops):
    density = pops[0] * float(weights_table[0])
    moment = [jnp.zeros_like(density), jnp.zeros_like(density), jnp.zeros_like(density)]
    for index in range(1, 19):
        term = pops[index] * float(weights_table[index])
        density = density + term
        for axis in range(3):
            if int(lattice[index][axis]) != 0:
                moment[axis] = moment[axis] + float(lattice[index][axis]) * term
    return density, [moment[axis] / density for axis in range(3)]


def collide(pops, coarse, interface):
    density, flow = macroscopic(pops)
    square = flow[0] * flow[0] + flow[1] * flow[1] + flow[2] * flow[2]
    inside = interface == 1
    posts = []
    for index in range(19):
        along = jnp.zeros_like(density)
        for axis in range(3):
            if int(lattice[index][axis]) != 0:
                along = along + float(lattice[index][axis]) * flow[axis]
        balance = density * (1.0 + 3.0 * along + 4.5 * along * along - 1.5 * square)
        relaxed = pops[index] - (pops[index] - balance) * inverse_tau
        posts.append(jnp.where(inside, coarse[index].astype(jnp.float32), relaxed))
    return jnp.stack(posts)


def stream(posts):
    pulled = []
    for index in range(19):
        move_x = int(lattice[index][0])
        move_y = int(lattice[index][1])
        move_z = int(lattice[index][2])
        moved = jnp.roll(posts[index], (move_z, move_y, move_x), axis=(0, 1, 2))
        back = posts[opposite[index]]
        if move_z == 1:
            moved = moved.at[0].set(back[0])
        if move_z == -1:
            moved = moved.at[-1].set(back[-1])
        pulled.append(moved)
    return jnp.stack(pulled)


def reference(pops, coarse_pops, interface, drop_vel, drop_frac, home, counts, dest):
    state = pops
    for substep in range(2):
        state = stream(collide(state, coarse_pops, interface))
    density, flow = macroscopic(state)
    cells_all = NZ * NY * NX
    flat_velocity = jnp.stack(flow).reshape(3, cells_all)

    device = jnp.arange(NBT, dtype=jnp.int32) // NBD
    pos_x = device // (N_GY * N_GZ)
    pos_y = (device // N_GZ) % N_GY
    pos_z = device % N_GZ
    cell_x = pos_x[:, None] * CX + home % CX
    cell_y = pos_y[:, None] * CY + (home // CX) % CY
    cell_z = pos_z[:, None] * CZ + home // (CX * CY)

    def stencil(offset):
        step_z = offset // 16
        step_y = (offset // 4) % 4
        step_x = offset % 4
        weight = kernel((step_z - 1) - drop_frac[2]) * kernel((step_y - 1) - drop_frac[1]) * kernel((step_x - 1) - drop_frac[0])
        layer = cell_z + step_z - 1
        inside = (layer >= 0) & (layer < NZ)
        flat = (jnp.clip(layer, 0, NZ - 1) * NY + (cell_y + step_y - 1) % NY) * NX + (cell_x + step_x - 1) % NX
        return weight, inside, flat.astype(jnp.int32)

    def gather_step(total, offset):
        weight, inside, flat = stencil(offset)
        sample = flat_velocity[:, flat]
        return total + jnp.where(inside, weight, 0.0) * sample, None

    offsets = jnp.arange(64, dtype=jnp.int32)
    sampled = lax.scan(gather_step, jnp.zeros((3, NBT, 128), jnp.float32), offsets)[0]
    moved = drop_vel + relax * (sampled - drop_vel)
    live = (jnp.arange(128, dtype=jnp.int32)[None, :] < counts[:, None])[None]
    push = jnp.where(live, couple * (moved - sampled), 0.0)

    def spread_step(total, offset):
        weight, inside, flat = stencil(offset)
        target = jnp.where(inside, flat, cells_all)
        return total.at[:, target].add(weight * push, mode="drop"), None

    force = lax.scan(spread_step, jnp.zeros((3, cells_all), jnp.float32), offsets)[0].reshape(3, NZ, NY, NX)

    states = jnp.where(live, jnp.concatenate([moved, drop_frac + moved], axis=0), 0.0)
    travel_x = dest % 3 - 1
    travel_y = (dest // 3) % 3 - 1
    travel_z = dest // 9 - 1
    target = (((pos_x + travel_x) % N_GX) * N_GY + (pos_y + travel_y) % N_GY) * N_GZ + (pos_z + travel_z) % N_GZ
    grouped = dest.reshape(DEVICES, NBD)
    order = jnp.arange(NBD, dtype=jnp.int32)
    earlier = (grouped[:, :, None] == grouped[:, None, :]) & (order[None, None, :] < order[None, :, None])
    rank = jnp.sum(earlier.astype(jnp.int32), axis=2).reshape(NBT)
    lane = jnp.where(dest < 13, dest, dest - 1)
    slot = jnp.where(dest == 13, device * SLOTS + jnp.arange(NBT, dtype=jnp.int32) % NBD,
                     target * SLOTS + NBD + lane * CAP + rank).astype(jnp.int32)
    arrived = jnp.zeros((6, DEVICES * SLOTS, 128), jnp.float32).at[:, slot].set(states)
    return state, force, arrived
```

```python
import functools
import math

import jax
import jax.numpy as jnp
import numpy as np
from jax import lax
from jax.experimental import pallas as pl
from jax.experimental.pallas import tpu as pltpu
from jax.sharding import PartitionSpec as P

TILE = 8
CAP = 2


lattice = np.array(
    [
        [0, 0, 0],
        [1, 0, 0],
        [-1, 0, 0],
        [0, 1, 0],
        [0, -1, 0],
        [0, 0, 1],
        [0, 0, -1],
        [1, 1, 0],
        [-1, -1, 0],
        [1, -1, 0],
        [-1, 1, 0],
        [1, 0, 1],
        [-1, 0, -1],
        [1, 0, -1],
        [-1, 0, 1],
        [0, 1, 1],
        [0, -1, -1],
        [0, 1, -1],
        [0, -1, 1],
    ]
)
weights_table = np.array([1.0 / 3.0] + [1.0 / 18.0] * 6 + [1.0 / 36.0] * 12)
opposite = [0, 2, 1, 4, 3, 6, 5, 8, 7, 10, 9, 12, 11, 14, 13, 16, 15, 18, 17]
inverse_tau = 0.8
relax = 0.5
couple = 8.0
highest = lax.Precision.HIGHEST


def with_halo(cells, sides, width, closed):
    for axis, dim in sides:
        count = lax.axis_size(axis)
        ends = count if closed else count - 1
        head = lax.slice_in_dim(cells, 0, width, axis=dim)
        tail = lax.slice_in_dim(cells, cells.shape[dim] - width, cells.shape[dim], axis=dim)
        cells = jnp.concatenate(
            [
                lax.ppermute(tail, axis, [(i, (i + 1) % count) for i in range(ends)]),
                cells,
                lax.ppermute(head, axis, [((i + 1) % count, i) for i in range(ends)]),
            ],
            axis=dim,
        )
    return cells


def kernel(distance):
    return 0.25 * (1.0 + jnp.cos(math.pi * 0.5 * distance))


def macroscopic(pops):
    density = pops[0] * float(weights_table[0])
    moment = [jnp.zeros_like(density), jnp.zeros_like(density), jnp.zeros_like(density)]
    for index in range(1, 19):
        term = pops[index] * float(weights_table[index])
        density = density + term
        for axis in range(3):
            if int(lattice[index][axis]) != 0:
                moment[axis] = moment[axis] + float(lattice[index][axis]) * term
    return (density, [moment[axis] / density for axis in range(3)])


def collide(pops, coarse, interface):
    density, flow = macroscopic(pops)
    square = flow[0] * flow[0] + flow[1] * flow[1] + flow[2] * flow[2]
    inside = interface == 1
    posts = []
    for index in range(19):
        along = jnp.zeros_like(density)
        for axis in range(3):
            if int(lattice[index][axis]) != 0:
                along = along + float(lattice[index][axis]) * flow[axis]
        balance = density * (1.0 + 3.0 * along + 4.5 * along * along - 1.5 * square)
        relaxed = pops[index] - (pops[index] - balance) * inverse_tau
        posts.append(jnp.where(inside, coarse[index].astype(jnp.float32), relaxed))
    return jnp.stack(posts)


def window(source, index, grown, shape):
    starts = [
        grown[0] * (1 - int(lattice[index][2])),
        grown[1] * (1 - int(lattice[index][1])),
        grown[2] * (1 - int(lattice[index][0])),
    ]
    return source[
        starts[0] : starts[0] + shape[0],
        starts[1] : starts[1] + shape[1],
        starts[2] : starts[2] + shape[2],
    ]


def axis_pull(posts):
    shape = posts.shape[1:]
    cross_z = [index for index in range(19) if int(lattice[index][2]) != 0]
    cross_y = [index for index in range(19) if int(lattice[index][1]) != 0]
    cross_x = [index for index in range(19) if int(lattice[index][0]) != 0]
    part_z = with_halo(jnp.stack([posts[index] for index in cross_z]), (("gz", 1),), 1, False)
    into_y = []
    for index in cross_y:
        if index in cross_z:
            into_y.append(part_z[cross_z.index(index)])
        else:
            into_y.append(jnp.pad(posts[index], ((1, 1), (0, 0), (0, 0))))
    part_y = with_halo(jnp.stack(into_y), (("gy", 2),), 1, True)
    into_x = []
    for index in cross_x:
        if index in cross_y:
            into_x.append(part_y[cross_y.index(index)])
        elif index in cross_z:
            into_x.append(jnp.pad(part_z[cross_z.index(index)], ((0, 0), (1, 1), (0, 0))))
        else:
            into_x.append(jnp.pad(posts[index], ((1, 1), (1, 1), (0, 0))))
    part_x = with_halo(jnp.stack(into_x), (("gx", 3),), 1, True)
    pulled = []
    for index in range(19):
        if index in cross_x:
            pulled.append(window(part_x[cross_x.index(index)], index, (1, 1, 1), shape))
        elif index in cross_y:
            pulled.append(window(part_y[cross_y.index(index)], index, (1, 1, 0), shape))
        elif index in cross_z:
            pulled.append(window(part_z[cross_z.index(index)], index, (1, 0, 0), shape))
        else:
            pulled.append(posts[index])
    return pulled


def wall_fix(pulled, posts, bottom, top):
    fixed = []
    for index in range(19):
        value = pulled[index]
        if int(lattice[index][2]) == 1:
            value = jnp.where(bottom, posts[opposite[index]], value)
        if int(lattice[index][2]) == -1:
            value = jnp.where(top, posts[opposite[index]], value)
        fixed.append(value)
    return jnp.stack(fixed)


def row_weights(offset, frac):
    span = lax.broadcasted_iota(jnp.int32, (1, TILE + 4), 1)
    distance = span - 2 - offset[:, None] - frac[:, None]
    return jnp.where(jnp.abs(distance) < 2.0, kernel(distance), 0.0)


def fold(array, dim, inner):
    core = lax.slice_in_dim(array, 4, inner + 4, axis=dim)
    lower = lax.slice_in_dim(array, 0, 2, axis=dim)
    upper = lax.slice_in_dim(array, inner + 6, inner + 8, axis=dim)
    low_pad = [(0, 0)] * array.ndim
    high_pad = [(0, 0)] * array.ndim
    low_pad[dim] = (0, inner - 2)
    high_pad[dim] = (inner - 2, 0)
    return core + jnp.pad(lower, low_pad) + jnp.pad(upper, high_pad)


def phis(frac):
    angle = frac * (0.5 * math.pi)
    sine = 0.25 * jnp.sin(angle)
    cosine = 0.25 * jnp.cos(angle)
    return (0.25 - sine, 0.25 + cosine, 0.25 + sine, 0.25 - cosine)


def split(value):
    high = value.astype(jnp.bfloat16)
    return high, (value - high.astype(jnp.float32)).astype(jnp.bfloat16)


def pick(step, parts):
    value = jnp.where(step == 0, parts[0], 0.0)
    for index in range(1, 4):
        value = jnp.where(step == index, parts[index], value)
    return value


def dots(left, right, dims):
    return lax.dot_general(left, right, (dims, ((), ())), preferred_element_type=jnp.float32)


def droplet_body(size, counts_ref, vel_ref, speed_ref, frac_ref, home_ref, spread_ref, state_ref,
                 vel_high, vel_low, row_high, row_low, push_high, push_low, plane_ref):
    depth, height, width = size
    blocks = home_ref.shape[0]
    layers, rows, lanes = depth + 3, height + 8, width + 128
    high, low = split(vel_ref[...].reshape(3 * layers * rows, lanes))
    vel_high[...] = high
    vel_low[...] = low
    row_high[...] = jnp.zeros_like(row_high)
    row_low[...] = jnp.zeros_like(row_low)
    used = width + 16
    span_x = lax.broadcasted_iota(jnp.int32, (used, 128), 0) + 1
    span_y = lax.broadcasted_iota(jnp.int32, (rows, 128), 0)
    span_y = jnp.where(span_y >= height + 4, span_y - rows, span_y) + 1
    span_z = lax.broadcasted_iota(jnp.int32, (layers, 128), 0)
    last = lax.broadcasted_iota(jnp.int32, (16, 128), 0) == 15
    slots = lax.broadcasted_iota(jnp.int32, (1, 128), 1)

    def pair(number):
        for half in range(2):
            block = 2 * number + half
            side = pl.ds(half * 128, 128)
            cell = home_ref[pl.ds(block, 1), :]
            cell_x = cell & (width - 1) if width & (width - 1) == 0 else cell % width
            cell_y = cell // width % height
            cell_z = cell // (width * height)
            part_x = phis(frac_ref[0, pl.ds(block, 1), :])
            part_y = phis(frac_ref[1, pl.ds(block, 1), :])
            part_z = phis(frac_ref[2, pl.ds(block, 1), :])
            high, low = split(pick(span_x - cell_x, part_x))
            row_high[0:used, side] = high
            row_low[0:used, side] = low
            high, low = split(jnp.where(last & (cell_x == 0), part_x[0], 0.0))
            row_high[lanes - 16 : lanes, side] = high
            row_low[lanes - 16 : lanes, side] = low
            weight_y = pick(span_y - cell_y, part_y)
            weight_z = pick(span_z - cell_z, part_z)
            for layer in range(layers):
                plane_ref[layer, :, side] = weight_y * weight_z[layer : layer + 1, :]
        along_high = row_high[...]
        along_low = row_low[...]
        sums = (
            dots(vel_high[...], along_high, ((1,), (0,)))
            + dots(vel_low[...], along_high, ((1,), (0,)))
            + dots(vel_high[...], along_low, ((1,), (0,)))
        ).reshape(3, layers, rows, 256)
        plane = plane_ref[...]
        sampled = jnp.sum(jnp.sum(sums * plane[None], axis=1), axis=1)
        for half in range(2):
            block = 2 * number + half
            live = slots < counts_ref[block]
            for axis in range(3):
                sample = sampled[axis : axis + 1, half * 128 : half * 128 + 128]
                speed = speed_ref[axis, pl.ds(block, 1), :]
                frac = frac_ref[axis, pl.ds(block, 1), :]
                moved = speed + relax * (sample - speed)
                push = jnp.where(live, couple * (moved - sample), 0.0)
                state_ref[axis, pl.ds(block, 1), :] = jnp.where(live, moved, 0.0)
                state_ref[3 + axis, pl.ds(block, 1), :] = jnp.where(live, frac + moved, 0.0)
                high, low = split(
                    (plane[:, :, half * 128 : half * 128 + 128] * push[None]).reshape(layers * rows, 128)
                )
                where = pl.ds(axis * layers * rows, layers * rows)
                push_high[where, half * 128 : half * 128 + 128] = high
                push_low[where, half * 128 : half * 128 + 128] = low
        patch = (
            dots(push_high[...], along_high, ((1,), (1,)))
            + dots(push_low[...], along_high, ((1,), (1,)))
            + dots(push_high[...], along_low, ((1,), (1,)))
        ).reshape(3, layers, rows, lanes)
        return patch

    spread_ref[...] = pair(0)

    def step(number, carry):
        spread_ref[...] += pair(number)
        return carry

    lax.fori_loop(1, blocks // 2, step, 0)


def droplets(velocity, drop_vel, drop_frac, home, counts, size):
    depth, height, width = size
    blocks = home.shape[0]
    layers, rows, lanes = depth + 3, height + 8, width + 128
    flat = 3 * layers * rows
    vmem = pl.BlockSpec(memory_space=pltpu.VMEM)
    return pl.pallas_call(
        functools.partial(droplet_body, size),
        out_shape=(
            jax.ShapeDtypeStruct((3, layers, rows, lanes), jnp.float32),
            jax.ShapeDtypeStruct((6, blocks, 128), jnp.float32),
        ),
        in_specs=[pl.BlockSpec(memory_space=pltpu.SMEM), vmem, vmem, vmem, vmem],
        out_specs=(vmem, vmem),
        scratch_shapes=[
            pltpu.VMEM((flat, lanes), jnp.bfloat16),
            pltpu.VMEM((flat, lanes), jnp.bfloat16),
            pltpu.VMEM((lanes, 256), jnp.bfloat16),
            pltpu.VMEM((lanes, 256), jnp.bfloat16),
            pltpu.VMEM((flat, 256), jnp.bfloat16),
            pltpu.VMEM((flat, 256), jnp.bfloat16),
            pltpu.VMEM((layers, rows, 256), jnp.float32),
        ],
        compiler_params=pltpu.CompilerParams(vmem_limit_bytes=48 * 1024 * 1024),
    )(counts, velocity, drop_vel, drop_frac, home)


def local(pops, coarse_pops, interface, drop_vel, drop_frac, home, counts, dest):
    level = lax.axis_index("gz")
    levels = lax.axis_size("gz")
    depth, height, width = interface.shape
    rows = lax.broadcasted_iota(jnp.int32, (depth, 1, 1), 0)
    bottom = (level == 0) & (rows == 0)
    top = (level == levels - 1) & (rows == depth - 1)
    state = pops
    for substep in range(2):
        posts = collide(state, coarse_pops, interface)
        pulled = axis_pull(posts)
        state = wall_fix(pulled, posts, bottom, top)
    density, flow = macroscopic(state)
    velocity = jnp.stack(flow)
    velocity_ext = with_halo(velocity, (("gx", 3), ("gy", 2), ("gz", 1)), 2, True)
    rim_rows = lax.broadcasted_iota(jnp.int32, (1, depth + 4, 1, 1), 1)
    keep = jnp.logical_not(
        (level == 0) & (rim_rows < 2) | (level == levels - 1) & (rim_rows >= depth + 2)
    )
    velocity_ext = jnp.where(keep, velocity_ext, 0.0)
    blocks = home.shape[0]
    circle = velocity_ext[:, 1:]
    circle = jnp.pad(
        jnp.concatenate([circle[:, :, 2:], jnp.zeros_like(circle[:, :, :5]), circle[:, :, 1:2]], axis=2),
        ((0, 0), (0, 0), (0, 0), (0, 0)),
    )
    lanes = jnp.zeros(circle.shape[:3] + (125,), jnp.float32)
    circle = jnp.concatenate([circle[..., 2:], lanes, circle[..., 1:2]], axis=3)
    spread, states = droplets(
        circle, drop_vel, drop_frac, home, counts, (depth, height, width)
    )
    spread = jnp.concatenate(
        [jnp.zeros_like(spread[..., :1]), spread[..., -1:], spread[..., : width + 2]], axis=3
    )
    spread = jnp.concatenate(
        [jnp.zeros_like(spread[:, :, :1]), spread[:, :, -1:], spread[:, :, : height + 2]], axis=2
    )
    spread = jnp.concatenate([jnp.zeros_like(spread[:, :1]), spread], axis=1)
    spread = jnp.where(keep, spread, 0.0)
    force_ext = with_halo(spread, (("gx", 3), ("gy", 2), ("gz", 1)), 2, True)
    force = fold(fold(fold(force_ext, 1, depth), 2, height), 3, width)
    order = lax.broadcasted_iota(jnp.int32, (blocks,), 0)
    earlier = (dest[:, None] == dest[None, :]) & (order[None, :] < order[:, None])
    rank = jnp.sum(earlier.astype(jnp.int32), axis=1)
    moving = dest != 13
    slot = jnp.where(moving, dest * CAP + rank, 27 * CAP)
    outbox = jnp.zeros((6, 27 * CAP, 128), jnp.float32).at[:, slot].set(states, mode="drop")
    outbox = outbox.reshape(6, 3, 3, 3, CAP, 128)
    arrived_box = with_halo(outbox, (("gx", 3), ("gy", 2), ("gz", 1)), 1, True)
    inbox = arrived_box[:, 4::-2, 4::-2, 4::-2].reshape(6, 27 * CAP, 128)
    incoming = jnp.concatenate([inbox[:, : 13 * CAP], inbox[:, 14 * CAP :]], axis=1)
    staying = jnp.where(moving[None, :, None], 0.0, states)
    arrived = jnp.concatenate([staying, incoming], axis=1)
    return (state, force, arrived)


def solution(mesh):
    return jax.shard_map(
        local,
        mesh=mesh,
        in_specs=(
            P(None, "gz", "gy", "gx"),
            P(None, "gz", "gy", "gx"),
            P("gz", "gy", "gx"),
            P(None, ("gx", "gy", "gz"), None),
            P(None, ("gx", "gy", "gz"), None),
            P(("gx", "gy", "gz"), None),
            P(("gx", "gy", "gz")),
            P(("gx", "gy", "gz")),
        ),
        out_specs=(
            P(None, "gz", "gy", "gx"),
            P(None, "gz", "gy", "gx"),
            P(None, ("gx", "gy", "gz"), None),
        ),
        check_vma=False,
    )
```

```python
import functools
import math

import jax
import jax.numpy as jnp
import numpy as np
from jax import lax
from jax.experimental import pallas as pl
from jax.experimental.pallas import tpu as pltpu
from jax.sharding import PartitionSpec as P

TILE = 8
CAP = 2


lattice = np.array(
    [
        [0, 0, 0],
        [1, 0, 0],
        [-1, 0, 0],
        [0, 1, 0],
        [0, -1, 0],
        [0, 0, 1],
        [0, 0, -1],
        [1, 1, 0],
        [-1, -1, 0],
        [1, -1, 0],
        [-1, 1, 0],
        [1, 0, 1],
        [-1, 0, -1],
        [1, 0, -1],
        [-1, 0, 1],
        [0, 1, 1],
        [0, -1, -1],
        [0, 1, -1],
        [0, -1, 1],
    ]
)
weights_table = np.array([1.0 / 3.0] + [1.0 / 18.0] * 6 + [1.0 / 36.0] * 12)
opposite = [0, 2, 1, 4, 3, 6, 5, 8, 7, 10, 9, 12, 11, 14, 13, 16, 15, 18, 17]
inverse_tau = 0.8
relax = 0.5
couple = 8.0
highest = lax.Precision.HIGHEST


def with_halo(cells, sides, width, closed):
    for axis, dim in sides:
        count = lax.axis_size(axis)
        ends = count if closed else count - 1
        head = lax.slice_in_dim(cells, 0, width, axis=dim)
        tail = lax.slice_in_dim(cells, cells.shape[dim] - width, cells.shape[dim], axis=dim)
        cells = jnp.concatenate(
            [
                lax.ppermute(tail, axis, [(i, (i + 1) % count) for i in range(ends)]),
                cells,
                lax.ppermute(head, axis, [((i + 1) % count, i) for i in range(ends)]),
            ],
            axis=dim,
        )
    return cells


def fold(array, dim, inner):
    core = lax.slice_in_dim(array, 4, inner + 4, axis=dim)
    lower = lax.slice_in_dim(array, 0, 2, axis=dim)
    upper = lax.slice_in_dim(array, inner + 6, inner + 8, axis=dim)
    low_pad = [(0, 0)] * array.ndim
    high_pad = [(0, 0)] * array.ndim
    low_pad[dim] = (0, inner - 2)
    high_pad[dim] = (inner - 2, 0)
    return core + jnp.pad(lower, low_pad) + jnp.pad(upper, high_pad)


ways = [tuple(int(part) for part in lattice[index][::-1]) for index in range(19)] + [(0, 0, 0)]
channels = len(ways)
LOW = 3
HIGH = 4


def low_reach(way):
    return 2 + way


def high_reach(way):
    return 3 - way


def rim(kind):
    count, reach = (LOW, low_reach) if kind == "low" else (HIGH, high_reach)
    return [
        (step, channel)
        for step in range(1, count + 1)
        for channel in range(channels)
        if step <= reach(ways[channel][0])
    ]


def rim_count(kind):
    return LOW if kind == "low" else HIGH


def rim_sides(levels):
    if levels == 2:
        return [("low", 1, 0, 0), ("high", 0, 1, 0)]
    return [("low", None, None, 0), ("high", None, None, 1)]


def rim_sizes(levels):
    sides = [(len(rim(kind)), rim_count(kind)) for kind, _, _, _ in rim_sides(levels)]
    return [max(sides)] if levels == 2 else sides


def guarded(level, guard, action):
    if guard is None:
        action()
    else:
        pl.when(level == guard)(action)


def row_table(depth, levels):
    high_at, low_at = 0, 0
    own, own_strips, rims, strips = [], [], {}, {}

    def entry(channel, bounces=False):
        nonlocal high_at, low_at
        way_z, way, _ = ways[channel]
        above, below = high_reach(way), low_reach(way)
        if bounces and way_z != 0:
            above, below = max(above, HIGH - 1), max(below, LOW - 1)
        place = (high_at, low_at, above, below)
        high_at, low_at = high_at + place[2], low_at + place[3]
        return place

    def strip():
        nonlocal high_at, low_at
        place = (high_at, low_at, HIGH, LOW)
        high_at, low_at = high_at + HIGH, low_at + LOW
        return place

    for layer in range(depth):
        for channel in range(channels):
            own.append((layer, channel, entry(channel, layer in (0, depth - 1))))
        own_strips.append((strip(), strip()))
    start = (high_at, low_at)
    most = start
    for kind, _, _, _ in rim_sides(levels):
        if levels == 2:
            high_at, low_at = start
        rims[kind] = [(step, channel, entry(channel)) for step, channel in rim(kind)]
        strips[kind] = [(strip(), strip()) for _ in range(rim_count(kind))]
        most = (max(most[0], high_at), max(most[1], low_at))
    return own, own_strips, rims, strips, [-(-count // 8) * 8 for count in most]


def moments(cells):
    density = cells[0] * float(weights_table[0])
    moment = [None, None, None]
    face, edge = float(weights_table[1]), float(weights_table[7])
    edge_sum = cells[7]
    for index in range(8, 19):
        edge_sum = edge_sum + cells[index]
    face_sum = cells[1]
    for index in range(2, 7):
        face_sum = face_sum + cells[index]
    density = density + face * face_sum + edge * edge_sum
    for axis in range(3):
        total = {}
        for group, indices in ((face, range(1, 7)), (edge, range(7, 19))):
            plus, minus = None, None
            for index in indices:
                way = int(lattice[index][axis])
                if way == 1:
                    plus = cells[index] if plus is None else plus + cells[index]
                if way == -1:
                    minus = cells[index] if minus is None else minus + cells[index]
            total[group] = plus - minus
        moment[axis] = face * total[face] + edge * total[edge]
    return density, moment


def relaxed(cells):
    density, moment = moments(cells)
    inverse = 1.0 / density
    flow = [part * inverse for part in moment]
    square = flow[0] * flow[0] + flow[1] * flow[1] + flow[2] * flow[2]
    scale = density * inverse_tau
    base = scale * (1.0 - 1.5 * square)
    keep = 1.0 - inverse_tau
    posts = [None] * 19
    posts[0] = keep * cells[0] + base
    for index in range(1, 19, 2):
        along = None
        for axis in range(3):
            way = int(lattice[index][axis])
            if way != 0:
                part = flow[axis] if way == 1 else -flow[axis]
                along = part if along is None else along + part
        odd = 3.0 * scale * along
        even = base + (4.5 * scale) * (along * along)
        posts[index] = keep * cells[index] + (even + odd)
        posts[index + 1] = keep * cells[index + 1] + (even - odd)
    return posts


def lane_roll(value, shift):
    shift = shift % value.shape[-1]
    return value if shift == 0 else pltpu.roll(value, shift, value.ndim - 1)


def first_body(levels, level_ref, pops_ref, coarse_ref, interface_ref, posts_ref, *outs):
    depth, height, width = interface_ref.shape
    sides = rim_sides(levels)
    slots = len(rim_sizes(levels))
    rims = outs[:slots]
    right_ref, left_ref = outs[slots : slots + 2]
    right_rims = outs[slots + 2 : 2 * slots + 2]
    left_rims = outs[2 * slots + 2 :]
    level = level_ref[0]
    lane = lax.broadcasted_iota(jnp.int32, (height, 128), 1)

    def layer_step(layer, carry):
        mask = interface_ref[layer]
        inside = mask == 1
        posts = relaxed([pops_ref[index, layer] for index in range(19)])
        posts = [
            jnp.where(inside, coarse_ref[index, layer].astype(jnp.float32), posts[index])
            for index in range(19)
        ] + [mask.astype(jnp.float32)]
        right, left = jnp.zeros((height, 128), jnp.float32), jnp.zeros((height, 128), jnp.float32)
        for channel in range(channels):
            posts_ref[channel, layer] = posts[channel]
            here = (lane >= 4 * channel) & (lane < 4 * channel + 4)
            right = jnp.where(here, lane_roll(posts[channel][:, width - 128 :], 4 * channel + 4), right)
            left = jnp.where(here, lane_roll(posts[channel][:, :128], 4 * channel), left)
        right_ref[layer] = right
        left_ref[layer] = left
        return carry

    lax.fori_loop(0, depth, layer_step, 0)
    for kind, _, sender, slot in sides:

        def pack(kind=kind, slot=slot):
            for place, (step, channel) in enumerate(rim(kind)):
                rims[slot][place] = posts_ref[channel, depth - step if kind == "low" else step - 1]
            for step in range(1, rim_count(kind) + 1):
                layer = depth - step if kind == "low" else step - 1
                right_rims[slot][step - 1] = right_ref[layer]
                left_rims[slot][step - 1] = left_ref[layer]

        guarded(level, sender, pack)


def rows_body(levels, level_ref, posts_ref, low_ref, high_ref, *rest):
    depth, height = posts_ref.shape[1:3]
    slots = len(rim_sizes(levels))
    rims, low_rims, high_rims = rest[:slots], rest[slots : 2 * slots], rest[2 * slots : 3 * slots]
    down_ref, up_ref = rest[3 * slots :]
    own, own_strips, rim_rows, rim_strips, _ = row_table(depth, levels)

    def put(place, source, *index):
        down_at, up_at, down_rows, up_rows = place
        down_ref[down_at : down_at + down_rows, :] = source[(*index, slice(0, down_rows))]
        up_ref[up_at : up_at + up_rows, :] = source[(*index, slice(height - up_rows, height))]

    for layer, channel, place in own:
        put(place, posts_ref, channel, layer)
    for layer in range(depth):
        put(own_strips[layer][0], low_ref, layer)
        put(own_strips[layer][1], high_ref, layer)
    for kind, receiver, _, slot in rim_sides(levels):

        def pack(kind=kind, slot=slot):
            for at, (_, _, place) in enumerate(rim_rows[kind]):
                put(place, rims[slot], at)
            for step, (low, high) in enumerate(rim_strips[kind]):
                put(low, low_rims[slot], step)
                put(high, high_rims[slot], step)

        guarded(level_ref[0], receiver, pack)


def steps_body(levels, level_ref, posts_ref, low_ref, high_ref, *rest):
    depth, height, width = posts_ref.shape[1:]
    slots = len(rim_sizes(levels))
    rims, low_rims, high_rims = rest[:slots], rest[slots : 2 * slots], rest[2 * slots : 3 * slots]
    above_ref, below_ref, pops_ref, vel_ref, ext, strip_low, strip_high, pulled, second = rest[3 * slots :]
    own, own_strips, rim_rows, rim_strips, _ = row_table(depth, levels)
    level = level_ref[0]
    rows, lanes = height + 8, width + 128
    main = slice(0, width)

    def place_rows(target, index, place, cols):
        above_at, below_at, above_rows, below_rows = place
        target[(*index, slice(height, height + above_rows), cols)] = above_ref[
            above_at : above_at + above_rows, :
        ]
        target[(*index, slice(rows - below_rows, rows), cols)] = below_ref[
            below_at : below_at + below_rows, :
        ]

    whole = slice(None)
    for layer, channel, place in own:
        ext[channel, LOW + layer, :height, main] = posts_ref[channel, layer]
        place_rows(ext, (channel, LOW + layer), place, main)
    for layer in range(depth):
        for strip, source, place in (
            (strip_low, low_ref, own_strips[layer][0]),
            (strip_high, high_ref, own_strips[layer][1]),
        ):
            strip[LOW + layer, :height, :] = source[layer]
            place_rows(strip, (LOW + layer,), place, whole)
    for kind, receiver, _, slot in rim_sides(levels):

        def unpack(kind=kind, slot=slot):
            def at_layer(step):
                return LOW - step if kind == "low" else LOW + depth + step - 1

            for at, (step, channel, place) in enumerate(rim_rows[kind]):
                ext[channel, at_layer(step), :height, main] = rims[slot][at]
                place_rows(ext, (channel, at_layer(step)), place, main)
            for step in range(1, rim_count(kind) + 1):
                for strip, source, place in (
                    (strip_low, low_rims[slot], rim_strips[kind][step - 1][0]),
                    (strip_high, high_rims[slot], rim_strips[kind][step - 1][1]),
                ):
                    strip[at_layer(step), :height, :] = source[step - 1]
                    place_rows(strip, (at_layer(step),), place, whole)

        guarded(level, receiver, unpack)

    lane = lax.broadcasted_iota(jnp.int32, (rows, 128), 1)

    def strip_step(layer, carry):
        low, high = strip_low[layer], strip_high[layer]
        for channel in range(channels):
            ext[channel, layer, :, width:] = jnp.where(
                lane < 64, lane_roll(high, -4 * channel), lane_roll(low, 124 - 4 * channel)
            )
        return carry

    lax.fori_loop(0, LOW + depth + HIGH, strip_step, 0)

    def pull(source, layer, at):
        bottom = (level == 0) & (layer == 0)
        top = (level == levels - 1) & (layer == depth - 1)
        for index in range(19):
            way_z, way_y, way_x = ways[index]
            value = source[index, at - way_z]
            if way_x != 0:
                value = pltpu.roll(value, way_x % lanes, 1)
            if way_y != 0:
                value = pltpu.roll(value, way_y % rows, 0)
            if way_z != 0:
                wall = bottom if way_z == 1 else top
                value = jnp.where(wall, source[opposite[index], at], value)
            pulled[index] = value

    tiles = [
        (slice(row, row + 8), slice(col, col + 128))
        for row in range(0, rows, 8)
        for col in range(0, lanes, 128)
    ]

    def first_step(number, carry):
        at = number + 1
        pull(ext, at - LOW, at)
        for tile in tiles:
            posts = relaxed([pulled[(index, *tile)] for index in range(19)])
            inside = ext[(19, at, *tile)] > 0.5
            for index in range(19):
                second[(index, number, *tile)] = jnp.where(inside, ext[(index, at, *tile)], posts[index])
        return carry

    lax.fori_loop(0, depth + LOW + HIGH - 2, first_step, 0)

    row_at = lax.broadcasted_iota(jnp.int32, (8, 128), 0)
    lane_at = lax.broadcasted_iota(jnp.int32, (8, 128), 1)

    def second_step(number, carry):
        layer = number - 1
        pull(second, layer, number + 1)
        keep = jnp.logical_not((level == 0) & (layer < 0) | (level == levels - 1) & (layer >= depth))
        for tile in tiles:
            density, moment = moments([pulled[(index, *tile)] for index in range(19)])
            inverse = 1.0 / density
            row = row_at + tile[0].start
            col = lane_at + tile[1].start
            valid = ((row < height + 2) | (row == rows - 1)) & ((col < width + 2) | (col == lanes - 1))
            for axis in range(3):
                vel_ref[(axis, number, *tile)] = jnp.where(valid & keep, moment[axis] * inverse, 0.0)
        return carry

    lax.fori_loop(0, 1, second_step, 0)

    def second_inner(number, carry):
        second_step(number, carry)
        for index in range(19):
            pops_ref[index, number - 1] = pulled[index, :height, main]
        return carry

    lax.fori_loop(1, depth + 1, second_inner, 0)
    lax.fori_loop(depth + 1, depth + 3, second_step, 0)


def call(body, outs, ins, scratch=()):
    vmem = pl.BlockSpec(memory_space=pltpu.VMEM)
    return pl.pallas_call(
        body,
        out_shape=[jax.ShapeDtypeStruct(shape, jnp.float32) for shape in outs],
        in_specs=[pl.BlockSpec(memory_space=pltpu.SMEM)] + [vmem] * (len(ins) - 1),
        out_specs=[vmem] * len(outs),
        scratch_shapes=list(scratch),
        compiler_params=pltpu.CompilerParams(vmem_limit_bytes=56 * 1024 * 1024),
    )(*ins)


def shifted(value, axis, step):
    count = lax.axis_size(axis)
    return lax.ppermute(value, axis, [(i, (i + step) % count) for i in range(count)])


def to_level(value, kind, levels, step=0):
    count = lax.axis_size("gx")
    pairs = []
    for at in range(levels):
        other = 1 - at if levels == 2 else at + 1 if kind == "low" else at - 1
        if 0 <= other < levels:
            pairs.append((at, other))
    if step == 0:
        return lax.ppermute(value, "gz", pairs)
    return lax.ppermute(
        value,
        ("gx", "gz"),
        [
            (x * levels + at, (x + step) % count * levels + other)
            for x in range(count)
            for at, other in pairs
        ],
    )


def two_substeps(pops, coarse_pops, interface):
    level = lax.axis_index("gz").astype(jnp.int32).reshape(1)
    levels = lax.axis_size("gz")
    depth, height, width = interface.shape
    sizes = rim_sizes(levels)
    slots = len(sizes)
    kinds = ["low", "high"][:slots]
    rims_of = [(size, height, width) for size, _ in sizes]
    strips_of = [(count, height, 128) for _, count in sizes]
    outs = call(
        functools.partial(first_body, levels),
        [(channels, depth, height, width)] + rims_of + [(depth, height, 128)] * 2 + strips_of * 2,
        [level, pops, coarse_pops, interface],
    )
    posts, rims = outs[0], outs[1 : slots + 1]
    right, left = outs[slots + 1 : slots + 3]
    right_rims, left_rims = outs[slots + 3 : 2 * slots + 3], outs[2 * slots + 3 :]
    low = shifted(right, "gx", 1)
    high = shifted(left, "gx", -1)
    low_rims = [to_level(value, kind, levels, 1) for value, kind in zip(right_rims, kinds)]
    high_rims = [to_level(value, kind, levels, -1) for value, kind in zip(left_rims, kinds)]
    rims = [to_level(value, kind, levels) for value, kind in zip(rims, kinds)]
    given = [level, posts, low, high, *rims, *low_rims, *high_rims]
    counts = row_table(depth, levels)[-1]
    down, up = call(
        functools.partial(rows_body, levels), [(count, width) for count in counts], given
    )
    above = shifted(down, "gy", -1)
    below = shifted(up, "gy", 1)
    rows, lanes = height + 8, width + 128
    layers = depth + LOW + HIGH
    return call(
        functools.partial(steps_body, levels),
        [pops.shape, (3, depth + 3, rows, lanes)],
        given + [above, below],
        [
            pltpu.VMEM((channels, layers, rows, lanes), jnp.float32),
            pltpu.VMEM((layers, rows, 128), jnp.float32),
            pltpu.VMEM((layers, rows, 128), jnp.float32),
            pltpu.VMEM((19, rows, lanes), jnp.float32),
            pltpu.VMEM((19, layers - 2, rows, lanes), jnp.float32),
        ],
    )


def phis(frac):
    angle = frac * (0.5 * math.pi)
    sine = 0.25 * jnp.sin(angle)
    cosine = 0.25 * jnp.cos(angle)
    return (0.25 - sine, 0.25 + cosine, 0.25 + sine, 0.25 - cosine)


def split(value):
    high = value.astype(jnp.bfloat16)
    return high, (value - high.astype(jnp.float32)).astype(jnp.bfloat16)


def pick(step, parts):
    value = jnp.where(step == 0, parts[0], 0.0)
    for index in range(1, 4):
        value = jnp.where(step == index, parts[index], value)
    return value


def dots(left, right, dims):
    return lax.dot_general(left, right, (dims, ((), ())), preferred_element_type=jnp.float32)


def droplet_body(size, counts_ref, vel_ref, speed_ref, frac_ref, home_ref, spread_ref, state_ref,
                 vel_high, vel_low, row_high, row_low, push_high, push_low, plane_ref):
    depth, height, width = size
    blocks = home_ref.shape[0]
    layers, rows, lanes = depth + 3, height + 8, width + 128
    high, low = split(vel_ref[...].reshape(3 * layers * rows, lanes))
    vel_high[...] = high
    vel_low[...] = low
    row_high[...] = jnp.zeros_like(row_high)
    row_low[...] = jnp.zeros_like(row_low)
    used = width + 16
    span_x = lax.broadcasted_iota(jnp.int32, (used, 128), 0) + 1
    span_y = lax.broadcasted_iota(jnp.int32, (rows, 128), 0)
    span_y = jnp.where(span_y >= height + 4, span_y - rows, span_y) + 1
    span_z = lax.broadcasted_iota(jnp.int32, (layers, 128), 0)
    last = lax.broadcasted_iota(jnp.int32, (16, 128), 0) == 15
    slots = lax.broadcasted_iota(jnp.int32, (1, 128), 1)

    def pair(number):
        for half in range(2):
            block = 2 * number + half
            side = pl.ds(half * 128, 128)
            cell = home_ref[pl.ds(block, 1), :]
            cell_x = cell & (width - 1) if width & (width - 1) == 0 else cell % width
            cell_y = cell // width % height
            cell_z = cell // (width * height)
            part_x = phis(frac_ref[0, pl.ds(block, 1), :])
            part_y = phis(frac_ref[1, pl.ds(block, 1), :])
            part_z = phis(frac_ref[2, pl.ds(block, 1), :])
            high, low = split(pick(span_x - cell_x, part_x))
            row_high[0:used, side] = high
            row_low[0:used, side] = low
            high, low = split(jnp.where(last & (cell_x == 0), part_x[0], 0.0))
            row_high[lanes - 16 : lanes, side] = high
            row_low[lanes - 16 : lanes, side] = low
            weight_y = pick(span_y - cell_y, part_y)
            weight_z = pick(span_z - cell_z, part_z)
            for layer in range(layers):
                plane_ref[layer, :, side] = weight_y * weight_z[layer : layer + 1, :]
        along_high = row_high[...]
        along_low = row_low[...]
        sums = (
            dots(vel_high[...], along_high, ((1,), (0,)))
            + dots(vel_low[...], along_high, ((1,), (0,)))
            + dots(vel_high[...], along_low, ((1,), (0,)))
        ).reshape(3, layers, rows, 256)
        plane = plane_ref[...]
        sampled = jnp.sum(jnp.sum(sums * plane[None], axis=1), axis=1)
        for half in range(2):
            block = 2 * number + half
            live = slots < counts_ref[block]
            for axis in range(3):
                sample = sampled[axis : axis + 1, half * 128 : half * 128 + 128]
                speed = speed_ref[axis, pl.ds(block, 1), :]
                frac = frac_ref[axis, pl.ds(block, 1), :]
                moved = speed + relax * (sample - speed)
                push = jnp.where(live, couple * (moved - sample), 0.0)
                state_ref[axis, pl.ds(block, 1), :] = jnp.where(live, moved, 0.0)
                state_ref[3 + axis, pl.ds(block, 1), :] = jnp.where(live, frac + moved, 0.0)
                high, low = split(
                    (plane[:, :, half * 128 : half * 128 + 128] * push[None]).reshape(layers * rows, 128)
                )
                where = pl.ds(axis * layers * rows, layers * rows)
                push_high[where, half * 128 : half * 128 + 128] = high
                push_low[where, half * 128 : half * 128 + 128] = low
        patch = (
            dots(push_high[...], along_high, ((1,), (1,)))
            + dots(push_low[...], along_high, ((1,), (1,)))
            + dots(push_high[...], along_low, ((1,), (1,)))
        ).reshape(3, layers, rows, lanes)
        return patch

    spread_ref[...] = pair(0)

    def step(number, carry):
        spread_ref[...] += pair(number)
        return carry

    lax.fori_loop(1, blocks // 2, step, 0)


def droplets(velocity, drop_vel, drop_frac, home, counts, size):
    depth, height, width = size
    blocks = home.shape[0]
    layers, rows, lanes = depth + 3, height + 8, width + 128
    flat = 3 * layers * rows
    vmem = pl.BlockSpec(memory_space=pltpu.VMEM)
    return pl.pallas_call(
        functools.partial(droplet_body, size),
        out_shape=(
            jax.ShapeDtypeStruct((3, layers, rows, lanes), jnp.float32),
            jax.ShapeDtypeStruct((6, blocks, 128), jnp.float32),
        ),
        in_specs=[pl.BlockSpec(memory_space=pltpu.SMEM), vmem, vmem, vmem, vmem],
        out_specs=(vmem, vmem),
        scratch_shapes=[
            pltpu.VMEM((flat, lanes), jnp.bfloat16),
            pltpu.VMEM((flat, lanes), jnp.bfloat16),
            pltpu.VMEM((lanes, 256), jnp.bfloat16),
            pltpu.VMEM((lanes, 256), jnp.bfloat16),
            pltpu.VMEM((flat, 256), jnp.bfloat16),
            pltpu.VMEM((flat, 256), jnp.bfloat16),
            pltpu.VMEM((layers, rows, 256), jnp.float32),
        ],
        compiler_params=pltpu.CompilerParams(vmem_limit_bytes=48 * 1024 * 1024),
    )(counts, velocity, drop_vel, drop_frac, home)


def local(pops, coarse_pops, interface, drop_vel, drop_frac, home, counts, dest):
    level = lax.axis_index("gz")
    levels = lax.axis_size("gz")
    depth, height, width = interface.shape
    state, circle = two_substeps(pops, coarse_pops, interface)
    rim_rows = lax.broadcasted_iota(jnp.int32, (1, depth + 4, 1, 1), 1)
    keep = jnp.logical_not(
        (level == 0) & (rim_rows < 2) | (level == levels - 1) & (rim_rows >= depth + 2)
    )
    blocks = home.shape[0]
    spread, states = droplets(
        circle, drop_vel, drop_frac, home, counts, (depth, height, width)
    )
    spread = jnp.concatenate(
        [jnp.zeros_like(spread[..., :1]), spread[..., -1:], spread[..., : width + 2]], axis=3
    )
    spread = jnp.concatenate(
        [jnp.zeros_like(spread[:, :, :1]), spread[:, :, -1:], spread[:, :, : height + 2]], axis=2
    )
    spread = jnp.concatenate([jnp.zeros_like(spread[:, :1]), spread], axis=1)
    spread = jnp.where(keep, spread, 0.0)
    force_ext = with_halo(spread, (("gx", 3), ("gy", 2), ("gz", 1)), 2, True)
    force = fold(fold(fold(force_ext, 1, depth), 2, height), 3, width)
    order = lax.broadcasted_iota(jnp.int32, (blocks,), 0)
    earlier = (dest[:, None] == dest[None, :]) & (order[None, :] < order[:, None])
    rank = jnp.sum(earlier.astype(jnp.int32), axis=1)
    moving = dest != 13
    slot = jnp.where(moving, dest * CAP + rank, 27 * CAP)
    outbox = jnp.zeros((6, 27 * CAP, 128), jnp.float32).at[:, slot].set(states, mode="drop")
    outbox = outbox.reshape(6, 3, 3, 3, CAP, 128)
    arrived_box = with_halo(outbox, (("gx", 3), ("gy", 2), ("gz", 1)), 1, True)
    inbox = arrived_box[:, 4::-2, 4::-2, 4::-2].reshape(6, 27 * CAP, 128)
    incoming = jnp.concatenate([inbox[:, : 13 * CAP], inbox[:, 14 * CAP :]], axis=1)
    staying = jnp.where(moving[None, :, None], 0.0, states)
    arrived = jnp.concatenate([staying, incoming], axis=1)
    return (state, force, arrived)


def solution(mesh):
    return jax.shard_map(
        local,
        mesh=mesh,
        in_specs=(
            P(None, "gz", "gy", "gx"),
            P(None, "gz", "gy", "gx"),
            P("gz", "gy", "gx"),
            P(None, ("gx", "gy", "gz"), None),
            P(None, ("gx", "gy", "gz"), None),
            P(("gx", "gy", "gz"), None),
            P(("gx", "gy", "gz")),
            P(("gx", "gy", "gz")),
        ),
        out_specs=(
            P(None, "gz", "gy", "gx"),
            P(None, "gz", "gy", "gx"),
            P(None, ("gx", "gy", "gz"), None),
        ),
        check_vma=False,
    )
```

```python
import functools
import math

import jax
import jax.numpy as jnp
import numpy as np
from jax import lax
from jax.experimental import pallas as pl
from jax.experimental.pallas import tpu as pltpu
from jax.sharding import PartitionSpec as P

CAP = 2


lattice = np.array(
    [
        [0, 0, 0],
        [1, 0, 0],
        [-1, 0, 0],
        [0, 1, 0],
        [0, -1, 0],
        [0, 0, 1],
        [0, 0, -1],
        [1, 1, 0],
        [-1, -1, 0],
        [1, -1, 0],
        [-1, 1, 0],
        [1, 0, 1],
        [-1, 0, -1],
        [1, 0, -1],
        [-1, 0, 1],
        [0, 1, 1],
        [0, -1, -1],
        [0, 1, -1],
        [0, -1, 1],
    ]
)
weights_table = np.array([1.0 / 3.0] + [1.0 / 18.0] * 6 + [1.0 / 36.0] * 12)
opposite = [0, 2, 1, 4, 3, 6, 5, 8, 7, 10, 9, 12, 11, 14, 13, 16, 15, 18, 17]
inverse_tau = 0.8
relax = 0.5
couple = 8.0


def call(body, outs, ins, scalars=1, scratch=()):
    vmem = pl.BlockSpec(memory_space=pltpu.VMEM)
    return pl.pallas_call(
        body,
        out_shape=[jax.ShapeDtypeStruct(shape, jnp.float32) for shape in outs],
        in_specs=[pl.BlockSpec(memory_space=pltpu.SMEM)] * scalars + [vmem] * (len(ins) - scalars),
        out_specs=[vmem] * len(outs),
        scratch_shapes=list(scratch),
        compiler_params=pltpu.CompilerParams(vmem_limit_bytes=56 * 1024 * 1024),
    )(*ins)


ways = [tuple(int(part) for part in lattice[index][::-1]) for index in range(19)] + [(0, 0, 0)]
channels = len(ways)
LOW = 3
HIGH = 4


def low_reach(way):
    return 2 + way


def high_reach(way):
    return 3 - way


def rim(kind):
    count, reach = (LOW, low_reach) if kind == "low" else (HIGH, high_reach)
    return [
        (step, channel)
        for step in range(1, count + 1)
        for channel in range(channels)
        if step <= reach(ways[channel][0])
    ]


def rim_count(kind):
    return LOW if kind == "low" else HIGH


def rim_sides(levels):
    if levels == 2:
        return [("low", 1, 0, 0), ("high", 0, 1, 0)]
    return [("low", None, None, 0), ("high", None, None, 1)]


def rim_sizes(levels):
    sides = [(len(rim(kind)), rim_count(kind)) for kind, _, _, _ in rim_sides(levels)]
    return [max(sides)] if levels == 2 else sides


def guarded(level, guard, action):
    if guard is None:
        action()
    else:
        pl.when(level == guard)(action)


def row_table(depth, levels):
    high_at, low_at = 0, 0
    own, own_strips, rims, strips = [], [], {}, {}

    def entry(channel, bounces=False):
        nonlocal high_at, low_at
        way_z, way, _ = ways[channel]
        above, below = high_reach(way), low_reach(way)
        if bounces and way_z != 0:
            above, below = max(above, HIGH - 1), max(below, LOW - 1)
        place = (high_at, low_at, above, below)
        high_at, low_at = high_at + place[2], low_at + place[3]
        return place

    def strip():
        nonlocal high_at, low_at
        place = (high_at, low_at, HIGH, LOW)
        high_at, low_at = high_at + HIGH, low_at + LOW
        return place

    for layer in range(depth):
        for channel in range(channels):
            own.append((layer, channel, entry(channel, layer in (0, depth - 1))))
        own_strips.append((strip(), strip()))
    start = (high_at, low_at)
    most = start
    for kind, _, _, _ in rim_sides(levels):
        if levels == 2:
            high_at, low_at = start
        rims[kind] = [(step, channel, entry(channel)) for step, channel in rim(kind)]
        strips[kind] = [(strip(), strip()) for _ in range(rim_count(kind))]
        most = (max(most[0], high_at), max(most[1], low_at))
    return own, own_strips, rims, strips, [-(-count // 8) * 8 for count in most]


def moments(cells):
    density = cells[0] * float(weights_table[0])
    moment = [None, None, None]
    face, edge = float(weights_table[1]), float(weights_table[7])
    edge_sum = cells[7]
    for index in range(8, 19):
        edge_sum = edge_sum + cells[index]
    face_sum = cells[1]
    for index in range(2, 7):
        face_sum = face_sum + cells[index]
    density = density + face * face_sum + edge * edge_sum
    for axis in range(3):
        total = {}
        for group, indices in ((face, range(1, 7)), (edge, range(7, 19))):
            plus, minus = None, None
            for index in indices:
                way = int(lattice[index][axis])
                if way == 1:
                    plus = cells[index] if plus is None else plus + cells[index]
                if way == -1:
                    minus = cells[index] if minus is None else minus + cells[index]
            total[group] = plus - minus
        moment[axis] = face * total[face] + edge * total[edge]
    return density, moment


def relaxed(cells):
    density, moment = moments(cells)
    inverse = 1.0 / density
    flow = [part * inverse for part in moment]
    square = flow[0] * flow[0] + flow[1] * flow[1] + flow[2] * flow[2]
    scale = density * inverse_tau
    base = scale * (1.0 - 1.5 * square)
    keep = 1.0 - inverse_tau
    posts = [None] * 19
    posts[0] = keep * cells[0] + base
    for index in range(1, 19, 2):
        along = None
        for axis in range(3):
            way = int(lattice[index][axis])
            if way != 0:
                part = flow[axis] if way == 1 else -flow[axis]
                along = part if along is None else along + part
        odd = 3.0 * scale * along
        even = base + (4.5 * scale) * (along * along)
        posts[index] = keep * cells[index] + (even + odd)
        posts[index + 1] = keep * cells[index + 1] + (even - odd)
    return posts


def lane_roll(value, shift):
    shift = shift % value.shape[-1]
    return value if shift == 0 else pltpu.roll(value, shift, value.ndim - 1)


def first_body(levels, level_ref, pops_ref, coarse_ref, interface_ref, posts_ref, *outs):
    depth, height, width = interface_ref.shape
    sides = rim_sides(levels)
    slots = len(rim_sizes(levels))
    rims = outs[:slots]
    right_ref, left_ref = outs[slots : slots + 2]
    right_rims = outs[slots + 2 : 2 * slots + 2]
    left_rims = outs[2 * slots + 2 :]
    level = level_ref[0]
    lane = lax.broadcasted_iota(jnp.int32, (height, 128), 1)

    def layer_step(layer, carry):
        mask = interface_ref[layer]
        inside = mask == 1
        posts = relaxed([pops_ref[index, layer] for index in range(19)])
        posts = [
            jnp.where(inside, coarse_ref[index, layer].astype(jnp.float32), posts[index])
            for index in range(19)
        ] + [mask.astype(jnp.float32)]
        right, left = jnp.zeros((height, 128), jnp.float32), jnp.zeros((height, 128), jnp.float32)
        for channel in range(channels):
            posts_ref[channel, layer] = posts[channel]
            here = (lane >= 4 * channel) & (lane < 4 * channel + 4)
            right = jnp.where(here, lane_roll(posts[channel][:, width - 128 :], 4 * channel + 4), right)
            left = jnp.where(here, lane_roll(posts[channel][:, :128], 4 * channel), left)
        right_ref[layer] = right
        left_ref[layer] = left
        return carry

    lax.fori_loop(0, depth, layer_step, 0)
    for kind, _, sender, slot in sides:

        def pack(kind=kind, slot=slot):
            for place, (step, channel) in enumerate(rim(kind)):
                rims[slot][place] = posts_ref[channel, depth - step if kind == "low" else step - 1]
            for step in range(1, rim_count(kind) + 1):
                layer = depth - step if kind == "low" else step - 1
                right_rims[slot][step - 1] = right_ref[layer]
                left_rims[slot][step - 1] = left_ref[layer]

        guarded(level, sender, pack)


def rows_body(levels, level_ref, posts_ref, low_ref, high_ref, *rest):
    depth, height = posts_ref.shape[1:3]
    slots = len(rim_sizes(levels))
    rims, low_rims, high_rims = rest[:slots], rest[slots : 2 * slots], rest[2 * slots : 3 * slots]
    down_ref, up_ref = rest[3 * slots :]
    own, own_strips, rim_rows, rim_strips, _ = row_table(depth, levels)

    def put(place, source, *index):
        down_at, up_at, down_rows, up_rows = place
        down_ref[down_at : down_at + down_rows, :] = source[(*index, slice(0, down_rows))]
        up_ref[up_at : up_at + up_rows, :] = source[(*index, slice(height - up_rows, height))]

    for layer, channel, place in own:
        put(place, posts_ref, channel, layer)
    for layer in range(depth):
        put(own_strips[layer][0], low_ref, layer)
        put(own_strips[layer][1], high_ref, layer)
    for kind, receiver, _, slot in rim_sides(levels):

        def pack(kind=kind, slot=slot):
            for at, (_, _, place) in enumerate(rim_rows[kind]):
                put(place, rims[slot], at)
            for step, (low, high) in enumerate(rim_strips[kind]):
                put(low, low_rims[slot], step)
                put(high, high_rims[slot], step)

        guarded(level_ref[0], receiver, pack)


def steps_body(
    levels, level_ref, posts_ref, low_ref, high_ref, rims, low_rims, high_rims, above_ref, below_ref,
    pops_ref, vel_ref, ext, strip_low, strip_high, pulled, second,
):
    depth, height, width = posts_ref.shape[1:]
    own, own_strips, rim_rows, rim_strips, _ = row_table(depth, levels)
    level = level_ref[0]
    rows, lanes = height + 8, width + 128
    main = slice(0, width)

    def place_rows(target, index, place, cols):
        above_at, below_at, above_rows, below_rows = place
        target[(*index, slice(height, height + above_rows), cols)] = above_ref[
            above_at : above_at + above_rows, :
        ]
        target[(*index, slice(rows - below_rows, rows), cols)] = below_ref[
            below_at : below_at + below_rows, :
        ]

    whole = slice(None)
    for layer, channel, place in own:
        ext[channel, LOW + layer, :height, main] = posts_ref[channel, layer]
        place_rows(ext, (channel, LOW + layer), place, main)
    for layer in range(depth):
        for strip, source, place in (
            (strip_low, low_ref, own_strips[layer][0]),
            (strip_high, high_ref, own_strips[layer][1]),
        ):
            strip[LOW + layer, :height, :] = source[layer]
            place_rows(strip, (LOW + layer,), place, whole)
    for kind, receiver, _, slot in rim_sides(levels):

        def unpack(kind=kind, slot=slot):
            def at_layer(step):
                return LOW - step if kind == "low" else LOW + depth + step - 1

            for at, (step, channel, place) in enumerate(rim_rows[kind]):
                ext[channel, at_layer(step), :height, main] = rims[slot][at]
                place_rows(ext, (channel, at_layer(step)), place, main)
            for step in range(1, rim_count(kind) + 1):
                for strip, source, place in (
                    (strip_low, low_rims[slot], rim_strips[kind][step - 1][0]),
                    (strip_high, high_rims[slot], rim_strips[kind][step - 1][1]),
                ):
                    strip[at_layer(step), :height, :] = source[step - 1]
                    place_rows(strip, (at_layer(step),), place, whole)

        guarded(level, receiver, unpack)

    lane = lax.broadcasted_iota(jnp.int32, (rows, 128), 1)

    def strip_step(layer, carry):
        low, high = strip_low[layer], strip_high[layer]
        for channel in range(channels):
            ext[channel, layer, :, width:] = jnp.where(
                lane < 64, lane_roll(high, -4 * channel), lane_roll(low, 124 - 4 * channel)
            )
        return carry

    lax.fori_loop(0, LOW + depth + HIGH, strip_step, 0)

    def pull(source, layer, at):
        bottom = (level == 0) & (layer == 0)
        top = (level == levels - 1) & (layer == depth - 1)
        for index in range(19):
            way_z, way_y, way_x = ways[index]
            value = source[index, at - way_z]
            if way_x != 0:
                value = pltpu.roll(value, way_x % lanes, 1)
            if way_y != 0:
                value = pltpu.roll(value, way_y % rows, 0)
            if way_z != 0:
                wall = bottom if way_z == 1 else top
                value = jnp.where(wall, source[opposite[index], at], value)
            pulled[index] = value

    tiles = [
        (slice(row, row + 8), slice(col, col + 128))
        for row in range(0, rows, 8)
        for col in range(0, lanes, 128)
    ]

    def first_step(number, carry):
        at = number + 1
        pull(ext, at - LOW, at)
        for tile in tiles:
            posts = relaxed([pulled[(index, *tile)] for index in range(19)])
            inside = ext[(19, at, *tile)] > 0.5
            for index in range(19):
                second[(index, number, *tile)] = jnp.where(inside, ext[(index, at, *tile)], posts[index])
        return carry

    lax.fori_loop(0, depth + LOW + HIGH - 2, first_step, 0)

    row_at = lax.broadcasted_iota(jnp.int32, (8, 128), 0)
    lane_at = lax.broadcasted_iota(jnp.int32, (8, 128), 1)

    def second_step(number, carry):
        layer = number - 1
        pull(second, layer, number + 1)
        keep = jnp.logical_not((level == 0) & (layer < 0) | (level == levels - 1) & (layer >= depth))
        for tile in tiles:
            density, moment = moments([pulled[(index, *tile)] for index in range(19)])
            inverse = 1.0 / density
            row = row_at + tile[0].start
            col = lane_at + tile[1].start
            valid = ((row < height + 2) | (row == rows - 1)) & ((col < width + 2) | (col == lanes - 1))
            for axis in range(3):
                vel_ref[(axis, number, *tile)] = jnp.where(valid & keep, moment[axis] * inverse, 0.0)
        return carry

    lax.fori_loop(0, 1, second_step, 0)

    def second_inner(number, carry):
        second_step(number, carry)
        for index in range(19):
            pops_ref[index, number - 1] = pulled[index, :height, main]
        return carry

    lax.fori_loop(1, depth + 1, second_inner, 0)
    lax.fori_loop(depth + 1, depth + 3, second_step, 0)


def shifted(value, axis, step):
    count = lax.axis_size(axis)
    return lax.ppermute(value, axis, [(i, (i + step) % count) for i in range(count)])


def to_level(value, kind, levels, side=None, step=0):
    pairs = []
    for at in range(levels):
        other = 1 - at if levels == 2 else at + 1 if kind in ("low", "up") else at - 1
        if 0 <= other < levels:
            pairs.append((at, other))
    if side is None:
        return lax.ppermute(value, "gz", pairs)
    count = lax.axis_size(side)
    return lax.ppermute(
        value,
        (side, "gz"),
        [
            (brick * levels + at, (brick + step) % count * levels + other)
            for brick in range(count)
            for at, other in pairs
        ],
    )


def wide_exchange(level, pops, coarse_pops, interface):
    levels = lax.axis_size("gz")
    depth, height, width = interface.shape
    sizes = rim_sizes(levels)
    slots = len(sizes)
    kinds = ["low", "high"][:slots]
    rims_of = [(size, height, width) for size, _ in sizes]
    strips_of = [(count, height, 128) for _, count in sizes]
    outs = call(
        functools.partial(first_body, levels),
        [(channels, depth, height, width)] + rims_of + [(depth, height, 128)] * 2 + strips_of * 2,
        [level, pops, coarse_pops, interface],
    )
    posts, rims = outs[0], outs[1 : slots + 1]
    right, left = outs[slots + 1 : slots + 3]
    right_rims, left_rims = outs[slots + 3 : 2 * slots + 3], outs[2 * slots + 3 :]
    low = shifted(right, "gx", 1)
    high = shifted(left, "gx", -1)
    low_rims = [to_level(value, kind, levels, "gx", 1) for value, kind in zip(right_rims, kinds)]
    high_rims = [to_level(value, kind, levels, "gx", -1) for value, kind in zip(left_rims, kinds)]
    rims = [to_level(value, kind, levels) for value, kind in zip(rims, kinds)]
    given = [level, posts, low, high, *rims, *low_rims, *high_rims]
    counts = row_table(depth, levels)[-1]
    down, up = call(
        functools.partial(rows_body, levels), [(count, width) for count in counts], given
    )
    above = shifted(down, "gy", -1)
    below = shifted(up, "gy", 1)
    return given + [above, below]


def phis(frac):
    angle = frac * (0.5 * math.pi)
    sine = 0.25 * jnp.sin(angle)
    cosine = 0.25 * jnp.cos(angle)
    return (0.25 - sine, 0.25 + cosine, 0.25 + sine, 0.25 - cosine)


def split(value):
    high = value.astype(jnp.bfloat16)
    return high, (value - high.astype(jnp.float32)).astype(jnp.bfloat16)


def pick(step, parts):
    value = jnp.where(step == 0, parts[0], 0.0)
    for index in range(1, 4):
        value = jnp.where(step == index, parts[index], value)
    return value


def dots(left, right, dims):
    return lax.dot_general(left, right, (dims, ((), ())), preferred_element_type=jnp.float32)


def droplet_body(
    size, counts_ref, dest_ref, vel_ref, speed_ref, frac_ref, home_ref, spread_ref, stay_ref, state_ref,
    vel_high, vel_low, row_high, row_low, push_high, push_low, plane_ref,
):
    depth, height, width = size
    blocks = home_ref.shape[0]
    layers, rows, lanes = depth + 3, height + 8, width + 128
    high, low = split(vel_ref[...].reshape(3 * layers * rows, lanes))
    vel_high[...] = high
    vel_low[...] = low
    row_high[...] = jnp.zeros_like(row_high)
    row_low[...] = jnp.zeros_like(row_low)
    used = width + 16
    span_x = lax.broadcasted_iota(jnp.int32, (used, 128), 0) + 1
    span_y = lax.broadcasted_iota(jnp.int32, (rows, 128), 0)
    span_y = jnp.where(span_y >= height + 4, span_y - rows, span_y) + 1
    span_z = lax.broadcasted_iota(jnp.int32, (layers, 128), 0)
    last = lax.broadcasted_iota(jnp.int32, (16, 128), 0) == 15
    slots = lax.broadcasted_iota(jnp.int32, (1, 128), 1)

    def pair(number):
        for half in range(2):
            block = 2 * number + half
            side = pl.ds(half * 128, 128)
            cell = home_ref[pl.ds(block, 1), :]
            cell_x = cell & (width - 1) if width & (width - 1) == 0 else cell % width
            cell_y = cell // width % height
            cell_z = cell // (width * height)
            part_x = phis(frac_ref[0, pl.ds(block, 1), :])
            part_y = phis(frac_ref[1, pl.ds(block, 1), :])
            part_z = phis(frac_ref[2, pl.ds(block, 1), :])
            high, low = split(pick(span_x - cell_x, part_x))
            row_high[0:used, side] = high
            row_low[0:used, side] = low
            high, low = split(jnp.where(last & (cell_x == 0), part_x[0], 0.0))
            row_high[lanes - 16 : lanes, side] = high
            row_low[lanes - 16 : lanes, side] = low
            weight_y = pick(span_y - cell_y, part_y)
            weight_z = pick(span_z - cell_z, part_z)
            for layer in range(layers):
                plane_ref[layer, :, side] = weight_y * weight_z[layer : layer + 1, :]
        along_high = row_high[...]
        along_low = row_low[...]
        sums = (
            dots(vel_high[...], along_high, ((1,), (0,)))
            + dots(vel_low[...], along_high, ((1,), (0,)))
            + dots(vel_high[...], along_low, ((1,), (0,)))
        ).reshape(3, layers, rows, 256)
        plane = plane_ref[...]
        sampled = jnp.sum(jnp.sum(sums * plane[None], axis=1), axis=1)
        for half in range(2):
            block = 2 * number + half
            live = slots < counts_ref[block]
            for axis in range(3):
                sample = sampled[axis : axis + 1, half * 128 : half * 128 + 128]
                speed = speed_ref[axis, pl.ds(block, 1), :]
                frac = frac_ref[axis, pl.ds(block, 1), :]
                moved = speed + relax * (sample - speed)
                push = jnp.where(live, couple * (moved - sample), 0.0)
                stays = live & (dest_ref[block] == 13)
                for at, value in ((axis, moved), (3 + axis, frac + moved)):
                    state_ref[block, at : at + 1, :] = jnp.where(live, value, 0.0)
                    stay_ref[at, pl.ds(block, 1), :] = jnp.where(stays, value, 0.0)
                high, low = split(
                    (plane[:, :, half * 128 : half * 128 + 128] * push[None]).reshape(layers * rows, 128)
                )
                where = pl.ds(axis * layers * rows, layers * rows)
                push_high[where, half * 128 : half * 128 + 128] = high
                push_low[where, half * 128 : half * 128 + 128] = low
        patch = (
            dots(push_high[...], along_high, ((1,), (1,)))
            + dots(push_low[...], along_high, ((1,), (1,)))
            + dots(push_high[...], along_low, ((1,), (1,)))
        ).reshape(3, layers, rows, lanes)
        return patch

    spread_ref[...] = pair(0)

    def step(number, carry):
        spread_ref[...] += pair(number)
        return carry

    lax.fori_loop(1, blocks // 2, step, 0)


def force_sides(levels):
    if levels == 2:
        return [("up", 0, 1, 0), ("down", 1, 0, 0)]
    return [("up", None, None, 0), ("down", None, None, 1)]


GROUP = 6 * 8


def group_at(way_z, way_y):
    return (way_z + 1) * 3 + way_y + 1


def message_rows(depth):
    return [8 * 8, 2 * 4 * depth, 4 * depth, 2 * 8, 8]


def pack_body(
    levels, level_ref, dest_ref, spread_ref, state_ref, own_ref, side_ref,
    to_levels, north_ref, south_ref, north_levels, south_levels, outbox, strip, taken,
):
    depth, height, width = own_ref.shape[1:]
    level = level_ref[0]
    layers, rows = depth + 3, height + 8
    lane = lax.broadcasted_iota(jnp.int32, (rows, 128), 1)
    for layer in range(layers):
        value = jnp.zeros((rows, 128), jnp.float32)
        for axis in range(3):
            here = (lane >= 4 * axis) & (lane < 4 * axis + 3)
            value = jnp.where(here, lane_roll(spread_ref[axis, layer, :, width:], 4 * axis + 1), value)
        strip[layer] = value
    for code in range(27):
        taken[code] = 0
    outbox[...] = jnp.zeros_like(outbox)
    for block in range(state_ref.shape[0]):
        code = dest_ref[block]

        @pl.when(code != 13)
        def _():
            rank = taken[code]
            outbox[code * CAP + rank] = state_ref[block]
            taken[code] = rank + 1

    def force(part, layer, cut):
        return spread_ref[part, layer, cut, 0:width] if part < 3 else strip[layer, cut, :]

    def blocks(target, way_z, way_y):
        base = target.shape[0] - GROUP
        for slot in range(6):
            target[base + 8 * slot : base + 8 * slot + 8, :] = outbox[6 * group_at(way_z, way_y) + slot]

    main, north, south = slice(0, height), slice(height, height + 2), slice(rows - 1, rows)
    for part in range(4):
        for layer in range(depth):
            own_ref[part, layer] = force(part, layer + 1, main)
            at = part * depth + layer
            north_ref[2 * at : 2 * at + 2, :] = force(part, layer + 1, north)
            south_ref[at : at + 1, :] = force(part, layer + 1, south)
    blocks(north_ref, 0, 1)
    blocks(south_ref, 0, -1)
    for slot in range(2):
        side_ref[slot] = outbox[6 * group_at(0, 0) + slot]
        side_ref[2 + slot] = outbox[6 * group_at(0, 0) + 4 + slot]
    for kind, sender, _, slot in force_sides(levels):

        def pack(kind=kind, slot=slot):
            for part in range(4):
                for step in range(2 if kind == "up" else 1):
                    layer = depth + 1 + step if kind == "up" else 0
                    at = 2 * part + step
                    to_levels[slot][8 * at : 8 * at + 8, :] = force(part, layer, main)
                    north_levels[slot][2 * at : 2 * at + 2, :] = force(part, layer, north)
                    south_levels[slot][at : at + 1, :] = force(part, layer, south)
            way = 1 if kind == "up" else -1
            blocks(to_levels[slot], way, 0)
            blocks(north_levels[slot], way, 1)
            blocks(south_levels[slot], way, -1)

        guarded(level, sender, pack)


def main_body(levels, level_ref, counts_ref, dest_ref, *rest):
    slots = len(rim_sizes(levels))
    posts_ref, low_ref, high_ref = rest[:3]
    rims, low_rims, high_rims = (rest[3 + slots * at : 3 + slots * at + slots] for at in range(3))
    rest = rest[3 + 3 * slots :]
    above_ref, below_ref, speed_ref, frac_ref, home_ref = rest[:5]
    pops_ref, own_ref, stay_ref, side_ref, north_ref, south_ref = rest[5:11]
    to_levels, north_levels, south_levels = (rest[11 + slots * at : 11 + slots * at + slots] for at in range(3))
    rest = rest[11 + 3 * slots :]
    vel_ref, spread_ref, state_ref, outbox, strip, taken = rest[:6]
    steps_body(
        levels, level_ref, posts_ref, low_ref, high_ref, rims, low_rims, high_rims, above_ref, below_ref,
        pops_ref, vel_ref, *rest[6:11],
    )
    droplet_body(
        posts_ref.shape[1:], counts_ref, dest_ref, vel_ref, speed_ref, frac_ref, home_ref,
        spread_ref, stay_ref, state_ref, *rest[11:],
    )
    pack_body(
        levels, level_ref, dest_ref, spread_ref, state_ref, own_ref, side_ref,
        to_levels, north_ref, south_ref, north_levels, south_levels, outbox, strip, taken,
    )


def gather_body(levels, level_ref, own_ref, side_ref, *rest):
    depth, height, width = own_ref.shape[1:]
    slots = len(rim_sizes(levels))
    north_ref, south_ref = rest[:2]
    from_levels, north_levels, south_levels = (rest[2 + slots * at : 2 + slots * at + slots] for at in range(3))
    force_ref, right_ref, left_ref, total = rest[2 + 3 * slots :]
    base = depth * height
    total[...] = own_ref[...]
    right_ref[base:, :] = jnp.zeros((right_ref.shape[0] - base, width), jnp.float32)
    left_ref[base:, :] = jnp.zeros((left_ref.shape[0] - base, width), jnp.float32)
    last = slice(height - 1, height)
    for part in range(4):
        for layer in range(depth):
            at = part * depth + layer
            total[part, layer, 0:2, :] += north_ref[2 * at : 2 * at + 2, :]
            total[part, layer, last, :] += south_ref[at : at + 1, :]

    def blocks(source, way_z, way_y):
        at = base + 16 * group_at(way_z, way_y)
        start = source.shape[0] - GROUP
        left_ref[at : at + 16, :] = source[start : start + 16, :]
        right_ref[at : at + 16, :] = source[start + 32 : start + 48, :]

    at = base + 16 * group_at(0, 0)
    for slot in range(2):
        left_ref[at + 8 * slot : at + 8 * slot + 8, :] = side_ref[slot]
        right_ref[at + 8 * slot : at + 8 * slot + 8, :] = side_ref[2 + slot]
    blocks(north_ref, 0, 1)
    blocks(south_ref, 0, -1)
    for kind, _, receiver, slot in force_sides(levels):

        def take(kind=kind, slot=slot):
            for part in range(4):
                for step in range(2 if kind == "up" else 1):
                    layer = step if kind == "up" else depth - 1
                    at = 2 * part + step
                    total[part, layer] += from_levels[slot][8 * at : 8 * at + 8, :]
                    total[part, layer, 0:2, :] += north_levels[slot][2 * at : 2 * at + 2, :]
                    total[part, layer, last, :] += south_levels[slot][at : at + 1, :]
            way = 1 if kind == "up" else -1
            blocks(from_levels[slot], way, 0)
            blocks(north_levels[slot], way, 1)
            blocks(south_levels[slot], way, -1)

        guarded(level_ref[0], receiver, take)
    for layer in range(depth):
        for axis in range(3):
            force_ref[axis, layer] = total[axis, layer]
        for target in (right_ref, left_ref):
            target[layer * height : layer * height + height, :] = total[3, layer]


def last_body(levels, level_ref, part_ref, stay_ref, *rest):
    depth, height, width = part_ref.shape[1:]
    slots = len(rim_sizes(levels))
    north_ref, south_ref = rest[:2]
    from_levels, north_levels, south_levels = (rest[2 + slots * at : 2 + slots * at + slots] for at in range(3))
    right_ref, left_ref, force_ref, arrived_ref = rest[2 + 3 * slots :]
    blocks = stay_ref.shape[1]
    base = depth * height
    lane = lax.broadcasted_iota(jnp.int32, (height, 128), 1)
    for layer in range(depth):
        rows = slice(layer * height, layer * height + height)
        before, after = right_ref[rows, :128], left_ref[rows, :128]
        for axis in range(3):
            first = jnp.where(lane < 2, lane_roll(before, -4 * axis - 1), 0.0)
            final = jnp.where(lane == 127, lane_roll(after, 127 - 4 * axis), 0.0)
            force_ref[axis, layer] = part_ref[axis, layer]
            force_ref[axis, layer, :, 0:128] += first
            force_ref[axis, layer, :, width - 128 : width] += final
    arrived_ref[:, 0:blocks, :] = stay_ref[...]

    def put(source, start, way_z, way_y, way_x):
        code = group_at(way_z, way_y) * 3 + way_x + 1
        at = blocks + CAP * (code if code < 13 else code - 1)
        for slot in range(CAP):
            for axis in range(6):
                if source is None:
                    value = jnp.zeros((1, 128), jnp.float32)
                else:
                    value = source[start + 8 * slot + axis : start + 8 * slot + axis + 1, :]
                arrived_ref[axis, at + slot : at + slot + 1, :] = value

    for way_z in (-1, 0, 1):
        for way_y in (-1, 0, 1):
            for way_x, source in ((1, right_ref), (-1, left_ref)):
                put(source, base + 16 * group_at(way_z, way_y), way_z, way_y, way_x)
    middle = 16

    def put_group(source, way_z, way_y):
        put(source, None if source is None else source.shape[0] - GROUP + middle, way_z, way_y, 0)

    put_group(north_ref, 0, 1)
    put_group(south_ref, 0, -1)
    for kind, _, receiver, slot in force_sides(levels):
        way = 1 if kind == "up" else -1

        def take(way=way, slot=slot):
            put_group(from_levels[slot], way, 0)
            put_group(north_levels[slot], way, 1)
            put_group(south_levels[slot], way, -1)

        def clear(way=way):
            for way_y in (-1, 0, 1):
                put_group(None, way, way_y)

        guarded(level_ref[0], receiver, take)
        if receiver is not None:
            guarded(level_ref[0], 1 - receiver, clear)


def local(pops, coarse_pops, interface, drop_vel, drop_frac, home, counts, dest):
    level = lax.axis_index("gz").astype(jnp.int32).reshape(1)
    levels = lax.axis_size("gz")
    depth, height, width = interface.shape
    blocks = home.shape[0]
    kinds = ["up", "down"][: len(rim_sizes(levels))]
    slots = len(kinds)
    given = wide_exchange(level, pops, coarse_pops, interface)
    layers, rows, lanes = depth + 3, height + 8, width + 128
    flat = 3 * layers * rows
    deep = depth + LOW + HIGH
    sizes = [(count + GROUP, width) for count in message_rows(depth)]
    outs = call(
        functools.partial(main_body, levels),
        [pops.shape, (4, depth, height, width), (6, blocks, 128), (4, 8, 128), sizes[1], sizes[2]]
        + [sizes[0]] * slots
        + [sizes[3]] * slots
        + [sizes[4]] * slots,
        [given[0], counts, dest] + given[1:] + [drop_vel, drop_frac, home],
        3,
        [
            pltpu.VMEM((3, layers, rows, lanes), jnp.float32),
            pltpu.VMEM((3, layers, rows, lanes), jnp.float32),
            pltpu.VMEM((blocks, 8, 128), jnp.float32),
            pltpu.VMEM((27 * CAP, 8, 128), jnp.float32),
            pltpu.VMEM((layers, rows, 128), jnp.float32),
            pltpu.SMEM((27,), jnp.int32),
            pltpu.VMEM((channels, deep, rows, lanes), jnp.float32),
            pltpu.VMEM((deep, rows, 128), jnp.float32),
            pltpu.VMEM((deep, rows, 128), jnp.float32),
            pltpu.VMEM((19, rows, lanes), jnp.float32),
            pltpu.VMEM((19, deep - 2, rows, lanes), jnp.float32),
            pltpu.VMEM((flat, lanes), jnp.bfloat16),
            pltpu.VMEM((flat, lanes), jnp.bfloat16),
            pltpu.VMEM((lanes, 256), jnp.bfloat16),
            pltpu.VMEM((lanes, 256), jnp.bfloat16),
            pltpu.VMEM((flat, 256), jnp.bfloat16),
            pltpu.VMEM((flat, 256), jnp.bfloat16),
            pltpu.VMEM((layers, rows, 256), jnp.float32),
        ],
    )
    state, own, stay, side, north, south = outs[:6]
    to_levels, north_levels, south_levels = (outs[6 + slots * at : 6 + slots * at + slots] for at in range(3))
    received = [shifted(north, "gy", 1), shifted(south, "gy", -1)]
    received += [to_level(value, kind, levels) for value, kind in zip(to_levels, kinds)]
    received += [to_level(value, kind, levels, "gy", 1) for value, kind in zip(north_levels, kinds)]
    received += [to_level(value, kind, levels, "gy", -1) for value, kind in zip(south_levels, kinds)]
    side_rows = (depth * height + 9 * 16, width)
    part, right, left = call(
        functools.partial(gather_body, levels),
        [(3, depth, height, width), side_rows, side_rows],
        [level, own, side] + received,
        1,
        [pltpu.VMEM((4, depth, height, width), jnp.float32)],
    )
    force, arrived = call(
        functools.partial(last_body, levels),
        [(3, depth, height, width), (6, blocks + 26 * CAP, 128)],
        [level, part, stay] + received + [shifted(right, "gx", 1), shifted(left, "gx", -1)],
    )
    return state, force, arrived


def solution(mesh):
    return jax.shard_map(
        local,
        mesh=mesh,
        in_specs=(
            P(None, "gz", "gy", "gx"),
            P(None, "gz", "gy", "gx"),
            P("gz", "gy", "gx"),
            P(None, ("gx", "gy", "gz"), None),
            P(None, ("gx", "gy", "gz"), None),
            P(("gx", "gy", "gz"), None),
            P(("gx", "gy", "gz")),
            P(("gx", "gy", "gz")),
        ),
        out_specs=(
            P(None, "gz", "gy", "gx"),
            P(None, "gz", "gy", "gx"),
            P(None, ("gx", "gy", "gz"), None),
        ),
        check_vma=False,
    )
```

```python
import functools
import math

import jax
import jax.numpy as jnp
import numpy as np
from jax import lax
from jax.experimental import pallas as pl
from jax.experimental.pallas import tpu as pltpu
from jax.sharding import PartitionSpec as P

CAP = 2


lattice = np.array(
    [
        [0, 0, 0],
        [1, 0, 0],
        [-1, 0, 0],
        [0, 1, 0],
        [0, -1, 0],
        [0, 0, 1],
        [0, 0, -1],
        [1, 1, 0],
        [-1, -1, 0],
        [1, -1, 0],
        [-1, 1, 0],
        [1, 0, 1],
        [-1, 0, -1],
        [1, 0, -1],
        [-1, 0, 1],
        [0, 1, 1],
        [0, -1, -1],
        [0, 1, -1],
        [0, -1, 1],
    ]
)
weights_table = np.array([1.0 / 3.0] + [1.0 / 18.0] * 6 + [1.0 / 36.0] * 12)
opposite = [0, 2, 1, 4, 3, 6, 5, 8, 7, 10, 9, 12, 11, 14, 13, 16, 15, 18, 17]
inverse_tau = 0.8
relax = 0.5
couple = 8.0


def call(body, outs, ins, scalars=1, scratch=(), cost=None):
    vmem = pl.BlockSpec(memory_space=pltpu.VMEM)
    return pl.pallas_call(
        body,
        out_shape=[jax.ShapeDtypeStruct(shape, jnp.float32) for shape in outs],
        in_specs=[pl.BlockSpec(memory_space=pltpu.SMEM)] * scalars + [vmem] * (len(ins) - scalars),
        out_specs=[vmem] * len(outs),
        scratch_shapes=list(scratch),
        cost_estimate=cost,
        compiler_params=pltpu.CompilerParams(vmem_limit_bytes=56 * 1024 * 1024),
    )(*ins)


ways = [tuple(int(part) for part in lattice[index][::-1]) for index in range(19)] + [(0, 0, 0)]
channels = len(ways)
LOW = 3
HIGH = 4


def low_reach(way):
    return 2 + way


def high_reach(way):
    return 3 - way


def rim(kind):
    count, reach = (LOW, low_reach) if kind == "low" else (HIGH, high_reach)
    return [
        (step, channel)
        for step in range(1, count + 1)
        for channel in range(channels)
        if step <= reach(ways[channel][0])
    ]


def rim_count(kind):
    return LOW if kind == "low" else HIGH


def rim_sides(levels):
    if levels == 2:
        return [("low", 1, 0, 0), ("high", 0, 1, 0)]
    return [("low", None, None, 0), ("high", None, None, 1)]


def rim_sizes(levels):
    sizes = [len(rim(kind)) for kind, _, _, _ in rim_sides(levels)]
    return [max(sizes)] if levels == 2 else sizes


def guarded(level, guard, action):
    if guard is None:
        action()
    else:
        pl.when(level == guard)(action)


def row_places(cells):
    places, high_at, low_at = [], 0, 0
    for channel, bounces in cells:
        way_z, way, _ = ways[channel]
        above, below = high_reach(way), low_reach(way)
        if bounces and way_z != 0:
            above, below = max(above, HIGH - 1), max(below, LOW - 1)
        places.append((high_at, low_at, above, below))
        high_at, low_at = high_at + above, low_at + below
    return places, (-(-high_at // 8) * 8, -(-low_at // 8) * 8)


def own_rows(depth):
    cells = [(layer, channel) for layer in range(depth) for channel in range(channels)]
    places, sizes = row_places([(channel, layer in (0, depth - 1)) for layer, channel in cells])
    return [(layer, channel, place) for (layer, channel), place in zip(cells, places)], sizes


def rim_rows(kind):
    places, sizes = row_places([(channel, False) for _, channel in rim(kind)])
    return [(step, channel, place) for (step, channel), place in zip(rim(kind), places)], sizes


def rim_row_sizes(levels):
    sizes = [rim_rows(kind)[1] for kind, _, _, _ in rim_sides(levels)]
    return [tuple(max(part) for part in zip(*sizes))] if levels == 2 else sizes


def moments(cells):
    density = cells[0] * float(weights_table[0])
    moment = [None, None, None]
    face, edge = float(weights_table[1]), float(weights_table[7])
    edge_sum = cells[7]
    for index in range(8, 19):
        edge_sum = edge_sum + cells[index]
    face_sum = cells[1]
    for index in range(2, 7):
        face_sum = face_sum + cells[index]
    density = density + face * face_sum + edge * edge_sum
    for axis in range(3):
        total = {}
        for group, indices in ((face, range(1, 7)), (edge, range(7, 19))):
            plus, minus = None, None
            for index in indices:
                way = int(lattice[index][axis])
                if way == 1:
                    plus = cells[index] if plus is None else plus + cells[index]
                if way == -1:
                    minus = cells[index] if minus is None else minus + cells[index]
            total[group] = plus - minus
        moment[axis] = face * total[face] + edge * total[edge]
    return density, moment


def relaxed(cells):
    density, moment = moments(cells)
    inverse = 1.0 / density
    flow = [part * inverse for part in moment]
    square = flow[0] * flow[0] + flow[1] * flow[1] + flow[2] * flow[2]
    scale = density * inverse_tau
    base = scale * (1.0 - 1.5 * square)
    keep = 1.0 - inverse_tau
    posts = [None] * 19
    posts[0] = keep * cells[0] + base
    for index in range(1, 19, 2):
        along = None
        for axis in range(3):
            way = int(lattice[index][axis])
            if way != 0:
                part = flow[axis] if way == 1 else -flow[axis]
                along = part if along is None else along + part
        odd = 3.0 * scale * along
        even = base + (4.5 * scale) * (along * along)
        posts[index] = keep * cells[index] + (even + odd)
        posts[index + 1] = keep * cells[index + 1] + (even - odd)
    return posts


def lane_roll(value, shift):
    shift = shift % value.shape[-1]
    return value if shift == 0 else pltpu.roll(value, shift, value.ndim - 1)


def first_body(levels, level_ref, pops_ref, coarse_ref, interface_ref, posts_ref, down_ref, up_ref, *outs):
    depth, height, width = interface_ref.shape
    slots = len(rim_sizes(levels))
    rims, down_rims, up_rims = (outs[slots * at : slots * at + slots] for at in range(3))
    own = own_rows(depth)[0]
    for layer in range(depth):
        mask = interface_ref[layer]
        inside = mask == 1
        posts = relaxed([pops_ref[index, layer] for index in range(19)])
        posts = [
            jnp.where(inside, coarse_ref[index, layer].astype(jnp.float32), posts[index])
            for index in range(19)
        ] + [mask.astype(jnp.float32)]
        for channel in range(channels):
            posts_ref[channel, layer] = posts[channel]
            down_at, up_at, down, up = own[layer * channels + channel][2]
            down_ref[down_at : down_at + down, :] = posts[channel][:down, :]
            up_ref[up_at : up_at + up, :] = posts[channel][height - up :, :]
    for kind, _, sender, slot in rim_sides(levels):

        def pack(kind=kind, slot=slot):
            for at, (step, channel, place) in enumerate(rim_rows(kind)[0]):
                cells = posts_ref[channel, depth - step if kind == "low" else step - 1]
                rims[slot][at] = cells
                down_at, up_at, down, up = place
                down_rims[slot][down_at : down_at + down, :] = cells[:down, :]
                up_rims[slot][up_at : up_at + up, :] = cells[height - up :, :]

        guarded(level_ref[0], sender, pack)


def unpack(levels, level, posts_ref, above_ref, below_ref, rims, above_rims, below_rims, ext):
    depth, height = posts_ref.shape[1:3]
    rows = height + 8

    def put(channel, at, cells, place, above, below):
        above_at, below_at, above_rows, below_rows = place
        ext[channel, at, :height, :] = cells
        ext[channel, at, height : height + above_rows, :] = above[above_at : above_at + above_rows, :]
        ext[channel, at, rows - below_rows : rows, :] = below[below_at : below_at + below_rows, :]

    for layer, channel, place in own_rows(depth)[0]:
        put(channel, LOW + layer, posts_ref[channel, layer], place, above_ref, below_ref)
    for kind, receiver, _, slot in rim_sides(levels):

        def take(kind=kind, slot=slot):
            for at, (step, channel, place) in enumerate(rim_rows(kind)[0]):
                layer = LOW - step if kind == "low" else LOW + depth + step - 1
                put(channel, layer, rims[slot][at], place, above_rims[slot], below_rims[slot])

        guarded(level, receiver, take)


def split_given(levels, rest):
    slots = len(rim_sizes(levels))
    parts = [rest[3 + slots * at : 3 + slots * at + slots] for at in range(3)]
    return rest[:3], parts, rest[3 + 3 * slots :]


def strip_body(levels, level_ref, *rest):
    (posts_ref, above_ref, below_ref), parts, (strip_ref, ext) = split_given(levels, rest)
    unpack(levels, level_ref[0], posts_ref, above_ref, below_ref, *parts, ext)
    layers, rows, width = ext.shape[1:]
    lane = lax.broadcasted_iota(jnp.int32, (rows, 128), 1)

    def channel_step(channel, carry):
        value = jnp.zeros((rows, 128), jnp.float32)
        for layer in range(layers):
            cells = ext[channel, layer]
            if width > 128:
                cells = jnp.where(lane < 64, cells[:, :128], cells[:, width - 128 :])
            value = jnp.where(lane // 8 == layer, lane_roll(cells, 8 * layer + 4), value)
        strip_ref[channel] = value
        return carry

    lax.fori_loop(0, channels, channel_step, 0)


def inner_body(levels, level_ref, *rest):
    (posts_ref, above_ref, below_ref), parts, rest = split_given(levels, rest)
    pops_ref, vel_ref, ext, pulled, second = rest
    level = level_ref[0]
    unpack(levels, level, posts_ref, above_ref, below_ref, *parts, ext)
    depth, height, width = posts_ref.shape[1:]
    rows = height + 8

    def pull(source, layer, at):
        bottom = (level == 0) & (layer == 0)
        top = (level == levels - 1) & (layer == depth - 1)
        for index in range(19):
            way_z, way_y, way_x = ways[index]
            value = source[index, at - way_z]
            if way_x != 0:
                value = pltpu.roll(value, way_x % width, 1)
            if way_y != 0:
                value = pltpu.roll(value, way_y % rows, 0)
            if way_z != 0:
                wall = bottom if way_z == 1 else top
                value = jnp.where(wall, source[opposite[index], at], value)
            pulled[index] = value

    tiles = [
        (slice(row, row + 8), slice(col, col + 128))
        for row in range(0, rows, 8)
        for col in range(0, width, 128)
    ]

    def first_step(number, carry):
        at = number + 1
        pull(ext, at - LOW, at)
        for tile in tiles:
            posts = relaxed([pulled[(index, *tile)] for index in range(19)])
            inside = ext[(19, at, *tile)] > 0.5
            for index in range(19):
                second[(index, number, *tile)] = jnp.where(inside, ext[(index, at, *tile)], posts[index])
        return carry

    lax.fori_loop(0, depth + LOW + HIGH - 2, first_step, 0)

    def second_step(number, carry):
        pull(second, number - 1, number + 1)
        for tile in tiles:
            density, moment = moments([pulled[(index, *tile)] for index in range(19)])
            inverse = 1.0 / density
            for axis in range(3):
                vel_ref[(axis, number, *tile)] = moment[axis] * inverse
        return carry

    def second_inner(number, carry):
        second_step(number, carry)
        for index in range(19):
            pops_ref[index, number - 1] = pulled[index, :height, :]
        return carry

    lax.fori_loop(0, 1, second_step, 0)
    lax.fori_loop(1, depth + 1, second_inner, 0)
    lax.fori_loop(depth + 1, depth + 3, second_step, 0)


def edge_body(
    levels, level_ref, strip_ref, left_ref, right_ref, inner_pops, inner_vel,
    pops_ref, vel_ref, sides, pulled, second,
):
    depth, height, width = pops_ref.shape[1:]
    rows, lanes = height + 8, width + 128
    level = level_ref[0]
    lane = lax.broadcasted_iota(jnp.int32, (rows, 128), 1)
    before = lane % 8 < 4
    bottom = (lane // 8 == LOW) & (level == 0)
    top = (lane // 8 == LOW + depth - 1) & (level == levels - 1)
    for channel in range(channels):
        own = strip_ref[channel]
        sides[0, channel] = jnp.where(before, left_ref[channel], own)
        sides[1, channel] = jnp.where(before, own, right_ref[channel])

    def pull(source, side, target):
        for index in range(19):
            way_z, way_y, way_x = ways[index]
            value = lane_roll(source[side, index], 8 * way_z + way_x)
            if way_y != 0:
                value = pltpu.roll(value, way_y % rows, 0)
            if way_z != 0:
                value = jnp.where(bottom if way_z == 1 else top, source[side, opposite[index]], value)
            target[side, index] = value

    speeds = [[], []]
    for side in range(2):
        pull(sides, side, pulled)
        for row in range(0, rows, 8):
            cut = slice(row, row + 8)
            posts = relaxed([pulled[side, index, cut] for index in range(19)])
            inside = sides[side, 19, cut] > 0.5
            for index in range(19):
                second[side, index, cut] = jnp.where(inside, sides[side, index, cut], posts[index])
        pull(second, side, pulled)
        density, moment = moments([pulled[side, index] for index in range(19)])
        inverse = 1.0 / density
        speeds[side] = [part * inverse for part in moment]

    near = lane[:height]
    near = (near < 2) | (near >= 126)
    front = before[:height]
    for index in range(19):
        value = jnp.where(front, pulled[1, index, :height], pulled[0, index, :height])
        for layer in range(depth):
            turned = lane_roll(value, -(8 * (layer + LOW) + 4))
            for col in range(0, width, 128):
                cells = inner_pops[index, layer, :, col : col + 128]
                if col == 0 or col == width - 128:
                    mask = near if width == 128 else near & ((lane[:height] < 64) == (col == 0))
                    cells = jnp.where(mask, turned, cells)
                pops_ref[index, layer, :, col : col + 128] = cells
    row = lax.broadcasted_iota(jnp.int32, (rows, 128), 0)
    valid = (row < height + 2) | (row == rows - 1)
    beyond = (lane < 2) | (lane == 127)
    for axis in range(3):
        main = jnp.where(before, speeds[1][axis], speeds[0][axis])
        rest = jnp.where(before, speeds[0][axis], speeds[1][axis])
        for layer in range(depth + 3):
            keep = valid
            if layer == 0:
                keep = valid & (level != 0)
            if layer > depth:
                keep = valid & (level != levels - 1)
            shift = -(8 * (layer - 1 + LOW) + 4)
            turned = lane_roll(main, shift)
            for col in range(0, width, 128):
                cells = inner_vel[axis, layer, :, col : col + 128]
                if col == 0 or col == width - 128:
                    mask = (lane < 2) & (col == 0) | (lane >= 126) & (col == width - 128)
                    cells = jnp.where(mask, turned, cells)
                vel_ref[axis, layer, :, col : col + 128] = jnp.where(keep, cells, 0.0)
            vel_ref[axis, layer, :, width:] = jnp.where(keep & beyond, lane_roll(rest, shift), 0.0)


def shifted(value, axis, step):
    count = lax.axis_size(axis)
    return lax.ppermute(value, axis, [(i, (i + step) % count) for i in range(count)])


def to_level(value, kind, levels, side=None, step=0):
    pairs = []
    for at in range(levels):
        other = 1 - at if levels == 2 else at + 1 if kind in ("low", "up") else at - 1
        if 0 <= other < levels:
            pairs.append((at, other))
    if side is None:
        return lax.ppermute(value, "gz", pairs)
    count = lax.axis_size(side)
    return lax.ppermute(
        value,
        (side, "gz"),
        [
            (brick * levels + at, (brick + step) % count * levels + other)
            for brick in range(count)
            for at, other in pairs
        ],
    )


def wide_exchange(level, pops, coarse_pops, interface):
    levels = lax.axis_size("gz")
    depth, height, width = interface.shape
    sizes = rim_sizes(levels)
    slots = len(sizes)
    kinds = ["low", "high"][:slots]
    down_sizes, up_sizes = zip(*rim_row_sizes(levels))
    outs = call(
        functools.partial(first_body, levels),
        [(channels, depth, height, width)]
        + [(size, width) for size in own_rows(depth)[1]]
        + [(size, height, width) for size in sizes]
        + [(size, width) for size in down_sizes + up_sizes],
        [level, pops, coarse_pops, interface],
    )
    posts, down, up = outs[:3]
    rims, down_rims, up_rims = (outs[3 + slots * at : 3 + slots * at + slots] for at in range(3))
    given = [level, posts, shifted(down, "gy", -1), shifted(up, "gy", 1)]
    given += [to_level(value, kind, levels) for value, kind in zip(rims, kinds)]
    given += [to_level(value, kind, levels, "gy", -1) for value, kind in zip(down_rims, kinds)]
    given += [to_level(value, kind, levels, "gy", 1) for value, kind in zip(up_rims, kinds)]
    deep, rows = depth + LOW + HIGH, height + 8
    ext = pltpu.VMEM((channels, deep, rows, width), jnp.float32)
    (strip,) = call(functools.partial(strip_body, levels), [(channels, rows, 128)], given, 1, [ext])
    left, right = shifted(strip, "gx", 1), shifted(strip, "gx", -1)
    inner_pops, inner_vel = call(
        functools.partial(inner_body, levels),
        [pops.shape, (3, depth + 3, rows, width)],
        given,
        1,
        [
            ext,
            pltpu.VMEM((19, rows, width), jnp.float32),
            pltpu.VMEM((19, deep - 2, rows, width), jnp.float32),
        ],
        pl.CostEstimate(flops=10**8, bytes_accessed=1 << 22, transcendentals=0),
    )
    return [strip, left, right, inner_pops, inner_vel]


def phis(frac):
    angle = frac * (0.5 * math.pi)
    sine = 0.25 * jnp.sin(angle)
    cosine = 0.25 * jnp.cos(angle)
    return (0.25 - sine, 0.25 + cosine, 0.25 + sine, 0.25 - cosine)


def split(value):
    high = value.astype(jnp.bfloat16)
    return high, (value - high.astype(jnp.float32)).astype(jnp.bfloat16)


def pick(step, parts):
    value = jnp.where(step == 0, parts[0], 0.0)
    for index in range(1, 4):
        value = jnp.where(step == index, parts[index], value)
    return value


def dots(left, right, dims):
    return lax.dot_general(left, right, (dims, ((), ())), preferred_element_type=jnp.float32)


def droplet_body(
    size, counts_ref, dest_ref, vel_ref, speed_ref, frac_ref, home_ref, spread_ref, stay_ref, state_ref,
    vel_high, vel_low, row_high, row_low, push_high, push_low, plane_ref,
):
    depth, height, width = size
    blocks = home_ref.shape[0]
    layers, rows, lanes = depth + 3, height + 8, width + 128
    high, low = split(vel_ref[...].reshape(3 * layers * rows, lanes))
    vel_high[...] = high
    vel_low[...] = low
    row_high[...] = jnp.zeros_like(row_high)
    row_low[...] = jnp.zeros_like(row_low)
    used = width + 16
    span_x = lax.broadcasted_iota(jnp.int32, (used, 128), 0) + 1
    span_y = lax.broadcasted_iota(jnp.int32, (rows, 128), 0)
    span_y = jnp.where(span_y >= height + 4, span_y - rows, span_y) + 1
    span_z = lax.broadcasted_iota(jnp.int32, (layers, 128), 0)
    last = lax.broadcasted_iota(jnp.int32, (16, 128), 0) == 15
    slots = lax.broadcasted_iota(jnp.int32, (1, 128), 1)

    def pair(number):
        for half in range(2):
            block = 2 * number + half
            side = pl.ds(half * 128, 128)
            cell = home_ref[pl.ds(block, 1), :]
            cell_x = cell & (width - 1) if width & (width - 1) == 0 else cell % width
            cell_y = cell // width % height
            cell_z = cell // (width * height)
            part_x = phis(frac_ref[0, pl.ds(block, 1), :])
            part_y = phis(frac_ref[1, pl.ds(block, 1), :])
            part_z = phis(frac_ref[2, pl.ds(block, 1), :])
            high, low = split(pick(span_x - cell_x, part_x))
            row_high[0:used, side] = high
            row_low[0:used, side] = low
            high, low = split(jnp.where(last & (cell_x == 0), part_x[0], 0.0))
            row_high[lanes - 16 : lanes, side] = high
            row_low[lanes - 16 : lanes, side] = low
            weight_y = pick(span_y - cell_y, part_y)
            weight_z = pick(span_z - cell_z, part_z)
            for layer in range(layers):
                plane_ref[layer, :, side] = weight_y * weight_z[layer : layer + 1, :]
        along_high = row_high[...]
        along_low = row_low[...]
        sums = (
            dots(vel_high[...], along_high, ((1,), (0,)))
            + dots(vel_low[...], along_high, ((1,), (0,)))
            + dots(vel_high[...], along_low, ((1,), (0,)))
        ).reshape(3, layers, rows, 256)
        plane = plane_ref[...]
        sampled = jnp.sum(jnp.sum(sums * plane[None], axis=1), axis=1)
        for half in range(2):
            block = 2 * number + half
            live = slots < counts_ref[block]
            for axis in range(3):
                sample = sampled[axis : axis + 1, half * 128 : half * 128 + 128]
                speed = speed_ref[axis, pl.ds(block, 1), :]
                frac = frac_ref[axis, pl.ds(block, 1), :]
                moved = speed + relax * (sample - speed)
                push = jnp.where(live, couple * (moved - sample), 0.0)
                stays = live & (dest_ref[block] == 13)
                for at, value in ((axis, moved), (3 + axis, frac + moved)):
                    state_ref[block, at : at + 1, :] = jnp.where(live, value, 0.0)
                    stay_ref[at, pl.ds(block, 1), :] = jnp.where(stays, value, 0.0)
                high, low = split(
                    (plane[:, :, half * 128 : half * 128 + 128] * push[None]).reshape(layers * rows, 128)
                )
                where = pl.ds(axis * layers * rows, layers * rows)
                push_high[where, half * 128 : half * 128 + 128] = high
                push_low[where, half * 128 : half * 128 + 128] = low
        patch = (
            dots(push_high[...], along_high, ((1,), (1,)))
            + dots(push_low[...], along_high, ((1,), (1,)))
            + dots(push_high[...], along_low, ((1,), (1,)))
        ).reshape(3, layers, rows, lanes)
        return patch

    spread_ref[...] = pair(0)

    def step(number, carry):
        spread_ref[...] += pair(number)
        return carry

    lax.fori_loop(1, blocks // 2, step, 0)


def force_sides(levels):
    if levels == 2:
        return [("up", 0, 1, 0), ("down", 1, 0, 0)]
    return [("up", None, None, 0), ("down", None, None, 1)]


GROUP = 6 * 8


def group_at(way_z, way_y):
    return (way_z + 1) * 3 + way_y + 1


def message_rows(depth):
    return [8 * 8, 2 * 4 * depth, 4 * depth, 2 * 8, 8]


def pack_body(
    levels, level_ref, dest_ref, spread_ref, state_ref, own_ref, side_ref,
    to_levels, north_ref, south_ref, north_levels, south_levels, outbox, strip, taken,
):
    depth, height, width = own_ref.shape[1:]
    level = level_ref[0]
    layers, rows = depth + 3, height + 8
    lane = lax.broadcasted_iota(jnp.int32, (rows, 128), 1)
    for layer in range(layers):
        value = jnp.zeros((rows, 128), jnp.float32)
        for axis in range(3):
            here = (lane >= 4 * axis) & (lane < 4 * axis + 3)
            value = jnp.where(here, lane_roll(spread_ref[axis, layer, :, width:], 4 * axis + 1), value)
        strip[layer] = value
    for code in range(27):
        taken[code] = 0
    outbox[...] = jnp.zeros_like(outbox)
    for block in range(state_ref.shape[0]):
        code = dest_ref[block]

        @pl.when(code != 13)
        def _():
            rank = taken[code]
            outbox[code * CAP + rank] = state_ref[block]
            taken[code] = rank + 1

    def force(part, layer, cut):
        return spread_ref[part, layer, cut, 0:width] if part < 3 else strip[layer, cut, :]

    def blocks(target, way_z, way_y):
        base = target.shape[0] - GROUP
        for slot in range(6):
            target[base + 8 * slot : base + 8 * slot + 8, :] = outbox[6 * group_at(way_z, way_y) + slot]

    main, north, south = slice(0, height), slice(height, height + 2), slice(rows - 1, rows)
    for part in range(4):
        for layer in range(depth):
            own_ref[part, layer] = force(part, layer + 1, main)
            at = part * depth + layer
            north_ref[2 * at : 2 * at + 2, :] = force(part, layer + 1, north)
            south_ref[at : at + 1, :] = force(part, layer + 1, south)
    blocks(north_ref, 0, 1)
    blocks(south_ref, 0, -1)
    for slot in range(2):
        side_ref[slot] = outbox[6 * group_at(0, 0) + slot]
        side_ref[2 + slot] = outbox[6 * group_at(0, 0) + 4 + slot]
    for kind, sender, _, slot in force_sides(levels):

        def pack(kind=kind, slot=slot):
            for part in range(4):
                for step in range(2 if kind == "up" else 1):
                    layer = depth + 1 + step if kind == "up" else 0
                    at = 2 * part + step
                    to_levels[slot][8 * at : 8 * at + 8, :] = force(part, layer, main)
                    north_levels[slot][2 * at : 2 * at + 2, :] = force(part, layer, north)
                    south_levels[slot][at : at + 1, :] = force(part, layer, south)
            way = 1 if kind == "up" else -1
            blocks(to_levels[slot], way, 0)
            blocks(north_levels[slot], way, 1)
            blocks(south_levels[slot], way, -1)

        guarded(level, sender, pack)


def main_body(
    levels, level_ref, counts_ref, dest_ref, strip_ref, left_ref, right_ref, inner_pops, inner_vel,
    speed_ref, frac_ref, home_ref, pops_ref, own_ref, stay_ref, side_ref, north_ref, south_ref, *rest,
):
    slots = len(rim_sizes(levels))
    to_levels, north_levels, south_levels = (rest[slots * at : slots * at + slots] for at in range(3))
    rest = rest[3 * slots :]
    vel_ref, spread_ref, state_ref, outbox, strip, taken = rest[:6]
    edge_body(
        levels, level_ref, strip_ref, left_ref, right_ref, inner_pops, inner_vel, pops_ref, vel_ref, *rest[6:9]
    )
    droplet_body(
        pops_ref.shape[1:], counts_ref, dest_ref, vel_ref, speed_ref, frac_ref, home_ref,
        spread_ref, stay_ref, state_ref, *rest[9:],
    )
    pack_body(
        levels, level_ref, dest_ref, spread_ref, state_ref, own_ref, side_ref,
        to_levels, north_ref, south_ref, north_levels, south_levels, outbox, strip, taken,
    )


def gather_body(levels, level_ref, own_ref, side_ref, *rest):
    depth, height, width = own_ref.shape[1:]
    slots = len(rim_sizes(levels))
    north_ref, south_ref = rest[:2]
    from_levels, north_levels, south_levels = (rest[2 + slots * at : 2 + slots * at + slots] for at in range(3))
    force_ref, right_ref, left_ref, total = rest[2 + 3 * slots :]
    base = depth * height
    total[...] = own_ref[...]
    right_ref[base:, :] = jnp.zeros((right_ref.shape[0] - base, width), jnp.float32)
    left_ref[base:, :] = jnp.zeros((left_ref.shape[0] - base, width), jnp.float32)
    last = slice(height - 1, height)
    for part in range(4):
        for layer in range(depth):
            at = part * depth + layer
            total[part, layer, 0:2, :] += north_ref[2 * at : 2 * at + 2, :]
            total[part, layer, last, :] += south_ref[at : at + 1, :]

    def blocks(source, way_z, way_y):
        at = base + 16 * group_at(way_z, way_y)
        start = source.shape[0] - GROUP
        left_ref[at : at + 16, :] = source[start : start + 16, :]
        right_ref[at : at + 16, :] = source[start + 32 : start + 48, :]

    at = base + 16 * group_at(0, 0)
    for slot in range(2):
        left_ref[at + 8 * slot : at + 8 * slot + 8, :] = side_ref[slot]
        right_ref[at + 8 * slot : at + 8 * slot + 8, :] = side_ref[2 + slot]
    blocks(north_ref, 0, 1)
    blocks(south_ref, 0, -1)
    for kind, _, receiver, slot in force_sides(levels):

        def take(kind=kind, slot=slot):
            for part in range(4):
                for step in range(2 if kind == "up" else 1):
                    layer = step if kind == "up" else depth - 1
                    at = 2 * part + step
                    total[part, layer] += from_levels[slot][8 * at : 8 * at + 8, :]
                    total[part, layer, 0:2, :] += north_levels[slot][2 * at : 2 * at + 2, :]
                    total[part, layer, last, :] += south_levels[slot][at : at + 1, :]
            way = 1 if kind == "up" else -1
            blocks(from_levels[slot], way, 0)
            blocks(north_levels[slot], way, 1)
            blocks(south_levels[slot], way, -1)

        guarded(level_ref[0], receiver, take)
    for layer in range(depth):
        for axis in range(3):
            force_ref[axis, layer] = total[axis, layer]
        for target in (right_ref, left_ref):
            target[layer * height : layer * height + height, :] = total[3, layer]


def last_body(levels, level_ref, part_ref, stay_ref, *rest):
    depth, height, width = part_ref.shape[1:]
    slots = len(rim_sizes(levels))
    north_ref, south_ref = rest[:2]
    from_levels, north_levels, south_levels = (rest[2 + slots * at : 2 + slots * at + slots] for at in range(3))
    right_ref, left_ref, force_ref, arrived_ref = rest[2 + 3 * slots :]
    blocks = stay_ref.shape[1]
    base = depth * height
    lane = lax.broadcasted_iota(jnp.int32, (height, 128), 1)
    for layer in range(depth):
        rows = slice(layer * height, layer * height + height)
        before, after = right_ref[rows, :128], left_ref[rows, :128]
        for axis in range(3):
            first = jnp.where(lane < 2, lane_roll(before, -4 * axis - 1), 0.0)
            final = jnp.where(lane == 127, lane_roll(after, 127 - 4 * axis), 0.0)
            force_ref[axis, layer] = part_ref[axis, layer]
            force_ref[axis, layer, :, 0:128] += first
            force_ref[axis, layer, :, width - 128 : width] += final
    arrived_ref[:, 0:blocks, :] = stay_ref[...]

    def put(source, start, way_z, way_y, way_x):
        code = group_at(way_z, way_y) * 3 + way_x + 1
        at = blocks + CAP * (code if code < 13 else code - 1)
        for slot in range(CAP):
            for axis in range(6):
                if source is None:
                    value = jnp.zeros((1, 128), jnp.float32)
                else:
                    value = source[start + 8 * slot + axis : start + 8 * slot + axis + 1, :]
                arrived_ref[axis, at + slot : at + slot + 1, :] = value

    for way_z in (-1, 0, 1):
        for way_y in (-1, 0, 1):
            for way_x, source in ((1, right_ref), (-1, left_ref)):
                put(source, base + 16 * group_at(way_z, way_y), way_z, way_y, way_x)
    middle = 16

    def put_group(source, way_z, way_y):
        put(source, None if source is None else source.shape[0] - GROUP + middle, way_z, way_y, 0)

    put_group(north_ref, 0, 1)
    put_group(south_ref, 0, -1)
    for kind, _, receiver, slot in force_sides(levels):
        way = 1 if kind == "up" else -1

        def take(way=way, slot=slot):
            put_group(from_levels[slot], way, 0)
            put_group(north_levels[slot], way, 1)
            put_group(south_levels[slot], way, -1)

        def clear(way=way):
            for way_y in (-1, 0, 1):
                put_group(None, way, way_y)

        guarded(level_ref[0], receiver, take)
        if receiver is not None:
            guarded(level_ref[0], 1 - receiver, clear)


def local(pops, coarse_pops, interface, drop_vel, drop_frac, home, counts, dest):
    level = lax.axis_index("gz").astype(jnp.int32).reshape(1)
    levels = lax.axis_size("gz")
    depth, height, width = interface.shape
    blocks = home.shape[0]
    kinds = ["up", "down"][: len(rim_sizes(levels))]
    slots = len(kinds)
    given = wide_exchange(level, pops, coarse_pops, interface)
    layers, rows, lanes = depth + 3, height + 8, width + 128
    flat = 3 * layers * rows
    sizes = [(count + GROUP, width) for count in message_rows(depth)]
    outs = call(
        functools.partial(main_body, levels),
        [pops.shape, (4, depth, height, width), (6, blocks, 128), (4, 8, 128), sizes[1], sizes[2]]
        + [sizes[0]] * slots
        + [sizes[3]] * slots
        + [sizes[4]] * slots,
        [level, counts, dest] + given + [drop_vel, drop_frac, home],
        3,
        [
            pltpu.VMEM((3, layers, rows, lanes), jnp.float32),
            pltpu.VMEM((3, layers, rows, lanes), jnp.float32),
            pltpu.VMEM((blocks, 8, 128), jnp.float32),
            pltpu.VMEM((27 * CAP, 8, 128), jnp.float32),
            pltpu.VMEM((layers, rows, 128), jnp.float32),
            pltpu.SMEM((27,), jnp.int32),
            pltpu.VMEM((2, channels, rows, 128), jnp.float32),
            pltpu.VMEM((2, 19, rows, 128), jnp.float32),
            pltpu.VMEM((2, 19, rows, 128), jnp.float32),
            pltpu.VMEM((flat, lanes), jnp.bfloat16),
            pltpu.VMEM((flat, lanes), jnp.bfloat16),
            pltpu.VMEM((lanes, 256), jnp.bfloat16),
            pltpu.VMEM((lanes, 256), jnp.bfloat16),
            pltpu.VMEM((flat, 256), jnp.bfloat16),
            pltpu.VMEM((flat, 256), jnp.bfloat16),
            pltpu.VMEM((layers, rows, 256), jnp.float32),
        ],
    )
    state, own, stay, side, north, south = outs[:6]
    to_levels, north_levels, south_levels = (outs[6 + slots * at : 6 + slots * at + slots] for at in range(3))
    received = [shifted(north, "gy", 1), shifted(south, "gy", -1)]
    received += [to_level(value, kind, levels) for value, kind in zip(to_levels, kinds)]
    received += [to_level(value, kind, levels, "gy", 1) for value, kind in zip(north_levels, kinds)]
    received += [to_level(value, kind, levels, "gy", -1) for value, kind in zip(south_levels, kinds)]
    side_rows = (depth * height + 9 * 16, width)
    part, right, left = call(
        functools.partial(gather_body, levels),
        [(3, depth, height, width), side_rows, side_rows],
        [level, own, side] + received,
        1,
        [pltpu.VMEM((4, depth, height, width), jnp.float32)],
    )
    force, arrived = call(
        functools.partial(last_body, levels),
        [(3, depth, height, width), (6, blocks + 26 * CAP, 128)],
        [level, part, stay] + received + [shifted(right, "gx", 1), shifted(left, "gx", -1)],
    )
    return state, force, arrived


def solution(mesh):
    return jax.shard_map(
        local,
        mesh=mesh,
        in_specs=(
            P(None, "gz", "gy", "gx"),
            P(None, "gz", "gy", "gx"),
            P("gz", "gy", "gx"),
            P(None, ("gx", "gy", "gz"), None),
            P(None, ("gx", "gy", "gz"), None),
            P(("gx", "gy", "gz"), None),
            P(("gx", "gy", "gz")),
            P(("gx", "gy", "gz")),
        ),
        out_specs=(
            P(None, "gz", "gy", "gx"),
            P(None, "gz", "gy", "gx"),
            P(None, ("gx", "gy", "gz"), None),
        ),
        check_vma=False,
    )
```

```python
import functools
import math

import jax
import jax.numpy as jnp
import numpy as np
from jax import lax
from jax.experimental import pallas as pl
from jax.experimental.pallas import tpu as pltpu
from jax.sharding import PartitionSpec as P

CAP = 2


lattice = np.array(
    [
        [0, 0, 0],
        [1, 0, 0],
        [-1, 0, 0],
        [0, 1, 0],
        [0, -1, 0],
        [0, 0, 1],
        [0, 0, -1],
        [1, 1, 0],
        [-1, -1, 0],
        [1, -1, 0],
        [-1, 1, 0],
        [1, 0, 1],
        [-1, 0, -1],
        [1, 0, -1],
        [-1, 0, 1],
        [0, 1, 1],
        [0, -1, -1],
        [0, 1, -1],
        [0, -1, 1],
    ]
)
weights_table = np.array([1.0 / 3.0] + [1.0 / 18.0] * 6 + [1.0 / 36.0] * 12)
opposite = [0, 2, 1, 4, 3, 6, 5, 8, 7, 10, 9, 12, 11, 14, 13, 16, 15, 18, 17]
inverse_tau = 0.8
relax = 0.5
couple = 8.0


def call(body, outs, ins, scalars=1, scratch=(), cost=None):
    vmem = pl.BlockSpec(memory_space=pltpu.VMEM)
    return pl.pallas_call(
        body,
        out_shape=[jax.ShapeDtypeStruct(shape, jnp.float32) for shape in outs],
        in_specs=[pl.BlockSpec(memory_space=pltpu.SMEM)] * scalars + [vmem] * (len(ins) - scalars),
        out_specs=[vmem] * len(outs),
        scratch_shapes=list(scratch),
        cost_estimate=cost,
        compiler_params=pltpu.CompilerParams(vmem_limit_bytes=56 * 1024 * 1024),
    )(*ins)


ways = [tuple(int(part) for part in lattice[index][::-1]) for index in range(19)] + [(0, 0, 0)]
channels = len(ways)
LOW = 3
HIGH = 4


def low_reach(way):
    return 2 + way


def high_reach(way):
    return 3 - way


def rim(kind):
    count, reach = (LOW, low_reach) if kind == "low" else (HIGH, high_reach)
    return [
        (step, channel)
        for step in range(1, count + 1)
        for channel in range(channels)
        if step <= reach(ways[channel][0])
    ]


def rim_count(kind):
    return LOW if kind == "low" else HIGH


def rim_sides(levels):
    if levels == 2:
        return [("low", 1, 0, 0), ("high", 0, 1, 0)]
    return [("low", None, None, 0), ("high", None, None, 1)]


def rim_sizes(levels):
    sizes = [len(rim(kind)) for kind, _, _, _ in rim_sides(levels)]
    return [max(sizes)] if levels == 2 else sizes


def guarded(level, guard, action):
    if guard is None:
        action()
    else:
        pl.when(level == guard)(action)


def row_places(cells):
    places, high_at, low_at = [], 0, 0
    for channel, bounces in cells:
        way_z, way, _ = ways[channel]
        above, below = high_reach(way), low_reach(way)
        if bounces and way_z != 0:
            above, below = max(above, HIGH - 1), max(below, LOW - 1)
        places.append((high_at, low_at, above, below))
        high_at, low_at = high_at + above, low_at + below
    return places, (-(-high_at // 8) * 8, -(-low_at // 8) * 8)


def own_rows(depth):
    cells = [(layer, channel) for layer in range(depth) for channel in range(channels)]
    places, sizes = row_places([(channel, layer in (0, depth - 1)) for layer, channel in cells])
    return [(layer, channel, place) for (layer, channel), place in zip(cells, places)], sizes


def rim_rows(kind):
    places, sizes = row_places([(channel, False) for _, channel in rim(kind)])
    return [(step, channel, place) for (step, channel), place in zip(rim(kind), places)], sizes


def rim_row_sizes(levels):
    sizes = [rim_rows(kind)[1] for kind, _, _, _ in rim_sides(levels)]
    return [tuple(max(part) for part in zip(*sizes))] if levels == 2 else sizes


def moments(cells):
    density = cells[0] * float(weights_table[0])
    moment = [None, None, None]
    face, edge = float(weights_table[1]), float(weights_table[7])
    edge_sum = cells[7]
    for index in range(8, 19):
        edge_sum = edge_sum + cells[index]
    face_sum = cells[1]
    for index in range(2, 7):
        face_sum = face_sum + cells[index]
    density = density + face * face_sum + edge * edge_sum
    for axis in range(3):
        total = {}
        for group, indices in ((face, range(1, 7)), (edge, range(7, 19))):
            plus, minus = None, None
            for index in indices:
                way = int(lattice[index][axis])
                if way == 1:
                    plus = cells[index] if plus is None else plus + cells[index]
                if way == -1:
                    minus = cells[index] if minus is None else minus + cells[index]
            total[group] = plus - minus
        moment[axis] = face * total[face] + edge * total[edge]
    return density, moment


def relaxed(cells):
    density, moment = moments(cells)
    inverse = 1.0 / density
    flow = [part * inverse for part in moment]
    square = flow[0] * flow[0] + flow[1] * flow[1] + flow[2] * flow[2]
    scale = density * inverse_tau
    base = scale * (1.0 - 1.5 * square)
    keep = 1.0 - inverse_tau
    posts = [None] * 19
    posts[0] = keep * cells[0] + base
    for index in range(1, 19, 2):
        along = None
        for axis in range(3):
            way = int(lattice[index][axis])
            if way != 0:
                part = flow[axis] if way == 1 else -flow[axis]
                along = part if along is None else along + part
        odd = 3.0 * scale * along
        even = base + (4.5 * scale) * (along * along)
        posts[index] = keep * cells[index] + (even + odd)
        posts[index + 1] = keep * cells[index + 1] + (even - odd)
    return posts


def lane_roll(value, shift):
    shift = shift % value.shape[-1]
    return value if shift == 0 else pltpu.roll(value, shift, value.ndim - 1)


def first_body(levels, level_ref, pops_ref, coarse_ref, interface_ref, posts_ref, down_ref, up_ref, *outs):
    depth, height, width = interface_ref.shape
    slots = len(rim_sizes(levels))
    rims, down_rims, up_rims = (outs[slots * at : slots * at + slots] for at in range(3))
    own = own_rows(depth)[0]
    for layer in range(depth):
        mask = interface_ref[layer]
        inside = mask == 1
        posts = relaxed([pops_ref[index, layer] for index in range(19)])
        posts = [
            jnp.where(inside, coarse_ref[index, layer].astype(jnp.float32), posts[index])
            for index in range(19)
        ] + [mask.astype(jnp.float32)]
        for channel in range(channels):
            posts_ref[channel, layer] = posts[channel]
            down_at, up_at, down, up = own[layer * channels + channel][2]
            down_ref[down_at : down_at + down, :] = posts[channel][:down, :]
            up_ref[up_at : up_at + up, :] = posts[channel][height - up :, :]
    for kind, _, sender, slot in rim_sides(levels):

        def pack(kind=kind, slot=slot):
            for at, (step, channel, place) in enumerate(rim_rows(kind)[0]):
                cells = posts_ref[channel, depth - step if kind == "low" else step - 1]
                rims[slot][at] = cells
                down_at, up_at, down, up = place
                down_rims[slot][down_at : down_at + down, :] = cells[:down, :]
                up_rims[slot][up_at : up_at + up, :] = cells[height - up :, :]

        guarded(level_ref[0], sender, pack)


def unpack(levels, level, posts_ref, above_ref, below_ref, rims, above_rims, below_rims, ext):
    depth, height = posts_ref.shape[1:3]
    rows = height + 8

    def put(channel, at, cells, place, above, below):
        above_at, below_at, above_rows, below_rows = place
        ext[channel, at, :height, :] = cells
        ext[channel, at, height : height + above_rows, :] = above[above_at : above_at + above_rows, :]
        ext[channel, at, rows - below_rows : rows, :] = below[below_at : below_at + below_rows, :]

    for layer, channel, place in own_rows(depth)[0]:
        put(channel, LOW + layer, posts_ref[channel, layer], place, above_ref, below_ref)
    for kind, receiver, _, slot in rim_sides(levels):

        def take(kind=kind, slot=slot):
            for at, (step, channel, place) in enumerate(rim_rows(kind)[0]):
                layer = LOW - step if kind == "low" else LOW + depth + step - 1
                put(channel, layer, rims[slot][at], place, above_rims[slot], below_rims[slot])

        guarded(level, receiver, take)


def split_given(levels, rest):
    slots = len(rim_sizes(levels))
    parts = [rest[3 + slots * at : 3 + slots * at + slots] for at in range(3)]
    return rest[:3], parts, rest[3 + 3 * slots :]


def strip_body(levels, level_ref, *rest):
    (posts_ref, above_ref, below_ref), parts, (strip_ref, ext) = split_given(levels, rest)
    unpack(levels, level_ref[0], posts_ref, above_ref, below_ref, *parts, ext)
    layers, rows, width = ext.shape[1:]
    lane = lax.broadcasted_iota(jnp.int32, (rows, 128), 1)

    def channel_step(channel, carry):
        value = jnp.zeros((rows, 128), jnp.float32)
        for layer in range(layers):
            cells = ext[channel, layer]
            if width > 128:
                cells = jnp.where(lane < 64, cells[:, :128], cells[:, width - 128 :])
            value = jnp.where(lane // 8 == layer, lane_roll(cells, 8 * layer + 4), value)
        strip_ref[channel] = value
        return carry

    lax.fori_loop(0, channels, channel_step, 0)


def inner_body(levels, level_ref, *rest):
    (posts_ref, above_ref, below_ref), parts, rest = split_given(levels, rest)
    pops_ref, vel_ref, ext, pulled, second = rest
    level = level_ref[0]
    unpack(levels, level, posts_ref, above_ref, below_ref, *parts, ext)
    depth, height, width = posts_ref.shape[1:]
    rows = height + 8

    def pull(source, layer, at):
        bottom = (level == 0) & (layer == 0)
        top = (level == levels - 1) & (layer == depth - 1)
        for index in range(19):
            way_z, way_y, way_x = ways[index]
            value = source[index, at - way_z]
            if way_x != 0:
                value = pltpu.roll(value, way_x % width, 1)
            if way_y != 0:
                value = pltpu.roll(value, way_y % rows, 0)
            if way_z != 0:
                wall = bottom if way_z == 1 else top
                value = jnp.where(wall, source[opposite[index], at], value)
            pulled[index] = value

    tiles = [
        (slice(row, row + 8), slice(col, col + 128))
        for row in range(0, rows, 8)
        for col in range(0, width, 128)
    ]

    def first_step(number, carry):
        at = number + 1
        pull(ext, at - LOW, at)
        for tile in tiles:
            posts = relaxed([pulled[(index, *tile)] for index in range(19)])
            inside = ext[(19, at, *tile)] > 0.5
            for index in range(19):
                second[(index, number, *tile)] = jnp.where(inside, ext[(index, at, *tile)], posts[index])
        return carry

    lax.fori_loop(0, depth + LOW + HIGH - 2, first_step, 0)

    def second_step(number, carry):
        pull(second, number - 1, number + 1)
        for tile in tiles:
            density, moment = moments([pulled[(index, *tile)] for index in range(19)])
            inverse = 1.0 / density
            for axis in range(3):
                vel_ref[(axis, number, *tile)] = moment[axis] * inverse
        return carry

    def second_inner(number, carry):
        second_step(number, carry)
        for index in range(19):
            pops_ref[index, number - 1] = pulled[index, :height, :]
        return carry

    lax.fori_loop(0, 1, second_step, 0)
    lax.fori_loop(1, depth + 1, second_inner, 0)
    lax.fori_loop(depth + 1, depth + 3, second_step, 0)


def edge_body(
    levels, level_ref, strip_ref, left_ref, right_ref, inner_pops, inner_vel,
    pops_ref, vel_ref, beyond_ref, sides, pulled, second,
):
    depth, height, width = pops_ref.shape[1:]
    rows = height + 8
    level = level_ref[0]
    lane = lax.broadcasted_iota(jnp.int32, (rows, 128), 1)
    before = lane % 8 < 4
    bottom = (lane // 8 == LOW) & (level == 0)
    top = (lane // 8 == LOW + depth - 1) & (level == levels - 1)
    for channel in range(channels):
        own = strip_ref[channel]
        sides[0, channel] = jnp.where(before, left_ref[channel], own)
        sides[1, channel] = jnp.where(before, own, right_ref[channel])

    def pull(source, side, target):
        for index in range(19):
            way_z, way_y, way_x = ways[index]
            value = lane_roll(source[side, index], 8 * way_z + way_x)
            if way_y != 0:
                value = pltpu.roll(value, way_y % rows, 0)
            if way_z != 0:
                value = jnp.where(bottom if way_z == 1 else top, source[side, opposite[index]], value)
            target[side, index] = value

    speeds = [[], []]
    for side in range(2):
        pull(sides, side, pulled)
        for row in range(0, rows, 8):
            cut = slice(row, row + 8)
            posts = relaxed([pulled[side, index, cut] for index in range(19)])
            inside = sides[side, 19, cut] > 0.5
            for index in range(19):
                second[side, index, cut] = jnp.where(inside, sides[side, index, cut], posts[index])
        pull(second, side, pulled)
        density, moment = moments([pulled[side, index] for index in range(19)])
        inverse = 1.0 / density
        speeds[side] = [part * inverse for part in moment]

    near = lane[:height]
    near = (near < 2) | (near >= 126)
    front = before[:height]
    for index in range(19):
        value = jnp.where(front, pulled[1, index, :height], pulled[0, index, :height])
        for layer in range(depth):
            turned = lane_roll(value, -(8 * (layer + LOW) + 4))
            for col in range(0, width, 128):
                cells = inner_pops[index, layer, :, col : col + 128]
                if col == 0 or col == width - 128:
                    mask = near if width == 128 else near & ((lane[:height] < 64) == (col == 0))
                    cells = jnp.where(mask, turned, cells)
                pops_ref[index, layer, :, col : col + 128] = cells
    row = lax.broadcasted_iota(jnp.int32, (rows, 128), 0)
    valid = (row < height + 2) | (row == rows - 1)
    outside = (lane < 2) | (lane == 127)
    table = table_rows(depth, height)
    vel_ref[...] = jnp.zeros_like(vel_ref)
    beyond_ref[...] = jnp.zeros_like(beyond_ref)

    def put(target, axis, layer, cols, cells):
        at = axis * table + layer * (height + 3)
        target[at : at + 1, cols] = cells[rows - 1 :, :]
        target[at + 1 : at + height + 3, cols] = cells[: height + 2, :]

    for axis in range(3):
        main = jnp.where(before, speeds[1][axis], speeds[0][axis])
        rest = jnp.where(before, speeds[0][axis], speeds[1][axis])
        for layer in range(depth + 3):
            keep = valid
            if layer == 0:
                keep = valid & (level != 0)
            if layer > depth:
                keep = valid & (level != levels - 1)
            shift = -(8 * (layer - 1 + LOW) + 4)
            turned = lane_roll(main, shift)
            for col in range(0, width, 128):
                cells = inner_vel[axis, layer, :, col : col + 128]
                if col == 0 or col == width - 128:
                    mask = (lane < 2) & (col == 0) | (lane >= 126) & (col == width - 128)
                    cells = jnp.where(mask, turned, cells)
                put(vel_ref, axis, layer, slice(col, col + 128), jnp.where(keep, cells, 0.0))
            put(beyond_ref, axis, layer, slice(0, 128), jnp.where(keep & outside, lane_roll(rest, shift), 0.0))


def shifted(value, axis, step):
    count = lax.axis_size(axis)
    return lax.ppermute(value, axis, [(i, (i + step) % count) for i in range(count)])


def to_level(value, kind, levels, side=None, step=0):
    pairs = []
    for at in range(levels):
        other = 1 - at if levels == 2 else at + 1 if kind in ("low", "up") else at - 1
        if 0 <= other < levels:
            pairs.append((at, other))
    if side is None:
        return lax.ppermute(value, "gz", pairs)
    count = lax.axis_size(side)
    return lax.ppermute(
        value,
        (side, "gz"),
        [
            (brick * levels + at, (brick + step) % count * levels + other)
            for brick in range(count)
            for at, other in pairs
        ],
    )


def wide_exchange(level, pops, coarse_pops, interface):
    levels = lax.axis_size("gz")
    depth, height, width = interface.shape
    sizes = rim_sizes(levels)
    slots = len(sizes)
    kinds = ["low", "high"][:slots]
    down_sizes, up_sizes = zip(*rim_row_sizes(levels))
    outs = call(
        functools.partial(first_body, levels),
        [(channels, depth, height, width)]
        + [(size, width) for size in own_rows(depth)[1]]
        + [(size, height, width) for size in sizes]
        + [(size, width) for size in down_sizes + up_sizes],
        [level, pops, coarse_pops, interface],
    )
    posts, down, up = outs[:3]
    rims, down_rims, up_rims = (outs[3 + slots * at : 3 + slots * at + slots] for at in range(3))
    given = [level, posts, shifted(down, "gy", -1), shifted(up, "gy", 1)]
    given += [to_level(value, kind, levels) for value, kind in zip(rims, kinds)]
    given += [to_level(value, kind, levels, "gy", -1) for value, kind in zip(down_rims, kinds)]
    given += [to_level(value, kind, levels, "gy", 1) for value, kind in zip(up_rims, kinds)]
    deep, rows = depth + LOW + HIGH, height + 8
    ext = pltpu.VMEM((channels, deep, rows, width), jnp.float32)
    (strip,) = call(functools.partial(strip_body, levels), [(channels, rows, 128)], given, 1, [ext])
    left, right = shifted(strip, "gx", 1), shifted(strip, "gx", -1)
    inner_pops, inner_vel = call(
        functools.partial(inner_body, levels),
        [pops.shape, (3, depth + 3, rows, width)],
        given,
        1,
        [
            ext,
            pltpu.VMEM((19, rows, width), jnp.float32),
            pltpu.VMEM((19, deep - 2, rows, width), jnp.float32),
        ],
        pl.CostEstimate(flops=10**8, bytes_accessed=1 << 22, transcendentals=0),
    )
    return [strip, left, right, inner_pops, inner_vel]


def phis(frac):
    angle = frac * (0.5 * math.pi)
    sine = 0.25 * jnp.sin(angle)
    cosine = 0.25 * jnp.cos(angle)
    return (0.25 - sine, 0.25 + cosine, 0.25 + sine, 0.25 - cosine)


def split(value):
    high = value.astype(jnp.bfloat16)
    return high, (value - high.astype(jnp.float32)).astype(jnp.bfloat16)


def pick(step, parts):
    value = jnp.where(step == 0, parts[0], 0.0)
    for index in range(1, 4):
        value = jnp.where(step == index, parts[index], value)
    return value


def dots(left, right, dims):
    return lax.dot_general(left, right, (dims, ((), ())), preferred_element_type=jnp.float32)


def table_rows(depth, height):
    return -(-(depth + 3) * (height + 3) // 16) * 16


def droplet_body(
    size, counts_ref, dest_ref, vel_ref, beyond_ref, speed_ref, frac_ref, home_ref, spread_ref, outer_ref,
    stay_ref, state_ref, twice, mixed, along, push_high, push_low, plane_ref,
):
    depth, height, width = size
    blocks = home_ref.shape[0]
    layers, rows = depth + 3, height + 3
    table = table_rows(depth, height)
    high, low = split(vel_ref[...])
    twice[:, :width] = high
    twice[:, width:] = high
    mixed[:, :width] = low
    high, low = (part.astype(jnp.float32) for part in split(beyond_ref[...]))
    mixed[:, width:] = (high + lane_roll(low, 32) + lane_roll(high, 64)).astype(jnp.bfloat16)
    along[2 * width :, :] = jnp.zeros((128, along.shape[1]), jnp.bfloat16)
    plane_ref[:, layers * rows :, :] = jnp.zeros(
        (plane_ref.shape[0], table - layers * rows, 256), jnp.float32
    )
    span_x = lax.broadcasted_iota(jnp.int32, (width, 128), 0) + 1
    span_end = lax.broadcasted_iota(jnp.int32, (16, 128), 0)
    span_y = lax.broadcasted_iota(jnp.int32, (-(-rows // 8) * 8, 128), 0)
    span_z = lax.broadcasted_iota(jnp.int32, (-(-layers // 8) * 8, 128), 0)
    slots = lax.broadcasted_iota(jnp.int32, (1, 128), 1)

    def weigh(number):
        for half in range(2):
            block = 2 * number + half
            side = slice(block * 128, block * 128 + 128)
            cell = home_ref[block : block + 1, :]
            cell_x = cell % width
            cell_y = cell // width % height
            cell_z = cell // (width * height)
            part_x = phis(frac_ref[0, block : block + 1, :])
            part_y = phis(frac_ref[1, block : block + 1, :])
            part_z = phis(frac_ref[2, block : block + 1, :])
            high, low = split(pick(span_x - cell_x, part_x))
            along[0:width, side] = low
            along[width : 2 * width, side] = high
            high, low = split(pick(span_end + (width + 1) - cell_x, part_x))
            along[2 * width : 2 * width + 16, side] = high
            along[2 * width + 32 : 2 * width + 48, side] = high
            along[2 * width + 64 : 2 * width + 80, side] = low
            high, low = split(jnp.where((span_end == 15) & (cell_x == 0), part_x[0], 0.0))
            along[2 * width + 112 : 2 * width + 128, side] = high
            along[2 * width + 16 : 2 * width + 32, side] = high
            along[2 * width + 48 : 2 * width + 64, side] = low
            weight_y = pick(span_y - cell_y, part_y)[:rows]
            weight_z = pick(span_z - cell_z, part_z)
            for layer in range(layers):
                plane_ref[number % 2, layer * rows : layer * rows + rows, half * 128 : half * 128 + 128] = (
                    weight_y * weight_z[layer : layer + 1, :]
                )

    def sample(number):
        pair = slice(number * 256, number * 256 + 256)
        return dots(twice[...], along[0 : 2 * width, pair], ((1,), (0,))) + dots(
            mixed[...], along[width:, pair], ((1,), (0,))
        )

    def move(number, sums):
        plane = plane_ref[number % 2]
        for axis in range(3):
            where = slice(axis * table, axis * table + table)
            sampled = jnp.sum(sums[where] * plane, axis=0, keepdims=True)
            for half in range(2):
                block = 2 * number + half
                live = slots < counts_ref[block]
                sample = sampled[:, half * 128 : half * 128 + 128]
                speed = speed_ref[axis, block : block + 1, :]
                frac = frac_ref[axis, block : block + 1, :]
                moved = speed + relax * (sample - speed)
                push = jnp.where(live, couple * (moved - sample), 0.0)
                stays = live & (dest_ref[block] == 13)
                for at, value in ((axis, moved), (3 + axis, frac + moved)):
                    state_ref[block, at : at + 1, :] = jnp.where(live, value, 0.0)
                    stay_ref[at, block : block + 1, :] = jnp.where(stays, value, 0.0)
                high, low = split(plane[:, half * 128 : half * 128 + 128] * push)
                push_high[where, block * 128 : block * 128 + 128] = high
                push_low[where, block * 128 : block * 128 + 128] = low

    pairs = blocks // 2
    weigh(0)
    for number in range(pairs):
        sums = sample(number)
        if number + 1 < pairs:
            weigh(number + 1)
        move(number, sums)
    main = dots(push_high[...], along[0 : 2 * width, :], ((1,), (1,)))
    rest = dots(push_low[...], along[width:, :], ((1,), (1,)))
    outer = dots(push_high[...], along[2 * width :, :], ((1,), (1,)))
    spread_ref[...] = main[:, :width] + main[:, width:] + rest[:, :width]
    outer_ref[...] = outer + lane_roll(outer, -64) + rest[:, width:]


def force_sides(levels):
    if levels == 2:
        return [("up", 0, 1, 0), ("down", 1, 0, 0)]
    return [("up", None, None, 0), ("down", None, None, 1)]


GROUP = 6 * 8


def group_at(way_z, way_y):
    return (way_z + 1) * 3 + way_y + 1


def message_rows(depth):
    return [8 * 8, 2 * 4 * depth, 4 * depth, 2 * 8, 8]


def pack_body(
    levels, level_ref, dest_ref, spread_ref, outer_ref, state_ref, own_ref, side_ref,
    to_levels, north_ref, south_ref, north_levels, south_levels, outbox, strip, taken,
):
    depth, height, width = own_ref.shape[1:]
    level = level_ref[0]
    rows, table = height + 3, table_rows(depth, height)
    lane = lax.broadcasted_iota(jnp.int32, (table, 128), 1)
    value = jnp.zeros((table, 128), jnp.float32)
    for axis in range(3):
        here = (lane >= 4 * axis) & (lane < 4 * axis + 3)
        cells = outer_ref[axis * table : axis * table + table, :]
        value = jnp.where(here, lane_roll(cells, 4 * axis + 1), value)
    strip[...] = value
    for code in range(27):
        taken[code] = 0
    outbox[...] = jnp.zeros_like(outbox)
    for block in range(state_ref.shape[0]):
        code = dest_ref[block]

        @pl.when(code != 13)
        def _():
            rank = taken[code]
            outbox[code * CAP + rank] = state_ref[block]
            taken[code] = rank + 1

    def force(part, layer, cut):
        at = layer * rows
        if part < 3:
            return spread_ref[part * table + at + cut.start : part * table + at + cut.stop, :]
        return strip[at + cut.start : at + cut.stop, :]

    def blocks(target, way_z, way_y):
        base = target.shape[0] - GROUP
        for slot in range(6):
            target[base + 8 * slot : base + 8 * slot + 8, :] = outbox[6 * group_at(way_z, way_y) + slot]

    main, north, south = slice(1, height + 1), slice(height + 1, height + 3), slice(0, 1)
    for part in range(4):
        for layer in range(depth):
            own_ref[part, layer] = force(part, layer + 1, main)
            at = part * depth + layer
            north_ref[2 * at : 2 * at + 2, :] = force(part, layer + 1, north)
            south_ref[at : at + 1, :] = force(part, layer + 1, south)
    blocks(north_ref, 0, 1)
    blocks(south_ref, 0, -1)
    for slot in range(2):
        side_ref[slot] = outbox[6 * group_at(0, 0) + slot]
        side_ref[2 + slot] = outbox[6 * group_at(0, 0) + 4 + slot]
    for kind, sender, _, slot in force_sides(levels):

        def pack(kind=kind, slot=slot):
            for part in range(4):
                for step in range(2 if kind == "up" else 1):
                    layer = depth + 1 + step if kind == "up" else 0
                    at = 2 * part + step
                    to_levels[slot][8 * at : 8 * at + 8, :] = force(part, layer, main)
                    north_levels[slot][2 * at : 2 * at + 2, :] = force(part, layer, north)
                    south_levels[slot][at : at + 1, :] = force(part, layer, south)
            way = 1 if kind == "up" else -1
            blocks(to_levels[slot], way, 0)
            blocks(north_levels[slot], way, 1)
            blocks(south_levels[slot], way, -1)

        guarded(level, sender, pack)


def main_body(
    levels, level_ref, counts_ref, dest_ref, strip_ref, left_ref, right_ref, inner_pops, inner_vel,
    speed_ref, frac_ref, home_ref, pops_ref, own_ref, stay_ref, side_ref, north_ref, south_ref, *rest,
):
    slots = len(rim_sizes(levels))
    to_levels, north_levels, south_levels = (rest[slots * at : slots * at + slots] for at in range(3))
    rest = rest[3 * slots :]
    vel_ref, beyond_ref, spread_ref, outer_ref, state_ref, outbox, strip, taken = rest[:8]
    edge_body(
        levels, level_ref, strip_ref, left_ref, right_ref, inner_pops, inner_vel,
        pops_ref, vel_ref, beyond_ref, *rest[8:11],
    )
    droplet_body(
        pops_ref.shape[1:], counts_ref, dest_ref, vel_ref, beyond_ref, speed_ref, frac_ref, home_ref,
        spread_ref, outer_ref, stay_ref, state_ref, *rest[11:],
    )
    pack_body(
        levels, level_ref, dest_ref, spread_ref, outer_ref, state_ref, own_ref, side_ref,
        to_levels, north_ref, south_ref, north_levels, south_levels, outbox, strip, taken,
    )


def gather_body(levels, level_ref, own_ref, side_ref, *rest):
    depth, height, width = own_ref.shape[1:]
    slots = len(rim_sizes(levels))
    north_ref, south_ref = rest[:2]
    from_levels, north_levels, south_levels = (rest[2 + slots * at : 2 + slots * at + slots] for at in range(3))
    force_ref, right_ref, left_ref, total = rest[2 + 3 * slots :]
    base = depth * height
    total[...] = own_ref[...]
    right_ref[base:, :] = jnp.zeros((right_ref.shape[0] - base, width), jnp.float32)
    left_ref[base:, :] = jnp.zeros((left_ref.shape[0] - base, width), jnp.float32)
    last = slice(height - 1, height)
    for part in range(4):
        for layer in range(depth):
            at = part * depth + layer
            total[part, layer, 0:2, :] += north_ref[2 * at : 2 * at + 2, :]
            total[part, layer, last, :] += south_ref[at : at + 1, :]

    def blocks(source, way_z, way_y):
        at = base + 16 * group_at(way_z, way_y)
        start = source.shape[0] - GROUP
        left_ref[at : at + 16, :] = source[start : start + 16, :]
        right_ref[at : at + 16, :] = source[start + 32 : start + 48, :]

    at = base + 16 * group_at(0, 0)
    for slot in range(2):
        left_ref[at + 8 * slot : at + 8 * slot + 8, :] = side_ref[slot]
        right_ref[at + 8 * slot : at + 8 * slot + 8, :] = side_ref[2 + slot]
    blocks(north_ref, 0, 1)
    blocks(south_ref, 0, -1)
    for kind, _, receiver, slot in force_sides(levels):

        def take(kind=kind, slot=slot):
            for part in range(4):
                for step in range(2 if kind == "up" else 1):
                    layer = step if kind == "up" else depth - 1
                    at = 2 * part + step
                    total[part, layer] += from_levels[slot][8 * at : 8 * at + 8, :]
                    total[part, layer, 0:2, :] += north_levels[slot][2 * at : 2 * at + 2, :]
                    total[part, layer, last, :] += south_levels[slot][at : at + 1, :]
            way = 1 if kind == "up" else -1
            blocks(from_levels[slot], way, 0)
            blocks(north_levels[slot], way, 1)
            blocks(south_levels[slot], way, -1)

        guarded(level_ref[0], receiver, take)
    for layer in range(depth):
        for axis in range(3):
            force_ref[axis, layer] = total[axis, layer]
        for target in (right_ref, left_ref):
            target[layer * height : layer * height + height, :] = total[3, layer]


def last_body(levels, level_ref, part_ref, stay_ref, *rest):
    depth, height, width = part_ref.shape[1:]
    slots = len(rim_sizes(levels))
    north_ref, south_ref = rest[:2]
    from_levels, north_levels, south_levels = (rest[2 + slots * at : 2 + slots * at + slots] for at in range(3))
    right_ref, left_ref, force_ref, arrived_ref = rest[2 + 3 * slots :]
    blocks = stay_ref.shape[1]
    base = depth * height
    lane = lax.broadcasted_iota(jnp.int32, (height, 128), 1)
    for layer in range(depth):
        rows = slice(layer * height, layer * height + height)
        before, after = right_ref[rows, :128], left_ref[rows, :128]
        for axis in range(3):
            first = jnp.where(lane < 2, lane_roll(before, -4 * axis - 1), 0.0)
            final = jnp.where(lane == 127, lane_roll(after, 127 - 4 * axis), 0.0)
            force_ref[axis, layer] = part_ref[axis, layer]
            force_ref[axis, layer, :, 0:128] += first
            force_ref[axis, layer, :, width - 128 : width] += final
    arrived_ref[:, 0:blocks, :] = stay_ref[...]

    def put(source, start, way_z, way_y, way_x):
        code = group_at(way_z, way_y) * 3 + way_x + 1
        at = blocks + CAP * (code if code < 13 else code - 1)
        for slot in range(CAP):
            for axis in range(6):
                if source is None:
                    value = jnp.zeros((1, 128), jnp.float32)
                else:
                    value = source[start + 8 * slot + axis : start + 8 * slot + axis + 1, :]
                arrived_ref[axis, at + slot : at + slot + 1, :] = value

    for way_z in (-1, 0, 1):
        for way_y in (-1, 0, 1):
            for way_x, source in ((1, right_ref), (-1, left_ref)):
                put(source, base + 16 * group_at(way_z, way_y), way_z, way_y, way_x)
    middle = 16

    def put_group(source, way_z, way_y):
        put(source, None if source is None else source.shape[0] - GROUP + middle, way_z, way_y, 0)

    put_group(north_ref, 0, 1)
    put_group(south_ref, 0, -1)
    for kind, _, receiver, slot in force_sides(levels):
        way = 1 if kind == "up" else -1

        def take(way=way, slot=slot):
            put_group(from_levels[slot], way, 0)
            put_group(north_levels[slot], way, 1)
            put_group(south_levels[slot], way, -1)

        def clear(way=way):
            for way_y in (-1, 0, 1):
                put_group(None, way, way_y)

        guarded(level_ref[0], receiver, take)
        if receiver is not None:
            guarded(level_ref[0], 1 - receiver, clear)


def local(pops, coarse_pops, interface, drop_vel, drop_frac, home, counts, dest):
    level = lax.axis_index("gz").astype(jnp.int32).reshape(1)
    levels = lax.axis_size("gz")
    depth, height, width = interface.shape
    blocks = home.shape[0]
    kinds = ["up", "down"][: len(rim_sizes(levels))]
    slots = len(kinds)
    given = wide_exchange(level, pops, coarse_pops, interface)
    rows = height + 8
    table = table_rows(depth, height)
    sizes = [(count + GROUP, width) for count in message_rows(depth)]
    outs = call(
        functools.partial(main_body, levels),
        [pops.shape, (4, depth, height, width), (6, blocks, 128), (4, 8, 128), sizes[1], sizes[2]]
        + [sizes[0]] * slots
        + [sizes[3]] * slots
        + [sizes[4]] * slots,
        [level, counts, dest] + given + [drop_vel, drop_frac, home],
        3,
        [
            pltpu.VMEM((3 * table, width), jnp.float32),
            pltpu.VMEM((3 * table, 128), jnp.float32),
            pltpu.VMEM((3 * table, width), jnp.float32),
            pltpu.VMEM((3 * table, 128), jnp.float32),
            pltpu.VMEM((blocks, 8, 128), jnp.float32),
            pltpu.VMEM((27 * CAP, 8, 128), jnp.float32),
            pltpu.VMEM((table, 128), jnp.float32),
            pltpu.SMEM((27,), jnp.int32),
            pltpu.VMEM((2, channels, rows, 128), jnp.float32),
            pltpu.VMEM((2, 19, rows, 128), jnp.float32),
            pltpu.VMEM((2, 19, rows, 128), jnp.float32),
            pltpu.VMEM((3 * table, 2 * width), jnp.bfloat16),
            pltpu.VMEM((3 * table, width + 128), jnp.bfloat16),
            pltpu.VMEM((2 * width + 128, blocks * 128), jnp.bfloat16),
            pltpu.VMEM((3 * table, blocks * 128), jnp.bfloat16),
            pltpu.VMEM((3 * table, blocks * 128), jnp.bfloat16),
            pltpu.VMEM((2, table, 256), jnp.float32),
        ],
    )
    state, own, stay, side, north, south = outs[:6]
    to_levels, north_levels, south_levels = (outs[6 + slots * at : 6 + slots * at + slots] for at in range(3))
    received = [shifted(north, "gy", 1), shifted(south, "gy", -1)]
    received += [to_level(value, kind, levels) for value, kind in zip(to_levels, kinds)]
    received += [to_level(value, kind, levels, "gy", 1) for value, kind in zip(north_levels, kinds)]
    received += [to_level(value, kind, levels, "gy", -1) for value, kind in zip(south_levels, kinds)]
    side_rows = (depth * height + 9 * 16, width)
    part, right, left = call(
        functools.partial(gather_body, levels),
        [(3, depth, height, width), side_rows, side_rows],
        [level, own, side] + received,
        1,
        [pltpu.VMEM((4, depth, height, width), jnp.float32)],
    )
    force, arrived = call(
        functools.partial(last_body, levels),
        [(3, depth, height, width), (6, blocks + 26 * CAP, 128)],
        [level, part, stay] + received + [shifted(right, "gx", 1), shifted(left, "gx", -1)],
    )
    return state, force, arrived


def solution(mesh):
    return jax.shard_map(
        local,
        mesh=mesh,
        in_specs=(
            P(None, "gz", "gy", "gx"),
            P(None, "gz", "gy", "gx"),
            P("gz", "gy", "gx"),
            P(None, ("gx", "gy", "gz"), None),
            P(None, ("gx", "gy", "gz"), None),
            P(("gx", "gy", "gz"), None),
            P(("gx", "gy", "gz")),
            P(("gx", "gy", "gz")),
        ),
        out_specs=(
            P(None, "gz", "gy", "gx"),
            P(None, "gz", "gy", "gx"),
            P(None, ("gx", "gy", "gz"), None),
        ),
        check_vma=False,
    )
```

```python
import functools
import math

import jax
import jax.numpy as jnp
import numpy as np
from jax import lax
from jax.experimental import pallas as pl
from jax.experimental.pallas import tpu as pltpu
from jax.sharding import PartitionSpec as P

CAP = 2


lattice = np.array(
    [
        [0, 0, 0],
        [1, 0, 0],
        [-1, 0, 0],
        [0, 1, 0],
        [0, -1, 0],
        [0, 0, 1],
        [0, 0, -1],
        [1, 1, 0],
        [-1, -1, 0],
        [1, -1, 0],
        [-1, 1, 0],
        [1, 0, 1],
        [-1, 0, -1],
        [1, 0, -1],
        [-1, 0, 1],
        [0, 1, 1],
        [0, -1, -1],
        [0, 1, -1],
        [0, -1, 1],
    ]
)
weights_table = np.array([1.0 / 3.0] + [1.0 / 18.0] * 6 + [1.0 / 36.0] * 12)
opposite = [0, 2, 1, 4, 3, 6, 5, 8, 7, 10, 9, 12, 11, 14, 13, 16, 15, 18, 17]
inverse_tau = 0.8
relax = 0.5
couple = 8.0


def call(body, outs, ins, scalars=1, scratch=(), cost=None, heads=()):
    heads = dict(heads)
    arrays = ins[scalars:]
    landing = []
    for at, value in enumerate(arrays):
        count = heads.get(at, value.shape[0])
        landing.append(pltpu.VMEM((count,) + value.shape[1:], value.dtype))

    def whole(*refs):
        given = refs[scalars : len(ins)]
        made = refs[len(ins) : len(ins) + len(outs)]
        rest = refs[len(ins) + len(outs) :]
        landed, done, rest = rest[: len(arrays)], rest[len(arrays)], rest[len(arrays) + 1 :]
        copies = []
        for at, (source, target) in enumerate(zip(given, landed)):
            if at in heads:
                source = source.at[pl.ds(0, heads[at])]
            copies.append(pltpu.make_async_copy(source, target, done.at[at]))
        for copy in copies:
            copy.start()
        for copy in copies:
            copy.wait()
        body(*refs[:scalars], *landed, *made, *rest)

    vmem = pl.BlockSpec(memory_space=pltpu.VMEM)
    hbm = pl.BlockSpec(memory_space=pltpu.HBM)
    return pl.pallas_call(
        whole,
        out_shape=[jax.ShapeDtypeStruct(shape, jnp.float32) for shape in outs],
        in_specs=[pl.BlockSpec(memory_space=pltpu.SMEM)] * scalars + [hbm] * len(arrays),
        out_specs=[vmem] * len(outs),
        scratch_shapes=landing + [pltpu.SemaphoreType.DMA((len(arrays),))] + list(scratch),
        cost_estimate=cost,
        compiler_params=pltpu.CompilerParams(vmem_limit_bytes=64 * 1024 * 1024),
    )(*ins)


ways = [tuple(int(part) for part in lattice[index][::-1]) for index in range(19)] + [(0, 0, 0)]
channels = len(ways)
LOW = 3
HIGH = 4


def low_reach(way):
    return 2 + way


def high_reach(way):
    return 3 - way


def rim(kind):
    count, reach = (LOW, low_reach) if kind == "low" else (HIGH, high_reach)
    return [
        (step, channel)
        for step in range(1, count + 1)
        for channel in range(channels)
        if step <= reach(ways[channel][0])
    ]


def rim_count(kind):
    return LOW if kind == "low" else HIGH


def rim_sides(levels):
    if levels == 2:
        return [("low", 1, 0, 0), ("high", 0, 1, 0)]
    return [("low", None, None, 0), ("high", None, None, 1)]


def rim_sizes(levels):
    sizes = [FOUR + len(rim(kind)) for kind, _, _, _ in rim_sides(levels)]
    return [max(sizes)] if levels == 2 else sizes


def guarded(level, guard, action):
    if guard is None:
        action()
    else:
        pl.when(level == guard)(action)


def padded(count):
    return -(-count // 8) * 8


def reaches(channel, bounces):
    way_z, way, _ = ways[channel]
    above, below = high_reach(way), low_reach(way)
    if bounces and way_z != 0:
        above, below = max(above, HIGH - 1), max(below, LOW - 1)
    return above, below


def row_places(cells, start=(0, 0)):
    places, (high_at, low_at) = [], start
    for above, below in cells:
        places.append((high_at, low_at, above, below))
        high_at, low_at = high_at + above, low_at + below
    return places, (padded(high_at), padded(low_at))


def strip_rows():
    return row_places([reaches(channel, True) for channel in range(channels)])


def own_rows(depth):
    cells = [(layer, channel) for layer in range(depth) for channel in range(channels)]
    places, sizes = row_places(
        [reaches(channel, layer in (0, depth - 1)) for layer, channel in cells], strip_rows()[1]
    )
    return [(layer, channel, place) for (layer, channel), place in zip(cells, places)], sizes


FOUR = -(-channels // 4)


def rim_strip_rows():
    return row_places([(HIGH, LOW)] * FOUR)


def rim_rows(kind):
    places, sizes = row_places([reaches(channel, False) for _, channel in rim(kind)], rim_strip_rows()[1])
    return [(step, channel, place) for (step, channel), place in zip(rim(kind), places)], sizes


def rim_row_sizes(levels):
    sizes = [rim_rows(kind)[1] for kind, _, _, _ in rim_sides(levels)]
    return [tuple(max(part) for part in zip(*sizes))] if levels == 2 else sizes


def face_table(high):
    wants = []
    for channel in range(channels):
        way_z, _, way = ways[channel]
        count = high_reach(way) if high else low_reach(way)
        if way_z != 0:
            count = max(count, (HIGH if high else LOW) - 1)
        wants.append((-count, channel))
    free, table = [], []
    for count, channel in sorted(wants):
        tile = next((at for at, room in enumerate(free) if room >= -count), len(free))
        if tile == len(free):
            free.append(8)
        table.append((channel, tile, 8 - free[tile], -count))
        free[tile] += count
    return table, len(free)


def moments(cells):
    density = cells[0] * float(weights_table[0])
    moment = [None, None, None]
    face, edge = float(weights_table[1]), float(weights_table[7])
    edge_sum = cells[7]
    for index in range(8, 19):
        edge_sum = edge_sum + cells[index]
    face_sum = cells[1]
    for index in range(2, 7):
        face_sum = face_sum + cells[index]
    density = density + face * face_sum + edge * edge_sum
    for axis in range(3):
        total = {}
        for group, indices in ((face, range(1, 7)), (edge, range(7, 19))):
            plus, minus = None, None
            for index in indices:
                way = int(lattice[index][axis])
                if way == 1:
                    plus = cells[index] if plus is None else plus + cells[index]
                if way == -1:
                    minus = cells[index] if minus is None else minus + cells[index]
            total[group] = plus - minus
        moment[axis] = face * total[face] + edge * total[edge]
    return density, moment


def relaxed(cells):
    density, moment = moments(cells)
    inverse = 1.0 / density
    flow = [part * inverse for part in moment]
    square = flow[0] * flow[0] + flow[1] * flow[1] + flow[2] * flow[2]
    scale = density * inverse_tau
    base = scale * (1.0 - 1.5 * square)
    keep = 1.0 - inverse_tau
    posts = [None] * 19
    posts[0] = keep * cells[0] + base
    for index in range(1, 19, 2):
        along = None
        for axis in range(3):
            way = int(lattice[index][axis])
            if way != 0:
                part = flow[axis] if way == 1 else -flow[axis]
                along = part if along is None else along + part
        odd = 3.0 * scale * along
        even = base + (4.5 * scale) * (along * along)
        posts[index] = keep * cells[index] + (even + odd)
        posts[index + 1] = keep * cells[index + 1] + (even - odd)
    return posts


def lane_roll(value, shift):
    shift = shift % value.shape[-1]
    return value if shift == 0 else pltpu.roll(value, shift, value.ndim - 1)


def first_body(
    levels, level_ref, pops_ref, coarse_ref, interface_ref, posts_ref, strip_ref, down_ref, up_ref, *outs
):
    depth, height, width = interface_ref.shape
    slots = len(rim_sizes(levels))
    rims, down_rims, up_rims = (outs[slots * at : slots * at + slots] for at in range(3))
    lane = lax.broadcasted_iota(jnp.int32, (height, 128), 1)

    def put_rows(down, up, place, cells):
        down_at, up_at, down_rows, up_rows = place
        cols = slice(0, cells.shape[1])
        down[down_at : down_at + down_rows, cols] = cells[:down_rows, :]
        up[up_at : up_at + up_rows, cols] = cells[height - up_rows :, :]

    own = own_rows(depth)[0]
    for layer in range(depth):
        mask = interface_ref[layer]
        inside = mask == 1
        posts = relaxed([pops_ref[index, layer] for index in range(19)])
        posts = [
            jnp.where(inside, coarse_ref[index, layer].astype(jnp.float32), posts[index])
            for index in range(19)
        ] + [mask.astype(jnp.float32)]
        for channel in range(channels):
            posts_ref[channel, layer] = posts[channel]
            put_rows(down_ref, up_ref, own[layer * channels + channel][2], posts[channel])
    for channel in range(channels):
        value = jnp.zeros((height, 128), jnp.float32)
        for layer in range(depth):
            cells = posts_ref[channel, layer]
            if width > 128:
                cells = jnp.where(lane < 64, cells[:, :128], cells[:, width - 128 :])
            value = jnp.where(lane // 8 == LOW + layer, lane_roll(cells, 8 * (LOW + layer) + 4), value)
        strip_ref[channel] = value
        put_rows(down_ref, up_ref, strip_rows()[0][channel], value)
    for kind, _, sender, slot in rim_sides(levels):

        def pack(kind=kind, slot=slot):
            for tile in range(FOUR):
                value = jnp.zeros((height, 128), jnp.float32)
                for part in range(min(4, channels - 4 * tile)):
                    first = LOW + depth - 4 if kind == "low" else LOW
                    turned = lane_roll(strip_ref[4 * tile + part], 32 * part - 8 * first)
                    value = jnp.where(lane // 32 == part, turned, value)
                rims[slot][tile, :, 0:128] = value
                put_rows(down_rims[slot], up_rims[slot], rim_strip_rows()[0][tile], value)
            for at, (step, channel, place) in enumerate(rim_rows(kind)[0]):
                cells = posts_ref[channel, depth - step if kind == "low" else step - 1]
                rims[slot][FOUR + at] = cells
                put_rows(down_rims[slot], up_rims[slot], place, cells)

        guarded(level_ref[0], sender, pack)


def unpack(levels, level, posts_ref, above_ref, below_ref, rims, above_rims, below_rims, ext):
    depth, height = posts_ref.shape[1:3]
    rows = height + 8

    def put(channel, at, cells, place, above, below):
        above_at, below_at, above_rows, below_rows = place
        ext[channel, at, :height, :] = cells
        ext[channel, at, height : height + above_rows, :] = above[above_at : above_at + above_rows, :]
        ext[channel, at, rows - below_rows : rows, :] = below[below_at : below_at + below_rows, :]

    for layer, channel, place in own_rows(depth)[0]:
        put(channel, LOW + layer, posts_ref[channel, layer], place, above_ref, below_ref)
    for kind, receiver, _, slot in rim_sides(levels):

        def take(kind=kind, slot=slot):
            for at, (step, channel, place) in enumerate(rim_rows(kind)[0]):
                layer = LOW - step if kind == "low" else LOW + depth + step - 1
                put(channel, layer, rims[slot][FOUR + at], place, above_rims[slot], below_rims[slot])

        guarded(level, receiver, take)


def split_given(levels, rest):
    slots = len(rim_sizes(levels))
    parts = [rest[3 + slots * at : 3 + slots * at + slots] for at in range(3)]
    return rest[:3], parts, rest[3 + 3 * slots :]


def strip_body(levels, depth, level_ref, *rest):
    (own_ref, above_ref, below_ref), parts, rest = split_given(levels, rest)
    strip_ref, right_ref, left_ref, tiles = rest
    rows = strip_ref.shape[1]
    height = rows - 8
    lane = lax.broadcasted_iota(jnp.int32, (rows, 128), 1)
    layer_at = lane // 8

    def put(target, index, place, above, below):
        above_at, below_at, above_rows, below_rows = place
        target[index, height : height + above_rows, :] = above[above_at : above_at + above_rows, 0:128]
        target[index, rows - below_rows :, :] = below[below_at : below_at + below_rows, 0:128]

    for channel in range(channels):
        strip_ref[channel, 0:height, :] = own_ref[channel]
        put(strip_ref, channel, strip_rows()[0][channel], above_ref, below_ref)
    for kind, receiver, _, slot in rim_sides(levels):

        def take(kind=kind, slot=slot):
            rims, above_rims, below_rims = (part[slot] for part in parts)
            first = -1 if kind == "low" else LOW + depth
            here = layer_at < LOW if kind == "low" else layer_at >= LOW + depth
            for tile in range(FOUR):
                tiles[tile, 0:height, :] = rims[tile, :, 0:128]
                put(tiles, tile, rim_strip_rows()[0][tile], above_rims, below_rims)
                value = tiles[tile]
                for part in range(min(4, channels - 4 * tile)):
                    turned = lane_roll(value, 8 * first - 32 * part)
                    strip_ref[4 * tile + part] = jnp.where(here, turned, strip_ref[4 * tile + part])

        guarded(level_ref[0], receiver, take)
    spot = lane % 8
    for target, high in ((right_ref, False), (left_ref, True)):
        table, count = face_table(high)
        for tile in range(count):
            value = jnp.zeros((rows, 128), jnp.float32)
            for channel, at, first, cols in table:
                if at == tile:
                    turned = lane_roll(strip_ref[channel], first - (4 if high else 4 - cols))
                    value = jnp.where((spot >= first) & (spot < first + cols), turned, value)
            target[tile] = value


def inner_body(levels, level_ref, *rest):
    (posts_ref, above_ref, below_ref), parts, rest = split_given(levels, rest)
    pops_ref, vel_ref, ext, pulled, second = rest
    level = level_ref[0]
    unpack(levels, level, posts_ref, above_ref, below_ref, *parts, ext)
    depth, height, width = posts_ref.shape[1:]
    rows = height + 8

    def pull(source, layer, at):
        bottom = (level == 0) & (layer == 0)
        top = (level == levels - 1) & (layer == depth - 1)
        for index in range(19):
            way_z, way_y, way_x = ways[index]
            value = source[index, at - way_z]
            if way_x != 0:
                value = pltpu.roll(value, way_x % width, 1)
            if way_y != 0:
                value = pltpu.roll(value, way_y % rows, 0)
            if way_z != 0:
                wall = bottom if way_z == 1 else top
                value = jnp.where(wall, source[opposite[index], at], value)
            pulled[index] = value

    tiles = [
        (slice(row, row + 8), slice(col, col + 128))
        for row in range(0, rows, 8)
        for col in range(0, width, 128)
    ]

    def first_step(number, carry):
        at = number + 1
        pull(ext, at - LOW, at)
        for tile in tiles:
            posts = relaxed([pulled[(index, *tile)] for index in range(19)])
            inside = ext[(19, at, *tile)] > 0.5
            for index in range(19):
                second[(index, number, *tile)] = jnp.where(inside, ext[(index, at, *tile)], posts[index])
        return carry

    lax.fori_loop(0, depth + LOW + HIGH - 2, first_step, 0)

    def second_step(number, carry):
        pull(second, number - 1, number + 1)
        for tile in tiles:
            density, moment = moments([pulled[(index, *tile)] for index in range(19)])
            inverse = 1.0 / density
            for axis in range(3):
                vel_ref[(axis, number, *tile)] = moment[axis] * inverse
        return carry

    def second_inner(number, carry):
        second_step(number, carry)
        for index in range(19):
            pops_ref[index, number - 1] = pulled[index, :height, :]
        return carry

    lax.fori_loop(0, 1, second_step, 0)
    lax.fori_loop(1, depth + 1, second_inner, 0)
    lax.fori_loop(depth + 1, depth + 3, second_step, 0)


def edge_body(
    levels, level_ref, strip_ref, left_ref, right_ref, inner_pops, inner_vel,
    pops_ref, vel_ref, beyond_ref, sides, pulled, second,
):
    depth, height, width = pops_ref.shape[1:]
    rows = height + 8
    level = level_ref[0]
    lane = lax.broadcasted_iota(jnp.int32, (rows, 128), 1)
    before = lane % 8 < 4
    bottom = (lane // 8 == LOW) & (level == 0)
    top = (lane // 8 == LOW + depth - 1) & (level == levels - 1)
    for channel, tile, first, cols in face_table(False)[0]:
        turned = lane_roll(left_ref[tile], 4 - cols - first)
        sides[0, channel] = jnp.where(before, turned, strip_ref[channel])
    for channel, tile, first, _ in face_table(True)[0]:
        turned = lane_roll(right_ref[tile], 4 - first)
        sides[1, channel] = jnp.where(before, strip_ref[channel], turned)

    def pull(source, side, target):
        for index in range(19):
            way_z, way_y, way_x = ways[index]
            value = lane_roll(source[side, index], 8 * way_z + way_x)
            if way_y != 0:
                value = pltpu.roll(value, way_y % rows, 0)
            if way_z != 0:
                value = jnp.where(bottom if way_z == 1 else top, source[side, opposite[index]], value)
            target[side, index] = value

    speeds = [[], []]
    for side in range(2):
        pull(sides, side, pulled)
        for row in range(0, rows, 8):
            cut = slice(row, row + 8)
            posts = relaxed([pulled[side, index, cut] for index in range(19)])
            inside = sides[side, 19, cut] > 0.5
            for index in range(19):
                second[side, index, cut] = jnp.where(inside, sides[side, index, cut], posts[index])
        pull(second, side, pulled)
        density, moment = moments([pulled[side, index] for index in range(19)])
        inverse = 1.0 / density
        speeds[side] = [part * inverse for part in moment]

    near = lane[:height]
    near = (near < 2) | (near >= 126)
    front = before[:height]
    for index in range(19):
        value = jnp.where(front, pulled[1, index, :height], pulled[0, index, :height])
        for layer in range(depth):
            turned = lane_roll(value, -(8 * (layer + LOW) + 4))
            for col in range(0, width, 128):
                cells = inner_pops[index, layer, :, col : col + 128]
                if col == 0 or col == width - 128:
                    mask = near if width == 128 else near & ((lane[:height] < 64) == (col == 0))
                    cells = jnp.where(mask, turned, cells)
                pops_ref[index, layer, :, col : col + 128] = cells
    row = lax.broadcasted_iota(jnp.int32, (rows, 128), 0)
    valid = (row < height + 2) | (row == rows - 1)
    outside = (lane < 2) | (lane == 127)
    table = table_rows(depth, height)
    vel_ref[...] = jnp.zeros_like(vel_ref)
    beyond_ref[...] = jnp.zeros_like(beyond_ref)

    def put(target, axis, layer, cols, cells):
        at = axis * table + layer * (height + 3)
        target[at : at + 1, cols] = cells[rows - 1 :, :]
        target[at + 1 : at + height + 3, cols] = cells[: height + 2, :]

    for axis in range(3):
        main = jnp.where(before, speeds[1][axis], speeds[0][axis])
        rest = jnp.where(before, speeds[0][axis], speeds[1][axis])
        for layer in range(depth + 3):
            keep = valid
            if layer == 0:
                keep = valid & (level != 0)
            if layer > depth:
                keep = valid & (level != levels - 1)
            shift = -(8 * (layer - 1 + LOW) + 4)
            turned = lane_roll(main, shift)
            for col in range(0, width, 128):
                cells = inner_vel[axis, layer, :, col : col + 128]
                if col == 0 or col == width - 128:
                    mask = (lane < 2) & (col == 0) | (lane >= 126) & (col == width - 128)
                    cells = jnp.where(mask, turned, cells)
                put(vel_ref, axis, layer, slice(col, col + 128), jnp.where(keep, cells, 0.0))
            put(beyond_ref, axis, layer, slice(0, 128), jnp.where(keep & outside, lane_roll(rest, shift), 0.0))


def shifted(value, axis, step):
    count = lax.axis_size(axis)
    return lax.ppermute(value, axis, [(i, (i + step) % count) for i in range(count)])


def to_level(value, kind, levels, side=None, step=0):
    pairs = []
    for at in range(levels):
        other = 1 - at if levels == 2 else at + 1 if kind in ("low", "up") else at - 1
        if 0 <= other < levels:
            pairs.append((at, other))
    if side is None:
        return lax.ppermute(value, "gz", pairs)
    count = lax.axis_size(side)
    return lax.ppermute(
        value,
        (side, "gz"),
        [
            (brick * levels + at, (brick + step) % count * levels + other)
            for brick in range(count)
            for at, other in pairs
        ],
    )


def wide_exchange(level, pops, coarse_pops, interface):
    levels = lax.axis_size("gz")
    depth, height, width = interface.shape
    sizes = rim_sizes(levels)
    slots = len(sizes)
    kinds = ["low", "high"][:slots]
    down_sizes, up_sizes = zip(*rim_row_sizes(levels))
    outs = call(
        functools.partial(first_body, levels),
        [(channels, depth, height, width), (channels, height, 128)]
        + [(size, width) for size in own_rows(depth)[1]]
        + [(size, height, width) for size in sizes]
        + [(size, width) for size in down_sizes + up_sizes],
        [level, pops, coarse_pops, interface],
    )
    posts, own, down, up = outs[:4]
    rims, down_rims, up_rims = (outs[4 + slots * at : 4 + slots * at + slots] for at in range(3))
    given = [shifted(down, "gy", -1), shifted(up, "gy", 1)]
    given += [to_level(value, kind, levels) for value, kind in zip(rims, kinds)]
    given += [to_level(value, kind, levels, "gy", -1) for value, kind in zip(down_rims, kinds)]
    given += [to_level(value, kind, levels, "gy", 1) for value, kind in zip(up_rims, kinds)]
    deep, rows = depth + LOW + HIGH, height + 8
    ext = pltpu.VMEM((channels, deep, rows, width), jnp.float32)
    strip, right, left = call(
        functools.partial(strip_body, levels, depth),
        [(channels, rows, 128)] + [(face_table(high)[1], rows, 128) for high in (False, True)],
        [level, own] + given,
        1,
        [pltpu.VMEM((FOUR, rows, 128), jnp.float32)],
        heads=[(1, strip_rows()[1][0]), (2, strip_rows()[1][1])]
        + [(3 + at, FOUR) for at in range(slots)]
        + [(3 + slots + at, rim_strip_rows()[1][0]) for at in range(slots)]
        + [(3 + 2 * slots + at, rim_strip_rows()[1][1]) for at in range(slots)],
    )
    left, right = shifted(right, "gx", 1), shifted(left, "gx", -1)
    inner_pops, inner_vel = call(
        functools.partial(inner_body, levels),
        [pops.shape, (3, depth + 3, rows, width)],
        [level, posts] + given,
        1,
        [
            ext,
            pltpu.VMEM((19, rows, width), jnp.float32),
            pltpu.VMEM((19, deep - 2, rows, width), jnp.float32),
        ],
        pl.CostEstimate(flops=10**8, bytes_accessed=1 << 22, transcendentals=0),
    )
    return [strip, left, right, inner_pops, inner_vel]


def phis(frac):
    angle = frac * (0.5 * math.pi)
    sine = 0.25 * jnp.sin(angle)
    cosine = 0.25 * jnp.cos(angle)
    return (0.25 - sine, 0.25 + cosine, 0.25 + sine, 0.25 - cosine)


def split(value):
    high = value.astype(jnp.bfloat16)
    return high, (value - high.astype(jnp.float32)).astype(jnp.bfloat16)


def pick(step, parts):
    value = jnp.where(step == 0, parts[0], 0.0)
    for index in range(1, 4):
        value = jnp.where(step == index, parts[index], value)
    return value


def dots(left, right, dims):
    return lax.dot_general(left, right, (dims, ((), ())), preferred_element_type=jnp.float32)


def table_rows(depth, height):
    return -(-(depth + 3) * (height + 3) // 16) * 16


def droplet_body(
    size, counts_ref, dest_ref, vel_ref, beyond_ref, speed_ref, frac_ref, home_ref, spread_ref, outer_ref,
    stay_ref, state_ref, twice, mixed, along, push_high, push_low, plane_ref,
):
    depth, height, width = size
    blocks = home_ref.shape[0]
    layers, rows = depth + 3, height + 3
    table = table_rows(depth, height)
    high, low = split(vel_ref[...])
    twice[:, :width] = high
    twice[:, width:] = high
    mixed[:, :width] = low
    high, low = (part.astype(jnp.float32) for part in split(beyond_ref[...]))
    mixed[:, width:] = (high + lane_roll(low, 32) + lane_roll(high, 64)).astype(jnp.bfloat16)
    along[2 * width :, :] = jnp.zeros((128, along.shape[1]), jnp.bfloat16)
    plane_ref[:, layers * rows :, :] = jnp.zeros(
        (plane_ref.shape[0], table - layers * rows, 256), jnp.float32
    )
    span_x = lax.broadcasted_iota(jnp.int32, (width, 128), 0) + 1
    span_end = lax.broadcasted_iota(jnp.int32, (16, 128), 0)
    span_y = lax.broadcasted_iota(jnp.int32, (-(-rows // 8) * 8, 128), 0)
    span_z = lax.broadcasted_iota(jnp.int32, (-(-layers // 8) * 8, 128), 0)
    slots = lax.broadcasted_iota(jnp.int32, (1, 128), 1)

    def weigh(number):
        for half in range(2):
            block = 2 * number + half
            side = slice(block * 128, block * 128 + 128)
            cell = home_ref[block : block + 1, :]
            cell_x = cell % width
            cell_y = cell // width % height
            cell_z = cell // (width * height)
            part_x = phis(frac_ref[0, block : block + 1, :])
            part_y = phis(frac_ref[1, block : block + 1, :])
            part_z = phis(frac_ref[2, block : block + 1, :])
            high, low = split(pick(span_x - cell_x, part_x))
            along[0:width, side] = low
            along[width : 2 * width, side] = high
            high, low = split(pick(span_end + (width + 1) - cell_x, part_x))
            along[2 * width : 2 * width + 16, side] = high
            along[2 * width + 32 : 2 * width + 48, side] = high
            along[2 * width + 64 : 2 * width + 80, side] = low
            high, low = split(jnp.where((span_end == 15) & (cell_x == 0), part_x[0], 0.0))
            along[2 * width + 112 : 2 * width + 128, side] = high
            along[2 * width + 16 : 2 * width + 32, side] = high
            along[2 * width + 48 : 2 * width + 64, side] = low
            weight_y = pick(span_y - cell_y, part_y)[:rows]
            weight_z = pick(span_z - cell_z, part_z)
            for layer in range(layers):
                plane_ref[number % 2, layer * rows : layer * rows + rows, half * 128 : half * 128 + 128] = (
                    weight_y * weight_z[layer : layer + 1, :]
                )

    def sample(number):
        pair = slice(number * 256, number * 256 + 256)
        return dots(twice[...], along[0 : 2 * width, pair], ((1,), (0,))) + dots(
            mixed[...], along[width:, pair], ((1,), (0,))
        )

    def move(number, sums):
        plane = plane_ref[number % 2]
        for axis in range(3):
            where = slice(axis * table, axis * table + table)
            sampled = jnp.sum(sums[where] * plane, axis=0, keepdims=True)
            for half in range(2):
                block = 2 * number + half
                live = slots < counts_ref[block]
                sample = sampled[:, half * 128 : half * 128 + 128]
                speed = speed_ref[axis, block : block + 1, :]
                frac = frac_ref[axis, block : block + 1, :]
                moved = speed + relax * (sample - speed)
                push = jnp.where(live, couple * (moved - sample), 0.0)
                stays = live & (dest_ref[block] == 13)
                for at, value in ((axis, moved), (3 + axis, frac + moved)):
                    state_ref[block, at : at + 1, :] = jnp.where(live, value, 0.0)
                    stay_ref[at, block : block + 1, :] = jnp.where(stays, value, 0.0)
                high, low = split(plane[:, half * 128 : half * 128 + 128] * push)
                push_high[where, block * 128 : block * 128 + 128] = high
                push_low[where, block * 128 : block * 128 + 128] = low

    pairs = blocks // 2
    weigh(0)
    for number in range(pairs):
        sums = sample(number)
        if number + 1 < pairs:
            weigh(number + 1)
        move(number, sums)
    main = dots(push_high[...], along[0 : 2 * width, :], ((1,), (1,)))
    rest = dots(push_low[...], along[width:, :], ((1,), (1,)))
    outer = dots(push_high[...], along[2 * width :, :], ((1,), (1,)))
    spread_ref[...] = main[:, :width] + main[:, width:] + rest[:, :width]
    outer_ref[...] = outer + lane_roll(outer, -64) + rest[:, width:]


def force_sides(levels):
    if levels == 2:
        return [("up", 0, 1, 0), ("down", 1, 0, 0)]
    return [("up", None, None, 0), ("down", None, None, 1)]


GROUP = 6 * 8


def group_at(way_z, way_y):
    return (way_z + 1) * 3 + way_y + 1


def face_rows(depth, height):
    return -(-depth // 8) * height


def message_rows(depth):
    return [8 * 8, 2 * 4 * depth, 4 * depth, 2 * 8, 8]


def pack_body(
    levels, level_ref, dest_ref, spread_ref, outer_ref, state_ref, own_ref, side_ref,
    to_levels, north_ref, south_ref, north_levels, south_levels, outbox, strip, taken,
):
    depth, height, width = own_ref.shape[1:]
    level = level_ref[0]
    rows, table = height + 3, table_rows(depth, height)
    lane = lax.broadcasted_iota(jnp.int32, (table, 128), 1)
    value = jnp.zeros((table, 128), jnp.float32)
    for axis in range(3):
        here = (lane >= 4 * axis) & (lane < 4 * axis + 3)
        cells = outer_ref[axis * table : axis * table + table, :]
        value = jnp.where(here, lane_roll(cells, 4 * axis + 1), value)
    strip[...] = value
    for code in range(27):
        taken[code] = 0
    outbox[...] = jnp.zeros_like(outbox)
    for block in range(state_ref.shape[0]):
        code = dest_ref[block]

        @pl.when(code != 13)
        def _():
            rank = taken[code]
            outbox[code * CAP + rank] = state_ref[block]
            taken[code] = rank + 1

    def force(part, layer, cut):
        at = layer * rows
        if part < 3:
            return spread_ref[part * table + at + cut.start : part * table + at + cut.stop, :]
        return strip[at + cut.start : at + cut.stop, :]

    def blocks(target, way_z, way_y):
        base = target.shape[0] - GROUP
        for slot in range(6):
            target[base + 8 * slot : base + 8 * slot + 8, :] = outbox[6 * group_at(way_z, way_y) + slot]

    main, north, south = slice(1, height + 1), slice(height + 1, height + 3), slice(0, 1)
    for part in range(4):
        for layer in range(depth):
            own_ref[part, layer] = force(part, layer + 1, main)
            at = part * depth + layer
            north_ref[2 * at : 2 * at + 2, :] = force(part, layer + 1, north)
            south_ref[at : at + 1, :] = force(part, layer + 1, south)
    blocks(north_ref, 0, 1)
    blocks(south_ref, 0, -1)
    for slot in range(2):
        side_ref[slot] = outbox[6 * group_at(0, 0) + slot]
        side_ref[2 + slot] = outbox[6 * group_at(0, 0) + 4 + slot]
    for kind, sender, _, slot in force_sides(levels):

        def pack(kind=kind, slot=slot):
            for part in range(4):
                for step in range(2 if kind == "up" else 1):
                    layer = depth + 1 + step if kind == "up" else 0
                    at = 2 * part + step
                    to_levels[slot][8 * at : 8 * at + 8, :] = force(part, layer, main)
                    north_levels[slot][2 * at : 2 * at + 2, :] = force(part, layer, north)
                    south_levels[slot][at : at + 1, :] = force(part, layer, south)
            way = 1 if kind == "up" else -1
            blocks(to_levels[slot], way, 0)
            blocks(north_levels[slot], way, 1)
            blocks(south_levels[slot], way, -1)

        guarded(level, sender, pack)


def main_body(
    levels, level_ref, counts_ref, dest_ref, strip_ref, left_ref, right_ref, inner_pops, inner_vel,
    speed_ref, frac_ref, home_ref, pops_ref, own_ref, stay_ref, side_ref, north_ref, south_ref, *rest,
):
    slots = len(rim_sizes(levels))
    to_levels, north_levels, south_levels = (rest[slots * at : slots * at + slots] for at in range(3))
    rest = rest[3 * slots :]
    vel_ref, beyond_ref, spread_ref, outer_ref, state_ref, outbox, strip, taken = rest[:8]
    edge_body(
        levels, level_ref, strip_ref, left_ref, right_ref, inner_pops, inner_vel,
        pops_ref, vel_ref, beyond_ref, *rest[8:11],
    )
    droplet_body(
        pops_ref.shape[1:], counts_ref, dest_ref, vel_ref, beyond_ref, speed_ref, frac_ref, home_ref,
        spread_ref, outer_ref, stay_ref, state_ref, *rest[11:],
    )
    pack_body(
        levels, level_ref, dest_ref, spread_ref, outer_ref, state_ref, own_ref, side_ref,
        to_levels, north_ref, south_ref, north_levels, south_levels, outbox, strip, taken,
    )


def gather_body(levels, level_ref, own_ref, side_ref, *rest):
    depth, height, width = own_ref.shape[1:]
    slots = len(rim_sizes(levels))
    north_ref, south_ref = rest[:2]
    from_levels, north_levels, south_levels = (rest[2 + slots * at : 2 + slots * at + slots] for at in range(3))
    force_ref, right_ref, left_ref, total = rest[2 + 3 * slots :]
    base = face_rows(depth, height)
    total[...] = own_ref[...]
    right_ref[base:, :] = jnp.zeros((right_ref.shape[0] - base, width), jnp.float32)
    left_ref[base:, :] = jnp.zeros((left_ref.shape[0] - base, width), jnp.float32)
    last = slice(height - 1, height)
    for part in range(4):
        for layer in range(depth):
            at = part * depth + layer
            total[part, layer, 0:2, :] += north_ref[2 * at : 2 * at + 2, :]
            total[part, layer, last, :] += south_ref[at : at + 1, :]

    def blocks(source, way_z, way_y):
        at = base + 12 * group_at(way_z, way_y)
        start = source.shape[0] - GROUP
        for slot in range(CAP):
            rows = slice(at + 6 * slot, at + 6 * slot + 6)
            left_ref[rows, :] = source[start + 8 * slot : start + 8 * slot + 6, :]
            right_ref[rows, :] = source[start + 32 + 8 * slot : start + 38 + 8 * slot, :]

    at = base + 12 * group_at(0, 0)
    for slot in range(CAP):
        left_ref[at + 6 * slot : at + 6 * slot + 6, :] = side_ref[slot, 0:6, :]
        right_ref[at + 6 * slot : at + 6 * slot + 6, :] = side_ref[2 + slot, 0:6, :]
    blocks(north_ref, 0, 1)
    blocks(south_ref, 0, -1)
    for kind, _, receiver, slot in force_sides(levels):

        def take(kind=kind, slot=slot):
            for part in range(4):
                for step in range(2 if kind == "up" else 1):
                    layer = step if kind == "up" else depth - 1
                    at = 2 * part + step
                    total[part, layer] += from_levels[slot][8 * at : 8 * at + 8, :]
                    total[part, layer, 0:2, :] += north_levels[slot][2 * at : 2 * at + 2, :]
                    total[part, layer, last, :] += south_levels[slot][at : at + 1, :]
            way = 1 if kind == "up" else -1
            blocks(from_levels[slot], way, 0)
            blocks(north_levels[slot], way, 1)
            blocks(south_levels[slot], way, -1)

        guarded(level_ref[0], receiver, take)
    for layer in range(depth):
        for axis in range(3):
            force_ref[axis, layer] = total[axis, layer]
    lane = lax.broadcasted_iota(jnp.int32, (height, 128), 1)
    for tile in range(base // height):
        value = jnp.zeros((height, 128), jnp.float32)
        for layer in range(8 * tile, min(8 * tile + 8, depth)):
            part = layer - 8 * tile
            value = jnp.where(lane // 16 == part, lane_roll(total[3, layer, :, 0:128], 16 * part), value)
        for target in (right_ref, left_ref):
            target[tile * height : tile * height + height, 0:128] = value


def last_body(levels, level_ref, part_ref, stay_ref, *rest):
    depth, height, width = part_ref.shape[1:]
    slots = len(rim_sizes(levels))
    north_ref, south_ref = rest[:2]
    from_levels, north_levels, south_levels = (rest[2 + slots * at : 2 + slots * at + slots] for at in range(3))
    right_ref, left_ref, force_ref, arrived_ref = rest[2 + 3 * slots :]
    blocks = stay_ref.shape[1]
    base = face_rows(depth, height)
    lane = lax.broadcasted_iota(jnp.int32, (height, 128), 1)
    for layer in range(depth):
        rows = slice(layer // 8 * height, layer // 8 * height + height)
        before, after = right_ref[rows, :128], left_ref[rows, :128]
        for axis in range(3):
            at = 16 * (layer % 8) + 4 * axis
            first = jnp.where(lane < 2, lane_roll(before, -at - 1), 0.0)
            final = jnp.where(lane == 127, lane_roll(after, 127 - at), 0.0)
            force_ref[axis, layer] = part_ref[axis, layer]
            force_ref[axis, layer, :, 0:128] += first
            force_ref[axis, layer, :, width - 128 : width] += final
    arrived_ref[:, 0:blocks, :] = stay_ref[...]

    def put(source, start, stride, way_z, way_y, way_x):
        code = group_at(way_z, way_y) * 3 + way_x + 1
        at = blocks + CAP * (code if code < 13 else code - 1)
        for slot in range(CAP):
            for axis in range(6):
                if source is None:
                    value = jnp.zeros((1, 128), jnp.float32)
                else:
                    value = source[start + stride * slot + axis : start + stride * slot + axis + 1, :]
                arrived_ref[axis, at + slot : at + slot + 1, :] = value

    for way_z in (-1, 0, 1):
        for way_y in (-1, 0, 1):
            for way_x, source in ((1, right_ref), (-1, left_ref)):
                put(source, base + 12 * group_at(way_z, way_y), 6, way_z, way_y, way_x)
    middle = 16

    def put_group(source, way_z, way_y):
        put(source, None if source is None else source.shape[0] - GROUP + middle, 8, way_z, way_y, 0)

    put_group(north_ref, 0, 1)
    put_group(south_ref, 0, -1)
    for kind, _, receiver, slot in force_sides(levels):
        way = 1 if kind == "up" else -1

        def take(way=way, slot=slot):
            put_group(from_levels[slot], way, 0)
            put_group(north_levels[slot], way, 1)
            put_group(south_levels[slot], way, -1)

        def clear(way=way):
            for way_y in (-1, 0, 1):
                put_group(None, way, way_y)

        guarded(level_ref[0], receiver, take)
        if receiver is not None:
            guarded(level_ref[0], 1 - receiver, clear)


def local(pops, coarse_pops, interface, drop_vel, drop_frac, home, counts, dest):
    level = lax.axis_index("gz").astype(jnp.int32).reshape(1)
    levels = lax.axis_size("gz")
    depth, height, width = interface.shape
    blocks = home.shape[0]
    kinds = ["up", "down"][: len(rim_sizes(levels))]
    slots = len(kinds)
    given = wide_exchange(level, pops, coarse_pops, interface)
    rows = height + 8
    table = table_rows(depth, height)
    sizes = [(count + GROUP, width) for count in message_rows(depth)]
    outs = call(
        functools.partial(main_body, levels),
        [pops.shape, (4, depth, height, width), (6, blocks, 128), (4, 8, 128), sizes[1], sizes[2]]
        + [sizes[0]] * slots
        + [sizes[3]] * slots
        + [sizes[4]] * slots,
        [level, counts, dest] + given + [drop_vel, drop_frac, home],
        3,
        [
            pltpu.VMEM((3 * table, width), jnp.float32),
            pltpu.VMEM((3 * table, 128), jnp.float32),
            pltpu.VMEM((3 * table, width), jnp.float32),
            pltpu.VMEM((3 * table, 128), jnp.float32),
            pltpu.VMEM((blocks, 8, 128), jnp.float32),
            pltpu.VMEM((27 * CAP, 8, 128), jnp.float32),
            pltpu.VMEM((table, 128), jnp.float32),
            pltpu.SMEM((27,), jnp.int32),
            pltpu.VMEM((2, channels, rows, 128), jnp.float32),
            pltpu.VMEM((2, 19, rows, 128), jnp.float32),
            pltpu.VMEM((2, 19, rows, 128), jnp.float32),
            pltpu.VMEM((3 * table, 2 * width), jnp.bfloat16),
            pltpu.VMEM((3 * table, width + 128), jnp.bfloat16),
            pltpu.VMEM((2 * width + 128, blocks * 128), jnp.bfloat16),
            pltpu.VMEM((3 * table, blocks * 128), jnp.bfloat16),
            pltpu.VMEM((3 * table, blocks * 128), jnp.bfloat16),
            pltpu.VMEM((2, table, 256), jnp.float32),
        ],
    )
    state, own, stay, side, north, south = outs[:6]
    to_levels, north_levels, south_levels = (outs[6 + slots * at : 6 + slots * at + slots] for at in range(3))
    received = [shifted(north, "gy", 1), shifted(south, "gy", -1)]
    received += [to_level(value, kind, levels) for value, kind in zip(to_levels, kinds)]
    received += [to_level(value, kind, levels, "gy", 1) for value, kind in zip(north_levels, kinds)]
    received += [to_level(value, kind, levels, "gy", -1) for value, kind in zip(south_levels, kinds)]
    side_rows = (padded(face_rows(depth, height) + 9 * 6 * CAP), width)
    part, right, left = call(
        functools.partial(gather_body, levels),
        [(3, depth, height, width), side_rows, side_rows],
        [level, own, side] + received,
        1,
        [pltpu.VMEM((4, depth, height, width), jnp.float32)],
    )
    force, arrived = call(
        functools.partial(last_body, levels),
        [(3, depth, height, width), (6, blocks + 26 * CAP, 128)],
        [level, part, stay] + received + [shifted(right, "gx", 1), shifted(left, "gx", -1)],
    )
    return state, force, arrived


def solution(mesh):
    return jax.shard_map(
        local,
        mesh=mesh,
        in_specs=(
            P(None, "gz", "gy", "gx"),
            P(None, "gz", "gy", "gx"),
            P("gz", "gy", "gx"),
            P(None, ("gx", "gy", "gz"), None),
            P(None, ("gx", "gy", "gz"), None),
            P(("gx", "gy", "gz"), None),
            P(("gx", "gy", "gz")),
            P(("gx", "gy", "gz")),
        ),
        out_specs=(
            P(None, "gz", "gy", "gx"),
            P(None, "gz", "gy", "gx"),
            P(None, ("gx", "gy", "gz"), None),
        ),
        check_vma=False,
    )
```

```python
import functools
import math

import jax
import jax.numpy as jnp
import numpy as np
from jax import lax
from jax.experimental import pallas as pl
from jax.experimental.pallas import tpu as pltpu
from jax.sharding import PartitionSpec as P

CAP = 2


lattice = np.array(
    [
        [0, 0, 0],
        [1, 0, 0],
        [-1, 0, 0],
        [0, 1, 0],
        [0, -1, 0],
        [0, 0, 1],
        [0, 0, -1],
        [1, 1, 0],
        [-1, -1, 0],
        [1, -1, 0],
        [-1, 1, 0],
        [1, 0, 1],
        [-1, 0, -1],
        [1, 0, -1],
        [-1, 0, 1],
        [0, 1, 1],
        [0, -1, -1],
        [0, 1, -1],
        [0, -1, 1],
    ]
)
weights_table = np.array([1.0 / 3.0] + [1.0 / 18.0] * 6 + [1.0 / 36.0] * 12)
opposite = [0, 2, 1, 4, 3, 6, 5, 8, 7, 10, 9, 12, 11, 14, 13, 16, 15, 18, 17]
inverse_tau = 0.8
relax = 0.5
couple = 8.0


class Level:
    def __getitem__(self, _):
        return lax.axis_index("gz").astype(jnp.int32)


class Moving:
    def __init__(self, buffer, copy):
        self.buffer = buffer
        self.copy = copy

    def take(self):
        self.copy.wait()
        return self.buffer


def call(body, outs, arrays, scratch=(), cost=None, heads=(), late=(), kind=jnp.float32):
    heads = dict(heads)
    landing = []
    for at, value in enumerate(arrays):
        space = pltpu.SMEM if value.ndim == 1 else pltpu.VMEM
        landing.append(space((heads.get(at, value.shape[0]),) + value.shape[1:], value.dtype))

    def whole(*refs):
        given = refs[: len(arrays)]
        made = list(refs[len(arrays) : len(arrays) + len(outs)])
        rest = refs[len(arrays) + len(outs) :]
        landed, done, rest = list(rest[: len(arrays)]), rest[len(arrays)], rest[len(arrays) + 1 :]
        copies = []
        for at, (source, target) in enumerate(zip(given, landed)):
            if at in heads:
                source = source.at[pl.ds(0, heads[at])]
            copies.append(pltpu.make_async_copy(source, target, done.at[at]))
        for copy in copies:
            copy.start()
        for at, copy in enumerate(copies):
            if at in late:
                landed[at] = Moving(landed[at], copy)
            else:
                copy.wait()
        body(Level(), *landed, *made, *rest)

    vmem = pl.BlockSpec(memory_space=pltpu.VMEM)
    hbm = pl.BlockSpec(memory_space=pltpu.HBM)
    return pl.pallas_call(
        whole,
        out_shape=[
            jax.ShapeDtypeStruct(shape, kind[at] if isinstance(kind, list) else kind)
            for at, shape in enumerate(outs)
        ],
        in_specs=[hbm] * len(arrays),
        out_specs=[vmem] * len(outs),
        scratch_shapes=landing
        + [pltpu.SemaphoreType.DMA((len(arrays),))]
        + list(scratch),
        cost_estimate=cost,
        compiler_params=pltpu.CompilerParams(vmem_limit_bytes=64 * 1024 * 1024),
    )(*arrays)


ways = [tuple(int(part) for part in lattice[index][::-1]) for index in range(19)] + [(0, 0, 0)]
channels = len(ways)
LOW = 3
HIGH = 4


def low_reach(way):
    return 2 + way


def high_reach(way):
    return 3 - way


def rim(kind):
    count, reach = (LOW, low_reach) if kind == "low" else (HIGH, high_reach)
    return [
        (step, channel)
        for step in range(1, count + 1)
        for channel in range(channels)
        if step <= reach(ways[channel][0])
    ]


def rim_count(kind):
    return LOW if kind == "low" else HIGH


def rim_sides(levels):
    if levels == 2:
        return [("low", 1, 0, 0), ("high", 0, 1, 0)]
    return [("low", None, None, 0), ("high", None, None, 1)]


def rim_sizes(levels):
    sizes = [FOUR + len(rim(kind)) for kind, _, _, _ in rim_sides(levels)]
    return [max(sizes)] if levels == 2 else sizes


def guarded(level, guard, action):
    if guard is None:
        action()
    else:
        pl.when(level == guard)(action)


def padded(count):
    return -(-count // 8) * 8


def reaches(channel, bounces):
    way_z, way, _ = ways[channel]
    above, below = high_reach(way), low_reach(way)
    if bounces and way_z != 0:
        above, below = max(above, HIGH - 1), max(below, LOW - 1)
    return above, below


def row_places(cells, start=(0, 0)):
    places, (high_at, low_at) = [], start
    for above, below in cells:
        places.append((high_at, low_at, above, below))
        high_at, low_at = high_at + above, low_at + below
    return places, (padded(high_at), padded(low_at))


def strip_rows():
    return row_places([reaches(channel, True) for channel in range(channels)])


def own_rows(depth):
    cells = [(layer, channel) for layer in range(depth) for channel in range(channels)]
    places, sizes = row_places(
        [reaches(channel, layer in (0, depth - 1)) for layer, channel in cells], strip_rows()[1]
    )
    return [(layer, channel, place) for (layer, channel), place in zip(cells, places)], sizes


FOUR = -(-channels // 4)


def rim_strip_rows():
    return row_places([(HIGH, LOW)] * FOUR)


def rim_rows(kind):
    places, sizes = row_places([reaches(channel, False) for _, channel in rim(kind)], rim_strip_rows()[1])
    return [(step, channel, place) for (step, channel), place in zip(rim(kind), places)], sizes


def rim_row_sizes(levels):
    sizes = [rim_rows(kind)[1] for kind, _, _, _ in rim_sides(levels)]
    return [tuple(max(part) for part in zip(*sizes))] if levels == 2 else sizes


def face_table(high):
    wants = []
    for channel in range(channels):
        way_z, _, way = ways[channel]
        count = high_reach(way) if high else low_reach(way)
        if way_z != 0:
            count = max(count, (HIGH if high else LOW) - 1)
        wants.append((-count, channel))
    free, table = [], []
    for count, channel in sorted(wants):
        tile = next((at for at, room in enumerate(free) if room >= -count), len(free))
        if tile == len(free):
            free.append(8)
        table.append((channel, tile, 8 - free[tile], -count))
        free[tile] += count
    return table, len(free)


def moments(cells):
    density = cells[0] * float(weights_table[0])
    moment = [None, None, None]
    face, edge = float(weights_table[1]), float(weights_table[7])
    edge_sum = cells[7]
    for index in range(8, 19):
        edge_sum = edge_sum + cells[index]
    face_sum = cells[1]
    for index in range(2, 7):
        face_sum = face_sum + cells[index]
    density = density + face * face_sum + edge * edge_sum
    for axis in range(3):
        total = {}
        for group, indices in ((face, range(1, 7)), (edge, range(7, 19))):
            plus, minus = None, None
            for index in indices:
                way = int(lattice[index][axis])
                if way == 1:
                    plus = cells[index] if plus is None else plus + cells[index]
                if way == -1:
                    minus = cells[index] if minus is None else minus + cells[index]
            total[group] = plus - minus
        moment[axis] = face * total[face] + edge * total[edge]
    return density, moment


def relaxed(cells):
    density, moment = moments(cells)
    inverse = 1.0 / density
    flow = [part * inverse for part in moment]
    square = flow[0] * flow[0] + flow[1] * flow[1] + flow[2] * flow[2]
    scale = density * inverse_tau
    base = scale * (1.0 - 1.5 * square)
    keep = 1.0 - inverse_tau
    posts = [None] * 19
    posts[0] = keep * cells[0] + base
    for index in range(1, 19, 2):
        along = None
        for axis in range(3):
            way = int(lattice[index][axis])
            if way != 0:
                part = flow[axis] if way == 1 else -flow[axis]
                along = part if along is None else along + part
        odd = 3.0 * scale * along
        even = base + (4.5 * scale) * (along * along)
        posts[index] = keep * cells[index] + (even + odd)
        posts[index + 1] = keep * cells[index + 1] + (even - odd)
    return posts


def lane_roll(value, shift):
    shift = shift % value.shape[-1]
    return value if shift == 0 else pltpu.roll(value, shift, value.ndim - 1)


def first_body(
    levels, level_ref, pops_ref, coarse_ref, interface_ref, posts_ref, strip_ref, down_ref, up_ref, *outs
):
    depth, height, width = interface_ref.shape
    slots = len(rim_sizes(levels))
    rims, down_rims, up_rims = (outs[slots * at : slots * at + slots] for at in range(3))
    lane = lax.broadcasted_iota(jnp.int32, (height, 128), 1)

    def put_rows(down, up, place, cells):
        down_at, up_at, down_rows, up_rows = place
        cols = slice(0, cells.shape[1])
        down[down_at : down_at + down_rows, cols] = cells[:down_rows, :]
        up[up_at : up_at + up_rows, cols] = cells[height - up_rows :, :]

    own = own_rows(depth)[0]
    for layer in range(depth):
        mask = interface_ref[layer]
        inside = mask == 1
        posts = relaxed([pops_ref[index, layer] for index in range(19)])
        posts = [
            jnp.where(inside, coarse_ref[index, layer].astype(jnp.float32), posts[index])
            for index in range(19)
        ] + [mask.astype(jnp.float32)]
        for channel in range(channels):
            posts_ref[channel, layer] = posts[channel]
            put_rows(down_ref, up_ref, own[layer * channels + channel][2], posts[channel])
    for channel in range(channels):
        value = jnp.zeros((height, 128), jnp.float32)
        for layer in range(depth):
            cells = posts_ref[channel, layer]
            if width > 128:
                cells = jnp.where(lane < 64, cells[:, :128], cells[:, width - 128 :])
            value = jnp.where(lane // 8 == LOW + layer, lane_roll(cells, 8 * (LOW + layer) + 4), value)
        strip_ref[channel] = value
        put_rows(down_ref, up_ref, strip_rows()[0][channel], value)
    for kind, _, sender, slot in rim_sides(levels):

        def pack(kind=kind, slot=slot):
            for tile in range(FOUR):
                value = jnp.zeros((height, 128), jnp.float32)
                for part in range(min(4, channels - 4 * tile)):
                    first = LOW + depth - 4 if kind == "low" else LOW
                    turned = lane_roll(strip_ref[4 * tile + part], 32 * part - 8 * first)
                    value = jnp.where(lane // 32 == part, turned, value)
                rims[slot][tile, :, 0:128] = value
                put_rows(down_rims[slot], up_rims[slot], rim_strip_rows()[0][tile], value)
            for at, (step, channel, place) in enumerate(rim_rows(kind)[0]):
                cells = posts_ref[channel, depth - step if kind == "low" else step - 1]
                rims[slot][FOUR + at] = cells
                put_rows(down_rims[slot], up_rims[slot], place, cells)

        guarded(level_ref[0], sender, pack)


def unpack(levels, level, posts_ref, above_ref, below_ref, rims, above_rims, below_rims, ext):
    depth, height = posts_ref.shape[1:3]
    rows = height + 8

    def put(channel, at, cells, place, above, below):
        above_at, below_at, above_rows, below_rows = place
        ext[channel, at, :height, :] = cells
        ext[channel, at, height : height + above_rows, :] = above[above_at : above_at + above_rows, :]
        ext[channel, at, rows - below_rows : rows, :] = below[below_at : below_at + below_rows, :]

    for layer, channel, place in own_rows(depth)[0]:
        put(channel, LOW + layer, posts_ref[channel, layer], place, above_ref, below_ref)
    for kind, receiver, _, slot in rim_sides(levels):

        def take(kind=kind, slot=slot):
            for at, (step, channel, place) in enumerate(rim_rows(kind)[0]):
                layer = LOW - step if kind == "low" else LOW + depth + step - 1
                put(channel, layer, rims[slot][FOUR + at], place, above_rims[slot], below_rims[slot])

        guarded(level, receiver, take)


def split_given(levels, rest):
    slots = len(rim_sizes(levels))
    parts = [rest[3 + slots * at : 3 + slots * at + slots] for at in range(3)]
    return rest[:3], parts, rest[3 + 3 * slots :]


def strip_body(levels, depth, level_ref, *rest):
    (own_ref, above_ref, below_ref), parts, rest = split_given(levels, rest)
    _, strip_ref, right_ref, left_ref, tiles = rest
    rows = strip_ref.shape[1]
    height = rows - 8
    lane = lax.broadcasted_iota(jnp.int32, (rows, 128), 1)
    layer_at = lane // 8

    def put(target, index, place, above, below):
        above_at, below_at, above_rows, below_rows = place
        target[index, height : height + above_rows, :] = above[above_at : above_at + above_rows, 0:128]
        target[index, rows - below_rows :, :] = below[below_at : below_at + below_rows, 0:128]

    for channel in range(channels):
        strip_ref[channel, 0:height, :] = own_ref[channel]
        put(strip_ref, channel, strip_rows()[0][channel], above_ref, below_ref)
    for kind, receiver, _, slot in rim_sides(levels):

        def take(kind=kind, slot=slot):
            rims, above_rims, below_rims = (part[slot] for part in parts)
            first = -1 if kind == "low" else LOW + depth
            here = layer_at < LOW if kind == "low" else layer_at >= LOW + depth
            for tile in range(FOUR):
                tiles[tile, 0:height, :] = rims[tile, :, 0:128]
                put(tiles, tile, rim_strip_rows()[0][tile], above_rims, below_rims)
                value = tiles[tile]
                for part in range(min(4, channels - 4 * tile)):
                    turned = lane_roll(value, 8 * first - 32 * part)
                    strip_ref[4 * tile + part] = jnp.where(here, turned, strip_ref[4 * tile + part])

        guarded(level_ref[0], receiver, take)
    spot = lane % 8
    for target, high in ((right_ref, False), (left_ref, True)):
        table, count = face_table(high)
        for tile in range(count):
            value = jnp.zeros((rows, 128), jnp.float32)
            for channel, at, first, cols in table:
                if at == tile:
                    turned = lane_roll(strip_ref[channel], first - (4 if high else 4 - cols))
                    value = jnp.where((spot >= first) & (spot < first + cols), turned, value)
            target[tile] = value


def inner_body(levels, level_ref, *rest):
    (posts_ref, above_ref, below_ref), parts, rest = split_given(levels, rest)
    pops_ref, vel_ref, ext, pulled, second = rest
    level = level_ref[0]
    unpack(levels, level, posts_ref, above_ref, below_ref, *parts, ext)
    depth, height, width = posts_ref.shape[1:]
    rows = height + 8

    def pull(source, layer, at):
        bottom = (level == 0) & (layer == 0)
        top = (level == levels - 1) & (layer == depth - 1)
        for index in range(19):
            way_z, way_y, way_x = ways[index]
            value = source[index, at - way_z]
            if way_x != 0:
                value = pltpu.roll(value, way_x % width, 1)
            if way_y != 0:
                value = pltpu.roll(value, way_y % rows, 0)
            if way_z != 0:
                wall = bottom if way_z == 1 else top
                value = jnp.where(wall, source[opposite[index], at], value)
            pulled[index] = value

    tiles = [
        (slice(row, row + 8), slice(col, col + 128))
        for row in range(0, rows, 8)
        for col in range(0, width, 128)
    ]

    def first_step(number, carry):
        at = number + 1
        pull(ext, at - LOW, at)
        for tile in tiles:
            posts = relaxed([pulled[(index, *tile)] for index in range(19)])
            inside = ext[(19, at, *tile)] > 0.5
            for index in range(19):
                second[(index, number, *tile)] = jnp.where(inside, ext[(index, at, *tile)], posts[index])
        return carry

    first = jnp.where(level == 0, LOW - 1, 0)
    final = jnp.where(level == levels - 1, depth + LOW - 1, depth + LOW + HIGH - 2)
    lax.fori_loop(first, final, first_step, 0)

    def second_step(number, carry):
        pull(second, number - 1, number + 1)
        for tile in tiles:
            density, moment = moments([pulled[(index, *tile)] for index in range(19)])
            inverse = 1.0 / density
            for axis in range(3):
                vel_ref[(axis, number, *tile)] = moment[axis] * inverse
        return carry

    def second_inner(number, carry):
        second_step(number, carry)
        for index in range(19):
            pops_ref[index, number - 1] = pulled[index, :height, :]
        return carry

    lax.fori_loop(jnp.where(level == 0, 1, 0), 1, second_step, 0)
    lax.fori_loop(1, depth + 1, second_inner, 0)
    lax.fori_loop(depth + 1, jnp.where(level == levels - 1, depth + 1, depth + 3), second_step, 0)


def edge_body(
    size, levels, level_ref, strip_ref, left_ref, right_ref, inner_vel,
    edge_ref, vel_ref, beyond_ref, sides, pulled, second,
):
    depth, height, width = size
    rows = height + 8
    level = level_ref[0]
    lane = lax.broadcasted_iota(jnp.int32, (rows, 128), 1)
    before = lane % 8 < 4
    bottom = (lane // 8 == LOW) & (level == 0)
    top = (lane // 8 == LOW + depth - 1) & (level == levels - 1)
    for channel, tile, first, cols in face_table(False)[0]:
        turned = lane_roll(left_ref[tile], 4 - cols - first)
        sides[0, channel] = jnp.where(before, turned, strip_ref[channel])
    for channel, tile, first, _ in face_table(True)[0]:
        turned = lane_roll(right_ref[tile], 4 - first)
        sides[1, channel] = jnp.where(before, strip_ref[channel], turned)

    def pull(source, side, target):
        for index in range(19):
            way_z, way_y, way_x = ways[index]
            value = lane_roll(source[side, index], 8 * way_z + way_x)
            if way_y != 0:
                value = pltpu.roll(value, way_y % rows, 0)
            if way_z != 0:
                value = jnp.where(bottom if way_z == 1 else top, source[side, opposite[index]], value)
            target[side, index] = value

    speeds = [[], []]
    for side in range(2):
        pull(sides, side, pulled)
        for row in range(0, rows, 8):
            cut = slice(row, row + 8)
            posts = relaxed([pulled[side, index, cut] for index in range(19)])
            inside = sides[side, 19, cut] > 0.5
            for index in range(19):
                second[side, index, cut] = jnp.where(inside, sides[side, index, cut], posts[index])
        pull(second, side, pulled)
        density, moment = moments([pulled[side, index] for index in range(19)])
        inverse = 1.0 / density
        speeds[side] = [part * inverse for part in moment]

    row = lax.broadcasted_iota(jnp.int32, (rows, 128), 0)
    valid = (row < height + 2) | (row == rows - 1)
    outside = (lane < 2) | (lane == 127)
    vel_in = inner_vel.take()
    table = table_rows(depth, height)
    vel_ref[...] = jnp.zeros_like(vel_ref)
    beyond_ref[...] = jnp.zeros_like(beyond_ref)

    def put(target, axis, layer, cols, cells):
        at = axis * table + layer * (height + 3)
        target[at : at + 1, cols] = cells[rows - 1 :, :]
        target[at + 1 : at + height + 3, cols] = cells[: height + 2, :]

    for axis in range(3):
        main = jnp.where(before, speeds[1][axis], speeds[0][axis])
        rest = jnp.where(before, speeds[0][axis], speeds[1][axis])
        for layer in range(depth + 3):
            keep = valid
            if layer == 0:
                keep = valid & (level != 0)
            if layer > depth:
                keep = valid & (level != levels - 1)
            shift = -(8 * (layer - 1 + LOW) + 4)
            turned = lane_roll(main, shift)
            for col in range(0, width, 128):
                cells = vel_in[axis, layer, :, col : col + 128]
                if col == 0 or col == width - 128:
                    mask = (lane < 2) & (col == 0) | (lane >= 126) & (col == width - 128)
                    cells = jnp.where(mask, turned, cells)
                put(vel_ref, axis, layer, slice(col, col + 128), jnp.where(keep, cells, 0.0))
            put(beyond_ref, axis, layer, slice(0, 128), jnp.where(keep & outside, lane_roll(rest, shift), 0.0))
    for index in range(19):
        edge_ref[index] = jnp.where(before, pulled[1, index], pulled[0, index])[:height]


def patch_body(_, pops_in, edge_ref, pops_ref):
    depth, height, width = pops_ref.shape[1:]
    lane = lax.broadcasted_iota(jnp.int32, (height, 128), 1)
    for index in range(19):
        value = edge_ref[index]
        for layer in range(depth):
            turned = lane_roll(value, -(8 * (layer + LOW) + 4))
            for col in range(0, width, 128):
                cells = pops_in[index, layer, :, col : col + 128]
                if col == 0 or col == width - 128:
                    mask = (lane < 2) & (col == 0) | (lane >= 126) & (col == width - 128)
                    cells = jnp.where(mask, turned, cells)
                pops_ref[index, layer, :, col : col + 128] = cells


def long_cost():
    return pl.CostEstimate(flops=10**8, bytes_accessed=1 << 22, transcendentals=0)


def shifted(value, axis, step):
    count = lax.axis_size(axis)
    return lax.ppermute(value, axis, [(i, (i + step) % count) for i in range(count)])


def to_level(value, kind, levels, side=None, step=0):
    pairs = []
    for at in range(levels):
        other = 1 - at if levels == 2 else at + 1 if kind in ("low", "up") else at - 1
        if 0 <= other < levels:
            pairs.append((at, other))
    if side is None:
        return lax.ppermute(value, "gz", pairs)
    count = lax.axis_size(side)
    return lax.ppermute(
        value,
        (side, "gz"),
        [
            (brick * levels + at, (brick + step) % count * levels + other)
            for brick in range(count)
            for at, other in pairs
        ],
    )


def wide_exchange(pops, coarse_pops, interface, ready):
    levels = lax.axis_size("gz")
    depth, height, width = interface.shape
    sizes = rim_sizes(levels)
    slots = len(sizes)
    kinds = ["low", "high"][:slots]
    down_sizes, up_sizes = zip(*rim_row_sizes(levels))
    outs = call(
        functools.partial(first_body, levels),
        [(channels, depth, height, width), (channels, height, 128)]
        + [(size, width) for size in own_rows(depth)[1]]
        + [(size, height, width) for size in sizes]
        + [(size, width) for size in down_sizes + up_sizes],
        [pops, coarse_pops, interface],
    )
    posts, own, down, up = outs[:4]
    rims, down_rims, up_rims = (outs[4 + slots * at : 4 + slots * at + slots] for at in range(3))
    given = [shifted(down, "gy", -1), shifted(up, "gy", 1)]
    given += [to_level(value, kind, levels) for value, kind in zip(rims, kinds)]
    given += [to_level(value, kind, levels, "gy", -1) for value, kind in zip(down_rims, kinds)]
    given += [to_level(value, kind, levels, "gy", 1) for value, kind in zip(up_rims, kinds)]
    deep, rows = depth + LOW + HIGH, height + 8
    ext = pltpu.VMEM((channels, deep, rows, width), jnp.float32)
    strip, right, left = call(
        functools.partial(strip_body, levels, depth),
        [(channels, rows, 128)] + [(face_table(high)[1], rows, 128) for high in (False, True)],
        [own] + given + [ready],
        [pltpu.VMEM((FOUR, rows, 128), jnp.float32)],
        heads=[(1, strip_rows()[1][0]), (2, strip_rows()[1][1])]
        + [(3 + at, FOUR) for at in range(slots)]
        + [(3 + slots + at, rim_strip_rows()[1][0]) for at in range(slots)]
        + [(3 + 2 * slots + at, rim_strip_rows()[1][1]) for at in range(slots)],
    )
    left, right = shifted(right, "gx", 1), shifted(left, "gx", -1)
    inner_pops, inner_vel = call(
        functools.partial(inner_body, levels),
        [pops.shape, (3, depth + 3, rows, width)],
        [posts] + given,
        [
            ext,
            pltpu.VMEM((19, rows, width), jnp.float32),
            pltpu.VMEM((19, deep - 2, rows, width), jnp.float32),
        ],
        long_cost(),
    )
    return [strip, left, right, inner_pops, inner_vel]


def phis(frac):
    angle = frac * (0.5 * math.pi)
    sine = 0.25 * jnp.sin(angle)
    cosine = 0.25 * jnp.cos(angle)
    return (0.25 - sine, 0.25 + cosine, 0.25 + sine, 0.25 - cosine)


def split(value):
    high = value.astype(jnp.bfloat16)
    return high, (value - high.astype(jnp.float32)).astype(jnp.bfloat16)


def pick(step, parts):
    value = jnp.where(step == 0, parts[0], 0.0)
    for index in range(1, 4):
        value = jnp.where(step == index, parts[index], value)
    return value


def dots(left, right, dims):
    return lax.dot_general(left, right, (dims, ((), ())), preferred_element_type=jnp.float32)


def table_rows(depth, height):
    return -(-(depth + 3) * (height + 3) // 16) * 16


def weigh_body(size, _, frac_ref, home_ref, along, plane_ref, ready_ref):
    depth, height, width = size
    blocks = home_ref.shape[0]
    layers, rows = depth + 3, height + 3
    table = table_rows(depth, height)
    ready_ref[...] = jnp.zeros_like(ready_ref)
    along[2 * width :, :] = jnp.zeros((128, along.shape[1]), jnp.bfloat16)
    plane_ref[:, layers * rows :, :] = jnp.zeros(
        (plane_ref.shape[0], table - layers * rows, 256), jnp.float32
    )
    span_x = lax.broadcasted_iota(jnp.int32, (width, 128), 0) + 1
    span_end = lax.broadcasted_iota(jnp.int32, (16, 128), 0)
    span_y = lax.broadcasted_iota(jnp.int32, (padded(rows), 128), 0)
    span_z = lax.broadcasted_iota(jnp.int32, (padded(layers), 128), 0)
    for block in range(blocks):
        side = slice(block * 128, block * 128 + 128)
        cell = home_ref[block : block + 1, :]
        cell_x = cell % width
        cell_y = cell // width % height
        cell_z = cell // (width * height)
        part_x = phis(frac_ref[0, block : block + 1, :])
        part_y = phis(frac_ref[1, block : block + 1, :])
        part_z = phis(frac_ref[2, block : block + 1, :])
        high, low = split(pick(span_x - cell_x, part_x))
        along[0:width, side] = low
        along[width : 2 * width, side] = high
        high, low = split(pick(span_end + (width + 1) - cell_x, part_x))
        along[2 * width : 2 * width + 16, side] = high
        along[2 * width + 32 : 2 * width + 48, side] = high
        along[2 * width + 64 : 2 * width + 80, side] = low
        high, low = split(jnp.where((span_end == 15) & (cell_x == 0), part_x[0], 0.0))
        along[2 * width + 112 : 2 * width + 128, side] = high
        along[2 * width + 16 : 2 * width + 32, side] = high
        along[2 * width + 48 : 2 * width + 64, side] = low
        weight_y = pick(span_y - cell_y, part_y)[:rows]
        weight_z = pick(span_z - cell_z, part_z)
        half = block % 2 * 128
        for layer in range(layers):
            plane_ref[block // 2, layer * rows : layer * rows + rows, half : half + 128] = (
                weight_y * weight_z[layer : layer + 1, :]
            )


def droplet_body(
    size, counts_ref, dest_ref, vel_ref, beyond_ref, speed_ref, frac_ref, along_in, plane_in,
    spread_ref, outer_ref, stay_ref, state_ref, twice, mixed, push_high, push_low, meanwhile,
):
    depth, height, width = size
    blocks = state_ref.shape[0]
    table = table_rows(depth, height)
    high, low = split(vel_ref[...])
    twice[:, :width] = high
    twice[:, width:] = high
    mixed[:, :width] = low
    high, low = (part.astype(jnp.float32) for part in split(beyond_ref[...]))
    mixed[:, width:] = (high + lane_roll(low, 32) + lane_roll(high, 64)).astype(jnp.bfloat16)
    slots = lax.broadcasted_iota(jnp.int32, (1, 128), 1)
    along, plane_ref = along_in.take(), plane_in.take()

    def sample(number):
        pair = slice(number * 256, number * 256 + 256)
        return dots(twice[...], along[0 : 2 * width, pair], ((1,), (0,))) + dots(
            mixed[...], along[width:, pair], ((1,), (0,))
        )

    def move(number, sums):
        plane = plane_ref[number]
        for axis in range(3):
            where = slice(axis * table, axis * table + table)
            sampled = jnp.sum(sums[where] * plane, axis=0, keepdims=True)
            for half in range(2):
                block = 2 * number + half
                live = slots < counts_ref[block]
                sample = sampled[:, half * 128 : half * 128 + 128]
                speed = speed_ref[axis, block : block + 1, :]
                frac = frac_ref[axis, block : block + 1, :]
                moved = speed + relax * (sample - speed)
                push = jnp.where(live, couple * (moved - sample), 0.0)
                stays = live & (dest_ref[block] == 13)
                for at, value in ((axis, moved), (3 + axis, frac + moved)):
                    state_ref[block, at : at + 1, :] = jnp.where(live, value, 0.0)
                    stay_ref[at, block : block + 1, :] = jnp.where(stays, value, 0.0)
                high, low = split(plane[:, half * 128 : half * 128 + 128] * push)
                push_high[where, block * 128 : block * 128 + 128] = high
                push_low[where, block * 128 : block * 128 + 128] = low

    pairs = blocks // 2
    for number in range(pairs):
        move(number, sample(number))
    main = dots(push_high[...], along[0 : 2 * width, :], ((1,), (1,)))
    for action in meanwhile:
        action()
    rest = dots(push_low[...], along[width:, :], ((1,), (1,)))
    outer = dots(push_high[...], along[2 * width :, :], ((1,), (1,)))
    spread_ref[...] = main[:, :width] + main[:, width:] + rest[:, :width]
    outer_ref[...] = outer + lane_roll(outer, -64) + rest[:, width:]


def force_sides(levels):
    if levels == 2:
        return [("up", 0, 1, 0), ("down", 1, 0, 0)]
    return [("up", None, None, 0), ("down", None, None, 1)]


GROUP = 6 * 8


def group_at(way_z, way_y):
    return (way_z + 1) * 3 + way_y + 1


def face_rows(depth, height):
    return -(-depth // 8) * height


def message_rows(depth):
    return [8 * 8, 2 * 4 * depth, 4 * depth, 2 * 8, 8]


def pack_blocks(
    levels, level_ref, dest_ref, state_ref, side_ref,
    to_levels, north_ref, south_ref, north_levels, south_levels, outbox,
):
    level = level_ref[0]
    blocks = state_ref.shape[0]
    codes = [dest_ref[block] for block in range(blocks)]
    outbox[...] = jnp.zeros_like(outbox)
    for block in range(blocks):
        rank = jnp.int32(0)
        for earlier in range(block):
            rank = rank + (codes[earlier] == codes[block]).astype(jnp.int32)
        slot = jnp.where(codes[block] == 13, 27 * CAP, codes[block] * CAP + jnp.minimum(rank, CAP - 1))
        outbox[slot] = state_ref[block]

    def put(target, way_z, way_y):
        base = target.shape[0] - GROUP
        for slot in range(6):
            target[base + 8 * slot : base + 8 * slot + 8, :] = outbox[6 * group_at(way_z, way_y) + slot]

    put(north_ref, 0, 1)
    put(south_ref, 0, -1)
    for slot in range(CAP):
        side_ref[slot] = outbox[6 * group_at(0, 0) + slot]
        side_ref[CAP + slot] = outbox[6 * group_at(0, 0) + 4 + slot]
    ways_z = [(1 - 2 * level, 0)] if levels == 2 else [(1, 0), (-1, 1)]
    for way_z, slot in ways_z:
        put(to_levels[slot], way_z, 0)
        put(north_levels[slot], way_z, 1)
        put(south_levels[slot], way_z, -1)


def pack_force(
    levels, level_ref, spread_ref, outer_ref, own_ref,
    to_levels, north_ref, south_ref, north_levels, south_levels, strip,
):
    depth, height, width = own_ref.shape[1:]
    rows, table = height + 3, table_rows(depth, height)
    lane = lax.broadcasted_iota(jnp.int32, (table, 128), 1)
    value = jnp.zeros((table, 128), jnp.float32)
    for axis in range(3):
        here = (lane >= 4 * axis) & (lane < 4 * axis + 3)
        cells = outer_ref[axis * table : axis * table + table, :]
        value = jnp.where(here, lane_roll(cells, 4 * axis + 1), value)
    strip[...] = value

    def force(part, layer, cut):
        at = layer * rows
        if part < 3:
            return spread_ref[part * table + at + cut.start : part * table + at + cut.stop, :]
        return strip[at + cut.start : at + cut.stop, :]

    main, north, south = slice(1, height + 1), slice(height + 1, height + 3), slice(0, 1)
    for part in range(4):
        for layer in range(depth):
            own_ref[part, layer] = force(part, layer + 1, main)
            at = part * depth + layer
            north_ref[2 * at : 2 * at + 2, :] = force(part, layer + 1, north)
            south_ref[at : at + 1, :] = force(part, layer + 1, south)
    for kind, sender, _, slot in force_sides(levels):

        def pack(kind=kind, slot=slot):
            for part in range(4):
                for step in range(2 if kind == "up" else 1):
                    layer = depth + 1 + step if kind == "up" else 0
                    at = 2 * part + step
                    to_levels[slot][8 * at : 8 * at + 8, :] = force(part, layer, main)
                    north_levels[slot][2 * at : 2 * at + 2, :] = force(part, layer, north)
                    south_levels[slot][at : at + 1, :] = force(part, layer, south)

        guarded(level_ref[0], sender, pack)


def main_body(
    size, levels, level_ref, counts, dest, strip_ref, left_ref, right_ref, inner_vel,
    speed, frac, along, plane, edge_ref, own_ref, stay_ref, side_ref, north_ref, south_ref, *rest,
):
    slots = len(rim_sizes(levels))
    to_levels, north_levels, south_levels = (rest[slots * at : slots * at + slots] for at in range(3))
    rest = rest[3 * slots :]
    vel_ref, beyond_ref, spread_ref, outer_ref, state_ref, outbox, strip = rest[:7]
    counts_ref, dest_ref = counts.take(), dest.take()
    edge_body(
        size, levels, level_ref, strip_ref, left_ref, right_ref, inner_vel,
        edge_ref, vel_ref, beyond_ref, *rest[7:10],
    )

    def move_out():
        pack_blocks(
            levels, level_ref, dest_ref, state_ref, side_ref,
            to_levels, north_ref, south_ref, north_levels, south_levels, outbox,
        )

    droplet_body(
        size, counts_ref, dest_ref, vel_ref, beyond_ref, speed.take(), frac.take(), along, plane,
        spread_ref, outer_ref, stay_ref, state_ref, *rest[10:], [move_out],
    )
    pack_force(
        levels, level_ref, spread_ref, outer_ref, own_ref,
        to_levels, north_ref, south_ref, north_levels, south_levels, strip,
    )


def gather_body(levels, level_ref, own_ref, side_ref, *rest):
    depth, height, width = own_ref.shape[1:]
    slots = len(rim_sizes(levels))
    north_ref, south_ref = rest[:2]
    from_levels, north_levels, south_levels = (rest[2 + slots * at : 2 + slots * at + slots] for at in range(3))
    force_ref, right_ref, left_ref, total = rest[2 + 3 * slots :]
    base = face_rows(depth, height)
    total[...] = own_ref[...]
    right_ref[base:, :] = jnp.zeros((right_ref.shape[0] - base, width), jnp.float32)
    left_ref[base:, :] = jnp.zeros((left_ref.shape[0] - base, width), jnp.float32)
    last = slice(height - 1, height)
    for part in range(4):
        for layer in range(depth):
            at = part * depth + layer
            total[part, layer, 0:2, :] += north_ref[2 * at : 2 * at + 2, :]
            total[part, layer, last, :] += south_ref[at : at + 1, :]

    def blocks(source, way_z, way_y):
        at = base + 12 * group_at(way_z, way_y)
        start = source.shape[0] - GROUP
        for slot in range(CAP):
            rows = slice(at + 6 * slot, at + 6 * slot + 6)
            left_ref[rows, :] = source[start + 8 * slot : start + 8 * slot + 6, :]
            right_ref[rows, :] = source[start + 32 + 8 * slot : start + 38 + 8 * slot, :]

    at = base + 12 * group_at(0, 0)
    for slot in range(CAP):
        left_ref[at + 6 * slot : at + 6 * slot + 6, :] = side_ref[slot, 0:6, :]
        right_ref[at + 6 * slot : at + 6 * slot + 6, :] = side_ref[2 + slot, 0:6, :]
    blocks(north_ref, 0, 1)
    blocks(south_ref, 0, -1)
    for kind, _, receiver, slot in force_sides(levels):

        def take(kind=kind, slot=slot):
            for part in range(4):
                for step in range(2 if kind == "up" else 1):
                    layer = step if kind == "up" else depth - 1
                    at = 2 * part + step
                    total[part, layer] += from_levels[slot][8 * at : 8 * at + 8, :]
                    total[part, layer, 0:2, :] += north_levels[slot][2 * at : 2 * at + 2, :]
                    total[part, layer, last, :] += south_levels[slot][at : at + 1, :]
            way = 1 if kind == "up" else -1
            blocks(from_levels[slot], way, 0)
            blocks(north_levels[slot], way, 1)
            blocks(south_levels[slot], way, -1)

        guarded(level_ref[0], receiver, take)
    for layer in range(depth):
        for axis in range(3):
            force_ref[axis, layer] = total[axis, layer]
    lane = lax.broadcasted_iota(jnp.int32, (height, 128), 1)
    for tile in range(base // height):
        value = jnp.zeros((height, 128), jnp.float32)
        for layer in range(8 * tile, min(8 * tile + 8, depth)):
            part = layer - 8 * tile
            value = jnp.where(lane // 16 == part, lane_roll(total[3, layer, :, 0:128], 16 * part), value)
        for target in (right_ref, left_ref):
            target[tile * height : tile * height + height, 0:128] = value


def last_body(levels, level_ref, part_ref, stay_ref, *rest):
    depth, height, width = part_ref.shape[1:]
    slots = len(rim_sizes(levels))
    north_ref, south_ref = rest[:2]
    from_levels, north_levels, south_levels = (rest[2 + slots * at : 2 + slots * at + slots] for at in range(3))
    right_ref, left_ref, force_ref, arrived_ref = rest[2 + 3 * slots :]
    blocks = stay_ref.shape[1]
    base = face_rows(depth, height)
    lane = lax.broadcasted_iota(jnp.int32, (height, 128), 1)
    for layer in range(depth):
        rows = slice(layer // 8 * height, layer // 8 * height + height)
        before, after = right_ref[rows, :128], left_ref[rows, :128]
        for axis in range(3):
            at = 16 * (layer % 8) + 4 * axis
            first = jnp.where(lane < 2, lane_roll(before, -at - 1), 0.0)
            final = jnp.where(lane == 127, lane_roll(after, 127 - at), 0.0)
            force_ref[axis, layer] = part_ref[axis, layer]
            force_ref[axis, layer, :, 0:128] += first
            force_ref[axis, layer, :, width - 128 : width] += final
    arrived_ref[:, 0:blocks, :] = stay_ref[...]

    def put(source, start, stride, way_z, way_y, way_x):
        code = group_at(way_z, way_y) * 3 + way_x + 1
        at = blocks + CAP * (code if code < 13 else code - 1)
        for slot in range(CAP):
            for axis in range(6):
                if source is None:
                    value = jnp.zeros((1, 128), jnp.float32)
                else:
                    value = source[start + stride * slot + axis : start + stride * slot + axis + 1, :]
                arrived_ref[axis, at + slot : at + slot + 1, :] = value

    for way_z in (-1, 0, 1):
        for way_y in (-1, 0, 1):
            for way_x, source in ((1, right_ref), (-1, left_ref)):
                put(source, base + 12 * group_at(way_z, way_y), 6, way_z, way_y, way_x)
    middle = 16

    def put_group(source, way_z, way_y):
        put(source, None if source is None else source.shape[0] - GROUP + middle, 8, way_z, way_y, 0)

    put_group(north_ref, 0, 1)
    put_group(south_ref, 0, -1)
    for kind, _, receiver, slot in force_sides(levels):
        way = 1 if kind == "up" else -1

        def take(way=way, slot=slot):
            put_group(from_levels[slot], way, 0)
            put_group(north_levels[slot], way, 1)
            put_group(south_levels[slot], way, -1)

        def clear(way=way):
            for way_y in (-1, 0, 1):
                put_group(None, way, way_y)

        guarded(level_ref[0], receiver, take)
        if receiver is not None:
            guarded(level_ref[0], 1 - receiver, clear)


def local(pops, coarse_pops, interface, drop_vel, drop_frac, home, counts, dest):
    levels = lax.axis_size("gz")
    depth, height, width = interface.shape
    blocks = home.shape[0]
    kinds = ["up", "down"][: len(rim_sizes(levels))]
    slots = len(kinds)
    size = (depth, height, width)
    rows = height + 8
    table = table_rows(depth, height)
    along, plane, ready = call(
        functools.partial(weigh_body, size),
        [(2 * width + 128, blocks * 128), (blocks // 2, table, 256), (8, 128)],
        [drop_frac, home],
        cost=long_cost(),
        kind=[jnp.bfloat16, jnp.float32, jnp.float32],
    )
    strip, left, right, inner_pops, inner_vel = wide_exchange(pops, coarse_pops, interface, ready)
    sizes = [(count + GROUP, width) for count in message_rows(depth)]
    outs = call(
        functools.partial(main_body, size, levels),
        [(19, height, 128), (4, depth, height, width), (6, blocks, 128), (4, 8, 128), sizes[1], sizes[2]]
        + [sizes[0]] * slots
        + [sizes[3]] * slots
        + [sizes[4]] * slots,
        [counts, dest, strip, left, right, inner_vel, drop_vel, drop_frac, along, plane],
        [
            pltpu.VMEM((3 * table, width), jnp.float32),
            pltpu.VMEM((3 * table, 128), jnp.float32),
            pltpu.VMEM((3 * table, width), jnp.float32),
            pltpu.VMEM((3 * table, 128), jnp.float32),
            pltpu.VMEM((blocks, 8, 128), jnp.float32),
            pltpu.VMEM((27 * CAP + 1, 8, 128), jnp.float32),
            pltpu.VMEM((table, 128), jnp.float32),
            pltpu.VMEM((2, channels, rows, 128), jnp.float32),
            pltpu.VMEM((2, 19, rows, 128), jnp.float32),
            pltpu.VMEM((2, 19, rows, 128), jnp.float32),
            pltpu.VMEM((3 * table, 2 * width), jnp.bfloat16),
            pltpu.VMEM((3 * table, width + 128), jnp.bfloat16),
            pltpu.VMEM((3 * table, blocks * 128), jnp.bfloat16),
            pltpu.VMEM((3 * table, blocks * 128), jnp.bfloat16),
        ],
        late=(0, 1, 5, 6, 7, 8, 9),
    )
    edge, own, stay, side, north, south = outs[:6]
    to_levels, north_levels, south_levels = (outs[6 + slots * at : 6 + slots * at + slots] for at in range(3))
    received = [shifted(north, "gy", 1), shifted(south, "gy", -1)]
    received += [to_level(value, kind, levels) for value, kind in zip(to_levels, kinds)]
    received += [to_level(value, kind, levels, "gy", 1) for value, kind in zip(north_levels, kinds)]
    received += [to_level(value, kind, levels, "gy", -1) for value, kind in zip(south_levels, kinds)]
    (state,) = call(patch_body, [pops.shape], [inner_pops, edge], cost=long_cost())
    side_rows = (padded(face_rows(depth, height) + 9 * 6 * CAP), width)
    part, right, left = call(
        functools.partial(gather_body, levels),
        [(3, depth, height, width), side_rows, side_rows],
        [own, side] + received,
        [pltpu.VMEM((4, depth, height, width), jnp.float32)],
    )
    force, arrived = call(
        functools.partial(last_body, levels),
        [(3, depth, height, width), (6, blocks + 26 * CAP, 128)],
        [part, stay] + received + [shifted(right, "gx", 1), shifted(left, "gx", -1)],
    )
    return state, force, arrived


def solution(mesh):
    return jax.shard_map(
        local,
        mesh=mesh,
        in_specs=(
            P(None, "gz", "gy", "gx"),
            P(None, "gz", "gy", "gx"),
            P("gz", "gy", "gx"),
            P(None, ("gx", "gy", "gz"), None),
            P(None, ("gx", "gy", "gz"), None),
            P(("gx", "gy", "gz"), None),
            P(("gx", "gy", "gz")),
            P(("gx", "gy", "gz")),
        ),
        out_specs=(
            P(None, "gz", "gy", "gx"),
            P(None, "gz", "gy", "gx"),
            P(None, ("gx", "gy", "gz"), None),
        ),
        check_vma=False,
    )
```

```python
import functools
import math

import jax
import jax.numpy as jnp
import numpy as np
from jax import lax
from jax.experimental import pallas as pl
from jax.experimental.pallas import tpu as pltpu
from jax.sharding import PartitionSpec as P

CAP = 2


lattice = np.array(
    [
        [0, 0, 0],
        [1, 0, 0],
        [-1, 0, 0],
        [0, 1, 0],
        [0, -1, 0],
        [0, 0, 1],
        [0, 0, -1],
        [1, 1, 0],
        [-1, -1, 0],
        [1, -1, 0],
        [-1, 1, 0],
        [1, 0, 1],
        [-1, 0, -1],
        [1, 0, -1],
        [-1, 0, 1],
        [0, 1, 1],
        [0, -1, -1],
        [0, 1, -1],
        [0, -1, 1],
    ]
)
weights_table = np.array([1.0 / 3.0] + [1.0 / 18.0] * 6 + [1.0 / 36.0] * 12)
opposite = [0, 2, 1, 4, 3, 6, 5, 8, 7, 10, 9, 12, 11, 14, 13, 16, 15, 18, 17]
inverse_tau = 0.8
relax = 0.5
couple = 8.0


class Level:
    def __getitem__(self, _):
        return lax.axis_index("gz").astype(jnp.int32)


class Moving:
    def __init__(self, buffer, copy):
        self.buffer = buffer
        self.copy = copy

    def take(self):
        self.copy.wait()
        return self.buffer


def call(body, outs, arrays, scratch=(), cost=None, heads=(), late=(), kind=jnp.float32):
    heads = dict(heads)
    landing = []
    for at, value in enumerate(arrays):
        space = pltpu.SMEM if value.ndim == 1 else pltpu.VMEM
        landing.append(space((heads.get(at, value.shape[0]),) + value.shape[1:], value.dtype))

    def whole(*refs):
        given = refs[: len(arrays)]
        made = list(refs[len(arrays) : len(arrays) + len(outs)])
        rest = refs[len(arrays) + len(outs) :]
        landed, done, rest = list(rest[: len(arrays)]), rest[len(arrays)], rest[len(arrays) + 1 :]
        copies = []
        for at, (source, target) in enumerate(zip(given, landed)):
            if at in heads:
                source = source.at[pl.ds(0, heads[at])]
            copies.append(pltpu.make_async_copy(source, target, done.at[at]))
        for copy in copies:
            copy.start()
        for at, copy in enumerate(copies):
            if at in late:
                landed[at] = Moving(landed[at], copy)
            else:
                copy.wait()
        body(Level(), *landed, *made, *rest)

    vmem = pl.BlockSpec(memory_space=pltpu.VMEM)
    hbm = pl.BlockSpec(memory_space=pltpu.HBM)
    return pl.pallas_call(
        whole,
        out_shape=[
            jax.ShapeDtypeStruct(shape, kind[at] if isinstance(kind, list) else kind)
            for at, shape in enumerate(outs)
        ],
        in_specs=[hbm] * len(arrays),
        out_specs=[vmem] * len(outs),
        scratch_shapes=landing
        + [pltpu.SemaphoreType.DMA((len(arrays),))]
        + list(scratch),
        cost_estimate=cost,
        compiler_params=pltpu.CompilerParams(vmem_limit_bytes=64 * 1024 * 1024),
    )(*arrays)


ways = [tuple(int(part) for part in lattice[index][::-1]) for index in range(19)] + [(0, 0, 0)]
channels = len(ways)
LOW = 3
HIGH = 4


def low_reach(way):
    return 2 + way


def high_reach(way):
    return 3 - way


def rim(kind):
    side = 1 if kind == "low" else -1
    return [
        (step, channel)
        for step in (1, 2)
        for channel in range(channels)
        if step <= 1 + side * ways[channel][0]
    ]


def rim_sides(levels):
    if levels == 2:
        return [("low", 1, 0, 0), ("high", 0, 1, 0)]
    return [("low", None, None, 0), ("high", None, None, 1)]


def rim_sizes(levels):
    sizes = [FOUR + len(rim(kind)) for kind, _, _, _ in rim_sides(levels)]
    return [max(sizes)] if levels == 2 else sizes


def guarded(level, guard, action):
    if guard is None:
        action()
    else:
        pl.when(level == guard)(action)


def padded(count):
    return -(-count // 8) * 8


def reaches(channel, bounces):
    way_z, way, _ = ways[channel]
    above, below = high_reach(way), low_reach(way)
    if bounces and way_z != 0:
        above, below = max(above, HIGH - 1), max(below, LOW - 1)
    return above, below


def row_places(cells, start=(0, 0)):
    places, (high_at, low_at) = [], start
    for above, below in cells:
        places.append((high_at, low_at, above, below))
        high_at, low_at = high_at + above, low_at + below
    return places, (padded(high_at), padded(low_at))


def strip_rows():
    return row_places([reaches(channel, True) for channel in range(channels)])


def own_rows(depth):
    cells = [(layer, channel) for layer in range(depth) for channel in range(channels)]
    places, sizes = row_places(
        [reaches(channel, layer in (0, depth - 1)) for layer, channel in cells], strip_rows()[1]
    )
    return [(layer, channel, place) for (layer, channel), place in zip(cells, places)], sizes


FOUR = -(-channels // 4)


def rim_strip_rows():
    return row_places([(HIGH, LOW)] * FOUR)


def rim_rows(kind):
    places, sizes = row_places([reaches(channel, False) for _, channel in rim(kind)], rim_strip_rows()[1])
    return [(step, channel, place) for (step, channel), place in zip(rim(kind), places)], sizes


def rim_row_sizes(levels):
    sizes = [rim_rows(kind)[1] for kind, _, _, _ in rim_sides(levels)]
    return [tuple(max(part) for part in zip(*sizes))] if levels == 2 else sizes


def face_table(high):
    wants = []
    for channel in range(channels):
        way_z, _, way = ways[channel]
        count = high_reach(way) if high else low_reach(way)
        if way_z != 0:
            count = max(count, (HIGH if high else LOW) - 1)
        wants.append((-count, channel))
    free, table = [], []
    for count, channel in sorted(wants):
        tile = next((at for at, room in enumerate(free) if room >= -count), len(free))
        if tile == len(free):
            free.append(8)
        table.append((channel, tile, 8 - free[tile], -count))
        free[tile] += count
    return table, max(len(free), 9)


def moments(cells):
    density = cells[0] * float(weights_table[0])
    moment = [None, None, None]
    face, edge = float(weights_table[1]), float(weights_table[7])
    edge_sum = cells[7]
    for index in range(8, 19):
        edge_sum = edge_sum + cells[index]
    face_sum = cells[1]
    for index in range(2, 7):
        face_sum = face_sum + cells[index]
    density = density + face * face_sum + edge * edge_sum
    for axis in range(3):
        total = {}
        for group, indices in ((face, range(1, 7)), (edge, range(7, 19))):
            plus, minus = None, None
            for index in indices:
                way = int(lattice[index][axis])
                if way == 1:
                    plus = cells[index] if plus is None else plus + cells[index]
                if way == -1:
                    minus = cells[index] if minus is None else minus + cells[index]
            total[group] = plus - minus
        moment[axis] = face * total[face] + edge * total[edge]
    return density, moment


def relaxed(cells):
    density, moment = moments(cells)
    inverse = 1.0 / density
    flow = [part * inverse for part in moment]
    square = flow[0] * flow[0] + flow[1] * flow[1] + flow[2] * flow[2]
    scale = density * inverse_tau
    base = scale * (1.0 - 1.5 * square)
    keep = 1.0 - inverse_tau
    posts = [None] * 19
    posts[0] = keep * cells[0] + base
    for index in range(1, 19, 2):
        along = None
        for axis in range(3):
            way = int(lattice[index][axis])
            if way != 0:
                part = flow[axis] if way == 1 else -flow[axis]
                along = part if along is None else along + part
        odd = 3.0 * scale * along
        even = base + (4.5 * scale) * (along * along)
        posts[index] = keep * cells[index] + (even + odd)
        posts[index + 1] = keep * cells[index + 1] + (even - odd)
    return posts


def lane_roll(value, shift):
    shift = shift % value.shape[-1]
    return value if shift == 0 else pltpu.roll(value, shift, value.ndim - 1)


def first_body(
    levels, level_ref, pops_ref, coarse_ref, interface_ref, posts_ref, strip_ref, down_ref, up_ref, *outs
):
    depth, height, width = interface_ref.shape
    slots = len(rim_sizes(levels))
    rims, down_rims, up_rims = (outs[slots * at : slots * at + slots] for at in range(3))
    lane = lax.broadcasted_iota(jnp.int32, (height, 128), 1)

    def put_rows(down, up, place, cells):
        down_at, up_at, down_rows, up_rows = place
        cols = slice(0, cells.shape[1])
        down[down_at : down_at + down_rows, cols] = cells[:down_rows, :]
        up[up_at : up_at + up_rows, cols] = cells[height - up_rows :, :]

    own = own_rows(depth)[0]
    for layer in range(depth):
        mask = interface_ref[layer]
        inside = mask == 1
        posts = relaxed([pops_ref[index, layer] for index in range(19)])
        posts = [
            jnp.where(inside, coarse_ref[index, layer].astype(jnp.float32), posts[index])
            for index in range(19)
        ] + [mask.astype(jnp.float32)]
        for channel in range(channels):
            posts_ref[channel, layer] = posts[channel]
            put_rows(down_ref, up_ref, own[layer * channels + channel][2], posts[channel])
    for channel in range(channels):
        value = jnp.zeros((height, 128), jnp.float32)
        for layer in range(depth):
            cells = posts_ref[channel, layer]
            if width > 128:
                cells = jnp.where(lane < 64, cells[:, :128], cells[:, width - 128 :])
            value = jnp.where(lane // 8 == LOW + layer, lane_roll(cells, 8 * (LOW + layer) + 4), value)
        strip_ref[channel] = value
        put_rows(down_ref, up_ref, strip_rows()[0][channel], value)
    for kind, _, sender, slot in rim_sides(levels):

        def pack(kind=kind, slot=slot):
            for tile in range(FOUR):
                value = jnp.zeros((height, 128), jnp.float32)
                for part in range(min(4, channels - 4 * tile)):
                    first = LOW + depth - 4 if kind == "low" else LOW
                    turned = lane_roll(strip_ref[4 * tile + part], 32 * part - 8 * first)
                    value = jnp.where(lane // 32 == part, turned, value)
                rims[slot][tile, :, 0:128] = value
                put_rows(down_rims[slot], up_rims[slot], rim_strip_rows()[0][tile], value)
            for at, (step, channel, place) in enumerate(rim_rows(kind)[0]):
                cells = posts_ref[channel, depth - step if kind == "low" else step - 1]
                rims[slot][FOUR + at] = cells
                put_rows(down_rims[slot], up_rims[slot], place, cells)

        guarded(level_ref[0], sender, pack)


def unpack(levels, level, posts_ref, above_ref, below_ref, rims, above_rims, below_rims, ext):
    depth, height = posts_ref.shape[1:3]
    rows = height + 8

    def put(channel, at, cells, place, above, below):
        above_at, below_at, above_rows, below_rows = place
        ext[channel, at, :height, :] = cells
        ext[channel, at, height : height + above_rows, :] = above[above_at : above_at + above_rows, :]
        ext[channel, at, rows - below_rows : rows, :] = below[below_at : below_at + below_rows, :]

    for layer, channel, place in own_rows(depth)[0]:
        put(channel, LOW + layer, posts_ref[channel, layer], place, above_ref, below_ref)
    for kind, receiver, _, slot in rim_sides(levels):

        def take(kind=kind, slot=slot):
            for at, (step, channel, place) in enumerate(rim_rows(kind)[0]):
                layer = LOW - step if kind == "low" else LOW + depth + step - 1
                put(channel, layer, rims[slot][FOUR + at], place, above_rims[slot], below_rims[slot])

        guarded(level, receiver, take)


def split_given(levels, rest):
    slots = len(rim_sizes(levels))
    parts = [rest[3 + slots * at : 3 + slots * at + slots] for at in range(3)]
    return rest[:3], parts, rest[3 + 3 * slots :]


def strip_body(levels, depth, level_ref, *rest):
    (own_ref, above_ref, below_ref), parts, rest = split_given(levels, rest)
    _, strip_ref, right_ref, left_ref, tiles = rest
    rows = strip_ref.shape[1]
    height = rows - 8
    lane = lax.broadcasted_iota(jnp.int32, (rows, 128), 1)
    layer_at = lane // 8

    def put(target, index, place, above, below):
        above_at, below_at, above_rows, below_rows = place
        target[index, height : height + above_rows, :] = above[above_at : above_at + above_rows, 0:128]
        target[index, rows - below_rows :, :] = below[below_at : below_at + below_rows, 0:128]

    for channel in range(channels):
        strip_ref[channel, 0:height, :] = own_ref[channel]
        put(strip_ref, channel, strip_rows()[0][channel], above_ref, below_ref)
    for kind, receiver, _, slot in rim_sides(levels):

        def take(kind=kind, slot=slot):
            rims, above_rims, below_rims = (part[slot] for part in parts)
            first = -1 if kind == "low" else LOW + depth
            here = layer_at < LOW if kind == "low" else layer_at >= LOW + depth
            for tile in range(FOUR):
                tiles[tile, 0:height, :] = rims[tile, :, 0:128]
                put(tiles, tile, rim_strip_rows()[0][tile], above_rims, below_rims)
                value = tiles[tile]
                for part in range(min(4, channels - 4 * tile)):
                    turned = lane_roll(value, 8 * first - 32 * part)
                    strip_ref[4 * tile + part] = jnp.where(here, turned, strip_ref[4 * tile + part])

        guarded(level_ref[0], receiver, take)
    spot = lane % 8
    for target, high in ((right_ref, False), (left_ref, True)):
        table, count = face_table(high)
        for tile in range(count):
            value = jnp.zeros((rows, 128), jnp.float32)
            for channel, at, first, cols in table:
                if at == tile:
                    turned = lane_roll(strip_ref[channel], first - (4 if high else 4 - cols))
                    value = jnp.where((spot >= first) & (spot < first + cols), turned, value)
            target[tile] = value


def substeps(levels, level, size, ext, pulled, second):
    depth, height, width = size
    rows = height + 8

    def pull(source, layer, at, target):
        for index in range(19):
            way_z, way_y, way_x = ways[index]
            value = source[index, at - way_z]
            if way_x != 0:
                value = pltpu.roll(value, way_x % width, 1)
            if way_y != 0:
                value = pltpu.roll(value, way_y % rows, 0)
            if way_z == 1 and layer == 0:
                value = jnp.where(level == 0, source[opposite[index], at], value)
            if way_z == -1 and layer == depth - 1:
                value = jnp.where(level == levels - 1, source[opposite[index], at], value)
            target[index] = value

    tiles = [
        (slice(row, row + 8), slice(col, col + 128))
        for row in range(0, rows, 8)
        for col in range(0, width, 128)
    ]

    def first_steps(layers):
        for layer in layers:
            at = LOW + layer
            cells = pulled.at[at % pulled.shape[0]]
            pull(ext, layer, at, cells)
            for tile in tiles:
                posts = relaxed([cells[(index, *tile)] for index in range(19)])
                inside = ext[(19, at, *tile)] > 0.5
                for index in range(19):
                    second[(index, at - 1, *tile)] = jnp.where(
                        inside, ext[(index, at, *tile)], posts[index]
                    )

    def second_steps(layers, put):
        for layer in layers:
            at = LOW - 1 + layer
            cells = pulled.at[at % pulled.shape[0]]
            pull(second, layer, at, cells)
            for tile in tiles:
                density, moment = moments([cells[(index, *tile)] for index in range(19)])
                inverse = 1.0 / density
                for axis in range(3):
                    put(axis, layer, tile, moment[axis] * inverse)
            yield layer, cells

    return first_steps, second_steps


def inner_body(levels, level_ref, *rest):
    (posts_ref, above_ref, below_ref), parts, rest = split_given(levels, rest)
    pops_ref, vel_ref, ext, pulled, second = rest
    level = level_ref[0]
    unpack(levels, level, posts_ref, above_ref, below_ref, *parts, ext)
    depth, height, _ = size = posts_ref.shape[1:]
    first_steps, second_steps = substeps(levels, level, size, ext, pulled, second)

    def put(axis, layer, tile, value):
        vel_ref[(axis, layer, *tile)] = value

    pl.when(level != 0)(lambda: first_steps([-1]))
    pl.when(level != levels - 1)(lambda: first_steps([depth]))
    first_steps(range(depth))
    for layer, cells in second_steps(range(depth), put):
        for index in range(19):
            pops_ref[index, layer] = cells[index, :height, :]


def face_body(levels, level_ref, *rest):
    (posts_ref, above_ref, below_ref), parts, rest = split_given(levels, rest)
    slots = len(rim_sizes(levels))
    faces, (ext, pulled, second) = rest[:slots], rest[slots:]
    level = level_ref[0]
    unpack(levels, level, posts_ref, above_ref, below_ref, *parts, ext)
    size = posts_ref.shape[1:]
    depth = size[0]
    first_steps, second_steps = substeps(levels, level, size, ext, pulled, second)
    for kind, sender, _, slot in force_sides(levels):
        wanted = [depth - 1] if kind == "up" else [0, 1]

        def work(wanted=wanted, slot=slot):
            def put(axis, layer, tile, value):
                faces[slot][(axis, layer - wanted[0], *tile)] = value

            first_steps(range(wanted[0] - 1, wanted[-1] + 2))
            for _ in second_steps(wanted, put):
                pass

        guarded(level, sender, work)


def edge_body(
    size, levels, level_ref, strip_ref, left_ref, right_ref, inner_vel, faces,
    edge_ref, vel_ref, beyond_ref, sides, pulled, second,
):
    depth, height, width = size
    rows = height + 8
    level = level_ref[0]
    lane = lax.broadcasted_iota(jnp.int32, (rows, 128), 1)
    before = lane % 8 < 4
    bottom = (lane // 8 == LOW) & (level == 0)
    top = (lane // 8 == LOW + depth - 1) & (level == levels - 1)
    for channel, tile, first, cols in face_table(False)[0]:
        turned = lane_roll(left_ref[tile], 4 - cols - first)
        sides[0, channel] = jnp.where(before, turned, strip_ref[channel])
    for channel, tile, first, _ in face_table(True)[0]:
        turned = lane_roll(right_ref[tile], 4 - first)
        sides[1, channel] = jnp.where(before, strip_ref[channel], turned)

    def pull(source, side, target):
        for index in range(19):
            way_z, way_y, way_x = ways[index]
            value = lane_roll(source[side, index], 8 * way_z + way_x)
            if way_y != 0:
                value = pltpu.roll(value, way_y % rows, 0)
            if way_z != 0:
                value = jnp.where(bottom if way_z == 1 else top, source[side, opposite[index]], value)
            target[side, index] = value

    speeds = [[], []]
    for side in range(2):
        pull(sides, side, pulled)
        for row in range(0, rows, 8):
            cut = slice(row, row + 8)
            posts = relaxed([pulled[side, index, cut] for index in range(19)])
            inside = sides[side, 19, cut] > 0.5
            for index in range(19):
                second[side, index, cut] = jnp.where(inside, sides[side, index, cut], posts[index])
        pull(second, side, pulled)
        density, moment = moments([pulled[side, index] for index in range(19)])
        inverse = 1.0 / density
        speeds[side] = [part * inverse for part in moment]

    row = lax.broadcasted_iota(jnp.int32, (rows, 128), 0)
    valid = (row < height + 2) | (row == rows - 1)
    outside = (lane < 2) | (lane == 127)
    vel_in = inner_vel.take()
    faces = [face.take() for face in faces]

    def inner(axis, layer, cols):
        if layer == 0:
            return faces[0][axis, 0, :, cols]
        if layer > depth:
            return faces[-1][axis, layer - depth - 1, :, cols]
        return vel_in[axis, layer - 1, :, cols]

    table = table_rows(depth, height)
    vel_ref[...] = jnp.zeros_like(vel_ref)
    beyond_ref[...] = jnp.zeros_like(beyond_ref)

    def put(target, axis, layer, cols, cells):
        at = axis * table + layer * (height + 3)
        target[at : at + 1, cols] = cells[rows - 1 :, :]
        target[at + 1 : at + height + 3, cols] = cells[: height + 2, :]

    for axis in range(3):
        main = jnp.where(before, speeds[1][axis], speeds[0][axis])
        rest = jnp.where(before, speeds[0][axis], speeds[1][axis])
        for layer in range(depth + 3):
            keep = valid
            if layer == 0:
                keep = valid & (level != 0)
            if layer > depth:
                keep = valid & (level != levels - 1)
            shift = -(8 * (layer - 1 + LOW) + 4)
            turned = lane_roll(main, shift)
            for col in range(0, width, 128):
                cells = inner(axis, layer, slice(col, col + 128))
                if col == 0 or col == width - 128:
                    mask = (lane < 2) & (col == 0) | (lane >= 126) & (col == width - 128)
                    cells = jnp.where(mask, turned, cells)
                put(vel_ref, axis, layer, slice(col, col + 128), jnp.where(keep, cells, 0.0))
            put(beyond_ref, axis, layer, slice(0, 128), jnp.where(keep & outside, lane_roll(rest, shift), 0.0))
    for index in range(19):
        edge_ref[index] = jnp.where(before, pulled[1, index], pulled[0, index])[:height]


def patch_body(_, pops_in, edge_ref, pops_ref):
    depth, height, width = pops_ref.shape[1:]
    lane = lax.broadcasted_iota(jnp.int32, (height, 128), 1)
    for index in range(19):
        value = edge_ref[index]
        for layer in range(depth):
            turned = lane_roll(value, -(8 * (layer + LOW) + 4))
            for col in range(0, width, 128):
                cells = pops_in[index, layer, :, col : col + 128]
                if col == 0 or col == width - 128:
                    mask = (lane < 2) & (col == 0) | (lane >= 126) & (col == width - 128)
                    cells = jnp.where(mask, turned, cells)
                pops_ref[index, layer, :, col : col + 128] = cells


def long_cost():
    return pl.CostEstimate(flops=10**8, bytes_accessed=1 << 22, transcendentals=0)


def shifted(value, axis, step):
    count = lax.axis_size(axis)
    return lax.ppermute(value, axis, [(i, (i + step) % count) for i in range(count)])


def to_level(value, kind, levels, side=None, step=0):
    pairs = []
    for at in range(levels):
        other = 1 - at if levels == 2 else at + 1 if kind in ("low", "up") else at - 1
        if 0 <= other < levels:
            pairs.append((at, other))
    if side is None:
        return lax.ppermute(value, "gz", pairs)
    count = lax.axis_size(side)
    return lax.ppermute(
        value,
        (side, "gz"),
        [
            (brick * levels + at, (brick + step) % count * levels + other)
            for brick in range(count)
            for at, other in pairs
        ],
    )


def wide_exchange(pops, coarse_pops, interface, ready):
    levels = lax.axis_size("gz")
    depth, height, width = interface.shape
    sizes = rim_sizes(levels)
    slots = len(sizes)
    kinds = ["low", "high"][:slots]
    down_sizes, up_sizes = zip(*rim_row_sizes(levels))
    outs = call(
        functools.partial(first_body, levels),
        [(channels, depth, height, width), (channels, height, 128)]
        + [(size, width) for size in own_rows(depth)[1]]
        + [(size, height, width) for size in sizes]
        + [(size, width) for size in down_sizes + up_sizes],
        [pops, coarse_pops, interface],
    )
    posts, own, down, up = outs[:4]
    rims, down_rims, up_rims = (outs[4 + slots * at : 4 + slots * at + slots] for at in range(3))
    given = [shifted(down, "gy", -1), shifted(up, "gy", 1)]
    given += [to_level(value, kind, levels) for value, kind in zip(rims, kinds)]
    given += [to_level(value, kind, levels, "gy", -1) for value, kind in zip(down_rims, kinds)]
    given += [to_level(value, kind, levels, "gy", 1) for value, kind in zip(up_rims, kinds)]
    deep, rows = depth + LOW + HIGH, height + 8
    ext = pltpu.VMEM((channels, deep, rows, width), jnp.float32)
    strip, right, left = call(
        functools.partial(strip_body, levels, depth),
        [(channels, rows, 128)] + [(face_table(high)[1], rows, 128) for high in (False, True)],
        [own] + given + [ready],
        [pltpu.VMEM((FOUR, rows, 128), jnp.float32)],
        heads=[(1, strip_rows()[1][0]), (2, strip_rows()[1][1])]
        + [(3 + at, FOUR) for at in range(slots)]
        + [(3 + slots + at, rim_strip_rows()[1][0]) for at in range(slots)]
        + [(3 + 2 * slots + at, rim_strip_rows()[1][1]) for at in range(slots)],
    )
    left, right = shifted(right, "gx", 1), shifted(left, "gx", -1)
    scratch = [
        ext,
        pltpu.VMEM((4, 19, rows, width), jnp.float32),
        pltpu.VMEM((19, deep - 2, rows, width), jnp.float32),
    ]
    faces = call(
        functools.partial(face_body, levels), [(3, 2, rows, width)] * slots, [posts] + given, scratch
    )
    faces = [to_level(value, kind, levels) for value, kind in zip(faces, ["up", "down"])]
    inner_pops, inner_vel = call(
        functools.partial(inner_body, levels),
        [pops.shape, (3, depth, rows, width)],
        [posts] + given,
        scratch,
        long_cost(),
    )
    return strip, left, right, inner_pops, inner_vel, faces


def phis(frac):
    angle = frac * (0.5 * math.pi)
    sine = 0.25 * jnp.sin(angle)
    cosine = 0.25 * jnp.cos(angle)
    return (0.25 - sine, 0.25 + cosine, 0.25 + sine, 0.25 - cosine)


def split(value):
    high = value.astype(jnp.bfloat16)
    return high, (value - high.astype(jnp.float32)).astype(jnp.bfloat16)


def pick(step, parts):
    value = jnp.where(step == 0, parts[0], 0.0)
    for index in range(1, 4):
        value = jnp.where(step == index, parts[index], value)
    return value


def dots(left, right, dims):
    return lax.dot_general(left, right, (dims, ((), ())), preferred_element_type=jnp.float32)


def table_rows(depth, height):
    return -(-(depth + 3) * (height + 3) // 16) * 16


def weigh_body(size, _, frac_ref, home_ref, along, plane_ref, ready_ref):
    depth, height, width = size
    blocks = home_ref.shape[0]
    layers, rows = depth + 3, height + 3
    table = table_rows(depth, height)
    ready_ref[...] = jnp.zeros_like(ready_ref)
    along[2 * width :, :] = jnp.zeros((128, along.shape[1]), jnp.bfloat16)
    plane_ref[:, layers * rows :, :] = jnp.zeros(
        (plane_ref.shape[0], table - layers * rows, 256), jnp.float32
    )
    span_x = lax.broadcasted_iota(jnp.int32, (width, 128), 0) + 1
    span_end = lax.broadcasted_iota(jnp.int32, (16, 128), 0)
    span_y = lax.broadcasted_iota(jnp.int32, (padded(rows), 128), 0)
    span_z = lax.broadcasted_iota(jnp.int32, (padded(layers), 128), 0)
    for block in range(blocks):
        side = slice(block * 128, block * 128 + 128)
        cell = home_ref[block : block + 1, :]
        cell_x = cell % width
        cell_y = cell // width % height
        cell_z = cell // (width * height)
        part_x = phis(frac_ref[0, block : block + 1, :])
        part_y = phis(frac_ref[1, block : block + 1, :])
        part_z = phis(frac_ref[2, block : block + 1, :])
        high, low = split(pick(span_x - cell_x, part_x))
        along[0:width, side] = low
        along[width : 2 * width, side] = high
        high, low = split(pick(span_end + (width + 1) - cell_x, part_x))
        along[2 * width : 2 * width + 16, side] = high
        along[2 * width + 32 : 2 * width + 48, side] = high
        along[2 * width + 64 : 2 * width + 80, side] = low
        high, low = split(jnp.where((span_end == 15) & (cell_x == 0), part_x[0], 0.0))
        along[2 * width + 112 : 2 * width + 128, side] = high
        along[2 * width + 16 : 2 * width + 32, side] = high
        along[2 * width + 48 : 2 * width + 64, side] = low
        weight_y = pick(span_y - cell_y, part_y)[:rows]
        weight_z = pick(span_z - cell_z, part_z)
        half = block % 2 * 128
        for layer in range(layers):
            plane_ref[block // 2, layer * rows : layer * rows + rows, half : half + 128] = (
                weight_y * weight_z[layer : layer + 1, :]
            )


def droplet_body(
    size, counts_ref, dest_ref, vel_ref, beyond_ref, speed_ref, frac_ref, along_in, plane_in,
    spread_ref, outer_ref, stay_ref, state_ref, twice, mixed, push_high, push_low, meanwhile,
):
    depth, height, width = size
    blocks = state_ref.shape[0]
    table = table_rows(depth, height)
    high, low = split(vel_ref[...])
    twice[:, :width] = high
    twice[:, width:] = high
    mixed[:, :width] = low
    high, low = (part.astype(jnp.float32) for part in split(beyond_ref[...]))
    mixed[:, width:] = (high + lane_roll(low, 32) + lane_roll(high, 64)).astype(jnp.bfloat16)
    slots = lax.broadcasted_iota(jnp.int32, (1, 128), 1)
    along, plane_ref = along_in.take(), plane_in.take()

    def sample(number):
        pair = slice(number * 256, number * 256 + 256)
        return dots(twice[...], along[0 : 2 * width, pair], ((1,), (0,))) + dots(
            mixed[...], along[width:, pair], ((1,), (0,))
        )

    def move(number, sums):
        plane = plane_ref[number]
        for axis in range(3):
            where = slice(axis * table, axis * table + table)
            sampled = jnp.sum(sums[where] * plane, axis=0, keepdims=True)
            for half in range(2):
                block = 2 * number + half
                live = slots < counts_ref[block]
                sample = sampled[:, half * 128 : half * 128 + 128]
                speed = speed_ref[axis, block : block + 1, :]
                frac = frac_ref[axis, block : block + 1, :]
                moved = speed + relax * (sample - speed)
                push = jnp.where(live, couple * (moved - sample), 0.0)
                stays = live & (dest_ref[block] == 13)
                for at, value in ((axis, moved), (3 + axis, frac + moved)):
                    state_ref[block, at : at + 1, :] = jnp.where(live, value, 0.0)
                    stay_ref[at, block : block + 1, :] = jnp.where(stays, value, 0.0)
                high, low = split(plane[:, half * 128 : half * 128 + 128] * push)
                push_high[where, block * 128 : block * 128 + 128] = high
                push_low[where, block * 128 : block * 128 + 128] = low

    pairs = blocks // 2
    for number in range(pairs):
        move(number, sample(number))
    main = dots(push_high[...], along[0 : 2 * width, :], ((1,), (1,)))
    for action in meanwhile:
        action()
    rest = dots(push_low[...], along[width:, :], ((1,), (1,)))
    outer = dots(push_high[...], along[2 * width :, :], ((1,), (1,)))
    spread_ref[...] = main[:, :width] + main[:, width:] + rest[:, :width]
    outer_ref[...] = outer + lane_roll(outer, -64) + rest[:, width:]


def force_sides(levels):
    if levels == 2:
        return [("up", 0, 1, 0), ("down", 1, 0, 0)]
    return [("up", None, None, 0), ("down", None, None, 1)]


GROUP = 6 * 8


def group_at(way_z, way_y):
    return (way_z + 1) * 3 + way_y + 1


def face_rows(depth, height):
    return -(-depth // 8) * height


def message_rows(depth):
    return [8 * 8, 2 * 4 * depth, 4 * depth, 2 * 8, 8]


def pack_blocks(
    levels, level_ref, dest_ref, state_ref, side_ref,
    to_levels, north_ref, south_ref, north_levels, south_levels, outbox,
):
    level = level_ref[0]
    blocks = state_ref.shape[0]
    codes = [dest_ref[block] for block in range(blocks)]
    outbox[...] = jnp.zeros_like(outbox)
    for block in range(blocks):
        rank = jnp.int32(0)
        for earlier in range(block):
            rank = rank + (codes[earlier] == codes[block]).astype(jnp.int32)
        slot = jnp.where(codes[block] == 13, 27 * CAP, codes[block] * CAP + jnp.minimum(rank, CAP - 1))
        outbox[slot] = state_ref[block]

    def put(target, way_z, way_y):
        base = target.shape[0] - GROUP
        for slot in range(6):
            target[base + 8 * slot : base + 8 * slot + 8, :] = outbox[6 * group_at(way_z, way_y) + slot]

    put(north_ref, 0, 1)
    put(south_ref, 0, -1)
    for slot in range(CAP):
        side_ref[slot] = outbox[6 * group_at(0, 0) + slot]
        side_ref[CAP + slot] = outbox[6 * group_at(0, 0) + 4 + slot]
    ways_z = [(1 - 2 * level, 0)] if levels == 2 else [(1, 0), (-1, 1)]
    for way_z, slot in ways_z:
        put(to_levels[slot], way_z, 0)
        put(north_levels[slot], way_z, 1)
        put(south_levels[slot], way_z, -1)


def pack_force(
    levels, level_ref, spread_ref, outer_ref, own_ref,
    to_levels, north_ref, south_ref, north_levels, south_levels, strip,
):
    depth, height, width = own_ref.shape[1:]
    rows, table = height + 3, table_rows(depth, height)
    lane = lax.broadcasted_iota(jnp.int32, (table, 128), 1)
    value = jnp.zeros((table, 128), jnp.float32)
    for axis in range(3):
        here = (lane >= 4 * axis) & (lane < 4 * axis + 3)
        cells = outer_ref[axis * table : axis * table + table, :]
        value = jnp.where(here, lane_roll(cells, 4 * axis + 1), value)
    strip[...] = value

    def force(part, layer, cut):
        at = layer * rows
        if part < 3:
            return spread_ref[part * table + at + cut.start : part * table + at + cut.stop, :]
        return strip[at + cut.start : at + cut.stop, :]

    main, north, south = slice(1, height + 1), slice(height + 1, height + 3), slice(0, 1)
    for part in range(4):
        for layer in range(depth):
            own_ref[part, layer] = force(part, layer + 1, main)
            at = part * depth + layer
            north_ref[2 * at : 2 * at + 2, :] = force(part, layer + 1, north)
            south_ref[at : at + 1, :] = force(part, layer + 1, south)
    for kind, sender, _, slot in force_sides(levels):

        def pack(kind=kind, slot=slot):
            for part in range(4):
                for step in range(2 if kind == "up" else 1):
                    layer = depth + 1 + step if kind == "up" else 0
                    at = 2 * part + step
                    to_levels[slot][8 * at : 8 * at + 8, :] = force(part, layer, main)
                    north_levels[slot][2 * at : 2 * at + 2, :] = force(part, layer, north)
                    south_levels[slot][at : at + 1, :] = force(part, layer, south)

        guarded(level_ref[0], sender, pack)


def main_body(
    size, levels, level_ref, counts, dest, strip_ref, left_ref, right_ref, inner_vel,
    speed, frac, along, plane, *rest,
):
    slots = len(rim_sizes(levels))
    faces, rest = rest[:slots], rest[slots:]
    edge_ref, own_ref, stay_ref, side_ref, north_ref, south_ref = rest[:6]
    rest = rest[6:]
    to_levels, north_levels, south_levels = (rest[slots * at : slots * at + slots] for at in range(3))
    rest = rest[3 * slots :]
    vel_ref, beyond_ref, spread_ref, outer_ref, state_ref, outbox, strip = rest[:7]
    counts_ref, dest_ref = counts.take(), dest.take()
    edge_body(
        size, levels, level_ref, strip_ref, left_ref, right_ref, inner_vel, faces,
        edge_ref, vel_ref, beyond_ref, *rest[7:10],
    )

    def move_out():
        pack_blocks(
            levels, level_ref, dest_ref, state_ref, side_ref,
            to_levels, north_ref, south_ref, north_levels, south_levels, outbox,
        )

    droplet_body(
        size, counts_ref, dest_ref, vel_ref, beyond_ref, speed.take(), frac.take(), along, plane,
        spread_ref, outer_ref, stay_ref, state_ref, *rest[10:], [move_out],
    )
    pack_force(
        levels, level_ref, spread_ref, outer_ref, own_ref,
        to_levels, north_ref, south_ref, north_levels, south_levels, strip,
    )


def gather_body(levels, level_ref, own_ref, side_ref, *rest):
    depth, height, width = own_ref.shape[1:]
    slots = len(rim_sizes(levels))
    north_ref, south_ref = rest[:2]
    from_levels, north_levels, south_levels = (rest[2 + slots * at : 2 + slots * at + slots] for at in range(3))
    force_ref, right_ref, left_ref, total = rest[2 + 3 * slots :]
    base = face_rows(depth, height)
    total[...] = own_ref[...]
    right_ref[base:, :] = jnp.zeros((right_ref.shape[0] - base, width), jnp.float32)
    left_ref[base:, :] = jnp.zeros((left_ref.shape[0] - base, width), jnp.float32)
    last = slice(height - 1, height)
    for part in range(4):
        for layer in range(depth):
            at = part * depth + layer
            total[part, layer, 0:2, :] += north_ref[2 * at : 2 * at + 2, :]
            total[part, layer, last, :] += south_ref[at : at + 1, :]

    def blocks(source, way_z, way_y):
        at = base + 12 * group_at(way_z, way_y)
        start = source.shape[0] - GROUP
        for slot in range(CAP):
            rows = slice(at + 6 * slot, at + 6 * slot + 6)
            left_ref[rows, :] = source[start + 8 * slot : start + 8 * slot + 6, :]
            right_ref[rows, :] = source[start + 32 + 8 * slot : start + 38 + 8 * slot, :]

    at = base + 12 * group_at(0, 0)
    for slot in range(CAP):
        left_ref[at + 6 * slot : at + 6 * slot + 6, :] = side_ref[slot, 0:6, :]
        right_ref[at + 6 * slot : at + 6 * slot + 6, :] = side_ref[2 + slot, 0:6, :]
    blocks(north_ref, 0, 1)
    blocks(south_ref, 0, -1)
    for kind, _, receiver, slot in force_sides(levels):

        def take(kind=kind, slot=slot):
            for part in range(4):
                for step in range(2 if kind == "up" else 1):
                    layer = step if kind == "up" else depth - 1
                    at = 2 * part + step
                    total[part, layer] += from_levels[slot][8 * at : 8 * at + 8, :]
                    total[part, layer, 0:2, :] += north_levels[slot][2 * at : 2 * at + 2, :]
                    total[part, layer, last, :] += south_levels[slot][at : at + 1, :]
            way = 1 if kind == "up" else -1
            blocks(from_levels[slot], way, 0)
            blocks(north_levels[slot], way, 1)
            blocks(south_levels[slot], way, -1)

        guarded(level_ref[0], receiver, take)
    for layer in range(depth):
        for axis in range(3):
            force_ref[axis, layer] = total[axis, layer]
    lane = lax.broadcasted_iota(jnp.int32, (height, 128), 1)
    for tile in range(base // height):
        value = jnp.zeros((height, 128), jnp.float32)
        for layer in range(8 * tile, min(8 * tile + 8, depth)):
            part = layer - 8 * tile
            value = jnp.where(lane // 16 == part, lane_roll(total[3, layer, :, 0:128], 16 * part), value)
        for target in (right_ref, left_ref):
            target[tile * height : tile * height + height, 0:128] = value


def last_body(levels, level_ref, part_ref, stay_ref, *rest):
    depth, height, width = part_ref.shape[1:]
    slots = len(rim_sizes(levels))
    north_ref, south_ref = rest[:2]
    from_levels, north_levels, south_levels = (rest[2 + slots * at : 2 + slots * at + slots] for at in range(3))
    right_ref, left_ref, force_ref, arrived_ref = rest[2 + 3 * slots :]
    blocks = stay_ref.shape[1]
    base = face_rows(depth, height)
    lane = lax.broadcasted_iota(jnp.int32, (height, 128), 1)
    for layer in range(depth):
        rows = slice(layer // 8 * height, layer // 8 * height + height)
        before, after = right_ref[rows, :128], left_ref[rows, :128]
        for axis in range(3):
            at = 16 * (layer % 8) + 4 * axis
            first = jnp.where(lane < 2, lane_roll(before, -at - 1), 0.0)
            final = jnp.where(lane == 127, lane_roll(after, 127 - at), 0.0)
            force_ref[axis, layer] = part_ref[axis, layer]
            force_ref[axis, layer, :, 0:128] += first
            force_ref[axis, layer, :, width - 128 : width] += final
    arrived_ref[:, 0:blocks, :] = stay_ref[...]

    def put(source, start, stride, way_z, way_y, way_x):
        code = group_at(way_z, way_y) * 3 + way_x + 1
        at = blocks + CAP * (code if code < 13 else code - 1)
        for slot in range(CAP):
            for axis in range(6):
                if source is None:
                    value = jnp.zeros((1, 128), jnp.float32)
                else:
                    value = source[start + stride * slot + axis : start + stride * slot + axis + 1, :]
                arrived_ref[axis, at + slot : at + slot + 1, :] = value

    for way_z in (-1, 0, 1):
        for way_y in (-1, 0, 1):
            for way_x, source in ((1, right_ref), (-1, left_ref)):
                put(source, base + 12 * group_at(way_z, way_y), 6, way_z, way_y, way_x)
    middle = 16

    def put_group(source, way_z, way_y):
        put(source, None if source is None else source.shape[0] - GROUP + middle, 8, way_z, way_y, 0)

    put_group(north_ref, 0, 1)
    put_group(south_ref, 0, -1)
    for kind, _, receiver, slot in force_sides(levels):
        way = 1 if kind == "up" else -1

        def take(way=way, slot=slot):
            put_group(from_levels[slot], way, 0)
            put_group(north_levels[slot], way, 1)
            put_group(south_levels[slot], way, -1)

        def clear(way=way):
            for way_y in (-1, 0, 1):
                put_group(None, way, way_y)

        guarded(level_ref[0], receiver, take)
        if receiver is not None:
            guarded(level_ref[0], 1 - receiver, clear)


def local(pops, coarse_pops, interface, drop_vel, drop_frac, home, counts, dest):
    levels = lax.axis_size("gz")
    depth, height, width = interface.shape
    blocks = home.shape[0]
    kinds = ["up", "down"][: len(rim_sizes(levels))]
    slots = len(kinds)
    size = (depth, height, width)
    rows = height + 8
    table = table_rows(depth, height)
    along, plane, ready = call(
        functools.partial(weigh_body, size),
        [(2 * width + 128, blocks * 128), (blocks // 2, table, 256), (8, 128)],
        [drop_frac, home],
        cost=long_cost(),
        kind=[jnp.bfloat16, jnp.float32, jnp.float32],
    )
    strip, left, right, inner_pops, inner_vel, faces = wide_exchange(pops, coarse_pops, interface, ready)
    sizes = [(count + GROUP, width) for count in message_rows(depth)]
    outs = call(
        functools.partial(main_body, size, levels),
        [(19, height, 128), (4, depth, height, width), (6, blocks, 128), (4, 8, 128), sizes[1], sizes[2]]
        + [sizes[0]] * slots
        + [sizes[3]] * slots
        + [sizes[4]] * slots,
        [counts, dest, strip, left, right, inner_vel, drop_vel, drop_frac, along, plane] + faces,
        [
            pltpu.VMEM((3 * table, width), jnp.float32),
            pltpu.VMEM((3 * table, 128), jnp.float32),
            pltpu.VMEM((3 * table, width), jnp.float32),
            pltpu.VMEM((3 * table, 128), jnp.float32),
            pltpu.VMEM((blocks, 8, 128), jnp.float32),
            pltpu.VMEM((27 * CAP + 1, 8, 128), jnp.float32),
            pltpu.VMEM((table, 128), jnp.float32),
            pltpu.VMEM((2, channels, rows, 128), jnp.float32),
            pltpu.VMEM((2, 19, rows, 128), jnp.float32),
            pltpu.VMEM((2, 19, rows, 128), jnp.float32),
            pltpu.VMEM((3 * table, 2 * width), jnp.bfloat16),
            pltpu.VMEM((3 * table, width + 128), jnp.bfloat16),
            pltpu.VMEM((3 * table, blocks * 128), jnp.bfloat16),
            pltpu.VMEM((3 * table, blocks * 128), jnp.bfloat16),
        ],
        late=(0, 1, *range(5, 10 + slots)),
    )
    edge, own, stay, side, north, south = outs[:6]
    to_levels, north_levels, south_levels = (outs[6 + slots * at : 6 + slots * at + slots] for at in range(3))
    received = [shifted(north, "gy", 1), shifted(south, "gy", -1)]
    received += [to_level(value, kind, levels) for value, kind in zip(to_levels, kinds)]
    received += [to_level(value, kind, levels, "gy", 1) for value, kind in zip(north_levels, kinds)]
    received += [to_level(value, kind, levels, "gy", -1) for value, kind in zip(south_levels, kinds)]
    (state,) = call(patch_body, [pops.shape], [inner_pops, edge], cost=long_cost())
    side_rows = (padded(face_rows(depth, height) + 9 * 6 * CAP), width)
    part, right, left = call(
        functools.partial(gather_body, levels),
        [(3, depth, height, width), side_rows, side_rows],
        [own, side] + received,
        [pltpu.VMEM((4, depth, height, width), jnp.float32)],
    )
    force, arrived = call(
        functools.partial(last_body, levels),
        [(3, depth, height, width), (6, blocks + 26 * CAP, 128)],
        [part, stay] + received + [shifted(right, "gx", 1), shifted(left, "gx", -1)],
    )
    return state, force, arrived


def solution(mesh):
    return jax.shard_map(
        local,
        mesh=mesh,
        in_specs=(
            P(None, "gz", "gy", "gx"),
            P(None, "gz", "gy", "gx"),
            P("gz", "gy", "gx"),
            P(None, ("gx", "gy", "gz"), None),
            P(None, ("gx", "gy", "gz"), None),
            P(("gx", "gy", "gz"), None),
            P(("gx", "gy", "gz")),
            P(("gx", "gy", "gz")),
        ),
        out_specs=(
            P(None, "gz", "gy", "gx"),
            P(None, "gz", "gy", "gx"),
            P(None, ("gx", "gy", "gz"), None),
        ),
        check_vma=False,
    )
```

```python
import functools
import math

import jax
import jax.numpy as jnp
import numpy as np
from jax import lax
from jax.experimental import pallas as pl
from jax.experimental.pallas import tpu as pltpu
from jax.sharding import PartitionSpec as P

CAP = 2


lattice = np.array(
    [
        [0, 0, 0],
        [1, 0, 0],
        [-1, 0, 0],
        [0, 1, 0],
        [0, -1, 0],
        [0, 0, 1],
        [0, 0, -1],
        [1, 1, 0],
        [-1, -1, 0],
        [1, -1, 0],
        [-1, 1, 0],
        [1, 0, 1],
        [-1, 0, -1],
        [1, 0, -1],
        [-1, 0, 1],
        [0, 1, 1],
        [0, -1, -1],
        [0, 1, -1],
        [0, -1, 1],
    ]
)
weights_table = np.array([1.0 / 3.0] + [1.0 / 18.0] * 6 + [1.0 / 36.0] * 12)
opposite = [0, 2, 1, 4, 3, 6, 5, 8, 7, 10, 9, 12, 11, 14, 13, 16, 15, 18, 17]
inverse_tau = 0.8
relax = 0.5
couple = 8.0


class Level:
    def __getitem__(self, _):
        return lax.axis_index("gz").astype(jnp.int32)


class Moving:
    def __init__(self, buffer, copy):
        self.buffer = buffer
        self.copy = copy

    def take(self):
        self.copy.wait()
        return self.buffer


def call(body, outs, arrays, scratch=(), cost=None, heads=(), late=(), kind=jnp.float32):
    heads = dict(heads)
    landing = []
    for at, value in enumerate(arrays):
        space = pltpu.SMEM if value.ndim == 1 else pltpu.VMEM
        landing.append(space((heads.get(at, value.shape[0]),) + value.shape[1:], value.dtype))

    def whole(*refs):
        given = refs[: len(arrays)]
        made = list(refs[len(arrays) : len(arrays) + len(outs)])
        rest = refs[len(arrays) + len(outs) :]
        landed, done, rest = list(rest[: len(arrays)]), rest[len(arrays)], rest[len(arrays) + 1 :]
        copies = []
        for at, (source, target) in enumerate(zip(given, landed)):
            if at in heads:
                source = source.at[pl.ds(0, heads[at])]
            copies.append(pltpu.make_async_copy(source, target, done.at[at]))
        for copy in copies:
            copy.start()
        for at, copy in enumerate(copies):
            if at in late:
                landed[at] = Moving(landed[at], copy)
            else:
                copy.wait()
        body(Level(), *landed, *made, *rest)

    vmem = pl.BlockSpec(memory_space=pltpu.VMEM)
    hbm = pl.BlockSpec(memory_space=pltpu.HBM)
    return pl.pallas_call(
        whole,
        out_shape=[
            jax.ShapeDtypeStruct(shape, kind[at] if isinstance(kind, list) else kind)
            for at, shape in enumerate(outs)
        ],
        in_specs=[hbm] * len(arrays),
        out_specs=[vmem] * len(outs),
        scratch_shapes=landing
        + [pltpu.SemaphoreType.DMA((len(arrays),))]
        + list(scratch),
        cost_estimate=cost,
        compiler_params=pltpu.CompilerParams(vmem_limit_bytes=64 * 1024 * 1024),
    )(*arrays)


ways = [tuple(int(part) for part in lattice[index][::-1]) for index in range(19)] + [(0, 0, 0)]
channels = len(ways)
LOW = 3
HIGH = 4


def low_reach(way):
    return 2 + way


def high_reach(way):
    return 3 - way


def rim(kind):
    side = 1 if kind == "low" else -1
    return [
        (step, channel)
        for step in (1, 2)
        for channel in range(channels)
        if step <= 1 + side * ways[channel][0]
    ]


def rim_sides(levels):
    if levels == 2:
        return [("low", 1, 0, 0), ("high", 0, 1, 0)]
    return [("low", None, None, 0), ("high", None, None, 1)]


def rim_sizes(levels):
    sizes = [FOUR + len(rim(kind)) for kind, _, _, _ in rim_sides(levels)]
    return [max(sizes)] if levels == 2 else sizes


def guarded(level, guard, action):
    if guard is None:
        action()
    else:
        pl.when(level == guard)(action)


def padded(count):
    return -(-count // 8) * 8


def reaches(channel, bounces):
    way_z, way, _ = ways[channel]
    above, below = high_reach(way), low_reach(way)
    if bounces and way_z != 0:
        above, below = max(above, HIGH - 1), max(below, LOW - 1)
    return above, below


def row_places(cells, start=(0, 0)):
    places, (high_at, low_at) = [], start
    for above, below in cells:
        places.append((high_at, low_at, above, below))
        high_at, low_at = high_at + above, low_at + below
    return places, (padded(high_at), padded(low_at))


def strip_rows():
    return row_places([reaches(channel, True) for channel in range(channels)])


def own_rows(depth):
    cells = [(layer, channel) for layer in range(depth) for channel in range(channels)]
    places, sizes = row_places(
        [reaches(channel, layer in (0, depth - 1)) for layer, channel in cells], strip_rows()[1]
    )
    return [(layer, channel, place) for (layer, channel), place in zip(cells, places)], sizes


FOUR = -(-channels // 4)


def rim_strip_rows():
    return row_places([(HIGH, LOW)] * FOUR)


def rim_rows(kind):
    places, sizes = row_places([reaches(channel, False) for _, channel in rim(kind)], rim_strip_rows()[1])
    return [(step, channel, place) for (step, channel), place in zip(rim(kind), places)], sizes


def rim_row_sizes(levels):
    sizes = [rim_rows(kind)[1] for kind, _, _, _ in rim_sides(levels)]
    return [tuple(max(part) for part in zip(*sizes))] if levels == 2 else sizes


def face_table(high):
    wants = []
    for channel in range(channels):
        way_z, _, way = ways[channel]
        count = high_reach(way) if high else low_reach(way)
        if way_z != 0:
            count = max(count, (HIGH if high else LOW) - 1)
        wants.append((-count, channel))
    free, table = [], []
    for count, channel in sorted(wants):
        tile = next((at for at, room in enumerate(free) if room >= -count), len(free))
        if tile == len(free):
            free.append(8)
        table.append((channel, tile, 8 - free[tile], -count))
        free[tile] += count
    return table, len(free)


def moments(cells):
    density = cells[0] * float(weights_table[0])
    moment = [None, None, None]
    face, edge = float(weights_table[1]), float(weights_table[7])
    edge_sum = cells[7]
    for index in range(8, 19):
        edge_sum = edge_sum + cells[index]
    face_sum = cells[1]
    for index in range(2, 7):
        face_sum = face_sum + cells[index]
    density = density + face * face_sum + edge * edge_sum
    for axis in range(3):
        total = {}
        for group, indices in ((face, range(1, 7)), (edge, range(7, 19))):
            plus, minus = None, None
            for index in indices:
                way = int(lattice[index][axis])
                if way == 1:
                    plus = cells[index] if plus is None else plus + cells[index]
                if way == -1:
                    minus = cells[index] if minus is None else minus + cells[index]
            total[group] = plus - minus
        moment[axis] = face * total[face] + edge * total[edge]
    return density, moment


def relaxed(cells):
    density, moment = moments(cells)
    inverse = 1.0 / density
    flow = [part * inverse for part in moment]
    square = flow[0] * flow[0] + flow[1] * flow[1] + flow[2] * flow[2]
    scale = density * inverse_tau
    base = scale * (1.0 - 1.5 * square)
    keep = 1.0 - inverse_tau
    posts = [None] * 19
    posts[0] = keep * cells[0] + base
    for index in range(1, 19, 2):
        along = None
        for axis in range(3):
            way = int(lattice[index][axis])
            if way != 0:
                part = flow[axis] if way == 1 else -flow[axis]
                along = part if along is None else along + part
        odd = 3.0 * scale * along
        even = base + (4.5 * scale) * (along * along)
        posts[index] = keep * cells[index] + (even + odd)
        posts[index + 1] = keep * cells[index + 1] + (even - odd)
    return posts


def lane_roll(value, shift):
    shift = shift % value.shape[-1]
    return value if shift == 0 else pltpu.roll(value, shift, value.ndim - 1)


def first_body(
    levels, level_ref, pops_ref, coarse_ref, interface_ref, posts_ref, strip_ref, down_ref, up_ref, *outs
):
    depth, height, width = interface_ref.shape
    slots = len(rim_sizes(levels))
    rims, down_rims, up_rims = (outs[slots * at : slots * at + slots] for at in range(3))
    lane = lax.broadcasted_iota(jnp.int32, (height, 128), 1)

    def put_rows(down, up, place, cells):
        down_at, up_at, down_rows, up_rows = place
        cols = slice(0, cells.shape[1])
        down[down_at : down_at + down_rows, cols] = cells[:down_rows, :]
        up[up_at : up_at + up_rows, cols] = cells[height - up_rows :, :]

    own = own_rows(depth)[0]
    for layer in range(depth):
        mask = interface_ref[layer]
        inside = mask == 1
        posts = relaxed([pops_ref[index, layer] for index in range(19)])
        posts = [
            jnp.where(inside, coarse_ref[index, layer].astype(jnp.float32), posts[index])
            for index in range(19)
        ] + [mask.astype(jnp.float32)]
        for channel in range(channels):
            posts_ref[channel, layer] = posts[channel]
            put_rows(down_ref, up_ref, own[layer * channels + channel][2], posts[channel])
    for channel in range(channels):
        value = jnp.zeros((height, 128), jnp.float32)
        for layer in range(depth):
            cells = posts_ref[channel, layer]
            if width > 128:
                cells = jnp.where(lane < 64, cells[:, :128], cells[:, width - 128 :])
            value = jnp.where(lane // 8 == LOW + layer, lane_roll(cells, 8 * (LOW + layer) + 4), value)
        strip_ref[channel] = value
        put_rows(down_ref, up_ref, strip_rows()[0][channel], value)
    for kind, _, sender, slot in rim_sides(levels):

        def pack(kind=kind, slot=slot):
            for tile in range(FOUR):
                value = jnp.zeros((height, 128), jnp.float32)
                for part in range(min(4, channels - 4 * tile)):
                    first = LOW + depth - 4 if kind == "low" else LOW
                    turned = lane_roll(strip_ref[4 * tile + part], 32 * part - 8 * first)
                    value = jnp.where(lane // 32 == part, turned, value)
                rims[slot][tile, :, 0:128] = value
                put_rows(down_rims[slot], up_rims[slot], rim_strip_rows()[0][tile], value)
            for at, (step, channel, place) in enumerate(rim_rows(kind)[0]):
                cells = posts_ref[channel, depth - step if kind == "low" else step - 1]
                rims[slot][FOUR + at] = cells
                put_rows(down_rims[slot], up_rims[slot], place, cells)

        guarded(level_ref[0], sender, pack)


def unpack(levels, level, posts_ref, above_ref, below_ref, rims, above_rims, below_rims, ext):
    depth, height = posts_ref.shape[1:3]
    rows = height + 8

    def put(channel, at, cells, place, above, below):
        above_at, below_at, above_rows, below_rows = place
        ext[channel, at, :height, :] = cells
        ext[channel, at, height : height + above_rows, :] = above[above_at : above_at + above_rows, :]
        ext[channel, at, rows - below_rows : rows, :] = below[below_at : below_at + below_rows, :]

    for layer, channel, place in own_rows(depth)[0]:
        put(channel, LOW + layer, posts_ref[channel, layer], place, above_ref, below_ref)
    for kind, receiver, _, slot in rim_sides(levels):

        def take(kind=kind, slot=slot):
            for at, (step, channel, place) in enumerate(rim_rows(kind)[0]):
                layer = LOW - step if kind == "low" else LOW + depth + step - 1
                put(channel, layer, rims[slot][FOUR + at], place, above_rims[slot], below_rims[slot])

        guarded(level, receiver, take)


def split_given(levels, rest):
    slots = len(rim_sizes(levels))
    parts = [rest[3 + slots * at : 3 + slots * at + slots] for at in range(3)]
    return rest[:3], parts, rest[3 + 3 * slots :]


def strip_body(levels, depth, level_ref, *rest):
    (own_ref, above_ref, below_ref), parts, rest = split_given(levels, rest)
    _, strip_ref, right_ref, left_ref, tiles = rest
    rows = strip_ref.shape[1]
    height = rows - 8
    lane = lax.broadcasted_iota(jnp.int32, (rows, 128), 1)
    layer_at = lane // 8

    def put(target, index, place, above, below):
        above_at, below_at, above_rows, below_rows = place
        target[index, height : height + above_rows, :] = above[above_at : above_at + above_rows, 0:128]
        target[index, rows - below_rows :, :] = below[below_at : below_at + below_rows, 0:128]

    for channel in range(channels):
        strip_ref[channel, 0:height, :] = own_ref[channel]
        put(strip_ref, channel, strip_rows()[0][channel], above_ref, below_ref)
    for kind, receiver, _, slot in rim_sides(levels):

        def take(kind=kind, slot=slot):
            rims, above_rims, below_rims = (part[slot] for part in parts)
            first = -1 if kind == "low" else LOW + depth
            here = layer_at < LOW if kind == "low" else layer_at >= LOW + depth
            for tile in range(FOUR):
                tiles[tile, 0:height, :] = rims[tile, :, 0:128]
                put(tiles, tile, rim_strip_rows()[0][tile], above_rims, below_rims)
                value = tiles[tile]
                for part in range(min(4, channels - 4 * tile)):
                    turned = lane_roll(value, 8 * first - 32 * part)
                    strip_ref[4 * tile + part] = jnp.where(here, turned, strip_ref[4 * tile + part])

        guarded(level_ref[0], receiver, take)
    spot = lane % 8
    for target, high in ((right_ref, False), (left_ref, True)):
        table, count = face_table(high)
        for tile in range(count):
            value = jnp.zeros((rows, 128), jnp.float32)
            for channel, at, first, cols in table:
                if at == tile:
                    turned = lane_roll(strip_ref[channel], first - (4 if high else 4 - cols))
                    value = jnp.where((spot >= first) & (spot < first + cols), turned, value)
            target[tile] = value


def substeps(levels, level, size, ext, pulled, second):
    depth, height, width = size
    rows = height + 8

    def pull(source, layer, at, target):
        for index in range(19):
            way_z, way_y, way_x = ways[index]
            value = source[index, at - way_z]
            if way_x != 0:
                value = pltpu.roll(value, way_x % width, 1)
            if way_y != 0:
                value = pltpu.roll(value, way_y % rows, 0)
            if way_z == 1 and layer == 0:
                value = jnp.where(level == 0, source[opposite[index], at], value)
            if way_z == -1 and layer == depth - 1:
                value = jnp.where(level == levels - 1, source[opposite[index], at], value)
            target[index] = value

    tiles = [
        (slice(row, row + 8), slice(col, col + 128))
        for row in range(0, rows, 8)
        for col in range(0, width, 128)
    ]

    def first_steps(layers):
        for layer in layers:
            at = LOW + layer
            cells = pulled.at[at % pulled.shape[0]]
            pull(ext, layer, at, cells)
            for tile in tiles:
                posts = relaxed([cells[(index, *tile)] for index in range(19)])
                inside = ext[(19, at, *tile)] > 0.5
                for index in range(19):
                    second[(index, at - 1, *tile)] = jnp.where(
                        inside, ext[(index, at, *tile)], posts[index]
                    )

    def second_steps(layers, put):
        for layer in layers:
            at = LOW - 1 + layer
            cells = pulled.at[at % pulled.shape[0]]
            pull(second, layer, at, cells)
            for tile in tiles:
                density, moment = moments([cells[(index, *tile)] for index in range(19)])
                inverse = 1.0 / density
                for axis in range(3):
                    put(axis, layer, tile, moment[axis] * inverse)
            yield layer, cells

    return first_steps, second_steps


def inner_body(levels, level_ref, *rest):
    (posts_ref, above_ref, below_ref), parts, rest = split_given(levels, rest)
    pops_ref, vel_ref, ext, pulled, second = rest
    level = level_ref[0]
    unpack(levels, level, posts_ref, above_ref, below_ref, *parts, ext)
    depth, height, _ = size = posts_ref.shape[1:]
    first_steps, second_steps = substeps(levels, level, size, ext, pulled, second)

    def put(axis, layer, tile, value):
        vel_ref[(axis, layer, *tile)] = value

    pl.when(level != 0)(lambda: first_steps([-1]))
    pl.when(level != levels - 1)(lambda: first_steps([depth]))
    first_steps(range(depth))
    for layer, cells in second_steps(range(depth), put):
        for index in range(19):
            pops_ref[index, layer] = cells[index, :height, :]


def face_body(levels, level_ref, *rest):
    (posts_ref, above_ref, below_ref), parts, rest = split_given(levels, rest)
    slots = len(rim_sizes(levels))
    faces, (ext, pulled, second) = rest[:slots], rest[slots:]
    level = level_ref[0]
    unpack(levels, level, posts_ref, above_ref, below_ref, *parts, ext)
    depth, height, _ = size = posts_ref.shape[1:]
    first_steps, second_steps = substeps(levels, level, size, ext, pulled, second)
    for kind, sender, _, slot in force_sides(levels):
        wanted = [depth - 1] if kind == "up" else [0, 1]

        def work(wanted=wanted, slot=slot):
            def put(axis, layer, tile, value):
                at = (2 * axis + layer - wanted[0]) * (height + 3)
                row, cols = tile[0].start, tile[1]
                if row < height:
                    faces[slot][at + 1 + row : at + 9 + row, cols] = value
                else:
                    faces[slot][at + 1 + height : at + 3 + height, cols] = value[:2, :]
                    faces[slot][at : at + 1, cols] = value[7:, :]

            first_steps(range(wanted[0] - 1, wanted[-1] + 2))
            for _ in second_steps(wanted, put):
                pass

        guarded(level, sender, work)


def edge_body(
    size, levels, level_ref, strip_ref, left_ref, right_ref, inner_vel, faces,
    edge_ref, vel_ref, beyond_ref, sides, pulled, second,
):
    depth, height, width = size
    rows = height + 8
    level = level_ref[0]
    lane = lax.broadcasted_iota(jnp.int32, (rows, 128), 1)
    before = lane % 8 < 4
    bottom = (lane // 8 == LOW) & (level == 0)
    top = (lane // 8 == LOW + depth - 1) & (level == levels - 1)
    for channel, tile, first, cols in face_table(False)[0]:
        turned = lane_roll(left_ref[tile], 4 - cols - first)
        sides[0, channel] = jnp.where(before, turned, strip_ref[channel])
    for channel, tile, first, _ in face_table(True)[0]:
        turned = lane_roll(right_ref[tile], 4 - first)
        sides[1, channel] = jnp.where(before, strip_ref[channel], turned)

    def pull(source, side, target):
        for index in range(19):
            way_z, way_y, way_x = ways[index]
            value = lane_roll(source[side, index], 8 * way_z + way_x)
            if way_y != 0:
                value = pltpu.roll(value, way_y % rows, 0)
            if way_z != 0:
                value = jnp.where(bottom if way_z == 1 else top, source[side, opposite[index]], value)
            target[side, index] = value

    speeds = [[], []]
    for side in range(2):
        pull(sides, side, pulled)
        for row in range(0, rows, 8):
            cut = slice(row, row + 8)
            posts = relaxed([pulled[side, index, cut] for index in range(19)])
            inside = sides[side, 19, cut] > 0.5
            for index in range(19):
                second[side, index, cut] = jnp.where(inside, sides[side, index, cut], posts[index])
        pull(second, side, pulled)
        density, moment = moments([pulled[side, index] for index in range(19)])
        inverse = 1.0 / density
        speeds[side] = [part * inverse for part in moment]

    row = lax.broadcasted_iota(jnp.int32, (rows, 128), 0)
    valid = (row < height + 2) | (row == rows - 1)
    outside = (lane < 2) | (lane == 127)
    vel_in = inner_vel.take()
    faces = [face.take() for face in faces]

    def inner(axis, layer, cols):
        if 0 < layer <= depth:
            return vel_in[axis, layer - 1, :, cols]
        at = 2 * axis * (height + 3) if layer == 0 else (2 * axis + layer - depth - 1) * (height + 3)
        face = faces[0 if layer == 0 else -1]
        return jnp.concatenate(
            [
                face[at + 1 : at + height + 1, cols],
                face[at + height + 1 : at + height + 3, cols],
                jnp.zeros((5, 128), jnp.float32),
                face[at : at + 1, cols],
            ],
            axis=0,
        )

    table = table_rows(depth, height)
    vel_ref[...] = jnp.zeros_like(vel_ref)
    beyond_ref[...] = jnp.zeros_like(beyond_ref)

    def put(target, axis, layer, cols, cells):
        at = axis * table + layer * (height + 3)
        target[at : at + 1, cols] = cells[rows - 1 :, :]
        target[at + 1 : at + height + 3, cols] = cells[: height + 2, :]

    for axis in range(3):
        main = jnp.where(before, speeds[1][axis], speeds[0][axis])
        rest = jnp.where(before, speeds[0][axis], speeds[1][axis])
        for layer in range(depth + 3):
            keep = valid
            if layer == 0:
                keep = valid & (level != 0)
            if layer > depth:
                keep = valid & (level != levels - 1)
            shift = -(8 * (layer - 1 + LOW) + 4)
            turned = lane_roll(main, shift)
            for col in range(0, width, 128):
                cells = inner(axis, layer, slice(col, col + 128))
                if col == 0 or col == width - 128:
                    mask = (lane < 2) & (col == 0) | (lane >= 126) & (col == width - 128)
                    cells = jnp.where(mask, turned, cells)
                put(vel_ref, axis, layer, slice(col, col + 128), jnp.where(keep, cells, 0.0))
            put(beyond_ref, axis, layer, slice(0, 128), jnp.where(keep & outside, lane_roll(rest, shift), 0.0))
    for index in range(19):
        edge_ref[index] = jnp.where(before, pulled[1, index], pulled[0, index])[:height]


def patch_body(_, pops_in, edge_ref, pops_ref):
    depth, height, width = pops_ref.shape[1:]
    lane = lax.broadcasted_iota(jnp.int32, (height, 128), 1)
    for index in range(19):
        value = edge_ref[index]
        for layer in range(depth):
            turned = lane_roll(value, -(8 * (layer + LOW) + 4))
            for col in range(0, width, 128):
                cells = pops_in[index, layer, :, col : col + 128]
                if col == 0 or col == width - 128:
                    mask = (lane < 2) & (col == 0) | (lane >= 126) & (col == width - 128)
                    cells = jnp.where(mask, turned, cells)
                pops_ref[index, layer, :, col : col + 128] = cells


def long_cost():
    return pl.CostEstimate(flops=10**8, bytes_accessed=1 << 22, transcendentals=0)


def shifted(value, axis, step):
    count = lax.axis_size(axis)
    return lax.ppermute(value, axis, [(i, (i + step) % count) for i in range(count)])


def to_level(value, kind, levels, side=None, step=0):
    pairs = []
    for at in range(levels):
        other = 1 - at if levels == 2 else at + 1 if kind in ("low", "up") else at - 1
        if 0 <= other < levels:
            pairs.append((at, other))
    if side is None:
        return lax.ppermute(value, "gz", pairs)
    count = lax.axis_size(side)
    return lax.ppermute(
        value,
        (side, "gz"),
        [
            (brick * levels + at, (brick + step) % count * levels + other)
            for brick in range(count)
            for at, other in pairs
        ],
    )


def wide_exchange(pops, coarse_pops, interface, ready):
    levels = lax.axis_size("gz")
    depth, height, width = interface.shape
    sizes = rim_sizes(levels)
    slots = len(sizes)
    kinds = ["low", "high"][:slots]
    down_sizes, up_sizes = zip(*rim_row_sizes(levels))
    outs = call(
        functools.partial(first_body, levels),
        [(channels, depth, height, width), (channels, height, 128)]
        + [(size, width) for size in own_rows(depth)[1]]
        + [(size, height, width) for size in sizes]
        + [(size, width) for size in down_sizes + up_sizes],
        [pops, coarse_pops, interface],
    )
    posts, own, down, up = outs[:4]
    rims, down_rims, up_rims = (outs[4 + slots * at : 4 + slots * at + slots] for at in range(3))
    given = [shifted(down, "gy", -1), shifted(up, "gy", 1)]
    given += [to_level(value, kind, levels) for value, kind in zip(rims, kinds)]
    given += [to_level(value, kind, levels, "gy", -1) for value, kind in zip(down_rims, kinds)]
    given += [to_level(value, kind, levels, "gy", 1) for value, kind in zip(up_rims, kinds)]
    deep, rows = depth + LOW + HIGH, height + 8
    ext = pltpu.VMEM((channels, deep, rows, width), jnp.float32)
    strip, right, left = call(
        functools.partial(strip_body, levels, depth),
        [(channels, rows, 128)] + [(face_table(high)[1], rows, 128) for high in (False, True)],
        [own] + given + [ready],
        [pltpu.VMEM((FOUR, rows, 128), jnp.float32)],
        heads=[(1, strip_rows()[1][0]), (2, strip_rows()[1][1])]
        + [(3 + at, FOUR) for at in range(slots)]
        + [(3 + slots + at, rim_strip_rows()[1][0]) for at in range(slots)]
        + [(3 + 2 * slots + at, rim_strip_rows()[1][1]) for at in range(slots)],
    )
    left, right = shifted(right, "gx", 1), shifted(left, "gx", -1)
    scratch = [
        ext,
        pltpu.VMEM((4, 19, rows, width), jnp.float32),
        pltpu.VMEM((19, deep - 2, rows, width), jnp.float32),
    ]
    faces = call(
        functools.partial(face_body, levels), [(padded(6 * (height + 3)), width)] * slots, [posts] + given, scratch
    )
    faces = [to_level(value, kind, levels) for value, kind in zip(faces, ["up", "down"])]
    inner_pops, inner_vel = call(
        functools.partial(inner_body, levels),
        [pops.shape, (3, depth, rows, width)],
        [posts] + given,
        scratch,
        long_cost(),
    )
    return strip, left, right, inner_pops, inner_vel, faces


def phis(frac):
    angle = frac * (0.5 * math.pi)
    sine = 0.25 * jnp.sin(angle)
    cosine = 0.25 * jnp.cos(angle)
    return (0.25 - sine, 0.25 + cosine, 0.25 + sine, 0.25 - cosine)


def split(value):
    high = value.astype(jnp.bfloat16)
    return high, (value - high.astype(jnp.float32)).astype(jnp.bfloat16)


def pick(step, parts):
    value = jnp.where(step == 0, parts[0], 0.0)
    for index in range(1, 4):
        value = jnp.where(step == index, parts[index], value)
    return value


def dots(left, right, dims):
    return lax.dot_general(left, right, (dims, ((), ())), preferred_element_type=jnp.float32)


def table_rows(depth, height):
    return -(-(depth + 3) * (height + 3) // 16) * 16


def weigh_body(size, _, frac_ref, home_ref, along, plane_ref, ready_ref):
    depth, height, width = size
    blocks = home_ref.shape[0]
    layers, rows = depth + 3, height + 3
    table = table_rows(depth, height)
    ready_ref[...] = jnp.zeros_like(ready_ref)
    along[2 * width :, :] = jnp.zeros((128, along.shape[1]), jnp.bfloat16)
    plane_ref[:, layers * rows :, :] = jnp.zeros(
        (plane_ref.shape[0], table - layers * rows, 256), jnp.float32
    )
    span_x = lax.broadcasted_iota(jnp.int32, (width, 128), 0) + 1
    span_end = lax.broadcasted_iota(jnp.int32, (16, 128), 0)
    span_y = lax.broadcasted_iota(jnp.int32, (padded(rows), 128), 0)
    span_z = lax.broadcasted_iota(jnp.int32, (padded(layers), 128), 0)
    for block in range(blocks):
        side = slice(block * 128, block * 128 + 128)
        cell = home_ref[block : block + 1, :]
        cell_x = cell % width
        cell_y = cell // width % height
        cell_z = cell // (width * height)
        part_x = phis(frac_ref[0, block : block + 1, :])
        part_y = phis(frac_ref[1, block : block + 1, :])
        part_z = phis(frac_ref[2, block : block + 1, :])
        high, low = split(pick(span_x - cell_x, part_x))
        along[0:width, side] = low
        along[width : 2 * width, side] = high
        high, low = split(pick(span_end + (width + 1) - cell_x, part_x))
        along[2 * width : 2 * width + 16, side] = high
        along[2 * width + 32 : 2 * width + 48, side] = high
        along[2 * width + 64 : 2 * width + 80, side] = low
        high, low = split(jnp.where((span_end == 15) & (cell_x == 0), part_x[0], 0.0))
        along[2 * width + 112 : 2 * width + 128, side] = high
        along[2 * width + 16 : 2 * width + 32, side] = high
        along[2 * width + 48 : 2 * width + 64, side] = low
        weight_y = pick(span_y - cell_y, part_y)[:rows]
        weight_z = pick(span_z - cell_z, part_z)
        half = block % 2 * 128
        for layer in range(layers):
            plane_ref[block // 2, layer * rows : layer * rows + rows, half : half + 128] = (
                weight_y * weight_z[layer : layer + 1, :]
            )


def droplet_body(
    size, counts_ref, dest_ref, vel_ref, beyond_ref, speed_ref, frac_ref, along_in, plane_in,
    spread_ref, outer_ref, stay_ref, state_ref, twice, mixed, push_high, push_low, meanwhile,
):
    depth, height, width = size
    blocks = state_ref.shape[0]
    table = table_rows(depth, height)
    high, low = split(vel_ref[...])
    twice[:, :width] = high
    twice[:, width:] = high
    mixed[:, :width] = low
    high, low = (part.astype(jnp.float32) for part in split(beyond_ref[...]))
    mixed[:, width:] = (high + lane_roll(low, 32) + lane_roll(high, 64)).astype(jnp.bfloat16)
    slots = lax.broadcasted_iota(jnp.int32, (1, 128), 1)
    along, plane_ref = along_in.take(), plane_in.take()

    def sample(number):
        pair = slice(number * 256, number * 256 + 256)
        return dots(twice[...], along[0 : 2 * width, pair], ((1,), (0,))) + dots(
            mixed[...], along[width:, pair], ((1,), (0,))
        )

    def move(number, sums):
        plane = plane_ref[number]
        for axis in range(3):
            where = slice(axis * table, axis * table + table)
            sampled = jnp.sum(sums[where] * plane, axis=0, keepdims=True)
            for half in range(2):
                block = 2 * number + half
                live = slots < counts_ref[block]
                sample = sampled[:, half * 128 : half * 128 + 128]
                speed = speed_ref[axis, block : block + 1, :]
                frac = frac_ref[axis, block : block + 1, :]
                moved = speed + relax * (sample - speed)
                push = jnp.where(live, couple * (moved - sample), 0.0)
                stays = live & (dest_ref[block] == 13)
                for at, value in ((axis, moved), (3 + axis, frac + moved)):
                    state_ref[block, at : at + 1, :] = jnp.where(live, value, 0.0)
                    stay_ref[at, block : block + 1, :] = jnp.where(stays, value, 0.0)
                high, low = split(plane[:, half * 128 : half * 128 + 128] * push)
                push_high[where, block * 128 : block * 128 + 128] = high
                push_low[where, block * 128 : block * 128 + 128] = low

    pairs = blocks // 2
    for number in range(pairs):
        move(number, sample(number))
    main = dots(push_high[...], along[0 : 2 * width, :], ((1,), (1,)))
    for action in meanwhile:
        action()
    rest = dots(push_low[...], along[width:, :], ((1,), (1,)))
    outer = dots(push_high[...], along[2 * width :, :], ((1,), (1,)))
    spread_ref[...] = main[:, :width] + main[:, width:] + rest[:, :width]
    outer_ref[...] = outer + lane_roll(outer, -64) + rest[:, width:]


def force_sides(levels):
    if levels == 2:
        return [("up", 0, 1, 0), ("down", 1, 0, 0)]
    return [("up", None, None, 0), ("down", None, None, 1)]


GROUP = 6 * 8


def group_at(way_z, way_y):
    return (way_z + 1) * 3 + way_y + 1


def face_rows(depth, height):
    return -(-depth // 8) * height


def message_rows(depth):
    return [8 * 8, 2 * 4 * depth, 4 * depth, 2 * 8, 8]


def pack_blocks(
    levels, level_ref, dest_ref, state_ref, side_ref,
    to_levels, north_ref, south_ref, north_levels, south_levels, outbox,
):
    level = level_ref[0]
    blocks = state_ref.shape[0]
    codes = [dest_ref[block] for block in range(blocks)]
    outbox[...] = jnp.zeros_like(outbox)
    for block in range(blocks):
        rank = jnp.int32(0)
        for earlier in range(block):
            rank = rank + (codes[earlier] == codes[block]).astype(jnp.int32)
        slot = jnp.where(codes[block] == 13, 27 * CAP, codes[block] * CAP + jnp.minimum(rank, CAP - 1))
        outbox[slot] = state_ref[block]

    def put(target, way_z, way_y):
        base = target.shape[0] - GROUP
        for slot in range(6):
            target[base + 8 * slot : base + 8 * slot + 8, :] = outbox[6 * group_at(way_z, way_y) + slot]

    put(north_ref, 0, 1)
    put(south_ref, 0, -1)
    for slot in range(CAP):
        side_ref[slot] = outbox[6 * group_at(0, 0) + slot]
        side_ref[CAP + slot] = outbox[6 * group_at(0, 0) + 4 + slot]
    ways_z = [(1 - 2 * level, 0)] if levels == 2 else [(1, 0), (-1, 1)]
    for way_z, slot in ways_z:
        put(to_levels[slot], way_z, 0)
        put(north_levels[slot], way_z, 1)
        put(south_levels[slot], way_z, -1)


def pack_force(
    levels, level_ref, spread_ref, outer_ref, own_ref,
    to_levels, north_ref, south_ref, north_levels, south_levels, strip,
):
    depth, height, width = own_ref.shape[1:]
    rows, table = height + 3, table_rows(depth, height)
    lane = lax.broadcasted_iota(jnp.int32, (table, 128), 1)
    value = jnp.zeros((table, 128), jnp.float32)
    for axis in range(3):
        here = (lane >= 4 * axis) & (lane < 4 * axis + 3)
        cells = outer_ref[axis * table : axis * table + table, :]
        value = jnp.where(here, lane_roll(cells, 4 * axis + 1), value)
    strip[...] = value

    def force(part, layer, cut):
        at = layer * rows
        if part < 3:
            return spread_ref[part * table + at + cut.start : part * table + at + cut.stop, :]
        return strip[at + cut.start : at + cut.stop, :]

    main, north, south = slice(1, height + 1), slice(height + 1, height + 3), slice(0, 1)
    for part in range(4):
        for layer in range(depth):
            own_ref[part, layer] = force(part, layer + 1, main)
            at = part * depth + layer
            north_ref[2 * at : 2 * at + 2, :] = force(part, layer + 1, north)
            south_ref[at : at + 1, :] = force(part, layer + 1, south)
    for kind, sender, _, slot in force_sides(levels):

        def pack(kind=kind, slot=slot):
            for part in range(4):
                for step in range(2 if kind == "up" else 1):
                    layer = depth + 1 + step if kind == "up" else 0
                    at = 2 * part + step
                    to_levels[slot][8 * at : 8 * at + 8, :] = force(part, layer, main)
                    north_levels[slot][2 * at : 2 * at + 2, :] = force(part, layer, north)
                    south_levels[slot][at : at + 1, :] = force(part, layer, south)

        guarded(level_ref[0], sender, pack)


def main_body(
    size, levels, level_ref, counts, dest, strip_ref, left_ref, right_ref, inner_vel, *rest,
):
    slots = len(rim_sizes(levels))
    faces, (speed, frac, along, plane), rest = rest[:slots], rest[slots : slots + 4], rest[slots + 4 :]
    edge_ref, own_ref, stay_ref, side_ref, north_ref, south_ref = rest[:6]
    rest = rest[6:]
    to_levels, north_levels, south_levels = (rest[slots * at : slots * at + slots] for at in range(3))
    rest = rest[3 * slots :]
    vel_ref, beyond_ref, spread_ref, outer_ref, state_ref, outbox, strip = rest[:7]
    counts_ref, dest_ref = counts.take(), dest.take()
    edge_body(
        size, levels, level_ref, strip_ref, left_ref, right_ref, inner_vel, faces,
        edge_ref, vel_ref, beyond_ref, *rest[7:10],
    )

    def move_out():
        pack_blocks(
            levels, level_ref, dest_ref, state_ref, side_ref,
            to_levels, north_ref, south_ref, north_levels, south_levels, outbox,
        )

    droplet_body(
        size, counts_ref, dest_ref, vel_ref, beyond_ref, speed.take(), frac.take(), along, plane,
        spread_ref, outer_ref, stay_ref, state_ref, *rest[10:], [move_out],
    )
    pack_force(
        levels, level_ref, spread_ref, outer_ref, own_ref,
        to_levels, north_ref, south_ref, north_levels, south_levels, strip,
    )


def gather_body(levels, level_ref, own_ref, side_ref, *rest):
    depth, height, width = own_ref.shape[1:]
    slots = len(rim_sizes(levels))
    north_ref, south_ref = rest[:2]
    from_levels, north_levels, south_levels = (rest[2 + slots * at : 2 + slots * at + slots] for at in range(3))
    force_ref, right_ref, left_ref, total = rest[2 + 3 * slots :]
    base = face_rows(depth, height)
    total[...] = own_ref[...]
    right_ref[base:, :] = jnp.zeros((right_ref.shape[0] - base, width), jnp.float32)
    left_ref[base:, :] = jnp.zeros((left_ref.shape[0] - base, width), jnp.float32)
    last = slice(height - 1, height)
    for part in range(4):
        for layer in range(depth):
            at = part * depth + layer
            total[part, layer, 0:2, :] += north_ref[2 * at : 2 * at + 2, :]
            total[part, layer, last, :] += south_ref[at : at + 1, :]

    def blocks(source, way_z, way_y):
        at = base + 12 * group_at(way_z, way_y)
        start = source.shape[0] - GROUP
        for slot in range(CAP):
            rows = slice(at + 6 * slot, at + 6 * slot + 6)
            left_ref[rows, :] = source[start + 8 * slot : start + 8 * slot + 6, :]
            right_ref[rows, :] = source[start + 32 + 8 * slot : start + 38 + 8 * slot, :]

    at = base + 12 * group_at(0, 0)
    for slot in range(CAP):
        left_ref[at + 6 * slot : at + 6 * slot + 6, :] = side_ref[slot, 0:6, :]
        right_ref[at + 6 * slot : at + 6 * slot + 6, :] = side_ref[2 + slot, 0:6, :]
    blocks(north_ref, 0, 1)
    blocks(south_ref, 0, -1)
    for kind, _, receiver, slot in force_sides(levels):

        def take(kind=kind, slot=slot):
            for part in range(4):
                for step in range(2 if kind == "up" else 1):
                    layer = step if kind == "up" else depth - 1
                    at = 2 * part + step
                    total[part, layer] += from_levels[slot][8 * at : 8 * at + 8, :]
                    total[part, layer, 0:2, :] += north_levels[slot][2 * at : 2 * at + 2, :]
                    total[part, layer, last, :] += south_levels[slot][at : at + 1, :]
            way = 1 if kind == "up" else -1
            blocks(from_levels[slot], way, 0)
            blocks(north_levels[slot], way, 1)
            blocks(south_levels[slot], way, -1)

        guarded(level_ref[0], receiver, take)
    for layer in range(depth):
        for axis in range(3):
            force_ref[axis, layer] = total[axis, layer]
    lane = lax.broadcasted_iota(jnp.int32, (height, 128), 1)
    for tile in range(base // height):
        value = jnp.zeros((height, 128), jnp.float32)
        for layer in range(8 * tile, min(8 * tile + 8, depth)):
            part = layer - 8 * tile
            value = jnp.where(lane // 16 == part, lane_roll(total[3, layer, :, 0:128], 16 * part), value)
        for target in (right_ref, left_ref):
            target[tile * height : tile * height + height, 0:128] = value


def last_body(levels, level_ref, part_ref, stay_ref, *rest):
    depth, height, width = part_ref.shape[1:]
    slots = len(rim_sizes(levels))
    north_ref, south_ref = rest[:2]
    from_levels, north_levels, south_levels = (rest[2 + slots * at : 2 + slots * at + slots] for at in range(3))
    right_ref, left_ref, force_ref, arrived_ref = rest[2 + 3 * slots :]
    blocks = stay_ref.shape[1]
    base = face_rows(depth, height)
    lane = lax.broadcasted_iota(jnp.int32, (height, 128), 1)
    for layer in range(depth):
        rows = slice(layer // 8 * height, layer // 8 * height + height)
        before, after = right_ref[rows, :128], left_ref[rows, :128]
        for axis in range(3):
            at = 16 * (layer % 8) + 4 * axis
            first = jnp.where(lane < 2, lane_roll(before, -at - 1), 0.0)
            final = jnp.where(lane == 127, lane_roll(after, 127 - at), 0.0)
            force_ref[axis, layer] = part_ref[axis, layer]
            force_ref[axis, layer, :, 0:128] += first
            force_ref[axis, layer, :, width - 128 : width] += final
    arrived_ref[:, 0:blocks, :] = stay_ref[...]

    def put(source, start, stride, way_z, way_y, way_x):
        code = group_at(way_z, way_y) * 3 + way_x + 1
        at = blocks + CAP * (code if code < 13 else code - 1)
        for slot in range(CAP):
            for axis in range(6):
                if source is None:
                    value = jnp.zeros((1, 128), jnp.float32)
                else:
                    value = source[start + stride * slot + axis : start + stride * slot + axis + 1, :]
                arrived_ref[axis, at + slot : at + slot + 1, :] = value

    for way_z in (-1, 0, 1):
        for way_y in (-1, 0, 1):
            for way_x, source in ((1, right_ref), (-1, left_ref)):
                put(source, base + 12 * group_at(way_z, way_y), 6, way_z, way_y, way_x)
    middle = 16

    def put_group(source, way_z, way_y):
        put(source, None if source is None else source.shape[0] - GROUP + middle, 8, way_z, way_y, 0)

    put_group(north_ref, 0, 1)
    put_group(south_ref, 0, -1)
    for kind, _, receiver, slot in force_sides(levels):
        way = 1 if kind == "up" else -1

        def take(way=way, slot=slot):
            put_group(from_levels[slot], way, 0)
            put_group(north_levels[slot], way, 1)
            put_group(south_levels[slot], way, -1)

        def clear(way=way):
            for way_y in (-1, 0, 1):
                put_group(None, way, way_y)

        guarded(level_ref[0], receiver, take)
        if receiver is not None:
            guarded(level_ref[0], 1 - receiver, clear)


def local(pops, coarse_pops, interface, drop_vel, drop_frac, home, counts, dest):
    levels = lax.axis_size("gz")
    depth, height, width = interface.shape
    blocks = home.shape[0]
    kinds = ["up", "down"][: len(rim_sizes(levels))]
    slots = len(kinds)
    size = (depth, height, width)
    rows = height + 8
    table = table_rows(depth, height)
    along, plane, ready = call(
        functools.partial(weigh_body, size),
        [(2 * width + 128, blocks * 128), (blocks // 2, table, 256), (8, 128)],
        [drop_frac, home],
        cost=long_cost(),
        kind=[jnp.bfloat16, jnp.float32, jnp.float32],
    )
    strip, left, right, inner_pops, inner_vel, faces = wide_exchange(pops, coarse_pops, interface, ready)
    sizes = [(count + GROUP, width) for count in message_rows(depth)]
    outs = call(
        functools.partial(main_body, size, levels),
        [(19, height, 128), (4, depth, height, width), (6, blocks, 128), (4, 8, 128), sizes[1], sizes[2]]
        + [sizes[0]] * slots
        + [sizes[3]] * slots
        + [sizes[4]] * slots,
        [counts, dest, strip, left, right, inner_vel, *faces, drop_vel, drop_frac, along, plane],
        [
            pltpu.VMEM((3 * table, width), jnp.float32),
            pltpu.VMEM((3 * table, 128), jnp.float32),
            pltpu.VMEM((3 * table, width), jnp.float32),
            pltpu.VMEM((3 * table, 128), jnp.float32),
            pltpu.VMEM((blocks, 8, 128), jnp.float32),
            pltpu.VMEM((27 * CAP + 1, 8, 128), jnp.float32),
            pltpu.VMEM((table, 128), jnp.float32),
            pltpu.VMEM((2, channels, rows, 128), jnp.float32),
            pltpu.VMEM((2, 19, rows, 128), jnp.float32),
            pltpu.VMEM((2, 19, rows, 128), jnp.float32),
            pltpu.VMEM((3 * table, 2 * width), jnp.bfloat16),
            pltpu.VMEM((3 * table, width + 128), jnp.bfloat16),
            pltpu.VMEM((3 * table, blocks * 128), jnp.bfloat16),
            pltpu.VMEM((3 * table, blocks * 128), jnp.bfloat16),
        ],
        late=(0, 1, *range(5, 10 + slots)),
    )
    edge, own, stay, side, north, south = outs[:6]
    to_levels, north_levels, south_levels = (outs[6 + slots * at : 6 + slots * at + slots] for at in range(3))
    received = [shifted(north, "gy", 1), shifted(south, "gy", -1)]
    received += [to_level(value, kind, levels) for value, kind in zip(to_levels, kinds)]
    received += [to_level(value, kind, levels, "gy", 1) for value, kind in zip(north_levels, kinds)]
    received += [to_level(value, kind, levels, "gy", -1) for value, kind in zip(south_levels, kinds)]
    (state,) = call(patch_body, [pops.shape], [inner_pops, edge], cost=long_cost())
    side_rows = (padded(face_rows(depth, height) + 9 * 6 * CAP), width)
    part, right, left = call(
        functools.partial(gather_body, levels),
        [(3, depth, height, width), side_rows, side_rows],
        [own, side] + received,
        [pltpu.VMEM((4, depth, height, width), jnp.float32)],
    )
    force, arrived = call(
        functools.partial(last_body, levels),
        [(3, depth, height, width), (6, blocks + 26 * CAP, 128)],
        [part, stay] + received + [shifted(right, "gx", 1), shifted(left, "gx", -1)],
    )
    return state, force, arrived


def solution(mesh):
    return jax.shard_map(
        local,
        mesh=mesh,
        in_specs=(
            P(None, "gz", "gy", "gx"),
            P(None, "gz", "gy", "gx"),
            P("gz", "gy", "gx"),
            P(None, ("gx", "gy", "gz"), None),
            P(None, ("gx", "gy", "gz"), None),
            P(("gx", "gy", "gz"), None),
            P(("gx", "gy", "gz")),
            P(("gx", "gy", "gz")),
        ),
        out_specs=(
            P(None, "gz", "gy", "gx"),
            P(None, "gz", "gy", "gx"),
            P(None, ("gx", "gy", "gz"), None),
        ),
        check_vma=False,
    )
```

```python
import functools
import math

import jax
import jax.numpy as jnp
import numpy as np
from jax import lax
from jax.experimental import pallas as pl
from jax.experimental.pallas import tpu as pltpu
from jax.sharding import PartitionSpec as P

CAP = 2


lattice = np.array(
    [
        [0, 0, 0],
        [1, 0, 0],
        [-1, 0, 0],
        [0, 1, 0],
        [0, -1, 0],
        [0, 0, 1],
        [0, 0, -1],
        [1, 1, 0],
        [-1, -1, 0],
        [1, -1, 0],
        [-1, 1, 0],
        [1, 0, 1],
        [-1, 0, -1],
        [1, 0, -1],
        [-1, 0, 1],
        [0, 1, 1],
        [0, -1, -1],
        [0, 1, -1],
        [0, -1, 1],
    ]
)
weights_table = np.array([1.0 / 3.0] + [1.0 / 18.0] * 6 + [1.0 / 36.0] * 12)
opposite = [0, 2, 1, 4, 3, 6, 5, 8, 7, 10, 9, 12, 11, 14, 13, 16, 15, 18, 17]
inverse_tau = 0.8
relax = 0.5
couple = 8.0


class Level:
    def __getitem__(self, _):
        return lax.axis_index("gz").astype(jnp.int32)


class Moving:
    def __init__(self, buffer, copy):
        self.buffer = buffer
        self.copy = copy

    def take(self):
        self.copy.wait()
        return self.buffer


def call(body, outs, arrays, scratch=(), cost=None, heads=(), late=(), kind=jnp.float32):
    heads = dict(heads)
    landing = []
    for at, value in enumerate(arrays):
        space = pltpu.SMEM if value.ndim == 1 else pltpu.VMEM
        landing.append(space((heads.get(at, value.shape[0]),) + value.shape[1:], value.dtype))

    def whole(*refs):
        given = refs[: len(arrays)]
        made = list(refs[len(arrays) : len(arrays) + len(outs)])
        rest = refs[len(arrays) + len(outs) :]
        landed, done, rest = list(rest[: len(arrays)]), rest[len(arrays)], rest[len(arrays) + 1 :]
        copies = []
        for at, (source, target) in enumerate(zip(given, landed)):
            if at in heads:
                source = source.at[pl.ds(0, heads[at])]
            copies.append(pltpu.make_async_copy(source, target, done.at[at]))
        for copy in copies:
            copy.start()
        for at, copy in enumerate(copies):
            if at in late:
                landed[at] = Moving(landed[at], copy)
            else:
                copy.wait()
        body(Level(), *landed, *made, *rest)

    vmem = pl.BlockSpec(memory_space=pltpu.VMEM)
    hbm = pl.BlockSpec(memory_space=pltpu.HBM)
    return pl.pallas_call(
        whole,
        out_shape=[
            jax.ShapeDtypeStruct(shape, kind[at] if isinstance(kind, list) else kind)
            for at, shape in enumerate(outs)
        ],
        in_specs=[hbm] * len(arrays),
        out_specs=[vmem] * len(outs),
        scratch_shapes=landing
        + [pltpu.SemaphoreType.DMA((len(arrays),))]
        + list(scratch),
        cost_estimate=cost,
        compiler_params=pltpu.CompilerParams(vmem_limit_bytes=64 * 1024 * 1024),
    )(*arrays)


ways = [tuple(int(part) for part in lattice[index][::-1]) for index in range(19)] + [(0, 0, 0)]
channels = len(ways)
LOW = 3
HIGH = 4


def low_reach(way):
    return 2 + way


def high_reach(way):
    return 3 - way


def rim(kind):
    side = 1 if kind == "low" else -1
    return [
        (step, channel)
        for step in (1, 2)
        for channel in range(channels)
        if step <= 1 + side * ways[channel][0]
    ]


def rim_sides(levels):
    if levels == 2:
        return [("low", 1, 0, 0), ("high", 0, 1, 0)]
    return [("low", None, None, 0), ("high", None, None, 1)]


def rim_sizes(levels):
    sizes = [FOUR + len(rim(kind)) for kind, _, _, _ in rim_sides(levels)]
    return [max(sizes)] if levels == 2 else sizes


def guarded(level, guard, action):
    if guard is None:
        action()
    else:
        pl.when(level == guard)(action)


def padded(count):
    return -(-count // 8) * 8


def reaches(channel, bounces):
    way_z, way, _ = ways[channel]
    above, below = high_reach(way), low_reach(way)
    if bounces and way_z != 0:
        above, below = max(above, HIGH - 1), max(below, LOW - 1)
    return above, below


def row_places(cells, start=(0, 0)):
    places, (high_at, low_at) = [], start
    for above, below in cells:
        places.append((high_at, low_at, above, below))
        high_at, low_at = high_at + above, low_at + below
    return places, (padded(high_at), padded(low_at))


def strip_rows():
    return row_places([reaches(channel, True) for channel in range(channels)])


def own_rows(depth):
    cells = [(layer, channel) for layer in range(depth) for channel in range(channels)]
    places, sizes = row_places(
        [reaches(channel, layer in (0, depth - 1)) for layer, channel in cells], strip_rows()[1]
    )
    return [(layer, channel, place) for (layer, channel), place in zip(cells, places)], sizes


FOUR = -(-channels // 4)


def rim_strip_rows():
    return row_places([(HIGH, LOW)] * FOUR)


def rim_rows(kind):
    places, sizes = row_places([reaches(channel, False) for _, channel in rim(kind)], rim_strip_rows()[1])
    return [(step, channel, place) for (step, channel), place in zip(rim(kind), places)], sizes


def rim_row_sizes(levels):
    sizes = [rim_rows(kind)[1] for kind, _, _, _ in rim_sides(levels)]
    return [tuple(max(part) for part in zip(*sizes))] if levels == 2 else sizes


def face_table(high):
    wants = []
    for channel in range(channels):
        way_z, _, way = ways[channel]
        count = high_reach(way) if high else low_reach(way)
        if way_z != 0:
            count = max(count, (HIGH if high else LOW) - 1)
        wants.append((-count, channel))
    free, table = [], []
    for count, channel in sorted(wants):
        tile = next((at for at, room in enumerate(free) if room >= -count), len(free))
        if tile == len(free):
            free.append(8)
        table.append((channel, tile, 8 - free[tile], -count))
        free[tile] += count
    return table, len(free)


def moments(cells):
    density = cells[0] * float(weights_table[0])
    moment = [None, None, None]
    face, edge = float(weights_table[1]), float(weights_table[7])
    edge_sum = cells[7]
    for index in range(8, 19):
        edge_sum = edge_sum + cells[index]
    face_sum = cells[1]
    for index in range(2, 7):
        face_sum = face_sum + cells[index]
    density = density + face * face_sum + edge * edge_sum
    for axis in range(3):
        total = {}
        for group, indices in ((face, range(1, 7)), (edge, range(7, 19))):
            plus, minus = None, None
            for index in indices:
                way = int(lattice[index][axis])
                if way == 1:
                    plus = cells[index] if plus is None else plus + cells[index]
                if way == -1:
                    minus = cells[index] if minus is None else minus + cells[index]
            total[group] = plus - minus
        moment[axis] = face * total[face] + edge * total[edge]
    return density, moment


def relaxed(cells):
    density, moment = moments(cells)
    inverse = 1.0 / density
    flow = [part * inverse for part in moment]
    square = flow[0] * flow[0] + flow[1] * flow[1] + flow[2] * flow[2]
    scale = density * inverse_tau
    base = scale * (1.0 - 1.5 * square)
    keep = 1.0 - inverse_tau
    posts = [None] * 19
    posts[0] = keep * cells[0] + base
    for index in range(1, 19, 2):
        along = None
        for axis in range(3):
            way = int(lattice[index][axis])
            if way != 0:
                part = flow[axis] if way == 1 else -flow[axis]
                along = part if along is None else along + part
        odd = 3.0 * scale * along
        even = base + (4.5 * scale) * (along * along)
        posts[index] = keep * cells[index] + (even + odd)
        posts[index + 1] = keep * cells[index + 1] + (even - odd)
    return posts


def lane_roll(value, shift):
    shift = shift % value.shape[-1]
    return value if shift == 0 else pltpu.roll(value, shift, value.ndim - 1)


def first_body(
    levels, level_ref, pops_ref, coarse_ref, interface_ref, posts_ref, strip_ref, down_ref, up_ref, *outs
):
    depth, height, width = interface_ref.shape
    slots = len(rim_sizes(levels))
    rims, down_rims, up_rims = (outs[slots * at : slots * at + slots] for at in range(3))
    lane = lax.broadcasted_iota(jnp.int32, (height, 128), 1)

    def put_rows(down, up, place, cells):
        down_at, up_at, down_rows, up_rows = place
        cols = slice(0, cells.shape[1])
        down[down_at : down_at + down_rows, cols] = cells[:down_rows, :]
        up[up_at : up_at + up_rows, cols] = cells[height - up_rows :, :]

    own = own_rows(depth)[0]
    for layer in range(depth):
        mask = interface_ref[layer]
        inside = mask == 1
        posts = relaxed([pops_ref[index, layer] for index in range(19)])
        posts = [
            jnp.where(inside, coarse_ref[index, layer].astype(jnp.float32), posts[index])
            for index in range(19)
        ] + [mask.astype(jnp.float32)]
        for channel in range(channels):
            posts_ref[channel, layer] = posts[channel]
            put_rows(down_ref, up_ref, own[layer * channels + channel][2], posts[channel])
    for channel in range(channels):
        value = jnp.zeros((height, 128), jnp.float32)
        for layer in range(depth):
            cells = posts_ref[channel, layer]
            if width > 128:
                cells = jnp.where(lane < 64, cells[:, :128], cells[:, width - 128 :])
            value = jnp.where(lane // 8 == LOW + layer, lane_roll(cells, 8 * (LOW + layer) + 4), value)
        strip_ref[channel] = value
        put_rows(down_ref, up_ref, strip_rows()[0][channel], value)
    for kind, _, sender, slot in rim_sides(levels):

        def pack(kind=kind, slot=slot):
            for tile in range(FOUR):
                value = jnp.zeros((height, 128), jnp.float32)
                for part in range(min(4, channels - 4 * tile)):
                    first = LOW + depth - 4 if kind == "low" else LOW
                    turned = lane_roll(strip_ref[4 * tile + part], 32 * part - 8 * first)
                    value = jnp.where(lane // 32 == part, turned, value)
                rims[slot][tile, :, 0:128] = value
                put_rows(down_rims[slot], up_rims[slot], rim_strip_rows()[0][tile], value)
            for at, (step, channel, place) in enumerate(rim_rows(kind)[0]):
                cells = posts_ref[channel, depth - step if kind == "low" else step - 1]
                rims[slot][FOUR + at] = cells
                put_rows(down_rims[slot], up_rims[slot], place, cells)

        guarded(level_ref[0], sender, pack)


def unpack(levels, level, posts_ref, above_ref, below_ref, rims, above_rims, below_rims, ext):
    depth, height = posts_ref.shape[1:3]
    rows = height + 8

    def put(channel, at, cells, place, above, below):
        above_at, below_at, above_rows, below_rows = place
        ext[channel, at, :height, :] = cells
        ext[channel, at, height : height + above_rows, :] = above[above_at : above_at + above_rows, :]
        ext[channel, at, rows - below_rows : rows, :] = below[below_at : below_at + below_rows, :]

    for layer, channel, place in own_rows(depth)[0]:
        put(channel, LOW + layer, posts_ref[channel, layer], place, above_ref, below_ref)
    for kind, receiver, _, slot in rim_sides(levels):

        def take(kind=kind, slot=slot):
            for at, (step, channel, place) in enumerate(rim_rows(kind)[0]):
                layer = LOW - step if kind == "low" else LOW + depth + step - 1
                put(channel, layer, rims[slot][FOUR + at], place, above_rims[slot], below_rims[slot])

        guarded(level, receiver, take)


def split_given(levels, rest):
    slots = len(rim_sizes(levels))
    parts = [rest[3 + slots * at : 3 + slots * at + slots] for at in range(3)]
    return rest[:3], parts, rest[3 + 3 * slots :]


def strip_body(levels, depth, level_ref, *rest):
    (own_ref, above_ref, below_ref), parts, rest = split_given(levels, rest)
    _, strip_ref, right_ref, left_ref, tiles = rest
    rows = strip_ref.shape[1]
    height = rows - 8
    lane = lax.broadcasted_iota(jnp.int32, (rows, 128), 1)
    layer_at = lane // 8

    def put(target, index, place, above, below):
        above_at, below_at, above_rows, below_rows = place
        target[index, height : height + above_rows, :] = above[above_at : above_at + above_rows, 0:128]
        target[index, rows - below_rows :, :] = below[below_at : below_at + below_rows, 0:128]

    for channel in range(channels):
        strip_ref[channel, 0:height, :] = own_ref[channel]
        put(strip_ref, channel, strip_rows()[0][channel], above_ref, below_ref)
    for kind, receiver, _, slot in rim_sides(levels):

        def take(kind=kind, slot=slot):
            rims, above_rims, below_rims = (part[slot] for part in parts)
            first = -1 if kind == "low" else LOW + depth
            here = layer_at < LOW if kind == "low" else layer_at >= LOW + depth
            for tile in range(FOUR):
                tiles[tile, 0:height, :] = rims[tile, :, 0:128]
                put(tiles, tile, rim_strip_rows()[0][tile], above_rims, below_rims)
                value = tiles[tile]
                for part in range(min(4, channels - 4 * tile)):
                    turned = lane_roll(value, 8 * first - 32 * part)
                    strip_ref[4 * tile + part] = jnp.where(here, turned, strip_ref[4 * tile + part])

        guarded(level_ref[0], receiver, take)
    spot = lane % 8
    for target, high in ((right_ref, False), (left_ref, True)):
        table, count = face_table(high)
        for tile in range(count):
            value = jnp.zeros((rows, 128), jnp.float32)
            for channel, at, first, cols in table:
                if at == tile:
                    turned = lane_roll(strip_ref[channel], first - (4 if high else 4 - cols))
                    value = jnp.where((spot >= first) & (spot < first + cols), turned, value)
            target[tile] = value


def substeps(levels, level, size, ext, pulled, second):
    depth, height, width = size
    rows = height + 8

    def pull(source, layer, at, target):
        for index in range(19):
            way_z, way_y, way_x = ways[index]
            value = source[index, at - way_z]
            if way_x != 0:
                value = pltpu.roll(value, way_x % width, 1)
            if way_y != 0:
                value = pltpu.roll(value, way_y % rows, 0)
            if way_z == 1 and layer == 0:
                value = jnp.where(level == 0, source[opposite[index], at], value)
            if way_z == -1 and layer == depth - 1:
                value = jnp.where(level == levels - 1, source[opposite[index], at], value)
            target[index] = value

    tiles = [
        (slice(row, row + 8), slice(col, col + 128))
        for row in range(0, rows, 8)
        for col in range(0, width, 128)
    ]

    def first_steps(layers):
        for layer in layers:
            at = LOW + layer
            cells = pulled.at[at % pulled.shape[0]]
            pull(ext, layer, at, cells)
            for tile in tiles:
                posts = relaxed([cells[(index, *tile)] for index in range(19)])
                inside = ext[(19, at, *tile)] > 0.5
                for index in range(19):
                    second[(index, at - 1, *tile)] = jnp.where(
                        inside, ext[(index, at, *tile)], posts[index]
                    )

    def second_steps(layers, put):
        for layer in layers:
            at = LOW - 1 + layer
            cells = pulled.at[at % pulled.shape[0]]
            pull(second, layer, at, cells)
            for tile in tiles:
                density, moment = moments([cells[(index, *tile)] for index in range(19)])
                inverse = 1.0 / density
                for axis in range(3):
                    put(axis, layer, tile, moment[axis] * inverse)
            yield layer, cells

    return first_steps, second_steps


def inner_body(levels, level_ref, *rest):
    (posts_ref, above_ref, below_ref), parts, rest = split_given(levels, rest)
    pops_ref, vel_ref, ext, pulled, second = rest
    level = level_ref[0]
    unpack(levels, level, posts_ref, above_ref, below_ref, *parts, ext)
    depth, height, _ = size = posts_ref.shape[1:]
    first_steps, second_steps = substeps(levels, level, size, ext, pulled, second)

    def put(axis, layer, tile, value):
        vel_ref[(axis, layer, *tile)] = value

    pl.when(level != 0)(lambda: first_steps([-1]))
    pl.when(level != levels - 1)(lambda: first_steps([depth]))
    first_steps(range(depth))
    for layer, cells in second_steps(range(depth), put):
        for index in range(19):
            pops_ref[index, layer] = cells[index, :height, :]


def face_body(levels, level_ref, *rest):
    (posts_ref, above_ref, below_ref), parts, rest = split_given(levels, rest)
    slots = len(rim_sizes(levels))
    faces, (ext, pulled, second) = rest[:slots], rest[slots:]
    level = level_ref[0]
    unpack(levels, level, posts_ref, above_ref, below_ref, *parts, ext)
    depth, height, _ = size = posts_ref.shape[1:]
    first_steps, second_steps = substeps(levels, level, size, ext, pulled, second)
    for kind, sender, _, slot in force_sides(levels):
        wanted = [depth - 1] if kind == "up" else [0, 1]

        def work(wanted=wanted, slot=slot):
            def put(axis, layer, tile, value):
                at = (2 * axis + layer - wanted[0]) * (height + 3)
                row, cols = tile[0].start, tile[1]
                if row < height:
                    faces[slot][at + 1 + row : at + 9 + row, cols] = value
                else:
                    faces[slot][at + 1 + height : at + 3 + height, cols] = value[:2, :]
                    faces[slot][at : at + 1, cols] = value[7:, :]

            first_steps(range(wanted[0] - 1, wanted[-1] + 2))
            for _ in second_steps(wanted, put):
                pass

        guarded(level, sender, work)


def edge_body(
    size, levels, level_ref, strip_ref, left_ref, right_ref, inner_vel, faces,
    edge_ref, vel_ref, beyond_ref, sides, pulled, second,
):
    depth, height, width = size
    rows = height + 8
    level = level_ref[0]
    lane = lax.broadcasted_iota(jnp.int32, (rows, 128), 1)
    before = lane % 8 < 4
    bottom = (lane // 8 == LOW) & (level == 0)
    top = (lane // 8 == LOW + depth - 1) & (level == levels - 1)
    for channel, tile, first, cols in face_table(False)[0]:
        turned = lane_roll(left_ref[tile], 4 - cols - first)
        sides[0, channel] = jnp.where(before, turned, strip_ref[channel])
    for channel, tile, first, _ in face_table(True)[0]:
        turned = lane_roll(right_ref[tile], 4 - first)
        sides[1, channel] = jnp.where(before, strip_ref[channel], turned)

    def pull(source, side, target):
        for index in range(19):
            way_z, way_y, way_x = ways[index]
            value = lane_roll(source[side, index], 8 * way_z + way_x)
            if way_y != 0:
                value = pltpu.roll(value, way_y % rows, 0)
            if way_z != 0:
                value = jnp.where(bottom if way_z == 1 else top, source[side, opposite[index]], value)
            target[side, index] = value

    speeds = [[], []]
    for side in range(2):
        pull(sides, side, pulled)
        for row in range(0, rows, 8):
            cut = slice(row, row + 8)
            posts = relaxed([pulled[side, index, cut] for index in range(19)])
            inside = sides[side, 19, cut] > 0.5
            for index in range(19):
                second[side, index, cut] = jnp.where(inside, sides[side, index, cut], posts[index])
        pull(second, side, pulled)
        density, moment = moments([pulled[side, index] for index in range(19)])
        inverse = 1.0 / density
        speeds[side] = [part * inverse for part in moment]

    row = lax.broadcasted_iota(jnp.int32, (rows, 128), 0)
    valid = (row < height + 2) | (row == rows - 1)
    outside = (lane < 2) | (lane == 127)
    vel_in = inner_vel.take()
    faces = [face.take() for face in faces]

    def inner(axis, layer, cols):
        if 0 < layer <= depth:
            return vel_in[axis, layer - 1, :, cols]
        at = 2 * axis * (height + 3) if layer == 0 else (2 * axis + layer - depth - 1) * (height + 3)
        face = faces[0 if layer == 0 else -1]
        return jnp.concatenate(
            [
                face[at + 1 : at + height + 1, cols],
                face[at + height + 1 : at + height + 3, cols],
                jnp.zeros((5, 128), jnp.float32),
                face[at : at + 1, cols],
            ],
            axis=0,
        )

    table = table_rows(depth, height)
    vel_ref[...] = jnp.zeros_like(vel_ref)
    beyond_ref[...] = jnp.zeros_like(beyond_ref)

    def put(target, axis, layer, cols, cells):
        at = axis * table + layer * (height + 3)
        target[at : at + 1, cols] = cells[rows - 1 :, :]
        target[at + 1 : at + height + 3, cols] = cells[: height + 2, :]

    for axis in range(3):
        main = jnp.where(before, speeds[1][axis], speeds[0][axis])
        rest = jnp.where(before, speeds[0][axis], speeds[1][axis])
        for layer in range(depth + 3):
            keep = valid
            if layer == 0:
                keep = valid & (level != 0)
            if layer > depth:
                keep = valid & (level != levels - 1)
            shift = -(8 * (layer - 1 + LOW) + 4)
            turned = lane_roll(main, shift)
            for col in range(0, width, 128):
                cells = inner(axis, layer, slice(col, col + 128))
                if col == 0 or col == width - 128:
                    mask = (lane < 2) & (col == 0) | (lane >= 126) & (col == width - 128)
                    cells = jnp.where(mask, turned, cells)
                put(vel_ref, axis, layer, slice(col, col + 128), jnp.where(keep, cells, 0.0))
            put(beyond_ref, axis, layer, slice(0, 128), jnp.where(keep & outside, lane_roll(rest, shift), 0.0))
    for index in range(19):
        edge_ref[index] = jnp.where(before, pulled[1, index], pulled[0, index])[:height]


def patch_body(_, pops_in, edge_ref, pops_ref):
    depth, height, width = pops_ref.shape[1:]
    lane = lax.broadcasted_iota(jnp.int32, (height, 128), 1)
    for index in range(19):
        value = edge_ref[index]
        for layer in range(depth):
            turned = lane_roll(value, -(8 * (layer + LOW) + 4))
            for col in range(0, width, 128):
                cells = pops_in[index, layer, :, col : col + 128]
                if col == 0 or col == width - 128:
                    mask = (lane < 2) & (col == 0) | (lane >= 126) & (col == width - 128)
                    cells = jnp.where(mask, turned, cells)
                pops_ref[index, layer, :, col : col + 128] = cells


def long_cost():
    return pl.CostEstimate(flops=10**8, bytes_accessed=1 << 22, transcendentals=0)


def shifted(value, axis, step):
    count = lax.axis_size(axis)
    return lax.ppermute(value, axis, [(i, (i + step) % count) for i in range(count)])


def to_level(value, kind, levels, side=None, step=0):
    pairs = []
    for at in range(levels):
        other = 1 - at if levels == 2 else at + 1 if kind in ("low", "up") else at - 1
        if 0 <= other < levels:
            pairs.append((at, other))
    if side is None:
        return lax.ppermute(value, "gz", pairs)
    count = lax.axis_size(side)
    return lax.ppermute(
        value,
        (side, "gz"),
        [
            (brick * levels + at, (brick + step) % count * levels + other)
            for brick in range(count)
            for at, other in pairs
        ],
    )


def wide_exchange(pops, coarse_pops, interface, ready):
    levels = lax.axis_size("gz")
    depth, height, width = interface.shape
    sizes = rim_sizes(levels)
    slots = len(sizes)
    kinds = ["low", "high"][:slots]
    down_sizes, up_sizes = zip(*rim_row_sizes(levels))
    outs = call(
        functools.partial(first_body, levels),
        [(channels, depth, height, width), (channels, height, 128)]
        + [(size, width) for size in own_rows(depth)[1]]
        + [(size, height, width) for size in sizes]
        + [(size, width) for size in down_sizes + up_sizes],
        [pops, coarse_pops, interface],
    )
    posts, own, down, up = outs[:4]
    rims, down_rims, up_rims = (outs[4 + slots * at : 4 + slots * at + slots] for at in range(3))
    given = [shifted(down, "gy", -1), shifted(up, "gy", 1)]
    given += [to_level(value, kind, levels) for value, kind in zip(rims, kinds)]
    given += [to_level(value, kind, levels, "gy", -1) for value, kind in zip(down_rims, kinds)]
    given += [to_level(value, kind, levels, "gy", 1) for value, kind in zip(up_rims, kinds)]
    deep, rows = depth + LOW + HIGH, height + 8
    ext = pltpu.VMEM((channels, deep, rows, width), jnp.float32)
    strip, right, left = call(
        functools.partial(strip_body, levels, depth),
        [(channels, rows, 128)] + [(face_table(high)[1], rows, 128) for high in (False, True)],
        [own] + given + [ready],
        [pltpu.VMEM((FOUR, rows, 128), jnp.float32)],
        heads=[(1, strip_rows()[1][0]), (2, strip_rows()[1][1])]
        + [(3 + at, FOUR) for at in range(slots)]
        + [(3 + slots + at, rim_strip_rows()[1][0]) for at in range(slots)]
        + [(3 + 2 * slots + at, rim_strip_rows()[1][1]) for at in range(slots)],
    )
    left, right = shifted(right, "gx", 1), shifted(left, "gx", -1)
    scratch = [
        ext,
        pltpu.VMEM((4, 19, rows, width), jnp.float32),
        pltpu.VMEM((19, deep - 2, rows, width), jnp.float32),
    ]
    faces = call(
        functools.partial(face_body, levels), [(padded(6 * (height + 3)), width)] * slots, [posts] + given, scratch
    )
    faces = [to_level(value, kind, levels) for value, kind in zip(faces, ["up", "down"])]
    inner_pops, inner_vel = call(
        functools.partial(inner_body, levels),
        [pops.shape, (3, depth, rows, width)],
        [posts] + given,
        scratch,
        long_cost(),
    )
    return strip, left, right, inner_pops, inner_vel, faces


def phis(frac):
    angle = frac * (0.5 * math.pi)
    sine = 0.25 * jnp.sin(angle)
    cosine = 0.25 * jnp.cos(angle)
    return (0.25 - sine, 0.25 + cosine, 0.25 + sine, 0.25 - cosine)


def split(value):
    high = value.astype(jnp.bfloat16)
    return high, (value - high.astype(jnp.float32)).astype(jnp.bfloat16)


def pick(step, parts):
    value = jnp.where(step == 0, parts[0], 0.0)
    for index in range(1, 4):
        value = jnp.where(step == index, parts[index], value)
    return value


def dots(left, right, dims):
    return lax.dot_general(left, right, (dims, ((), ())), preferred_element_type=jnp.float32)


def table_rows(depth, height):
    return -(-(depth + 3) * (height + 3) // 16) * 16


def weigh_body(size, _, frac_ref, home_ref, along, plane_ref, ready_ref):
    depth, height, width = size
    blocks = home_ref.shape[0]
    layers, rows = depth + 3, height + 3
    table = table_rows(depth, height)
    ready_ref[...] = jnp.zeros_like(ready_ref)
    along[2 * width :, :] = jnp.zeros((128, along.shape[1]), jnp.bfloat16)
    plane_ref[:, layers * rows :, :] = jnp.zeros(
        (plane_ref.shape[0], table - layers * rows, 256), jnp.float32
    )
    span_x = lax.broadcasted_iota(jnp.int32, (width, 128), 0) + 1
    span_end = lax.broadcasted_iota(jnp.int32, (16, 128), 0)
    span_y = lax.broadcasted_iota(jnp.int32, (padded(rows), 128), 0)
    span_z = lax.broadcasted_iota(jnp.int32, (padded(layers), 128), 0)
    for block in range(blocks):
        side = slice(block * 128, block * 128 + 128)
        cell = home_ref[block : block + 1, :]
        cell_x = cell % width
        cell_y = cell // width % height
        cell_z = cell // (width * height)
        part_x = phis(frac_ref[0, block : block + 1, :])
        part_y = phis(frac_ref[1, block : block + 1, :])
        part_z = phis(frac_ref[2, block : block + 1, :])
        high, low = split(pick(span_x - cell_x, part_x))
        along[0:width, side] = low
        along[width : 2 * width, side] = high
        high, low = split(pick(span_end + (width + 1) - cell_x, part_x))
        along[2 * width : 2 * width + 16, side] = high
        along[2 * width + 32 : 2 * width + 48, side] = high
        along[2 * width + 64 : 2 * width + 80, side] = low
        high, low = split(jnp.where((span_end == 15) & (cell_x == 0), part_x[0], 0.0))
        along[2 * width + 112 : 2 * width + 128, side] = high
        along[2 * width + 16 : 2 * width + 32, side] = high
        along[2 * width + 48 : 2 * width + 64, side] = low
        weight_y = pick(span_y - cell_y, part_y)[:rows]
        weight_z = pick(span_z - cell_z, part_z)
        half = block % 2 * 128
        for layer in range(layers):
            plane_ref[block // 2, layer * rows : layer * rows + rows, half : half + 128] = (
                weight_y * weight_z[layer : layer + 1, :]
            )


def droplet_body(
    size, counts_ref, dest_ref, vel_ref, beyond_ref, speed_ref, frac_ref, along_in, plane_in,
    spread_ref, outer_ref, stay_ref, state_ref, twice, mixed, push_high, push_low, meanwhile,
):
    depth, height, width = size
    blocks = state_ref.shape[0]
    table = table_rows(depth, height)
    high, low = split(vel_ref[...])
    twice[:, :width] = high
    twice[:, width:] = high
    mixed[:, :width] = low
    high, low = (part.astype(jnp.float32) for part in split(beyond_ref[...]))
    mixed[:, width:] = (high + lane_roll(low, 32) + lane_roll(high, 64)).astype(jnp.bfloat16)
    slots = lax.broadcasted_iota(jnp.int32, (1, 128), 1)
    along, plane_ref = along_in.take(), plane_in.take()

    def sample(number):
        pair = slice(number * 256, number * 256 + 256)
        return dots(twice[...], along[0 : 2 * width, pair], ((1,), (0,))) + dots(
            mixed[...], along[width:, pair], ((1,), (0,))
        )

    def move(number, sums):
        plane = plane_ref[number]
        for axis in range(3):
            where = slice(axis * table, axis * table + table)
            sampled = jnp.sum(sums[where] * plane, axis=0, keepdims=True)
            for half in range(2):
                block = 2 * number + half
                live = slots < counts_ref[block]
                sample = sampled[:, half * 128 : half * 128 + 128]
                speed = speed_ref[axis, block : block + 1, :]
                frac = frac_ref[axis, block : block + 1, :]
                moved = speed + relax * (sample - speed)
                push = jnp.where(live, couple * (moved - sample), 0.0)
                stays = live & (dest_ref[block] == 13)
                for at, value in ((axis, moved), (3 + axis, frac + moved)):
                    state_ref[block, at : at + 1, :] = jnp.where(live, value, 0.0)
                    stay_ref[at, block : block + 1, :] = jnp.where(stays, value, 0.0)
                high, low = split(plane[:, half * 128 : half * 128 + 128] * push)
                push_high[where, block * 128 : block * 128 + 128] = high
                push_low[where, block * 128 : block * 128 + 128] = low

    pairs = blocks // 2
    for number in range(pairs):
        move(number, sample(number))
    outer = dots(push_high[...], along[2 * width :, :], ((1,), (1,)))
    rest = dots(push_low[...], along[width:, :], ((1,), (1,)))
    outer_ref[...] = outer + lane_roll(outer, -64) + rest[:, width:]
    spread_ref[...] = rest[:, :width]
    for action in meanwhile:
        action()
    main = dots(push_high[...], along[0 : 2 * width, :], ((1,), (1,)))
    spread_ref[...] += main[:, :width] + main[:, width:]


def force_sides(levels):
    if levels == 2:
        return [("up", 0, 1, 0), ("down", 1, 0, 0)]
    return [("up", None, None, 0), ("down", None, None, 1)]


GROUP = 6 * 8


def group_at(way_z, way_y):
    return (way_z + 1) * 3 + way_y + 1


def face_rows(depth, height):
    return -(-depth // 8) * height


def message_rows(depth):
    return [8 * 8, 2 * 4 * depth, 4 * depth, 2 * 8, 8]


def pack_blocks(
    levels, level_ref, dest_ref, state_ref, side_ref,
    to_levels, north_ref, south_ref, north_levels, south_levels, outbox,
):
    level = level_ref[0]
    blocks = state_ref.shape[0]
    codes = [dest_ref[block] for block in range(blocks)]
    outbox[...] = jnp.zeros_like(outbox)
    for block in range(blocks):
        rank = jnp.int32(0)
        for earlier in range(block):
            rank = rank + (codes[earlier] == codes[block]).astype(jnp.int32)
        slot = jnp.where(codes[block] == 13, 27 * CAP, codes[block] * CAP + jnp.minimum(rank, CAP - 1))
        outbox[slot] = state_ref[block]

    def put(target, way_z, way_y):
        base = target.shape[0] - GROUP
        for slot in range(6):
            target[base + 8 * slot : base + 8 * slot + 8, :] = outbox[6 * group_at(way_z, way_y) + slot]

    put(north_ref, 0, 1)
    put(south_ref, 0, -1)
    for slot in range(CAP):
        side_ref[slot] = outbox[6 * group_at(0, 0) + slot]
        side_ref[CAP + slot] = outbox[6 * group_at(0, 0) + 4 + slot]
    ways_z = [(1 - 2 * level, 0)] if levels == 2 else [(1, 0), (-1, 1)]
    for way_z, slot in ways_z:
        put(to_levels[slot], way_z, 0)
        put(north_levels[slot], way_z, 1)
        put(south_levels[slot], way_z, -1)


def pack_force(
    levels, level_ref, spread_ref, outer_ref, own_ref,
    to_levels, north_ref, south_ref, north_levels, south_levels, strip,
):
    depth, height, width = own_ref.shape[1:]
    rows, table = height + 3, table_rows(depth, height)
    lane = lax.broadcasted_iota(jnp.int32, (table, 128), 1)
    value = jnp.zeros((table, 128), jnp.float32)
    for axis in range(3):
        here = (lane >= 4 * axis) & (lane < 4 * axis + 3)
        cells = outer_ref[axis * table : axis * table + table, :]
        value = jnp.where(here, lane_roll(cells, 4 * axis + 1), value)
    strip[...] = value

    def force(part, layer, cut):
        at = layer * rows
        if part < 3:
            return spread_ref[part * table + at + cut.start : part * table + at + cut.stop, :]
        return strip[at + cut.start : at + cut.stop, :]

    main, north, south = slice(1, height + 1), slice(height + 1, height + 3), slice(0, 1)
    for part in range(4):
        for layer in range(depth):
            own_ref[part, layer] = force(part, layer + 1, main)
            at = part * depth + layer
            north_ref[2 * at : 2 * at + 2, :] = force(part, layer + 1, north)
            south_ref[at : at + 1, :] = force(part, layer + 1, south)
    for kind, sender, _, slot in force_sides(levels):

        def pack(kind=kind, slot=slot):
            for part in range(4):
                for step in range(2 if kind == "up" else 1):
                    layer = depth + 1 + step if kind == "up" else 0
                    at = 2 * part + step
                    to_levels[slot][8 * at : 8 * at + 8, :] = force(part, layer, main)
                    north_levels[slot][2 * at : 2 * at + 2, :] = force(part, layer, north)
                    south_levels[slot][at : at + 1, :] = force(part, layer, south)

        guarded(level_ref[0], sender, pack)


def main_body(
    size, levels, level_ref, counts, dest, strip_ref, left_ref, right_ref, inner_vel, *rest,
):
    slots = len(rim_sizes(levels))
    faces, (speed, frac, along, plane), rest = rest[:slots], rest[slots : slots + 4], rest[slots + 4 :]
    edge_ref, own_ref, stay_ref, side_ref, north_ref, south_ref = rest[:6]
    rest = rest[6:]
    to_levels, north_levels, south_levels = (rest[slots * at : slots * at + slots] for at in range(3))
    rest = rest[3 * slots :]
    vel_ref, beyond_ref, spread_ref, outer_ref, state_ref, outbox, strip = rest[:7]
    counts_ref, dest_ref = counts.take(), dest.take()
    edge_body(
        size, levels, level_ref, strip_ref, left_ref, right_ref, inner_vel, faces,
        edge_ref, vel_ref, beyond_ref, *rest[7:10],
    )

    def move_out():
        pack_blocks(
            levels, level_ref, dest_ref, state_ref, side_ref,
            to_levels, north_ref, south_ref, north_levels, south_levels, outbox,
        )

    droplet_body(
        size, counts_ref, dest_ref, vel_ref, beyond_ref, speed.take(), frac.take(), along, plane,
        spread_ref, outer_ref, stay_ref, state_ref, *rest[10:], [move_out],
    )
    pack_force(
        levels, level_ref, spread_ref, outer_ref, own_ref,
        to_levels, north_ref, south_ref, north_levels, south_levels, strip,
    )


def gather_body(levels, level_ref, own_ref, side_ref, *rest):
    depth, height, width = own_ref.shape[1:]
    slots = len(rim_sizes(levels))
    north_ref, south_ref = rest[:2]
    from_levels, north_levels, south_levels = (rest[2 + slots * at : 2 + slots * at + slots] for at in range(3))
    force_ref, right_ref, left_ref, total = rest[2 + 3 * slots :]
    base = face_rows(depth, height)
    total[...] = own_ref[...]
    right_ref[base:, :] = jnp.zeros((right_ref.shape[0] - base, width), jnp.float32)
    left_ref[base:, :] = jnp.zeros((left_ref.shape[0] - base, width), jnp.float32)
    last = slice(height - 1, height)
    for part in range(4):
        for layer in range(depth):
            at = part * depth + layer
            total[part, layer, 0:2, :] += north_ref[2 * at : 2 * at + 2, :]
            total[part, layer, last, :] += south_ref[at : at + 1, :]

    def blocks(source, way_z, way_y):
        at = base + 12 * group_at(way_z, way_y)
        start = source.shape[0] - GROUP
        for slot in range(CAP):
            rows = slice(at + 6 * slot, at + 6 * slot + 6)
            left_ref[rows, :] = source[start + 8 * slot : start + 8 * slot + 6, :]
            right_ref[rows, :] = source[start + 32 + 8 * slot : start + 38 + 8 * slot, :]

    at = base + 12 * group_at(0, 0)
    for slot in range(CAP):
        left_ref[at + 6 * slot : at + 6 * slot + 6, :] = side_ref[slot, 0:6, :]
        right_ref[at + 6 * slot : at + 6 * slot + 6, :] = side_ref[2 + slot, 0:6, :]
    blocks(north_ref, 0, 1)
    blocks(south_ref, 0, -1)
    for kind, _, receiver, slot in force_sides(levels):

        def take(kind=kind, slot=slot):
            for part in range(4):
                for step in range(2 if kind == "up" else 1):
                    layer = step if kind == "up" else depth - 1
                    at = 2 * part + step
                    total[part, layer] += from_levels[slot][8 * at : 8 * at + 8, :]
                    total[part, layer, 0:2, :] += north_levels[slot][2 * at : 2 * at + 2, :]
                    total[part, layer, last, :] += south_levels[slot][at : at + 1, :]
            way = 1 if kind == "up" else -1
            blocks(from_levels[slot], way, 0)
            blocks(north_levels[slot], way, 1)
            blocks(south_levels[slot], way, -1)

        guarded(level_ref[0], receiver, take)
    for layer in range(depth):
        for axis in range(3):
            force_ref[axis, layer] = total[axis, layer]
    lane = lax.broadcasted_iota(jnp.int32, (height, 128), 1)
    for tile in range(base // height):
        value = jnp.zeros((height, 128), jnp.float32)
        for layer in range(8 * tile, min(8 * tile + 8, depth)):
            part = layer - 8 * tile
            value = jnp.where(lane // 16 == part, lane_roll(total[3, layer, :, 0:128], 16 * part), value)
        for target in (right_ref, left_ref):
            target[tile * height : tile * height + height, 0:128] = value


def last_body(levels, level_ref, part_ref, stay_ref, *rest):
    depth, height, width = part_ref.shape[1:]
    slots = len(rim_sizes(levels))
    north_ref, south_ref = rest[:2]
    from_levels, north_levels, south_levels = (rest[2 + slots * at : 2 + slots * at + slots] for at in range(3))
    right_ref, left_ref, force_ref, arrived_ref = rest[2 + 3 * slots :]
    blocks = stay_ref.shape[1]
    base = face_rows(depth, height)
    lane = lax.broadcasted_iota(jnp.int32, (height, 128), 1)
    for layer in range(depth):
        rows = slice(layer // 8 * height, layer // 8 * height + height)
        before, after = right_ref[rows, :128], left_ref[rows, :128]
        for axis in range(3):
            at = 16 * (layer % 8) + 4 * axis
            first = jnp.where(lane < 2, lane_roll(before, -at - 1), 0.0)
            final = jnp.where(lane == 127, lane_roll(after, 127 - at), 0.0)
            force_ref[axis, layer] = part_ref[axis, layer]
            force_ref[axis, layer, :, 0:128] += first
            force_ref[axis, layer, :, width - 128 : width] += final
    arrived_ref[:, 0:blocks, :] = stay_ref[...]

    def put(source, start, stride, way_z, way_y, way_x):
        code = group_at(way_z, way_y) * 3 + way_x + 1
        at = blocks + CAP * (code if code < 13 else code - 1)
        for slot in range(CAP):
            for axis in range(6):
                if source is None:
                    value = jnp.zeros((1, 128), jnp.float32)
                else:
                    value = source[start + stride * slot + axis : start + stride * slot + axis + 1, :]
                arrived_ref[axis, at + slot : at + slot + 1, :] = value

    for way_z in (-1, 0, 1):
        for way_y in (-1, 0, 1):
            for way_x, source in ((1, right_ref), (-1, left_ref)):
                put(source, base + 12 * group_at(way_z, way_y), 6, way_z, way_y, way_x)
    middle = 16

    def put_group(source, way_z, way_y):
        put(source, None if source is None else source.shape[0] - GROUP + middle, 8, way_z, way_y, 0)

    put_group(north_ref, 0, 1)
    put_group(south_ref, 0, -1)
    for kind, _, receiver, slot in force_sides(levels):
        way = 1 if kind == "up" else -1

        def take(way=way, slot=slot):
            put_group(from_levels[slot], way, 0)
            put_group(north_levels[slot], way, 1)
            put_group(south_levels[slot], way, -1)

        def clear(way=way):
            for way_y in (-1, 0, 1):
                put_group(None, way, way_y)

        guarded(level_ref[0], receiver, take)
        if receiver is not None:
            guarded(level_ref[0], 1 - receiver, clear)


def local(pops, coarse_pops, interface, drop_vel, drop_frac, home, counts, dest):
    levels = lax.axis_size("gz")
    depth, height, width = interface.shape
    blocks = home.shape[0]
    kinds = ["up", "down"][: len(rim_sizes(levels))]
    slots = len(kinds)
    size = (depth, height, width)
    rows = height + 8
    table = table_rows(depth, height)
    along, plane, ready = call(
        functools.partial(weigh_body, size),
        [(2 * width + 128, blocks * 128), (blocks // 2, table, 256), (8, 128)],
        [drop_frac, home],
        cost=long_cost(),
        kind=[jnp.bfloat16, jnp.float32, jnp.float32],
    )
    strip, left, right, inner_pops, inner_vel, faces = wide_exchange(pops, coarse_pops, interface, ready)
    sizes = [(count + GROUP, width) for count in message_rows(depth)]
    outs = call(
        functools.partial(main_body, size, levels),
        [(19, height, 128), (4, depth, height, width), (6, blocks, 128), (4, 8, 128), sizes[1], sizes[2]]
        + [sizes[0]] * slots
        + [sizes[3]] * slots
        + [sizes[4]] * slots,
        [counts, dest, strip, left, right, inner_vel, *faces, drop_vel, drop_frac, along, plane],
        [
            pltpu.VMEM((3 * table, width), jnp.float32),
            pltpu.VMEM((3 * table, 128), jnp.float32),
            pltpu.VMEM((3 * table, width), jnp.float32),
            pltpu.VMEM((3 * table, 128), jnp.float32),
            pltpu.VMEM((blocks, 8, 128), jnp.float32),
            pltpu.VMEM((27 * CAP + 1, 8, 128), jnp.float32),
            pltpu.VMEM((table, 128), jnp.float32),
            pltpu.VMEM((2, channels, rows, 128), jnp.float32),
            pltpu.VMEM((2, 19, rows, 128), jnp.float32),
            pltpu.VMEM((2, 19, rows, 128), jnp.float32),
            pltpu.VMEM((3 * table, 2 * width), jnp.bfloat16),
            pltpu.VMEM((3 * table, width + 128), jnp.bfloat16),
            pltpu.VMEM((3 * table, blocks * 128), jnp.bfloat16),
            pltpu.VMEM((3 * table, blocks * 128), jnp.bfloat16),
        ],
        late=(0, 1, *range(5, 10 + slots)),
    )
    edge, own, stay, side, north, south = outs[:6]
    to_levels, north_levels, south_levels = (outs[6 + slots * at : 6 + slots * at + slots] for at in range(3))
    received = [shifted(north, "gy", 1), shifted(south, "gy", -1)]
    received += [to_level(value, kind, levels) for value, kind in zip(to_levels, kinds)]
    received += [to_level(value, kind, levels, "gy", 1) for value, kind in zip(north_levels, kinds)]
    received += [to_level(value, kind, levels, "gy", -1) for value, kind in zip(south_levels, kinds)]
    (state,) = call(patch_body, [pops.shape], [inner_pops, edge], cost=long_cost())
    side_rows = (padded(face_rows(depth, height) + 9 * 6 * CAP), width)
    part, right, left = call(
        functools.partial(gather_body, levels),
        [(3, depth, height, width), side_rows, side_rows],
        [own, side] + received,
        [pltpu.VMEM((4, depth, height, width), jnp.float32)],
    )
    force, arrived = call(
        functools.partial(last_body, levels),
        [(3, depth, height, width), (6, blocks + 26 * CAP, 128)],
        [part, stay] + received + [shifted(right, "gx", 1), shifted(left, "gx", -1)],
    )
    return state, force, arrived


def solution(mesh):
    return jax.shard_map(
        local,
        mesh=mesh,
        in_specs=(
            P(None, "gz", "gy", "gx"),
            P(None, "gz", "gy", "gx"),
            P("gz", "gy", "gx"),
            P(None, ("gx", "gy", "gz"), None),
            P(None, ("gx", "gy", "gz"), None),
            P(("gx", "gy", "gz"), None),
            P(("gx", "gy", "gz")),
            P(("gx", "gy", "gz")),
        ),
        out_specs=(
            P(None, "gz", "gy", "gx"),
            P(None, "gz", "gy", "gx"),
            P(None, ("gx", "gy", "gz"), None),
        ),
        check_vma=False,
    )
```

```python
import functools
import math

import jax
import jax.numpy as jnp
import numpy as np
from jax import lax
from jax.experimental import pallas as pl
from jax.experimental.pallas import tpu as pltpu
from jax.sharding import PartitionSpec as P

CAP = 2


lattice = np.array(
    [
        [0, 0, 0],
        [1, 0, 0],
        [-1, 0, 0],
        [0, 1, 0],
        [0, -1, 0],
        [0, 0, 1],
        [0, 0, -1],
        [1, 1, 0],
        [-1, -1, 0],
        [1, -1, 0],
        [-1, 1, 0],
        [1, 0, 1],
        [-1, 0, -1],
        [1, 0, -1],
        [-1, 0, 1],
        [0, 1, 1],
        [0, -1, -1],
        [0, 1, -1],
        [0, -1, 1],
    ]
)
weights_table = np.array([1.0 / 3.0] + [1.0 / 18.0] * 6 + [1.0 / 36.0] * 12)
opposite = [0, 2, 1, 4, 3, 6, 5, 8, 7, 10, 9, 12, 11, 14, 13, 16, 15, 18, 17]
inverse_tau = 0.8
relax = 0.5
couple = 8.0


class Level:
    later = ()

    def __getitem__(self, _):
        return lax.axis_index("gz").astype(jnp.int32)


class Moving:
    def __init__(self, buffer, copy):
        self.buffer = buffer
        self.copy = copy

    def take(self):
        self.copy.wait()
        return self.buffer


def call(body, outs, arrays, scratch=(), cost=None, heads=(), late=(), kind=jnp.float32, halves=()):
    heads = dict(heads)
    landing = []
    for at, value in enumerate(arrays):
        space = pltpu.SMEM if value.ndim == 1 else pltpu.VMEM
        landing.append(space((heads.get(at, value.shape[0]),) + value.shape[1:], value.dtype))

    def whole(*refs):
        given = refs[: len(arrays)]
        made = list(refs[len(arrays) : len(arrays) + len(outs)])
        rest = refs[len(arrays) + len(outs) :]
        landed, done, rest = list(rest[: len(arrays)]), rest[len(arrays)], rest[len(arrays) + 1 :]
        copies, level = [], Level()
        for at, (source, target) in enumerate(zip(given, landed)):
            if at in heads:
                source = source.at[pl.ds(0, heads[at])]
            copies.append(pltpu.make_async_copy(source, target, done.at[at, 0]))
        if halves:
            cuts = []
            for at, (source, target, dim) in enumerate(zip(given, landed, halves)):
                half = source.shape[dim] // 2
                for part, size in ((0, half), (1, source.shape[dim] - half)):
                    where = (slice(None),) * dim + (pl.ds(part * half, size),)
                    cuts.append(pltpu.make_async_copy(source.at[where], target.at[where], done.at[at, part]))
            copies, level.later = cuts[::2], cuts[1::2]
        for copy in [*copies, *level.later]:
            copy.start()
        for at, copy in enumerate(copies):
            if at in late:
                landed[at] = Moving(landed[at], copy)
            else:
                copy.wait()
        body(level, *landed, *made, *rest)

    vmem = pl.BlockSpec(memory_space=pltpu.VMEM)
    hbm = pl.BlockSpec(memory_space=pltpu.HBM)
    return pl.pallas_call(
        whole,
        out_shape=[
            jax.ShapeDtypeStruct(shape, kind[at] if isinstance(kind, list) else kind)
            for at, shape in enumerate(outs)
        ],
        in_specs=[hbm] * len(arrays),
        out_specs=[vmem] * len(outs),
        scratch_shapes=landing
        + [pltpu.SemaphoreType.DMA((len(arrays), 2))]
        + list(scratch),
        cost_estimate=cost,
        compiler_params=pltpu.CompilerParams(vmem_limit_bytes=64 * 1024 * 1024),
    )(*arrays)


ways = [tuple(int(part) for part in lattice[index][::-1]) for index in range(19)] + [(0, 0, 0)]
channels = len(ways)
LOW = 3
HIGH = 4


def low_reach(way):
    return 2 + way


def high_reach(way):
    return 3 - way


def rim(kind):
    side = 1 if kind == "low" else -1
    return [
        (step, channel)
        for step in (1, 2)
        for channel in range(channels)
        if step <= 1 + side * ways[channel][0]
    ]


def rim_sides(levels):
    if levels == 2:
        return [("low", 1, 0, 0), ("high", 0, 1, 0)]
    return [("low", None, None, 0), ("high", None, None, 1)]


def rim_sizes(levels):
    sizes = [FOUR + len(rim(kind)) for kind, _, _, _ in rim_sides(levels)]
    return [max(sizes)] if levels == 2 else sizes


def guarded(level, guard, action):
    if guard is None:
        action()
    else:
        pl.when(level == guard)(action)


def padded(count):
    return -(-count // 8) * 8


def reaches(channel, bounces):
    way_z, way, _ = ways[channel]
    above, below = high_reach(way), low_reach(way)
    if bounces and way_z != 0:
        above, below = max(above, HIGH - 1), max(below, LOW - 1)
    return above, below


def row_places(cells, start=(0, 0)):
    places, (high_at, low_at) = [], start
    for above, below in cells:
        places.append((high_at, low_at, above, below))
        high_at, low_at = high_at + above, low_at + below
    return places, (padded(high_at), padded(low_at))


def strip_rows():
    return row_places([reaches(channel, True) for channel in range(channels)])


def own_rows(depth):
    cells = [(layer, channel) for layer in range(depth) for channel in range(channels)]
    places, sizes = row_places(
        [reaches(channel, layer in (0, depth - 1)) for layer, channel in cells], strip_rows()[1]
    )
    return [(layer, channel, place) for (layer, channel), place in zip(cells, places)], sizes


FOUR = -(-channels // 4)


def rim_strip_rows():
    return row_places([(HIGH, LOW)] * FOUR)


def rim_rows(kind):
    places, sizes = row_places([reaches(channel, False) for _, channel in rim(kind)], rim_strip_rows()[1])
    return [(step, channel, place) for (step, channel), place in zip(rim(kind), places)], sizes


def rim_row_sizes(levels):
    sizes = [rim_rows(kind)[1] for kind, _, _, _ in rim_sides(levels)]
    return [tuple(max(part) for part in zip(*sizes))] if levels == 2 else sizes


def face_table(high):
    wants = []
    for channel in range(channels):
        way_z, _, way = ways[channel]
        count = high_reach(way) if high else low_reach(way)
        if way_z != 0:
            count = max(count, (HIGH if high else LOW) - 1)
        wants.append((-count, channel))
    free, table = [], []
    for count, channel in sorted(wants):
        tile = next((at for at, room in enumerate(free) if room >= -count), len(free))
        if tile == len(free):
            free.append(8)
        table.append((channel, tile, 8 - free[tile], -count))
        free[tile] += count
    return table, len(free)


def moments(cells):
    density = cells[0] * float(weights_table[0])
    moment = [None, None, None]
    face, edge = float(weights_table[1]), float(weights_table[7])
    edge_sum = cells[7]
    for index in range(8, 19):
        edge_sum = edge_sum + cells[index]
    face_sum = cells[1]
    for index in range(2, 7):
        face_sum = face_sum + cells[index]
    density = density + face * face_sum + edge * edge_sum
    for axis in range(3):
        total = {}
        for group, indices in ((face, range(1, 7)), (edge, range(7, 19))):
            plus, minus = None, None
            for index in indices:
                way = int(lattice[index][axis])
                if way == 1:
                    plus = cells[index] if plus is None else plus + cells[index]
                if way == -1:
                    minus = cells[index] if minus is None else minus + cells[index]
            total[group] = plus - minus
        moment[axis] = face * total[face] + edge * total[edge]
    return density, moment


def relaxed(cells):
    density, moment = moments(cells)
    inverse = 1.0 / density
    flow = [part * inverse for part in moment]
    square = flow[0] * flow[0] + flow[1] * flow[1] + flow[2] * flow[2]
    scale = density * inverse_tau
    base = scale * (1.0 - 1.5 * square)
    keep = 1.0 - inverse_tau
    posts = [None] * 19
    posts[0] = keep * cells[0] + base
    for index in range(1, 19, 2):
        along = None
        for axis in range(3):
            way = int(lattice[index][axis])
            if way != 0:
                part = flow[axis] if way == 1 else -flow[axis]
                along = part if along is None else along + part
        odd = 3.0 * scale * along
        even = base + (4.5 * scale) * (along * along)
        posts[index] = keep * cells[index] + (even + odd)
        posts[index + 1] = keep * cells[index + 1] + (even - odd)
    return posts


def lane_roll(value, shift):
    shift = shift % value.shape[-1]
    return value if shift == 0 else pltpu.roll(value, shift, value.ndim - 1)


def first_body(
    levels, level_ref, pops_ref, coarse_ref, interface_ref, posts_ref, strip_ref, down_ref, up_ref, *outs
):
    depth, height, width = interface_ref.shape
    slots = len(rim_sizes(levels))
    rims, down_rims, up_rims = (outs[slots * at : slots * at + slots] for at in range(3))
    lane = lax.broadcasted_iota(jnp.int32, (height, 128), 1)

    def put_rows(down, up, place, cells):
        down_at, up_at, down_rows, up_rows = place
        cols = slice(0, cells.shape[1])
        down[down_at : down_at + down_rows, cols] = cells[:down_rows, :]
        up[up_at : up_at + up_rows, cols] = cells[height - up_rows :, :]

    own = own_rows(depth)[0]
    for layer in range(depth):
        if layer == depth // 2:
            for copy in level_ref.later:
                copy.wait()
        mask = interface_ref[layer]
        inside = mask == 1
        posts = relaxed([pops_ref[index, layer] for index in range(19)])
        posts = [
            jnp.where(inside, coarse_ref[index, layer].astype(jnp.float32), posts[index])
            for index in range(19)
        ] + [mask.astype(jnp.float32)]
        for channel in range(channels):
            posts_ref[channel, layer] = posts[channel]
            put_rows(down_ref, up_ref, own[layer * channels + channel][2], posts[channel])
    for channel in range(channels):
        value = jnp.zeros((height, 128), jnp.float32)
        for layer in range(depth):
            cells = posts_ref[channel, layer]
            if width > 128:
                cells = jnp.where(lane < 64, cells[:, :128], cells[:, width - 128 :])
            value = jnp.where(lane // 8 == LOW + layer, lane_roll(cells, 8 * (LOW + layer) + 4), value)
        strip_ref[channel] = value
        put_rows(down_ref, up_ref, strip_rows()[0][channel], value)
    for kind, _, sender, slot in rim_sides(levels):

        def pack(kind=kind, slot=slot):
            for tile in range(FOUR):
                value = jnp.zeros((height, 128), jnp.float32)
                for part in range(min(4, channels - 4 * tile)):
                    first = LOW + depth - 4 if kind == "low" else LOW
                    turned = lane_roll(strip_ref[4 * tile + part], 32 * part - 8 * first)
                    value = jnp.where(lane // 32 == part, turned, value)
                rims[slot][tile, :, 0:128] = value
                put_rows(down_rims[slot], up_rims[slot], rim_strip_rows()[0][tile], value)
            for at, (step, channel, place) in enumerate(rim_rows(kind)[0]):
                cells = posts_ref[channel, depth - step if kind == "low" else step - 1]
                rims[slot][FOUR + at] = cells
                put_rows(down_rims[slot], up_rims[slot], place, cells)

        guarded(level_ref[0], sender, pack)


def unpack(levels, level, posts_ref, above_ref, below_ref, rims, above_rims, below_rims, ext):
    depth, height = posts_ref.shape[1:3]
    rows = height + 8

    def put(channel, at, cells, place, above, below):
        above_at, below_at, above_rows, below_rows = place
        ext[channel, at, :height, :] = cells
        ext[channel, at, height : height + above_rows, :] = above[above_at : above_at + above_rows, :]
        ext[channel, at, rows - below_rows : rows, :] = below[below_at : below_at + below_rows, :]

    for layer, channel, place in own_rows(depth)[0]:
        put(channel, LOW + layer, posts_ref[channel, layer], place, above_ref, below_ref)
    for kind, receiver, _, slot in rim_sides(levels):

        def take(kind=kind, slot=slot):
            for at, (step, channel, place) in enumerate(rim_rows(kind)[0]):
                layer = LOW - step if kind == "low" else LOW + depth + step - 1
                put(channel, layer, rims[slot][FOUR + at], place, above_rims[slot], below_rims[slot])

        guarded(level, receiver, take)


def split_given(levels, rest):
    slots = len(rim_sizes(levels))
    parts = [rest[3 + slots * at : 3 + slots * at + slots] for at in range(3)]
    return rest[:3], parts, rest[3 + 3 * slots :]


def strip_body(levels, depth, level_ref, *rest):
    (own_ref, above_ref, below_ref), parts, rest = split_given(levels, rest)
    _, strip_ref, right_ref, left_ref, tiles = rest
    rows = strip_ref.shape[1]
    height = rows - 8
    lane = lax.broadcasted_iota(jnp.int32, (rows, 128), 1)
    layer_at = lane // 8

    def put(target, index, place, above, below):
        above_at, below_at, above_rows, below_rows = place
        target[index, height : height + above_rows, :] = above[above_at : above_at + above_rows, 0:128]
        target[index, rows - below_rows :, :] = below[below_at : below_at + below_rows, 0:128]

    for channel in range(channels):
        strip_ref[channel, 0:height, :] = own_ref[channel]
        put(strip_ref, channel, strip_rows()[0][channel], above_ref, below_ref)
    for kind, receiver, _, slot in rim_sides(levels):

        def take(kind=kind, slot=slot):
            rims, above_rims, below_rims = (part[slot] for part in parts)
            first = -1 if kind == "low" else LOW + depth
            here = layer_at < LOW if kind == "low" else layer_at >= LOW + depth
            for tile in range(FOUR):
                tiles[tile, 0:height, :] = rims[tile, :, 0:128]
                put(tiles, tile, rim_strip_rows()[0][tile], above_rims, below_rims)
                value = tiles[tile]
                for part in range(min(4, channels - 4 * tile)):
                    turned = lane_roll(value, 8 * first - 32 * part)
                    strip_ref[4 * tile + part] = jnp.where(here, turned, strip_ref[4 * tile + part])

        guarded(level_ref[0], receiver, take)
    spot = lane % 8
    for target, high in ((right_ref, False), (left_ref, True)):
        table, count = face_table(high)
        for tile in range(count):
            value = jnp.zeros((rows, 128), jnp.float32)
            for channel, at, first, cols in table:
                if at == tile:
                    turned = lane_roll(strip_ref[channel], first - (4 if high else 4 - cols))
                    value = jnp.where((spot >= first) & (spot < first + cols), turned, value)
            target[tile] = value


def substeps(levels, level, size, ext, pulled, second):
    depth, height, width = size
    rows = height + 8

    def pull(source, layer, at, target):
        for index in range(19):
            way_z, way_y, way_x = ways[index]
            value = source[index, at - way_z]
            if way_x != 0:
                value = pltpu.roll(value, way_x % width, 1)
            if way_y != 0:
                value = pltpu.roll(value, way_y % rows, 0)
            if way_z == 1 and layer == 0:
                value = jnp.where(level == 0, source[opposite[index], at], value)
            if way_z == -1 and layer == depth - 1:
                value = jnp.where(level == levels - 1, source[opposite[index], at], value)
            target[index] = value

    tiles = [
        (slice(row, row + 8), slice(col, col + 128))
        for row in range(0, rows, 8)
        for col in range(0, width, 128)
    ]

    def first_steps(layers):
        for layer in layers:
            at = LOW + layer
            cells = pulled.at[at % pulled.shape[0]]
            pull(ext, layer, at, cells)
            for tile in tiles:
                posts = relaxed([cells[(index, *tile)] for index in range(19)])
                inside = ext[(19, at, *tile)] > 0.5
                for index in range(19):
                    second[(index, at - 1, *tile)] = jnp.where(
                        inside, ext[(index, at, *tile)], posts[index]
                    )

    def second_steps(layers, put):
        for layer in layers:
            at = LOW - 1 + layer
            cells = pulled.at[at % pulled.shape[0]]
            pull(second, layer, at, cells)
            for tile in tiles:
                density, moment = moments([cells[(index, *tile)] for index in range(19)])
                inverse = 1.0 / density
                for axis in range(3):
                    put(axis, layer, tile, moment[axis] * inverse)
            yield layer, cells

    return first_steps, second_steps


def inner_body(levels, level_ref, *rest):
    (posts_ref, above_ref, below_ref), parts, rest = split_given(levels, rest)
    pops_ref, vel_ref, ext, pulled, second = rest
    level = level_ref[0]
    unpack(levels, level, posts_ref, above_ref, below_ref, *parts, ext)
    depth, height, _ = size = posts_ref.shape[1:]
    first_steps, second_steps = substeps(levels, level, size, ext, pulled, second)

    def put(axis, layer, tile, value):
        vel_ref[(axis, layer, *tile)] = value

    pl.when(level != 0)(lambda: first_steps([-1]))
    pl.when(level != levels - 1)(lambda: first_steps([depth]))
    first_steps(range(depth))
    for layer, cells in second_steps(range(depth), put):
        for index in range(19):
            pops_ref[index, layer] = cells[index, :height, :]


def face_body(levels, level_ref, *rest):
    (posts_ref, above_ref, below_ref), parts, rest = split_given(levels, rest)
    slots = len(rim_sizes(levels))
    faces, (ext, pulled, second) = rest[:slots], rest[slots:]
    level = level_ref[0]
    unpack(levels, level, posts_ref, above_ref, below_ref, *parts, ext)
    depth, height, _ = size = posts_ref.shape[1:]
    first_steps, second_steps = substeps(levels, level, size, ext, pulled, second)
    for kind, sender, _, slot in force_sides(levels):
        wanted = [depth - 1] if kind == "up" else [0, 1]

        def work(wanted=wanted, slot=slot):
            def put(axis, layer, tile, value):
                at = (2 * axis + layer - wanted[0]) * (height + 3)
                row, cols = tile[0].start, tile[1]
                if row < height:
                    faces[slot][at + 1 + row : at + 9 + row, cols] = value
                else:
                    faces[slot][at + 1 + height : at + 3 + height, cols] = value[:2, :]
                    faces[slot][at : at + 1, cols] = value[7:, :]

            first_steps(range(wanted[0] - 1, wanted[-1] + 2))
            for _ in second_steps(wanted, put):
                pass

        guarded(level, sender, work)


def edge_body(
    size, levels, level_ref, strip_ref, left_ref, right_ref, inner_vel, faces,
    edge_ref, vel_ref, beyond_ref, sides, pulled, second,
):
    depth, height, width = size
    rows = height + 8
    level = level_ref[0]
    lane = lax.broadcasted_iota(jnp.int32, (rows, 128), 1)
    before = lane % 8 < 4
    bottom = (lane // 8 == LOW) & (level == 0)
    top = (lane // 8 == LOW + depth - 1) & (level == levels - 1)
    for channel, tile, first, cols in face_table(False)[0]:
        turned = lane_roll(left_ref[tile], 4 - cols - first)
        sides[0, channel] = jnp.where(before, turned, strip_ref[channel])
    for channel, tile, first, _ in face_table(True)[0]:
        turned = lane_roll(right_ref[tile], 4 - first)
        sides[1, channel] = jnp.where(before, strip_ref[channel], turned)

    def pull(source, side, target):
        for index in range(19):
            way_z, way_y, way_x = ways[index]
            value = lane_roll(source[side, index], 8 * way_z + way_x)
            if way_y != 0:
                value = pltpu.roll(value, way_y % rows, 0)
            if way_z != 0:
                value = jnp.where(bottom if way_z == 1 else top, source[side, opposite[index]], value)
            target[side, index] = value

    speeds = [[], []]
    for side in range(2):
        pull(sides, side, pulled)
        for row in range(0, rows, 8):
            cut = slice(row, row + 8)
            posts = relaxed([pulled[side, index, cut] for index in range(19)])
            inside = sides[side, 19, cut] > 0.5
            for index in range(19):
                second[side, index, cut] = jnp.where(inside, sides[side, index, cut], posts[index])
        pull(second, side, pulled)
        density, moment = moments([pulled[side, index] for index in range(19)])
        inverse = 1.0 / density
        speeds[side] = [part * inverse for part in moment]

    row = lax.broadcasted_iota(jnp.int32, (rows, 128), 0)
    valid = (row < height + 2) | (row == rows - 1)
    outside = (lane < 2) | (lane == 127)
    vel_in = inner_vel.take()
    faces = [face.take() for face in faces]

    def inner(axis, layer, cols):
        if 0 < layer <= depth:
            return vel_in[axis, layer - 1, :, cols]
        at = 2 * axis * (height + 3) if layer == 0 else (2 * axis + layer - depth - 1) * (height + 3)
        face = faces[0 if layer == 0 else -1]
        return jnp.concatenate(
            [
                face[at + 1 : at + height + 1, cols],
                face[at + height + 1 : at + height + 3, cols],
                jnp.zeros((5, 128), jnp.float32),
                face[at : at + 1, cols],
            ],
            axis=0,
        )

    table = table_rows(depth, height)
    vel_ref[...] = jnp.zeros_like(vel_ref)
    beyond_ref[...] = jnp.zeros_like(beyond_ref)

    def put(target, axis, layer, cols, cells):
        at = axis * table + layer * (height + 3)
        target[at : at + 1, cols] = cells[rows - 1 :, :]
        target[at + 1 : at + height + 3, cols] = cells[: height + 2, :]

    for axis in range(3):
        main = jnp.where(before, speeds[1][axis], speeds[0][axis])
        rest = jnp.where(before, speeds[0][axis], speeds[1][axis])
        for layer in range(depth + 3):
            keep = valid
            if layer == 0:
                keep = valid & (level != 0)
            if layer > depth:
                keep = valid & (level != levels - 1)
            shift = -(8 * (layer - 1 + LOW) + 4)
            turned = lane_roll(main, shift)
            for col in range(0, width, 128):
                cells = inner(axis, layer, slice(col, col + 128))
                if col == 0 or col == width - 128:
                    mask = (lane < 2) & (col == 0) | (lane >= 126) & (col == width - 128)
                    cells = jnp.where(mask, turned, cells)
                put(vel_ref, axis, layer, slice(col, col + 128), jnp.where(keep, cells, 0.0))
            put(beyond_ref, axis, layer, slice(0, 128), jnp.where(keep & outside, lane_roll(rest, shift), 0.0))
    for index in range(19):
        edge_ref[index] = jnp.where(before, pulled[1, index], pulled[0, index])[:height]


def patch_body(_, pops_in, edge_ref, pops_ref):
    depth, height, width = pops_ref.shape[1:]
    lane = lax.broadcasted_iota(jnp.int32, (height, 128), 1)
    for index in range(19):
        value = edge_ref[index]
        for layer in range(depth):
            turned = lane_roll(value, -(8 * (layer + LOW) + 4))
            for col in range(0, width, 128):
                cells = pops_in[index, layer, :, col : col + 128]
                if col == 0 or col == width - 128:
                    mask = (lane < 2) & (col == 0) | (lane >= 126) & (col == width - 128)
                    cells = jnp.where(mask, turned, cells)
                pops_ref[index, layer, :, col : col + 128] = cells


def long_cost():
    return pl.CostEstimate(flops=10**8, bytes_accessed=1 << 22, transcendentals=0)


def shifted(value, axis, step):
    count = lax.axis_size(axis)
    return lax.ppermute(value, axis, [(i, (i + step) % count) for i in range(count)])


def to_level(value, kind, levels, side=None, step=0):
    pairs = []
    for at in range(levels):
        other = 1 - at if levels == 2 else at + 1 if kind in ("low", "up") else at - 1
        if 0 <= other < levels:
            pairs.append((at, other))
    if side is None:
        return lax.ppermute(value, "gz", pairs)
    count = lax.axis_size(side)
    return lax.ppermute(
        value,
        (side, "gz"),
        [
            (brick * levels + at, (brick + step) % count * levels + other)
            for brick in range(count)
            for at, other in pairs
        ],
    )


def wide_exchange(pops, coarse_pops, interface, ready):
    levels = lax.axis_size("gz")
    depth, height, width = interface.shape
    sizes = rim_sizes(levels)
    slots = len(sizes)
    kinds = ["low", "high"][:slots]
    down_sizes, up_sizes = zip(*rim_row_sizes(levels))
    outs = call(
        functools.partial(first_body, levels),
        [(channels, depth, height, width), (channels, height, 128)]
        + [(size, width) for size in own_rows(depth)[1]]
        + [(size, height, width) for size in sizes]
        + [(size, width) for size in down_sizes + up_sizes],
        [pops, coarse_pops, interface],
        halves=(1, 1, 0),
    )
    posts, own, down, up = outs[:4]
    rims, down_rims, up_rims = (outs[4 + slots * at : 4 + slots * at + slots] for at in range(3))
    given = [shifted(down, "gy", -1), shifted(up, "gy", 1)]
    given += [to_level(value, kind, levels) for value, kind in zip(rims, kinds)]
    given += [to_level(value, kind, levels, "gy", -1) for value, kind in zip(down_rims, kinds)]
    given += [to_level(value, kind, levels, "gy", 1) for value, kind in zip(up_rims, kinds)]
    deep, rows = depth + LOW + HIGH, height + 8
    ext = pltpu.VMEM((channels, deep, rows, width), jnp.float32)
    strip, right, left = call(
        functools.partial(strip_body, levels, depth),
        [(channels, rows, 128)] + [(face_table(high)[1], rows, 128) for high in (False, True)],
        [own] + given + [ready],
        [pltpu.VMEM((FOUR, rows, 128), jnp.float32)],
        heads=[(1, strip_rows()[1][0]), (2, strip_rows()[1][1])]
        + [(3 + at, FOUR) for at in range(slots)]
        + [(3 + slots + at, rim_strip_rows()[1][0]) for at in range(slots)]
        + [(3 + 2 * slots + at, rim_strip_rows()[1][1]) for at in range(slots)],
    )
    left, right = shifted(right, "gx", 1), shifted(left, "gx", -1)
    scratch = [
        ext,
        pltpu.VMEM((4, 19, rows, width), jnp.float32),
        pltpu.VMEM((19, deep - 2, rows, width), jnp.float32),
    ]
    faces = call(
        functools.partial(face_body, levels), [(padded(6 * (height + 3)), width)] * slots, [posts] + given, scratch
    )
    faces = [to_level(value, kind, levels) for value, kind in zip(faces, ["up", "down"])]
    inner_pops, inner_vel = call(
        functools.partial(inner_body, levels),
        [pops.shape, (3, depth, rows, width)],
        [posts] + given,
        scratch,
        long_cost(),
    )
    return strip, left, right, inner_pops, inner_vel, faces


def phis(frac):
    angle = frac * (0.5 * math.pi)
    sine = 0.25 * jnp.sin(angle)
    cosine = 0.25 * jnp.cos(angle)
    return (0.25 - sine, 0.25 + cosine, 0.25 + sine, 0.25 - cosine)


def split(value):
    high = value.astype(jnp.bfloat16)
    return high, (value - high.astype(jnp.float32)).astype(jnp.bfloat16)


def pick(step, parts):
    value = jnp.where(step == 0, parts[0], 0.0)
    for index in range(1, 4):
        value = jnp.where(step == index, parts[index], value)
    return value


def dots(left, right, dims):
    return lax.dot_general(left, right, (dims, ((), ())), preferred_element_type=jnp.float32)


def table_rows(depth, height):
    return -(-(depth + 3) * (height + 3) // 16) * 16


def weigh_body(size, _, frac_ref, home_ref, along, plane_ref, ready_ref):
    depth, height, width = size
    blocks = home_ref.shape[0]
    layers, rows = depth + 3, height + 3
    table = table_rows(depth, height)
    ready_ref[...] = jnp.zeros_like(ready_ref)
    along[2 * width :, :] = jnp.zeros((128, along.shape[1]), jnp.bfloat16)
    plane_ref[:, layers * rows :, :] = jnp.zeros(
        (plane_ref.shape[0], table - layers * rows, 256), jnp.float32
    )
    span_x = lax.broadcasted_iota(jnp.int32, (width, 128), 0) + 1
    span_end = lax.broadcasted_iota(jnp.int32, (16, 128), 0)
    span_y = lax.broadcasted_iota(jnp.int32, (padded(rows), 128), 0)
    span_z = lax.broadcasted_iota(jnp.int32, (padded(layers), 128), 0)
    for block in range(blocks):
        side = slice(block * 128, block * 128 + 128)
        cell = home_ref[block : block + 1, :]
        cell_x = cell % width
        cell_y = cell // width % height
        cell_z = cell // (width * height)
        part_x = phis(frac_ref[0, block : block + 1, :])
        part_y = phis(frac_ref[1, block : block + 1, :])
        part_z = phis(frac_ref[2, block : block + 1, :])
        high, low = split(pick(span_x - cell_x, part_x))
        along[0:width, side] = low
        along[width : 2 * width, side] = high
        high, low = split(pick(span_end + (width + 1) - cell_x, part_x))
        along[2 * width : 2 * width + 16, side] = high
        along[2 * width + 32 : 2 * width + 48, side] = high
        along[2 * width + 64 : 2 * width + 80, side] = low
        high, low = split(jnp.where((span_end == 15) & (cell_x == 0), part_x[0], 0.0))
        along[2 * width + 112 : 2 * width + 128, side] = high
        along[2 * width + 16 : 2 * width + 32, side] = high
        along[2 * width + 48 : 2 * width + 64, side] = low
        weight_y = pick(span_y - cell_y, part_y)[:rows]
        weight_z = pick(span_z - cell_z, part_z)
        half = block % 2 * 128
        for layer in range(layers):
            plane_ref[block // 2, layer * rows : layer * rows + rows, half : half + 128] = (
                weight_y * weight_z[layer : layer + 1, :]
            )


def droplet_body(
    size, counts_ref, dest_ref, vel_ref, beyond_ref, speed_ref, frac_ref, along_in, plane_in,
    spread_ref, outer_ref, stay_ref, state_ref, twice, mixed, push_high, push_low, meanwhile,
):
    depth, height, width = size
    blocks = state_ref.shape[0]
    table = table_rows(depth, height)
    high, low = split(vel_ref[...])
    twice[:, :width] = high
    twice[:, width:] = high
    mixed[:, :width] = low
    high, low = (part.astype(jnp.float32) for part in split(beyond_ref[...]))
    mixed[:, width:] = (high + lane_roll(low, 32) + lane_roll(high, 64)).astype(jnp.bfloat16)
    slots = lax.broadcasted_iota(jnp.int32, (1, 128), 1)
    along, plane_ref = along_in.take(), plane_in.take()

    def sample(number):
        pair = slice(number * 256, number * 256 + 256)
        return dots(twice[...], along[0 : 2 * width, pair], ((1,), (0,))) + dots(
            mixed[...], along[width:, pair], ((1,), (0,))
        )

    def move(number, sums):
        plane = plane_ref[number]
        for axis in range(3):
            where = slice(axis * table, axis * table + table)
            sampled = jnp.sum(sums[where] * plane, axis=0, keepdims=True)
            for half in range(2):
                block = 2 * number + half
                live = slots < counts_ref[block]
                sample = sampled[:, half * 128 : half * 128 + 128]
                speed = speed_ref[axis, block : block + 1, :]
                frac = frac_ref[axis, block : block + 1, :]
                moved = speed + relax * (sample - speed)
                push = jnp.where(live, couple * (moved - sample), 0.0)
                stays = live & (dest_ref[block] == 13)
                for at, value in ((axis, moved), (3 + axis, frac + moved)):
                    state_ref[block, at : at + 1, :] = jnp.where(live, value, 0.0)
                    stay_ref[at, block : block + 1, :] = jnp.where(stays, value, 0.0)
                high, low = split(plane[:, half * 128 : half * 128 + 128] * push)
                push_high[where, block * 128 : block * 128 + 128] = high
                push_low[where, block * 128 : block * 128 + 128] = low

    pairs = blocks // 2
    for number in range(pairs):
        move(number, sample(number))
    outer = dots(push_high[...], along[2 * width :, :], ((1,), (1,)))
    rest = dots(push_low[...], along[width:, :], ((1,), (1,)))
    outer_ref[...] = outer + lane_roll(outer, -64) + rest[:, width:]
    spread_ref[...] = rest[:, :width]
    for action in meanwhile:
        action()
    main = dots(push_high[...], along[0 : 2 * width, :], ((1,), (1,)))
    spread_ref[...] += main[:, :width] + main[:, width:]


def force_sides(levels):
    if levels == 2:
        return [("up", 0, 1, 0), ("down", 1, 0, 0)]
    return [("up", None, None, 0), ("down", None, None, 1)]


GROUP = 6 * 8


def group_at(way_z, way_y):
    return (way_z + 1) * 3 + way_y + 1


def face_rows(depth, height):
    return -(-depth // 8) * height


def message_rows(depth):
    return [8 * 8, 2 * 4 * depth, 4 * depth, 2 * 8, 8]


def pack_blocks(
    levels, level_ref, dest_ref, state_ref, side_ref,
    to_levels, north_ref, south_ref, north_levels, south_levels, outbox,
):
    level = level_ref[0]
    blocks = state_ref.shape[0]
    codes = [dest_ref[block] for block in range(blocks)]
    outbox[...] = jnp.zeros_like(outbox)
    for block in range(blocks):
        rank = jnp.int32(0)
        for earlier in range(block):
            rank = rank + (codes[earlier] == codes[block]).astype(jnp.int32)
        slot = jnp.where(codes[block] == 13, 27 * CAP, codes[block] * CAP + jnp.minimum(rank, CAP - 1))
        outbox[slot] = state_ref[block]

    def put(target, way_z, way_y):
        base = target.shape[0] - GROUP
        for slot in range(6):
            target[base + 8 * slot : base + 8 * slot + 8, :] = outbox[6 * group_at(way_z, way_y) + slot]

    put(north_ref, 0, 1)
    put(south_ref, 0, -1)
    for slot in range(CAP):
        side_ref[slot] = outbox[6 * group_at(0, 0) + slot]
        side_ref[CAP + slot] = outbox[6 * group_at(0, 0) + 4 + slot]
    ways_z = [(1 - 2 * level, 0)] if levels == 2 else [(1, 0), (-1, 1)]
    for way_z, slot in ways_z:
        put(to_levels[slot], way_z, 0)
        put(north_levels[slot], way_z, 1)
        put(south_levels[slot], way_z, -1)


def pack_force(
    levels, level_ref, spread_ref, outer_ref, own_ref,
    to_levels, north_ref, south_ref, north_levels, south_levels, strip,
):
    depth, height, width = own_ref.shape[1:]
    rows, table = height + 3, table_rows(depth, height)
    lane = lax.broadcasted_iota(jnp.int32, (table, 128), 1)
    value = jnp.zeros((table, 128), jnp.float32)
    for axis in range(3):
        here = (lane >= 4 * axis) & (lane < 4 * axis + 3)
        cells = outer_ref[axis * table : axis * table + table, :]
        value = jnp.where(here, lane_roll(cells, 4 * axis + 1), value)
    strip[...] = value

    def force(part, layer, cut):
        at = layer * rows
        if part < 3:
            return spread_ref[part * table + at + cut.start : part * table + at + cut.stop, :]
        return strip[at + cut.start : at + cut.stop, :]

    main, north, south = slice(1, height + 1), slice(height + 1, height + 3), slice(0, 1)
    for part in range(4):
        for layer in range(depth):
            own_ref[part, layer] = force(part, layer + 1, main)
            at = part * depth + layer
            north_ref[2 * at : 2 * at + 2, :] = force(part, layer + 1, north)
            south_ref[at : at + 1, :] = force(part, layer + 1, south)
    for kind, sender, _, slot in force_sides(levels):

        def pack(kind=kind, slot=slot):
            for part in range(4):
                for step in range(2 if kind == "up" else 1):
                    layer = depth + 1 + step if kind == "up" else 0
                    at = 2 * part + step
                    to_levels[slot][8 * at : 8 * at + 8, :] = force(part, layer, main)
                    north_levels[slot][2 * at : 2 * at + 2, :] = force(part, layer, north)
                    south_levels[slot][at : at + 1, :] = force(part, layer, south)

        guarded(level_ref[0], sender, pack)


def main_body(
    size, levels, level_ref, counts, dest, strip_ref, left_ref, right_ref, inner_vel, *rest,
):
    slots = len(rim_sizes(levels))
    faces, (speed, frac, along, plane), rest = rest[:slots], rest[slots : slots + 4], rest[slots + 4 :]
    edge_ref, own_ref, stay_ref, side_ref, north_ref, south_ref = rest[:6]
    rest = rest[6:]
    to_levels, north_levels, south_levels = (rest[slots * at : slots * at + slots] for at in range(3))
    rest = rest[3 * slots :]
    vel_ref, beyond_ref, spread_ref, outer_ref, state_ref, outbox, strip = rest[:7]
    counts_ref, dest_ref = counts.take(), dest.take()
    edge_body(
        size, levels, level_ref, strip_ref, left_ref, right_ref, inner_vel, faces,
        edge_ref, vel_ref, beyond_ref, *rest[7:10],
    )

    def move_out():
        pack_blocks(
            levels, level_ref, dest_ref, state_ref, side_ref,
            to_levels, north_ref, south_ref, north_levels, south_levels, outbox,
        )

    droplet_body(
        size, counts_ref, dest_ref, vel_ref, beyond_ref, speed.take(), frac.take(), along, plane,
        spread_ref, outer_ref, stay_ref, state_ref, *rest[10:], [move_out],
    )
    pack_force(
        levels, level_ref, spread_ref, outer_ref, own_ref,
        to_levels, north_ref, south_ref, north_levels, south_levels, strip,
    )


def gather_body(levels, level_ref, own_ref, side_ref, *rest):
    depth, height, width = own_ref.shape[1:]
    slots = len(rim_sizes(levels))
    north_ref, south_ref = rest[:2]
    from_levels, north_levels, south_levels = (rest[2 + slots * at : 2 + slots * at + slots] for at in range(3))
    force_ref, right_ref, left_ref, total = rest[2 + 3 * slots :]
    base = face_rows(depth, height)
    total[...] = own_ref[...]
    right_ref[base:, :] = jnp.zeros((right_ref.shape[0] - base, width), jnp.float32)
    left_ref[base:, :] = jnp.zeros((left_ref.shape[0] - base, width), jnp.float32)
    last = slice(height - 1, height)
    for part in range(4):
        for layer in range(depth):
            at = part * depth + layer
            total[part, layer, 0:2, :] += north_ref[2 * at : 2 * at + 2, :]
            total[part, layer, last, :] += south_ref[at : at + 1, :]

    def blocks(source, way_z, way_y):
        at = base + 12 * group_at(way_z, way_y)
        start = source.shape[0] - GROUP
        for slot in range(CAP):
            rows = slice(at + 6 * slot, at + 6 * slot + 6)
            left_ref[rows, :] = source[start + 8 * slot : start + 8 * slot + 6, :]
            right_ref[rows, :] = source[start + 32 + 8 * slot : start + 38 + 8 * slot, :]

    at = base + 12 * group_at(0, 0)
    for slot in range(CAP):
        left_ref[at + 6 * slot : at + 6 * slot + 6, :] = side_ref[slot, 0:6, :]
        right_ref[at + 6 * slot : at + 6 * slot + 6, :] = side_ref[2 + slot, 0:6, :]
    blocks(north_ref, 0, 1)
    blocks(south_ref, 0, -1)
    for kind, _, receiver, slot in force_sides(levels):

        def take(kind=kind, slot=slot):
            for part in range(4):
                for step in range(2 if kind == "up" else 1):
                    layer = step if kind == "up" else depth - 1
                    at = 2 * part + step
                    total[part, layer] += from_levels[slot][8 * at : 8 * at + 8, :]
                    total[part, layer, 0:2, :] += north_levels[slot][2 * at : 2 * at + 2, :]
                    total[part, layer, last, :] += south_levels[slot][at : at + 1, :]
            way = 1 if kind == "up" else -1
            blocks(from_levels[slot], way, 0)
            blocks(north_levels[slot], way, 1)
            blocks(south_levels[slot], way, -1)

        guarded(level_ref[0], receiver, take)
    for layer in range(depth):
        for axis in range(3):
            force_ref[axis, layer] = total[axis, layer]
    lane = lax.broadcasted_iota(jnp.int32, (height, 128), 1)
    for tile in range(base // height):
        value = jnp.zeros((height, 128), jnp.float32)
        for layer in range(8 * tile, min(8 * tile + 8, depth)):
            part = layer - 8 * tile
            value = jnp.where(lane // 16 == part, lane_roll(total[3, layer, :, 0:128], 16 * part), value)
        for target in (right_ref, left_ref):
            target[tile * height : tile * height + height, 0:128] = value


def last_body(levels, level_ref, part_ref, stay_ref, *rest):
    depth, height, width = part_ref.shape[1:]
    slots = len(rim_sizes(levels))
    north_ref, south_ref = rest[:2]
    from_levels, north_levels, south_levels = (rest[2 + slots * at : 2 + slots * at + slots] for at in range(3))
    right_ref, left_ref, force_ref, arrived_ref = rest[2 + 3 * slots :]
    blocks = stay_ref.shape[1]
    base = face_rows(depth, height)
    lane = lax.broadcasted_iota(jnp.int32, (height, 128), 1)
    for layer in range(depth):
        rows = slice(layer // 8 * height, layer // 8 * height + height)
        before, after = right_ref[rows, :128], left_ref[rows, :128]
        for axis in range(3):
            at = 16 * (layer % 8) + 4 * axis
            first = jnp.where(lane < 2, lane_roll(before, -at - 1), 0.0)
            final = jnp.where(lane == 127, lane_roll(after, 127 - at), 0.0)
            force_ref[axis, layer] = part_ref[axis, layer]
            force_ref[axis, layer, :, 0:128] += first
            force_ref[axis, layer, :, width - 128 : width] += final
    arrived_ref[:, 0:blocks, :] = stay_ref[...]

    def put(source, start, stride, way_z, way_y, way_x):
        code = group_at(way_z, way_y) * 3 + way_x + 1
        at = blocks + CAP * (code if code < 13 else code - 1)
        for slot in range(CAP):
            for axis in range(6):
                if source is None:
                    value = jnp.zeros((1, 128), jnp.float32)
                else:
                    value = source[start + stride * slot + axis : start + stride * slot + axis + 1, :]
                arrived_ref[axis, at + slot : at + slot + 1, :] = value

    for way_z in (-1, 0, 1):
        for way_y in (-1, 0, 1):
            for way_x, source in ((1, right_ref), (-1, left_ref)):
                put(source, base + 12 * group_at(way_z, way_y), 6, way_z, way_y, way_x)
    middle = 16

    def put_group(source, way_z, way_y):
        put(source, None if source is None else source.shape[0] - GROUP + middle, 8, way_z, way_y, 0)

    put_group(north_ref, 0, 1)
    put_group(south_ref, 0, -1)
    for kind, _, receiver, slot in force_sides(levels):
        way = 1 if kind == "up" else -1

        def take(way=way, slot=slot):
            put_group(from_levels[slot], way, 0)
            put_group(north_levels[slot], way, 1)
            put_group(south_levels[slot], way, -1)

        def clear(way=way):
            for way_y in (-1, 0, 1):
                put_group(None, way, way_y)

        guarded(level_ref[0], receiver, take)
        if receiver is not None:
            guarded(level_ref[0], 1 - receiver, clear)


def local(pops, coarse_pops, interface, drop_vel, drop_frac, home, counts, dest):
    levels = lax.axis_size("gz")
    depth, height, width = interface.shape
    blocks = home.shape[0]
    kinds = ["up", "down"][: len(rim_sizes(levels))]
    slots = len(kinds)
    size = (depth, height, width)
    rows = height + 8
    table = table_rows(depth, height)
    along, plane, ready = call(
        functools.partial(weigh_body, size),
        [(2 * width + 128, blocks * 128), (blocks // 2, table, 256), (8, 128)],
        [drop_frac, home],
        cost=long_cost(),
        kind=[jnp.bfloat16, jnp.float32, jnp.float32],
    )
    strip, left, right, inner_pops, inner_vel, faces = wide_exchange(pops, coarse_pops, interface, ready)
    sizes = [(count + GROUP, width) for count in message_rows(depth)]
    outs = call(
        functools.partial(main_body, size, levels),
        [(19, height, 128), (4, depth, height, width), (6, blocks, 128), (4, 8, 128), sizes[1], sizes[2]]
        + [sizes[0]] * slots
        + [sizes[3]] * slots
        + [sizes[4]] * slots,
        [counts, dest, strip, left, right, inner_vel, *faces, drop_vel, drop_frac, along, plane],
        [
            pltpu.VMEM((3 * table, width), jnp.float32),
            pltpu.VMEM((3 * table, 128), jnp.float32),
            pltpu.VMEM((3 * table, width), jnp.float32),
            pltpu.VMEM((3 * table, 128), jnp.float32),
            pltpu.VMEM((blocks, 8, 128), jnp.float32),
            pltpu.VMEM((27 * CAP + 1, 8, 128), jnp.float32),
            pltpu.VMEM((table, 128), jnp.float32),
            pltpu.VMEM((2, channels, rows, 128), jnp.float32),
            pltpu.VMEM((2, 19, rows, 128), jnp.float32),
            pltpu.VMEM((2, 19, rows, 128), jnp.float32),
            pltpu.VMEM((3 * table, 2 * width), jnp.bfloat16),
            pltpu.VMEM((3 * table, width + 128), jnp.bfloat16),
            pltpu.VMEM((3 * table, blocks * 128), jnp.bfloat16),
            pltpu.VMEM((3 * table, blocks * 128), jnp.bfloat16),
        ],
        late=(0, 1, *range(5, 10 + slots)),
    )
    edge, own, stay, side, north, south = outs[:6]
    to_levels, north_levels, south_levels = (outs[6 + slots * at : 6 + slots * at + slots] for at in range(3))
    received = [shifted(north, "gy", 1), shifted(south, "gy", -1)]
    received += [to_level(value, kind, levels) for value, kind in zip(to_levels, kinds)]
    received += [to_level(value, kind, levels, "gy", 1) for value, kind in zip(north_levels, kinds)]
    received += [to_level(value, kind, levels, "gy", -1) for value, kind in zip(south_levels, kinds)]
    (state,) = call(patch_body, [pops.shape], [inner_pops, edge], cost=long_cost())
    side_rows = (padded(face_rows(depth, height) + 9 * 6 * CAP), width)
    part, right, left = call(
        functools.partial(gather_body, levels),
        [(3, depth, height, width), side_rows, side_rows],
        [own, side] + received,
        [pltpu.VMEM((4, depth, height, width), jnp.float32)],
    )
    force, arrived = call(
        functools.partial(last_body, levels),
        [(3, depth, height, width), (6, blocks + 26 * CAP, 128)],
        [part, stay] + received + [shifted(right, "gx", 1), shifted(left, "gx", -1)],
    )
    return state, force, arrived


def solution(mesh):
    return jax.shard_map(
        local,
        mesh=mesh,
        in_specs=(
            P(None, "gz", "gy", "gx"),
            P(None, "gz", "gy", "gx"),
            P("gz", "gy", "gx"),
            P(None, ("gx", "gy", "gz"), None),
            P(None, ("gx", "gy", "gz"), None),
            P(("gx", "gy", "gz"), None),
            P(("gx", "gy", "gz")),
            P(("gx", "gy", "gz")),
        ),
        out_specs=(
            P(None, "gz", "gy", "gx"),
            P(None, "gz", "gy", "gx"),
            P(None, ("gx", "gy", "gz"), None),
        ),
        check_vma=False,
    )
```
